32 devices in a mesh: groups: 2 (over y), graph: 4 (over x, core), mp: 4 (over z).
Axes of the slice: x: 2, y: 2, z: 4, core: 2. Of those that a mesh axis runs over, the one named last changes fastest.
Arguments:
- grid_lat: bfloat16 [16384, 512], P(('groups', 'graph', 'mp')), parts along dimension 0, may hold values from -6 to 6
- mesh_lat: bfloat16 [8192, 512], P(('groups', 'graph', 'mp')), parts along dimension 0, may hold values from -6 to 6
- cotangent: bfloat16 [8192, 512], P(('groups', 'graph', 'mp')), parts along dimension 0, may hold values from -6 to 6
- grid_send: int32 [512, 4], P(('groups', 'graph', 'mp')), parts along dimension 0, may hold values from 0 to 511
- g2m_slot: int32 [16384], P(('groups', 'graph', 'mp')), parts along dimension 0, may hold values from 0 to 63, as said below
- g2m_receiver: int32 [16384], P(('groups', 'graph', 'mp')), parts along dimension 0, may hold values from 0 to 255, as said below
- halo_send: int32 [512, 2], P(('groups', 'graph', 'mp')), parts along dimension 0, may hold values from 0 to 255
- mesh_sender: int32 [16384], P(('groups', 'graph', 'mp')), parts along dimension 0, may hold values from 0 to 287
- mesh_receiver: int32 [16384], P(('groups', 'graph', 'mp')), parts along dimension 0, may hold values from 0 to 255, as said below
- enc_edge_in: bfloat16 [1024, 512], P(None, 'mp'), may hold values from -0.1875 to 0.1875
- enc_edge_out: bfloat16 [512, 512], P('mp'), may hold values from -0.25 to 0.25
- enc_node_in: bfloat16 [1024, 512], P(None, 'mp'), may hold values from -0.1875 to 0.1875
- enc_node_out: bfloat16 [512, 512], P('mp'), may hold values from -0.25 to 0.25
- proc_edge_in: bfloat16 [1024, 512], P(None, 'mp'), may hold values from -0.1875 to 0.1875
- proc_edge_out: bfloat16 [512, 512], P('mp'), may hold values from -0.25 to 0.25
- proc_node_in: bfloat16 [1024, 512], P(None, 'mp'), may hold values from -0.1875 to 0.1875
- proc_node_out: bfloat16 [512, 512], P('mp'), may hold values from -0.25 to 0.25
Outputs:
- mesh_two: bfloat16 [8192, 512], P(('groups', 'graph', 'mp')), parts along dimension 0
- grid_grad: float32 [16384, 512], P(('groups', 'graph', 'mp')), parts along dimension 0
- mesh_grad: float32 [8192, 512], P(('groups', 'graph', 'mp')), parts along dimension 0
The draws below stay inside these ranges and needn't reach their ends.
There are 2 independent parts, one for each index of `groups`. The reference program is written for one: setup_inputs(seed, part) draws one part's arguments, and reference() takes and returns one part's arrays. A program takes and returns all parts, laid end to end along the dimension named above; an argument that names none is the same for every part. Nothing has to cross between parts.
Inputs may be any that keep to these rules, and one draw needn't show every extreme that they name: `g2m_slot`: an edge names only slots of a pair that hold a grid row its receiver's partition needs; slots of a pair that no edge names still hold valid rows. `g2m_receiver`: every mesh node of a device receives at least one grid-to-mesh edge. `mesh_receiver`: every mesh node of a device receives at least one mesh edge.
All inputs are finite; a program needn't handle non-finite values.
Results may differ from the reference program's by a relative error of at most 0.017.
Values may be sent and summed in bfloat16 or wider, within the bound.
No kernel may reach another device: no remote copies, remote signals or barrier semaphores. Data moves between devices by JAX's collectives and lax.ppermute only.
A program may use at most 64 MiB of HBM per device.

```python
import jax
import jax.numpy as jnp
from jax import lax

D = 512
G_DEV = 512
M_DEV = 256
E_DEV = 512
ME_DEV = 512
CAP = 4
HCAP = 2
PEERS = 16
GRID = 8192
MESH = 4096


def pair_counts(key):
    count_key, column_key = jax.random.split(key)
    counts = jax.random.randint(count_key, (PEERS, PEERS), 1, CAP + 1)
    column = jax.random.randint(column_key, (), 0, PEERS)
    full_column = jnp.arange(PEERS)[None, :] == column
    return (jnp.where(full_column, CAP, counts).astype(jnp.int32), column.astype(jnp.int32))


def shuffle_row(row_key, values):
    return jax.random.permutation(row_key, values)


def cover_rows(key, length, targets):
    fill_key, shuffle_key = jax.random.split(key)
    extra = jax.random.randint(fill_key, (PEERS, length - targets), 0, targets).astype(jnp.int32)
    base = jnp.broadcast_to(jnp.arange(targets, dtype=jnp.int32), (PEERS, targets))
    rows = jnp.concatenate([base, extra], axis=1)
    row_keys = jax.random.split(shuffle_key, PEERS)
    return jax.vmap(shuffle_row)(row_keys, rows).reshape(-1).astype(jnp.int32)


def draw_grid_send(key, part):
    key = jax.random.fold_in(key, 1)
    table = jax.random.randint(key, (PEERS * PEERS, CAP), 0, G_DEV).astype(jnp.int32)
    return table.at[0, 0].set(G_DEV - 1).at[0, 1].set(0)


def draw_g2m_slot(key, part):
    counts, full_owner = pair_counts(key)
    key = jax.random.fold_in(key, 2)
    source_key, column_key = jax.random.split(key)
    source = jax.random.randint(source_key, (PEERS, E_DEV), 0, PEERS).astype(jnp.int32)
    source = source.at[full_owner, 0].set(PEERS - 1).at[full_owner, 1].set(0)
    raw = jax.random.randint(column_key, (PEERS, E_DEV), 0, 1 << 20).astype(jnp.int32)
    owners = jnp.arange(PEERS, dtype=jnp.int32)[:, None]
    column = (raw % counts[source, owners]).astype(jnp.int32)
    column = column.at[full_owner, 0].set(CAP - 1).at[full_owner, 1].set(0)
    return (source * CAP + column).reshape(-1).astype(jnp.int32)


def draw_g2m_receiver(key, part):
    key = jax.random.fold_in(key, 3)
    return cover_rows(key, E_DEV, M_DEV)


def draw_halo_send(key, part):
    key = jax.random.fold_in(key, 4)
    table = jax.random.randint(key, (PEERS * PEERS, HCAP), 0, M_DEV).astype(jnp.int32)
    return table.at[0, 0].set(M_DEV - 1).at[1, 0].set(0)


def draw_mesh_sender(key, part):
    key = jax.random.fold_in(key, 5)
    coin_key, local_key, halo_key = jax.random.split(key, 3)
    coin = jax.random.randint(coin_key, (PEERS * ME_DEV,), 0, 2)
    local_rows = jax.random.randint(local_key, (PEERS * ME_DEV,), 0, M_DEV)
    halo_rows = M_DEV + jax.random.randint(halo_key, (PEERS * ME_DEV,), 0, PEERS * HCAP)
    sender = jnp.where(coin == 0, local_rows, halo_rows).astype(jnp.int32)
    return sender.at[0].set(M_DEV + PEERS * HCAP - 1).at[1].set(0)


def draw_mesh_receiver(key, part):
    key = jax.random.fold_in(key, 6)
    return cover_rows(key, ME_DEV, M_DEV)


def shard_levels(rng, shape, cuts, least, largest):
    def one(axis_at, shards_of):
        steps = jax.random.uniform(jax.random.fold_in(jax.random.fold_in(rng, 6), axis_at), (shards_of,), jnp.float32, least / len(cuts), largest / len(cuts))
        return jnp.repeat(jnp.exp(steps), shape[axis_at] // shards_of).reshape((-1,) + (1,) * (len(shape) - axis_at - 1))

    level = one(*cuts[0])
    for cut in cuts[1:]:
        level = level * one(*cut)
    return level


def normal_values(own_key, extent, width, reach, cuts=(), kind=jnp.bfloat16):
    values = jax.random.normal(own_key, extent, jnp.float32) * width
    if len(cuts) > 0:
        values = shard_levels(own_key, extent, cuts, -0.22, 0.18) * values
    return jnp.clip(values, min=-reach, max=reach).astype(kind)


def setup_inputs(seed: int = 0, part: int = 0) -> dict:
    streams_of = jax.random.split(jax.random.key(seed), 18)
    part_splits = jax.random.split(jax.random.fold_in(streams_of[17], part), 18)
    return {
        "grid_lat": normal_values(part_splits[0], (GRID, D), 1.0, 6.0, ((0, 16),)),
        "mesh_lat": normal_values(part_splits[1], (MESH, D), 1.0, 6.0, ((0, 16),)),
        "cotangent": normal_values(part_splits[2], (MESH, D), 1.0, 6.0, ((0, 16),)),
        "grid_send": draw_grid_send(jax.random.fold_in(jax.random.fold_in(streams_of[17], part), 71), part),
        "g2m_slot": draw_g2m_slot(jax.random.fold_in(jax.random.fold_in(streams_of[17], part), 71), part),
        "g2m_receiver": draw_g2m_receiver(jax.random.fold_in(jax.random.fold_in(streams_of[17], part), 71), part),
        "halo_send": draw_halo_send(jax.random.fold_in(jax.random.fold_in(streams_of[17], part), 71), part),
        "mesh_sender": draw_mesh_sender(jax.random.fold_in(jax.random.fold_in(streams_of[17], part), 71), part),
        "mesh_receiver": draw_mesh_receiver(jax.random.fold_in(jax.random.fold_in(streams_of[17], part), 71), part),
        "enc_edge_in": normal_values(streams_of[9], (2 * D, D), (2 * D) ** -0.5, 0.1875, ((1, 4),)),
        "enc_edge_out": normal_values(streams_of[10], (D, D), D ** -0.5, 0.25, ((0, 4),)),
        "enc_node_in": normal_values(streams_of[11], (2 * D, D), (2 * D) ** -0.5, 0.1875, ((1, 4),)),
        "enc_node_out": normal_values(streams_of[12], (D, D), D ** -0.5, 0.25, ((0, 4),)),
        "proc_edge_in": normal_values(streams_of[13], (2 * D, D), (2 * D) ** -0.5, 0.1875, ((1, 4),)),
        "proc_edge_out": normal_values(streams_of[14], (D, D), D ** -0.5, 0.25, ((0, 4),)),
        "proc_node_in": normal_values(streams_of[15], (2 * D, D), (2 * D) ** -0.5, 0.1875, ((1, 4),)),
        "proc_node_out": normal_values(streams_of[16], (D, D), D ** -0.5, 0.25, ((0, 4),)),
    }


def dense_trans(left, right):
    return lax.dot_general(left, right, (((1,), (1,)), ((), ())), preferred_element_type=jnp.float32)

def mlp_forward(inputs, w_first, w_second):
    before = jnp.dot(inputs, w_first, preferred_element_type=jnp.float32)
    hidden = jax.nn.silu(before).astype(jnp.bfloat16)
    summed = jnp.dot(hidden, w_second, preferred_element_type=jnp.float32)
    average = lax.optimization_barrier(jnp.mean(summed, axis=-1, keepdims=True))
    centered = summed - average
    rescale = lax.rsqrt(lax.optimization_barrier(jnp.mean(centered * centered, axis=-1, keepdims=True)) + 1e-05)
    normed = centered * rescale
    return (normed, (before, normed, rescale))

def mlp_backward(incoming, saved, w_first, w_second):
    before, normed, rescale = saved
    g_out = (incoming - lax.optimization_barrier(jnp.mean(incoming, axis=-1, keepdims=True)) - normed * lax.optimization_barrier(jnp.mean(incoming * normed, axis=-1, keepdims=True))) * rescale
    g_hidden = dense_trans(g_out.astype(jnp.bfloat16), w_second)
    logistic = jax.nn.sigmoid(before)
    g_before = (g_hidden * logistic * (1.0 + before * (1.0 - logistic))).astype(jnp.bfloat16)
    return dense_trans(g_before, w_first)

def reference(grid_lat, mesh_lat, cotangent, grid_send, g2m_slot, g2m_receiver, halo_send, mesh_sender, mesh_receiver, enc_edge_in, enc_edge_out, enc_node_in, enc_node_out, proc_edge_in, proc_edge_out, proc_node_in, proc_node_out):
    owners = jnp.arange(PEERS, dtype=jnp.int32)[:, None]
    send_table = grid_send.reshape(PEERS, PEERS, CAP)
    edge_slot = g2m_slot.reshape(PEERS, E_DEV)
    source = edge_slot // CAP
    grid_index = (source * G_DEV + send_table[source, owners, edge_slot % CAP]).reshape(-1)
    enc_target = (owners * M_DEV + g2m_receiver.reshape(PEERS, E_DEV)).reshape(-1)
    halo_table = halo_send.reshape(PEERS, PEERS, HCAP)
    sender = mesh_sender.reshape(PEERS, ME_DEV)
    halo_slot = jnp.maximum(sender - M_DEV, 0)
    halo_owner = halo_slot // HCAP
    remote = halo_owner * M_DEV + halo_table[halo_owner, owners, halo_slot % HCAP]
    proc_source = jnp.where(sender < M_DEV, owners * M_DEV + sender, remote).reshape(-1)
    proc_target = (owners * M_DEV + mesh_receiver.reshape(PEERS, ME_DEV)).reshape(-1)
    mesh_total = PEERS * M_DEV
    grid_total = PEERS * G_DEV
    features = mesh_lat.shape[1]
    edge_in = jnp.concatenate([grid_lat[grid_index], mesh_lat[enc_target]], axis=1)
    normed_e, saved_e = mlp_forward(edge_in, enc_edge_in, enc_edge_out)
    edge_latent = normed_e.astype(jnp.bfloat16)
    aggregate = jax.ops.segment_sum(edge_latent.astype(jnp.float32), enc_target, num_segments=mesh_total).astype(jnp.bfloat16)
    node_in = jnp.concatenate([mesh_lat, aggregate], axis=1)
    normed_n, saved_n = mlp_forward(node_in, enc_node_in, enc_node_out)
    mesh_one = (mesh_lat.astype(jnp.float32) + normed_n).astype(jnp.bfloat16)
    proc_in = jnp.concatenate([mesh_one[proc_source], mesh_one[proc_target]], axis=1)
    normed_p, saved_p = mlp_forward(proc_in, proc_edge_in, proc_edge_out)
    message = normed_p.astype(jnp.bfloat16)
    aggregate_two = jax.ops.segment_sum(message.astype(jnp.float32), proc_target, num_segments=mesh_total).astype(jnp.bfloat16)
    node_two = jnp.concatenate([mesh_one, aggregate_two], axis=1)
    normed_q, saved_q = mlp_forward(node_two, proc_node_in, proc_node_out)
    mesh_two = (mesh_one.astype(jnp.float32) + normed_q).astype(jnp.bfloat16)
    grad_two = cotangent.astype(jnp.float32)
    g_q = mlp_backward(grad_two, saved_q, proc_node_in, proc_node_out)
    grad_one = grad_two + g_q[:, :features]
    grad_msg = g_q[:, features:][proc_target]
    g_p = mlp_backward(grad_msg, saved_p, proc_edge_in, proc_edge_out)
    grad_one = grad_one + jax.ops.segment_sum(g_p[:, features:], proc_target, num_segments=mesh_total)
    grad_one = grad_one + jax.ops.segment_sum(g_p[:, :features], proc_source, num_segments=mesh_total)
    g_n = mlp_backward(grad_one, saved_n, enc_node_in, enc_node_out)
    mesh_grad = grad_one + g_n[:, :features]
    grad_edge = g_n[:, features:][enc_target]
    g_e = mlp_backward(grad_edge, saved_e, enc_edge_in, enc_edge_out)
    mesh_grad = mesh_grad + jax.ops.segment_sum(g_e[:, features:], enc_target, num_segments=mesh_total)
    grid_grad = jax.ops.segment_sum(g_e[:, :features], grid_index, num_segments=grid_total)
    return (mesh_two, grid_grad, mesh_grad)
```

```python
import functools

import jax
import jax.numpy as jnp
from jax import lax
from jax.experimental import pallas as pl
from jax.experimental.pallas import tpu as pltpu
from jax.sharding import PartitionSpec as P

F32 = jnp.float32
BF16 = jnp.bfloat16
LANES = 128
ROWS = 256
AXES = ("groups", "graph", "mp")
PEERS = ("graph", "mp")


def dot(left, right):
    return jnp.dot(left, right, preferred_element_type=F32)


def dot_trans(left, right):
    return lax.dot_general(left, right, (((1,), (1,)), ((), ())), preferred_element_type=F32)


def call(kernel, out_shape, *args):
    flops = 0
    return pl.pallas_call(
        kernel,
        out_shape=out_shape,
        in_specs=[pl.BlockSpec(memory_space=pltpu.VMEM)] * len(args),
        out_specs=[pl.BlockSpec(memory_space=pltpu.VMEM)] * len(out_shape),
        compiler_params=pltpu.CompilerParams(vmem_limit_bytes=40 * 1024 * 1024),
    )(*args)


def shape(rows, columns, dtype):
    return jax.ShapeDtypeStruct((rows, columns), dtype)


def weight_pair(ref, which, features):
    columns = features // LANES
    blocks = 2 * columns
    low = which * 192
    first = [
        jnp.concatenate([ref[p * columns + m, low : low + 128, :] for p in range(blocks)], axis=0)
        for m in range(columns)
    ]
    second = []
    for q in range(columns):
        parts = []
        for m in range(columns):
            for half in range(2):
                parts.append(ref[(half * columns + q) * columns + m, low + 128 : low + 192, :])
        second.append(jnp.concatenate(parts, axis=0))
    return jnp.concatenate(first, axis=1), jnp.concatenate(second, axis=1)


def pack_kernel(*refs):
    shards, (enc, proc), sem = refs[:8], refs[8:10], refs[10]
    plane = lax.axis_index("groups") * lax.axis_size("graph") + lax.axis_index("graph")
    half, quarter = plane // 4, plane % 4
    copies = []
    for i in range(4):
        out, low = (enc, proc)[i // 2], (i % 2) * 192
        row = pl.multiple_of(plane * 128, 128)
        copies.append(
            pltpu.make_async_copy(
                shards[2 * i].at[pl.ds(row, 128), :], out.at[pl.ds(low, 128), :], sem.at[2 * i]
            )
        )
        copies.append(
            pltpu.make_async_copy(
                shards[2 * i + 1].at[
                    pl.ds(pl.multiple_of(half * 64, 64), 64),
                    pl.ds(pl.multiple_of(quarter * 128, 128), 128),
                ],
                out.at[pl.ds(low + 128, 64), :],
                sem.at[2 * i + 1],
            )
        )
    for copy in copies:
        copy.start()
    for copy in copies:
        copy.wait()


def pack_whole(first, second):
    features = second.shape[1]
    columns = features // LANES
    blocks = 2 * columns
    one = first.reshape(blocks, 128, columns, 128).transpose(0, 2, 1, 3)
    two = second.reshape(columns, 2, 64, columns, 128).transpose(1, 3, 0, 2, 4)
    return jnp.concatenate(
        [one.reshape(blocks * columns, 128, 128), two.reshape(blocks * columns, 64, 128)], axis=1
    )


def gather_weights(shards):
    features = shards[1].shape[1]
    planes = lax.axis_size("groups") * lax.axis_size("graph")
    if features == 512 and planes == 8 and lax.axis_size("mp") == 4:
        enc, proc = pl.pallas_call(
            pack_kernel,
            out_shape=[shape(384, 128, BF16)] * 2,
            in_specs=[pl.BlockSpec(memory_space=pl.ANY)] * 8,
            out_specs=[pl.BlockSpec(memory_space=pl.ANY)] * 2,
            scratch_shapes=[pltpu.SemaphoreType.DMA((8,))],
            name="pack",
        )(*shards)
        return lax.all_gather(enc, AXES), lax.all_gather(proc, AXES)
    whole = [lax.all_gather(w, "mp", axis=1 - i % 2, tiled=True) for i, w in enumerate(shards)]
    packed = [pack_whole(whole[2 * i], whole[2 * i + 1]) for i in range(4)]
    return jnp.concatenate(packed[:2], axis=1), jnp.concatenate(packed[2:], axis=1)


def forward(inputs, first, second):
    before = dot(inputs, first)
    logistic = jax.nn.sigmoid(before)
    hidden = (before * logistic).astype(BF16)
    slope = logistic * (1.0 + before * (1.0 - logistic))
    summed = dot(hidden, second)
    centered = summed - jnp.mean(summed, axis=-1, keepdims=True)
    rescale = lax.rsqrt(jnp.mean(centered * centered, axis=-1, keepdims=True) + 1e-05)
    normed = centered * rescale
    return normed, slope.astype(BF16), normed.astype(BF16), rescale


def backward_hidden(incoming, slope, normed, rescale, second):
    normed = normed.astype(F32)
    g_out = (
        incoming
        - jnp.mean(incoming, axis=-1, keepdims=True)
        - normed * jnp.mean(incoming * normed, axis=-1, keepdims=True)
    ) * rescale
    return (dot_trans(g_out.astype(BF16), second) * slope.astype(F32)).astype(BF16)


def table(index_row, count):
    n = index_row.shape[1]
    return jnp.where(lax.broadcasted_iota(jnp.int32, (count, n), 0) == index_row, 1.0, 0.0)


def send_kernel(grid_ref, send_ref, outgoing_ref, table_ref):
    one = table(send_ref[...], grid_ref.shape[0])
    table_ref[...] = one.astype(BF16)
    outgoing_ref[...] = dot(one.T.astype(BF16), grid_ref[...]).astype(BF16)


def tables_kernel(
    mesh_ref,
    slot_ref,
    recv_e_ref,
    halo_ref,
    sender_ref,
    recv_p_ref,
    slot_t,
    slot_g,
    enc_t,
    enc_g,
    halo_t,
    halo_g,
    sender_t,
    sender_g,
    proc_t,
    proc_g,
    recv_rows,
):
    for index, scatter, gather in (
        (slot_ref, slot_t, slot_g),
        (recv_e_ref, enc_t, enc_g),
        (halo_ref, halo_t, halo_g),
        (sender_ref, sender_t, sender_g),
        (recv_p_ref, proc_t, proc_g),
    ):
        one = table(index[...], scatter.shape[0])
        scatter[...] = one.astype(BF16)
        gather[...] = one.T.astype(BF16)
    recv_rows[...] = dot(enc_g[...], mesh_ref[...]).astype(BF16)


def encode_kernel(
    mesh_ref,
    arrived_ref,
    slot_g,
    recv_rows,
    enc_t,
    halo_g,
    weights,
    one_ref,
    halo_ref,
    slope_e,
    normed_e,
    scale_e,
    slope_n,
    normed_n,
    scale_n,
):
    features = mesh_ref.shape[1]
    first, second = weight_pair(weights, 0, features)
    edges = slot_g.shape[0]
    for low in range(0, edges, ROWS):
        rows = pl.ds(low, ROWS)
        sent = dot(slot_g[rows, :], arrived_ref[...]).astype(BF16)
        inputs = jnp.concatenate([sent, recv_rows[rows, :]], axis=1)
        _, slope, normed, rescale = forward(inputs, first, second)
        slope_e[rows, :] = slope
        normed_e[rows, :] = normed
        scale_e[rows, :] = jnp.broadcast_to(rescale, (ROWS, LANES))
    aggregate = dot(enc_t[...], normed_e[...]).astype(BF16)
    first, second = weight_pair(weights, 1, features)
    mesh = mesh_ref[...]
    normed, slope, rounded, rescale = forward(
        jnp.concatenate([mesh, aggregate], axis=1), first, second
    )
    slope_n[...] = slope
    normed_n[...] = rounded
    scale_n[...] = jnp.broadcast_to(rescale, scale_n.shape)
    one_ref[...] = (mesh.astype(F32) + normed).astype(BF16)
    halo_ref[...] = dot(halo_g[...], one_ref[...]).astype(BF16)


def process_kernel(
    one_ref,
    halo_ref,
    cotangent_ref,
    sender_t,
    sender_g,
    proc_t,
    proc_g,
    weights,
    two_ref,
    grad_one_ref,
    grad_halo_ref,
    slope_p,
    normed_p,
    scale_p,
    ga_p,
):
    features = one_ref.shape[1]
    mesh_rows = one_ref.shape[0]
    edges = sender_g.shape[0]
    first, second = weight_pair(weights, 0, features)
    lookup = jnp.concatenate([one_ref[...], halo_ref[...]], axis=0)
    for low in range(0, edges, ROWS):
        rows = pl.ds(low, ROWS)
        sent = dot(sender_g[rows, :], lookup).astype(BF16)
        got = dot(proc_g[rows, :], one_ref[...]).astype(BF16)
        _, slope, normed, rescale = forward(jnp.concatenate([sent, got], axis=1), first, second)
        slope_p[rows, :] = slope
        normed_p[rows, :] = normed
        scale_p[rows, :] = jnp.broadcast_to(rescale, (ROWS, LANES))
    aggregate = dot(proc_t[...], normed_p[...]).astype(BF16)
    first_n, second_n = weight_pair(weights, 1, features)
    one = one_ref[...]
    normed, slope, rounded, rescale = forward(
        jnp.concatenate([one, aggregate], axis=1), first_n, second_n
    )
    two_ref[...] = (one.astype(F32) + normed).astype(BF16)
    cotangent = cotangent_ref[...].astype(F32)
    ga = backward_hidden(cotangent, slope, rounded, rescale, second_n)
    g_q = dot_trans(ga, first_n)
    g_msg = g_q[:, features:].astype(BF16)
    for low in range(0, edges, ROWS):
        rows = pl.ds(low, ROWS)
        incoming = dot(proc_g[rows, :], g_msg)
        ga_p[rows, :] = backward_hidden(
            incoming, slope_p[rows, :], normed_p[rows, :], scale_p[rows, 0:1], second
        )
    by_recv = dot(proc_t[...], ga_p[...]).astype(BF16)
    by_send = dot(sender_t[...], ga_p[...]).astype(BF16)
    g_send = dot_trans(by_send, first[:features, :])
    g_recv = dot_trans(by_recv, first[features:, :])
    grad_one_ref[...] = cotangent + g_q[:, :features] + g_recv + g_send[:mesh_rows, :]
    grad_halo_ref[...] = g_send[mesh_rows:, :].astype(BF16)


def decode_kernel(
    grad_one_ref,
    back_ref,
    halo_t,
    slope_e,
    normed_e,
    scale_e,
    slope_n,
    normed_n,
    scale_n,
    enc_t,
    enc_g,
    slot_t,
    weights,
    mesh_grad_ref,
    grad_slots_ref,
    ga_e,
):
    features = grad_one_ref.shape[1]
    edges = enc_g.shape[0]
    grad_one = grad_one_ref[...] + dot(halo_t[...], back_ref[...])
    first_n, second_n = weight_pair(weights, 1, features)
    ga = backward_hidden(grad_one, slope_n[...], normed_n[...], scale_n[:, 0:1], second_n)
    g_n = dot_trans(ga, first_n)
    g_edge = g_n[:, features:].astype(BF16)
    first, second = weight_pair(weights, 0, features)
    for low in range(0, edges, ROWS):
        rows = pl.ds(low, ROWS)
        incoming = dot(enc_g[rows, :], g_edge)
        ga_e[rows, :] = backward_hidden(
            incoming, slope_e[rows, :], normed_e[rows, :], scale_e[rows, 0:1], second
        )
    by_recv = dot(enc_t[...], ga_e[...]).astype(BF16)
    by_slot = dot(slot_t[...], ga_e[...]).astype(BF16)
    mesh_grad_ref[...] = grad_one + g_n[:, :features] + dot_trans(by_recv, first[features:, :])
    grad_slots_ref[...] = dot_trans(by_slot, first[:features, :]).astype(BF16)


def grid_kernel(table_ref, back_ref, out_ref):
    out_ref[...] = dot(table_ref[...], back_ref[...])


def exchange(rows, capacity):
    features = rows.shape[1]
    parts = rows.reshape(-1, capacity, features)
    return lax.all_to_all(parts, PEERS, split_axis=0, concat_axis=0, tiled=True).reshape(rows.shape)


def local(
    grid_lat,
    mesh_lat,
    cotangent,
    grid_send,
    g2m_slot,
    g2m_receiver,
    halo_send,
    mesh_sender,
    mesh_receiver,
    *shards,
):
    grid_rows, features = grid_lat.shape
    mesh_rows = mesh_lat.shape[0]
    edges = g2m_slot.shape[0]
    mesh_edges = mesh_sender.shape[0]
    slots, halos = grid_send.size, halo_send.size
    capacity, halo_capacity = grid_send.shape[1], halo_send.shape[1]
    enc_weights, proc_weights = gather_weights(shards)

    outgoing, grid_t = call(
        send_kernel,
        [shape(slots, features, BF16), shape(grid_rows, slots, BF16)],
        grid_lat,
        grid_send.reshape(1, slots),
    )
    arrived = exchange(outgoing, capacity)
    slot_t, slot_g, enc_t, enc_g, halo_t, halo_g, sender_t, sender_g, proc_t, proc_g, recv_rows = call(
        tables_kernel,
        [
            shape(slots, edges, BF16),
            shape(edges, slots, BF16),
            shape(mesh_rows, edges, BF16),
            shape(edges, mesh_rows, BF16),
            shape(mesh_rows, halos, BF16),
            shape(halos, mesh_rows, BF16),
            shape(mesh_rows + halos, mesh_edges, BF16),
            shape(mesh_edges, mesh_rows + halos, BF16),
            shape(mesh_rows, mesh_edges, BF16),
            shape(mesh_edges, mesh_rows, BF16),
            shape(edges, features, BF16),
        ],
        mesh_lat,
        g2m_slot.reshape(1, edges),
        g2m_receiver.reshape(1, edges),
        halo_send.reshape(1, halos),
        mesh_sender.reshape(1, mesh_edges),
        mesh_receiver.reshape(1, mesh_edges),
    )
    saved = [
        shape(edges, features, BF16),
        shape(edges, features, BF16),
        shape(edges, LANES, F32),
        shape(mesh_rows, features, BF16),
        shape(mesh_rows, features, BF16),
        shape(mesh_rows, LANES, F32),
    ]
    mesh_one, halo_out, *kept = call(
        encode_kernel,
        [shape(mesh_rows, features, BF16), shape(halos, features, BF16)] + saved,
        mesh_lat,
        arrived,
        slot_g,
        recv_rows,
        enc_t,
        halo_g,
        enc_weights,
    )
    halo_in = exchange(halo_out, halo_capacity)
    mesh_two, grad_one, grad_halo = pl.pallas_call(
        process_kernel,
        out_shape=[
            shape(mesh_rows, features, BF16),
            shape(mesh_rows, features, F32),
            shape(halos, features, BF16),
        ],
        in_specs=[pl.BlockSpec(memory_space=pltpu.VMEM)] * 8,
        out_specs=[pl.BlockSpec(memory_space=pltpu.VMEM)] * 3,
        scratch_shapes=[
            pltpu.VMEM((mesh_edges, features), BF16),
            pltpu.VMEM((mesh_edges, features), BF16),
            pltpu.VMEM((mesh_edges, LANES), F32),
            pltpu.VMEM((mesh_edges, features), BF16),
        ],
        compiler_params=pltpu.CompilerParams(vmem_limit_bytes=40 * 1024 * 1024),
    )(mesh_one, halo_in, cotangent, sender_t, sender_g, proc_t, proc_g, proc_weights)
    halo_back = exchange(grad_halo, halo_capacity)
    mesh_grad, grad_slots = pl.pallas_call(
        decode_kernel,
        out_shape=[shape(mesh_rows, features, F32), shape(slots, features, BF16)],
        in_specs=[pl.BlockSpec(memory_space=pltpu.VMEM)] * 13,
        out_specs=[pl.BlockSpec(memory_space=pltpu.VMEM)] * 2,
        scratch_shapes=[pltpu.VMEM((edges, features), BF16)],
        compiler_params=pltpu.CompilerParams(vmem_limit_bytes=40 * 1024 * 1024),
    )(grad_one, halo_back, halo_t, *kept, enc_t, enc_g, slot_t, enc_weights)
    returned = exchange(grad_slots, capacity)
    (grid_grad,) = call(grid_kernel, [shape(grid_rows, features, F32)], grid_t, returned)
    return (mesh_two, grid_grad, mesh_grad)


def solution(mesh):
    rows = P(AXES, None)
    flat = P(AXES)
    in_specs = (rows,) * 4 + (flat,) * 2 + (rows,) + (flat,) * 2 + (P(None, "mp"), P("mp", None)) * 4
    return jax.shard_map(
        local, mesh=mesh, in_specs=in_specs, out_specs=(rows,) * 3, check_vma=False
    )
```

```python
import functools

import jax
import jax.numpy as jnp
from jax import lax
from jax.experimental import pallas as pl
from jax.experimental.pallas import tpu as pltpu
from jax.sharding import PartitionSpec as P

F32 = jnp.float32
BF16 = jnp.bfloat16
LANES = 128
ROWS = 256
FEATURES = 512
AXES = ("groups", "graph", "mp")
PEERS = ("graph", "mp")


def dot(left, right):
    return jnp.dot(left, right, preferred_element_type=F32)


def dot_trans(left, right):
    return lax.dot_general(left, right, (((1,), (1,)), ((), ())), preferred_element_type=F32)


def call(kernel, out_shape, *args, weights=None, scratch=()):
    scratch = list(scratch)
    in_specs = [pl.BlockSpec(a.shape, functools.partial(origin, a.ndim)) for a in args]
    extra = []
    if weights is not None:
        place, sets = weights
        sizes = [len(arrays) for arrays in sets]
        extra = [a for arrays in sets for a in arrays]
        for arrays in sets:
            in_specs += [pl.BlockSpec(memory_space=pltpu.HBM)] * 2
            in_specs += [pl.BlockSpec(memory_space=pl.ANY)] * (len(arrays) - 2)
        for arrays in sets:
            scratch.append(pltpu.VMEM((2 * FEATURES, FEATURES), BF16))
            scratch.append(pltpu.VMEM((FEATURES, FEATURES), BF16))
        scratch.append(pltpu.SemaphoreType.DMA((len(sets), 2)))

    def body(*refs):
        if weights is None:
            return kernel(*refs)
        ins, refs = refs[: len(args)], refs[len(args) :]
        sources, refs = refs[: len(extra)], refs[len(extra) :]
        outs, refs = refs[: len(out_shape)], refs[len(out_shape) :]
        own, refs = refs[: len(scratch) - 2 * len(sets) - 1], refs[len(scratch) - 2 * len(sets) - 1 :]
        sem = refs[-1]
        held, low = [], 0
        for i, size in enumerate(sizes):
            one = (sources[low : low + size], refs[2 * i], refs[2 * i + 1], sem.at[i])
            low += size
            place(*one)
            held.append(one)
        kernel(held, *ins, *outs, *own)

    return pl.pallas_call(
        body,
        grid=(1,),
        out_shape=out_shape,
        in_specs=in_specs,
        out_specs=[pl.BlockSpec(s.shape, functools.partial(origin, len(s.shape))) for s in out_shape],
        scratch_shapes=scratch,
        name=kernel.__name__,
        compiler_params=pltpu.CompilerParams(vmem_limit_bytes=40 * 1024 * 1024),
    )(*args, *extra)


def origin(rank, step):
    return (0,) * rank


def taken(one):
    wait_weights(*one)
    return one[1][...], one[2][...]


def shape(rows, columns, dtype):
    return jax.ShapeDtypeStruct((rows, columns), dtype)


def pack_kernel(*refs):
    shards, outs, sem = refs[:8], refs[8:12], refs[12]
    plane = lax.axis_index("groups") * lax.axis_size("graph") + lax.axis_index("graph")
    copies = []
    for i, out in enumerate(outs):
        row = pl.multiple_of(plane * 128, 128)
        low = pl.multiple_of(plane // 4 * 64, 64)
        column = pl.multiple_of(plane % 4 * 128, 128)
        copies.append(
            pltpu.make_async_copy(
                shards[2 * i].at[pl.ds(row, 128), :], out.at[pl.ds(0, 128), :], sem.at[2 * i]
            )
        )
        copies.append(
            pltpu.make_async_copy(
                shards[2 * i + 1].at[pl.ds(low, 64), pl.ds(column, 128)],
                out.at[pl.ds(128, 64), :],
                sem.at[2 * i + 1],
            )
        )
    for copy in copies:
        copy.start()
    for copy in copies:
        copy.wait()


def place_pieces(refs, first, second, sem):
    (own_first, own_second), pieces = refs[:2], refs[2:]
    sem, sem_second = sem.at[0], sem.at[1]
    me = lax.axis_index("mp")
    plane = lax.axis_index("groups") * lax.axis_size("graph") + lax.axis_index("graph")
    column = pl.multiple_of(me * 128, 128)
    copies = [
        pltpu.make_async_copy(own_first, first.at[:, pl.ds(column, 128)], sem),
        pltpu.make_async_copy(own_second, second.at[pl.ds(column, 128), :], sem_second),
    ]
    for d, piece in enumerate(pieces):
        source = plane ^ d
        for step in range(3):
            m = (me + 3 - step) % 4
            copies.append(
                pltpu.make_async_copy(
                    piece.at[step, pl.ds(0, 128), :],
                    first.at[
                        pl.ds(pl.multiple_of(source * 128, 128), 128),
                        pl.ds(pl.multiple_of(m * 128, 128), 128),
                    ],
                    sem,
                )
            )
            copies.append(
                pltpu.make_async_copy(
                    piece.at[step, pl.ds(128, 64), :],
                    second.at[
                        pl.ds(pl.multiple_of(m * 128 + source // 4 * 64, 64), 64),
                        pl.ds(pl.multiple_of(source % 4 * 128, 128), 128),
                    ],
                    sem_second,
                )
            )
    for copy in copies:
        copy.start()


def place_whole(refs, first, second, sem):
    pltpu.make_async_copy(refs[0], first, sem.at[0]).start()
    pltpu.make_async_copy(refs[1], second, sem.at[1]).start()


def wait_weights(refs, first, second, sem):
    pltpu.make_async_copy(first, first, sem.at[0]).wait()
    pltpu.make_async_copy(second, second, sem.at[1]).wait()


def gather_weights(shards):
    planes = lax.axis_size("groups") * lax.axis_size("graph")
    if shards[1].shape[1] != 512 or planes != 8 or lax.axis_size("mp") != 4:
        whole = [lax.all_gather(w, "mp", axis=1 - i % 2, tiled=True) for i, w in enumerate(shards)]
        return place_whole, [whole[2 * i : 2 * i + 2] for i in range(4)]
    pieces = pl.pallas_call(
        pack_kernel,
        out_shape=[shape(192, 128, BF16)] * 4,
        in_specs=[pl.BlockSpec(memory_space=pltpu.HBM)] * 8,
        out_specs=[pl.BlockSpec(memory_space=pl.ANY)] * 4,
        scratch_shapes=[pltpu.SemaphoreType.DMA((8,))],
        name="pack",
    )(*shards)

    def across(x, flip):
        return lax.ppermute(x, ("groups", "graph"), [(p, p ^ flip) for p in range(8)])

    sets = []
    for i, piece in enumerate(pieces):
        along = [lax.ppermute(piece, "mp", [(m, (m + s) % 4) for m in range(4)]) for s in (1, 2, 3)]
        held = {0: jnp.stack(along)}
        for flip in (2, 4, 6):
            held[flip] = across(held[0], flip)
        for flip in (0, 2, 4, 6):
            held[flip + 1] = across(held[flip], 1)
        sets.append([shards[2 * i], shards[2 * i + 1]] + [held[d] for d in range(8)])
    return place_pieces, sets


def forward(inputs, first, second):
    before = dot(inputs, first)
    logistic = jax.nn.sigmoid(before)
    hidden = (before * logistic).astype(BF16)
    slope = logistic * (1.0 + before * (1.0 - logistic))
    summed = dot(hidden, second)
    centered = summed - jnp.mean(summed, axis=-1, keepdims=True)
    rescale = lax.rsqrt(jnp.mean(centered * centered, axis=-1, keepdims=True) + 1e-05)
    normed = centered * rescale
    return normed, slope.astype(BF16), normed.astype(BF16), rescale


def backward_hidden(incoming, slope, normed, rescale, second):
    normed = normed.astype(F32)
    g_out = (
        incoming
        - jnp.mean(incoming, axis=-1, keepdims=True)
        - normed * jnp.mean(incoming * normed, axis=-1, keepdims=True)
    ) * rescale
    return (dot_trans(g_out.astype(BF16), second) * slope.astype(F32)).astype(BF16)


def table(index_row, count):
    n = index_row.shape[1]
    return jnp.where(lax.broadcasted_iota(jnp.int32, (count, n), 0) == index_row, 1.0, 0.0)


def flat_row(index):
    count, width = index.shape
    at = lax.broadcasted_iota(jnp.int32, (count, count * width), 1)
    row = lax.broadcasted_iota(jnp.int32, (count, count * width), 0)
    spread = jnp.zeros_like(at)
    for c in range(width):
        spread = jnp.where(at % width == c, index[:, c : c + 1], spread)
    return jnp.sum(jnp.where(at // width == row, spread, 0), axis=0, keepdims=True)


def send_kernel(grid_ref, send_ref, outgoing_ref, table_ref):
    one = table(flat_row(send_ref[...]), grid_ref.shape[0])
    table_ref[...] = one.astype(BF16)
    outgoing_ref[...] = dot(one.T.astype(BF16), grid_ref[...]).astype(BF16)


def tables_kernel(
    mesh_ref,
    slot_ref,
    recv_e_ref,
    halo_ref,
    sender_ref,
    recv_p_ref,
    slot_t,
    slot_g,
    enc_t,
    enc_g,
    halo_t,
    halo_g,
    sender_t,
    sender_g,
    proc_t,
    proc_g,
    recv_rows,
):
    for index, scatter, gather in (
        (slot_ref, slot_t, slot_g),
        (recv_e_ref, enc_t, enc_g),
        (halo_ref, halo_t, halo_g),
        (sender_ref, sender_t, sender_g),
        (recv_p_ref, proc_t, proc_g),
    ):
        row = flat_row(index[...]) if index is halo_ref else index[...]
        one = table(row, scatter.shape[0])
        scatter[...] = one.astype(BF16)
        gather[...] = one.T.astype(BF16)
    recv_rows[...] = dot(enc_g[...], mesh_ref[...]).astype(BF16)


def encode_kernel(
    held,
    mesh_ref,
    arrived_ref,
    slot_g,
    recv_rows,
    enc_t,
    halo_g,
    one_ref,
    halo_ref,
    slope_e,
    normed_e,
    scale_e,
    slope_n,
    normed_n,
    scale_n,
):
    features = mesh_ref.shape[1]
    first, second = taken(held[0])
    edges = slot_g.shape[0]
    for low in range(0, edges, ROWS):
        rows = pl.ds(low, ROWS)
        sent = dot(slot_g[rows, :], arrived_ref[...]).astype(BF16)
        inputs = jnp.concatenate([sent, recv_rows[rows, :]], axis=1)
        _, slope, normed, rescale = forward(inputs, first, second)
        slope_e[rows, :] = slope
        normed_e[rows, :] = normed
        scale_e[rows, :] = jnp.broadcast_to(rescale, (ROWS, LANES))
    aggregate = dot(enc_t[...], normed_e[...]).astype(BF16)
    first, second = taken(held[1])
    mesh = mesh_ref[...]
    normed, slope, rounded, rescale = forward(
        jnp.concatenate([mesh, aggregate], axis=1), first, second
    )
    slope_n[...] = slope
    normed_n[...] = rounded
    scale_n[...] = jnp.broadcast_to(rescale, scale_n.shape)
    one_ref[...] = (mesh.astype(F32) + normed).astype(BF16)
    halo_ref[...] = dot(halo_g[...], one_ref[...]).astype(BF16)


def process_kernel(
    held,
    one_ref,
    halo_ref,
    cotangent_ref,
    sender_t,
    sender_g,
    proc_t,
    proc_g,
    two_ref,
    grad_one_ref,
    grad_halo_ref,
    slope_p,
    normed_p,
    scale_p,
    ga_p,
):
    features = one_ref.shape[1]
    mesh_rows = one_ref.shape[0]
    edges = sender_g.shape[0]
    first, second = taken(held[0])
    lookup = jnp.concatenate([one_ref[...], halo_ref[...]], axis=0)
    for low in range(0, edges, ROWS):
        rows = pl.ds(low, ROWS)
        sent = dot(sender_g[rows, :], lookup).astype(BF16)
        got = dot(proc_g[rows, :], one_ref[...]).astype(BF16)
        _, slope, normed, rescale = forward(jnp.concatenate([sent, got], axis=1), first, second)
        slope_p[rows, :] = slope
        normed_p[rows, :] = normed
        scale_p[rows, :] = jnp.broadcast_to(rescale, (ROWS, LANES))
    aggregate = dot(proc_t[...], normed_p[...]).astype(BF16)
    first_n, second_n = taken(held[1])
    one = one_ref[...]
    normed, slope, rounded, rescale = forward(
        jnp.concatenate([one, aggregate], axis=1), first_n, second_n
    )
    two_ref[...] = (one.astype(F32) + normed).astype(BF16)
    cotangent = cotangent_ref[...].astype(F32)
    ga = backward_hidden(cotangent, slope, rounded, rescale, second_n)
    g_q = dot_trans(ga, first_n)
    g_msg = g_q[:, features:].astype(BF16)
    for low in range(0, edges, ROWS):
        rows = pl.ds(low, ROWS)
        incoming = dot(proc_g[rows, :], g_msg)
        ga_p[rows, :] = backward_hidden(
            incoming, slope_p[rows, :], normed_p[rows, :], scale_p[rows, 0:1], second
        )
    by_recv = dot(proc_t[...], ga_p[...]).astype(BF16)
    by_send = dot(sender_t[...], ga_p[...]).astype(BF16)
    g_send = dot_trans(by_send, first[:features, :])
    g_recv = dot_trans(by_recv, first[features:, :])
    grad_one_ref[...] = cotangent + g_q[:, :features] + g_recv + g_send[:mesh_rows, :]
    grad_halo_ref[...] = g_send[mesh_rows:, :].astype(BF16)


def decode_kernel(
    held,
    grad_one_ref,
    back_ref,
    halo_t,
    slope_e,
    normed_e,
    scale_e,
    slope_n,
    normed_n,
    scale_n,
    enc_t,
    enc_g,
    slot_t,
    mesh_grad_ref,
    grad_slots_ref,
    ga_e,
):
    features = grad_one_ref.shape[1]
    edges = enc_g.shape[0]
    grad_one = grad_one_ref[...] + dot(halo_t[...], back_ref[...])
    first_n, second_n = taken(held[1])
    ga = backward_hidden(grad_one, slope_n[...], normed_n[...], scale_n[:, 0:1], second_n)
    g_n = dot_trans(ga, first_n)
    g_edge = g_n[:, features:].astype(BF16)
    first, second = taken(held[0])
    for low in range(0, edges, ROWS):
        rows = pl.ds(low, ROWS)
        incoming = dot(enc_g[rows, :], g_edge)
        ga_e[rows, :] = backward_hidden(
            incoming, slope_e[rows, :], normed_e[rows, :], scale_e[rows, 0:1], second
        )
    by_recv = dot(enc_t[...], ga_e[...]).astype(BF16)
    by_slot = dot(slot_t[...], ga_e[...]).astype(BF16)
    mesh_grad_ref[...] = grad_one + g_n[:, :features] + dot_trans(by_recv, first[features:, :])
    grad_slots_ref[...] = dot_trans(by_slot, first[:features, :]).astype(BF16)


def grid_kernel(table_ref, back_ref, out_ref):
    out_ref[...] = dot(table_ref[...], back_ref[...])


def exchange(rows, capacity):
    features = rows.shape[1]
    parts = rows.reshape(-1, capacity, features)
    return lax.all_to_all(parts, PEERS, split_axis=0, concat_axis=0, tiled=True).reshape(rows.shape)


def local(
    grid_lat,
    mesh_lat,
    cotangent,
    grid_send,
    g2m_slot,
    g2m_receiver,
    halo_send,
    mesh_sender,
    mesh_receiver,
    *shards,
):
    grid_rows, features = grid_lat.shape
    mesh_rows = mesh_lat.shape[0]
    edges = g2m_slot.shape[0]
    mesh_edges = mesh_sender.shape[0]
    slots, halos = grid_send.size, halo_send.size
    capacity, halo_capacity = grid_send.shape[1], halo_send.shape[1]
    place, sets = gather_weights(shards)

    outgoing, grid_t = call(
        send_kernel,
        [shape(slots, features, BF16), shape(grid_rows, slots, BF16)],
        grid_lat,
        grid_send,
    )
    arrived = exchange(outgoing, capacity)
    slot_t, slot_g, enc_t, enc_g, halo_t, halo_g, sender_t, sender_g, proc_t, proc_g, recv_rows = call(
        tables_kernel,
        [
            shape(slots, edges, BF16),
            shape(edges, slots, BF16),
            shape(mesh_rows, edges, BF16),
            shape(edges, mesh_rows, BF16),
            shape(mesh_rows, halos, BF16),
            shape(halos, mesh_rows, BF16),
            shape(mesh_rows + halos, mesh_edges, BF16),
            shape(mesh_edges, mesh_rows + halos, BF16),
            shape(mesh_rows, mesh_edges, BF16),
            shape(mesh_edges, mesh_rows, BF16),
            shape(edges, features, BF16),
        ],
        mesh_lat,
        g2m_slot.reshape(1, edges),
        g2m_receiver.reshape(1, edges),
        halo_send,
        mesh_sender.reshape(1, mesh_edges),
        mesh_receiver.reshape(1, mesh_edges),
    )
    saved = [
        shape(edges, features, BF16),
        shape(edges, features, BF16),
        shape(edges, LANES, F32),
        shape(mesh_rows, features, BF16),
        shape(mesh_rows, features, BF16),
        shape(mesh_rows, LANES, F32),
    ]
    mesh_one, halo_out, *kept = call(
        encode_kernel,
        [shape(mesh_rows, features, BF16), shape(halos, features, BF16)] + saved,
        mesh_lat,
        arrived,
        slot_g,
        recv_rows,
        enc_t,
        halo_g,
        weights=(place, sets[:2]),
    )
    halo_in = exchange(halo_out, halo_capacity)
    mesh_two, grad_one, grad_halo = call(
        process_kernel,
        [
            shape(mesh_rows, features, BF16),
            shape(mesh_rows, features, F32),
            shape(halos, features, BF16),
        ],
        mesh_one,
        halo_in,
        cotangent,
        sender_t,
        sender_g,
        proc_t,
        proc_g,
        weights=(place, sets[2:]),
        scratch=[
            pltpu.VMEM((mesh_edges, features), BF16),
            pltpu.VMEM((mesh_edges, features), BF16),
            pltpu.VMEM((mesh_edges, LANES), F32),
            pltpu.VMEM((mesh_edges, features), BF16),
        ],
    )
    halo_back = exchange(grad_halo, halo_capacity)
    mesh_grad, grad_slots = call(
        decode_kernel,
        [shape(mesh_rows, features, F32), shape(slots, features, BF16)],
        grad_one,
        halo_back,
        halo_t,
        *kept,
        enc_t,
        enc_g,
        slot_t,
        weights=(place, sets[:2]),
        scratch=[pltpu.VMEM((edges, features), BF16)],
    )
    returned = exchange(grad_slots, capacity)
    (grid_grad,) = call(grid_kernel, [shape(grid_rows, features, F32)], grid_t, returned)
    return (mesh_two, grid_grad, mesh_grad)


def solution(mesh):
    rows = P(AXES, None)
    flat = P(AXES)
    in_specs = (rows,) * 4 + (flat,) * 2 + (rows,) + (flat,) * 2 + (P(None, "mp"), P("mp", None)) * 4
    return jax.shard_map(
        local, mesh=mesh, in_specs=in_specs, out_specs=(rows,) * 3, check_vma=False
    )
```

```python
import functools

import jax
import jax.numpy as jnp
from jax import lax
from jax.experimental import pallas as pl
from jax.experimental.pallas import tpu as pltpu
from jax.sharding import PartitionSpec as P

F32 = jnp.float32
BF16 = jnp.bfloat16
LANES = 128
ROWS = 256
FEATURES = 512
AXES = ("groups", "graph", "mp")
PEERS = ("graph", "mp")


def dot(left, right):
    return jnp.dot(left, right, preferred_element_type=F32)


def dot_trans(left, right):
    return lax.dot_general(left, right, (((1,), (1,)), ((), ())), preferred_element_type=F32)


def shape(rows, columns, dtype):
    return pltpu.HBM((rows, columns), dtype)


def origin(rank, step):
    return (0,) * rank


def call(kernel, out_shape, *args, weights=(), scratch=()):
    scratch = list(scratch)
    in_specs = [pl.BlockSpec(a.shape, functools.partial(origin, a.ndim)) for a in args]
    in_specs += [pl.BlockSpec(memory_space=pl.ANY)] * len(weights)
    if weights:
        scratch.append(pltpu.VMEM((FEATURES, weights[0].shape[1]), BF16))
        scratch.append(pltpu.SemaphoreType.DMA)

    def body(*refs):
        if not weights:
            return kernel(*refs)
        ins, refs = refs[: len(args)], refs[len(args) :]
        sources, refs = refs[: len(weights)], refs[len(weights) :]
        held, sem = refs[-2:]
        low = 0
        for source in sources:
            rows = source.shape[0]
            pltpu.make_async_copy(source, held.at[pl.ds(low, rows), :], sem).start()
            low += rows
        kernel((held, sem), *ins, *refs[:-2])

    operands = [pltpu.with_memory_space_constraint(a, pltpu.HBM) for a in args] + list(weights)
    return pl.pallas_call(
        body,
        grid=(1,),
        out_shape=out_shape,
        in_specs=in_specs,
        out_specs=[pl.BlockSpec(s.shape, functools.partial(origin, len(s.shape))) for s in out_shape],
        scratch_shapes=scratch,
        name=kernel.__name__,
        compiler_params=pltpu.CompilerParams(vmem_limit_bytes=40 * 1024 * 1024),
    )(*operands)


def wait_weights(weights):
    held, sem = weights
    pltpu.make_async_copy(held, held, sem).wait()


def layers(weights, which):
    low = which * 3 * FEATURES
    held = weights[0]
    return (
        held[:, low : low + 2 * FEATURES],
        held[:, low + 2 * FEATURES : low + 3 * FEATURES],
    )


def prepare_kernel(*refs):
    shards, refs = refs[:8], refs[8:]
    grid_ref, send_ref, enc_own, proc_own, enc_piece, proc_piece, outgoing_ref, table_ref = refs
    plane = lax.axis_index("groups") * lax.axis_size("graph") + lax.axis_index("graph")
    for i in range(4):
        own, low = (enc_own, proc_own)[i // 2], i % 2 * 3 * FEATURES
        own[:, low : low + 2 * FEATURES] = shards[2 * i][...].astype(F32).T.astype(BF16)
        own[:, low + 2 * FEATURES : low + 3 * FEATURES] = shards[2 * i + 1][...]
    rows = enc_piece.shape[0]
    low = pl.multiple_of(plane * rows, rows)
    enc_piece[...] = enc_own[pl.ds(low, rows), :]
    proc_piece[...] = proc_own[pl.ds(low, rows), :]
    send_kernel(grid_ref, send_ref, outgoing_ref, table_ref)


def across(x, flip):
    planes = lax.axis_size("groups") * lax.axis_size("graph")
    return lax.ppermute(x, ("groups", "graph"), [(p, p ^ flip) for p in range(planes)])


def spread_along(piece):
    size = lax.axis_size("mp")
    return jnp.concatenate(
        [lax.ppermute(piece, "mp", [(m, (m + s) % size) for m in range(size)]) for s in range(1, size)]
    )


def spread_plane(own, first, second):
    blocks = [own, first, second]
    for flip in (2, 4, 6):
        block = across(first, flip)
        blocks += [block, across(block, 1)]
    return blocks


def start(grid_lat, grid_send, shards):
    grid_rows, features = grid_lat.shape
    slots, capacity = grid_send.size, grid_send.shape[1]
    sent = [shape(slots, features, BF16), shape(grid_rows, slots, BF16)]
    planes = lax.axis_size("groups") * lax.axis_size("graph")
    hidden = shards[1].shape[0]
    if planes != 8 or lax.axis_size("mp") != 4 or hidden != 128 or features != FEATURES:
        outgoing, grid_t = call(send_kernel, sent, grid_lat, grid_send)
        rows = []
        for i in range(4):
            rows.append(lax.all_gather(shards[2 * i], "mp", axis=1, tiled=True).T)
            rows.append(lax.all_gather(shards[2 * i + 1], "mp", axis=0, tiled=True))
        sets = [[jnp.concatenate(rows[:4], axis=1)], [jnp.concatenate(rows[4:], axis=1)]]
        return sets[0], sets[1], exchange(outgoing, capacity), grid_t
    enc_own, proc_own, enc_piece, proc_piece, outgoing, grid_t = call(
        prepare_kernel,
        [shape(hidden, 6 * features, BF16)] * 2
        + [shape(hidden // planes, 6 * features, BF16)] * 2
        + sent,
        *shards,
        grid_lat,
        grid_send,
    )
    first = spread_along(enc_piece)
    second = across(first, 1)
    outgoing, proc_piece, second = lax.optimization_barrier((outgoing, proc_piece, second))
    enc = spread_plane(enc_own, first, second)
    arrived = exchange(outgoing, capacity)
    first = spread_along(proc_piece)
    proc = spread_plane(proc_own, first, across(first, 1))
    return enc, proc, arrived, grid_t


def forward(inputs, first, second):
    before = dot_trans(inputs, first)
    logistic = jax.nn.sigmoid(before)
    hidden = (before * logistic).astype(BF16)
    slope = logistic * (1.0 + before * (1.0 - logistic))
    summed = dot(hidden, second)
    centered = summed - jnp.mean(summed, axis=-1, keepdims=True)
    rescale = lax.rsqrt(jnp.mean(centered * centered, axis=-1, keepdims=True) + 1e-05)
    normed = centered * rescale
    return normed, slope.astype(BF16), normed.astype(BF16), rescale


def backward_hidden(incoming, slope, normed, rescale, second):
    normed = normed.astype(F32)
    g_out = (
        incoming
        - jnp.mean(incoming, axis=-1, keepdims=True)
        - normed * jnp.mean(incoming * normed, axis=-1, keepdims=True)
    ) * rescale
    return (dot_trans(g_out.astype(BF16), second) * slope.astype(F32)).astype(BF16)


def table(index_row, count):
    n = index_row.shape[1]
    return jnp.where(lax.broadcasted_iota(jnp.int32, (count, n), 0) == index_row, 1.0, 0.0)


def flat_row(index):
    count, width = index.shape
    at = lax.broadcasted_iota(jnp.int32, (count, count * width), 1)
    row = lax.broadcasted_iota(jnp.int32, (count, count * width), 0)
    spread = jnp.zeros_like(at)
    for c in range(width):
        spread = jnp.where(at % width == c, index[:, c : c + 1], spread)
    return jnp.sum(jnp.where(at // width == row, spread, 0), axis=0, keepdims=True)


def send_kernel(grid_ref, send_ref, outgoing_ref, table_ref):
    one = table(flat_row(send_ref[...]), grid_ref.shape[0])
    table_ref[...] = one.astype(BF16)
    outgoing_ref[...] = dot(one.T.astype(BF16), grid_ref[...]).astype(BF16)


def tables_kernel(
    mesh_ref,
    slot_ref,
    recv_e_ref,
    halo_ref,
    sender_ref,
    recv_p_ref,
    slot_t,
    slot_g,
    enc_t,
    enc_g,
    halo_t,
    halo_g,
    sender_t,
    sender_g,
    proc_t,
    proc_g,
    recv_rows,
):
    for index, scatter, gather in (
        (slot_ref, slot_t, slot_g),
        (recv_e_ref, enc_t, enc_g),
        (halo_ref, halo_t, halo_g),
        (sender_ref, sender_t, sender_g),
        (recv_p_ref, proc_t, proc_g),
    ):
        row = flat_row(index[...]) if index is halo_ref else index[...]
        one = table(row, scatter.shape[0])
        scatter[...] = one.astype(BF16)
        gather[...] = one.T.astype(BF16)
    recv_rows[...] = dot(enc_g[...], mesh_ref[...]).astype(BF16)


def encode_kernel(
    weights,
    mesh_ref,
    arrived_ref,
    slot_g,
    recv_rows,
    enc_t,
    halo_g,
    one_ref,
    halo_ref,
    slope_e,
    normed_e,
    scale_e,
    slope_n,
    normed_n,
    scale_n,
):
    edges = slot_g.shape[0]
    wait_weights(weights)
    first, second = layers(weights, 0)
    for low in range(0, edges, ROWS):
        rows = pl.ds(low, ROWS)
        sent = dot(slot_g[rows, :], arrived_ref[...]).astype(BF16)
        inputs = jnp.concatenate([sent, recv_rows[rows, :]], axis=1)
        _, slope, normed, rescale = forward(inputs, first, second)
        slope_e[rows, :] = slope
        normed_e[rows, :] = normed
        scale_e[rows, :] = jnp.broadcast_to(rescale, (ROWS, LANES))
    aggregate = dot(enc_t[...], normed_e[...]).astype(BF16)
    first, second = layers(weights, 1)
    mesh = mesh_ref[...]
    normed, slope, rounded, rescale = forward(
        jnp.concatenate([mesh, aggregate], axis=1), first, second
    )
    slope_n[...] = slope
    normed_n[...] = rounded
    scale_n[...] = jnp.broadcast_to(rescale, scale_n.shape)
    one_ref[...] = (mesh.astype(F32) + normed).astype(BF16)
    halo_ref[...] = dot(halo_g[...], one_ref[...]).astype(BF16)


def process_kernel(
    weights,
    one_ref,
    halo_ref,
    cotangent_ref,
    sender_t,
    sender_g,
    proc_t,
    proc_g,
    two_ref,
    grad_one_ref,
    grad_halo_ref,
    slope_p,
    normed_p,
    scale_p,
    ga_p,
):
    features = one_ref.shape[1]
    mesh_rows = one_ref.shape[0]
    edges = sender_g.shape[0]
    wait_weights(weights)
    first, second = layers(weights, 0)
    lookup = jnp.concatenate([one_ref[...], halo_ref[...]], axis=0)
    for low in range(0, edges, ROWS):
        rows = pl.ds(low, ROWS)
        sent = dot(sender_g[rows, :], lookup).astype(BF16)
        got = dot(proc_g[rows, :], one_ref[...]).astype(BF16)
        _, slope, normed, rescale = forward(jnp.concatenate([sent, got], axis=1), first, second)
        slope_p[rows, :] = slope
        normed_p[rows, :] = normed
        scale_p[rows, :] = jnp.broadcast_to(rescale, (ROWS, LANES))
    aggregate = dot(proc_t[...], normed_p[...]).astype(BF16)
    first_n, second_n = layers(weights, 1)
    one = one_ref[...]
    normed, slope, rounded, rescale = forward(
        jnp.concatenate([one, aggregate], axis=1), first_n, second_n
    )
    two_ref[...] = (one.astype(F32) + normed).astype(BF16)
    cotangent = cotangent_ref[...].astype(F32)
    ga = backward_hidden(cotangent, slope, rounded, rescale, second_n)
    g_q = dot(ga, first_n)
    g_msg = g_q[:, features:].astype(BF16)
    for low in range(0, edges, ROWS):
        rows = pl.ds(low, ROWS)
        incoming = dot(proc_g[rows, :], g_msg)
        ga_p[rows, :] = backward_hidden(
            incoming, slope_p[rows, :], normed_p[rows, :], scale_p[rows, 0:1], second
        )
    by_recv = dot(proc_t[...], ga_p[...]).astype(BF16)
    by_send = dot(sender_t[...], ga_p[...]).astype(BF16)
    g_send = dot(by_send, first[:, :features])
    g_recv = dot(by_recv, first[:, features:])
    grad_one_ref[...] = cotangent + g_q[:, :features] + g_recv + g_send[:mesh_rows, :]
    grad_halo_ref[...] = g_send[mesh_rows:, :].astype(BF16)


def decode_kernel(
    weights,
    grad_one_ref,
    back_ref,
    halo_t,
    slope_e,
    normed_e,
    scale_e,
    slope_n,
    normed_n,
    scale_n,
    enc_t,
    enc_g,
    slot_t,
    mesh_grad_ref,
    grad_slots_ref,
    ga_e,
):
    features = grad_one_ref.shape[1]
    edges = enc_g.shape[0]
    grad_one = grad_one_ref[...] + dot(halo_t[...], back_ref[...])
    wait_weights(weights)
    first_n, second_n = layers(weights, 1)
    ga = backward_hidden(grad_one, slope_n[...], normed_n[...], scale_n[:, 0:1], second_n)
    g_n = dot(ga, first_n)
    g_edge = g_n[:, features:].astype(BF16)
    first, second = layers(weights, 0)
    for low in range(0, edges, ROWS):
        rows = pl.ds(low, ROWS)
        incoming = dot(enc_g[rows, :], g_edge)
        ga_e[rows, :] = backward_hidden(
            incoming, slope_e[rows, :], normed_e[rows, :], scale_e[rows, 0:1], second
        )
    by_recv = dot(enc_t[...], ga_e[...]).astype(BF16)
    by_slot = dot(slot_t[...], ga_e[...]).astype(BF16)
    mesh_grad_ref[...] = grad_one + g_n[:, :features] + dot(by_recv, first[:, features:])
    grad_slots_ref[...] = dot(by_slot, first[:, :features]).astype(BF16)


def grid_kernel(table_ref, back_ref, out_ref):
    out_ref[...] = dot(table_ref[...], back_ref[...])


def exchange(rows, capacity):
    features = rows.shape[1]
    parts = rows.reshape(-1, capacity, features)
    return lax.all_to_all(parts, PEERS, split_axis=0, concat_axis=0, tiled=True).reshape(rows.shape)


def local(
    grid_lat,
    mesh_lat,
    cotangent,
    grid_send,
    g2m_slot,
    g2m_receiver,
    halo_send,
    mesh_sender,
    mesh_receiver,
    *shards,
):
    grid_rows, features = grid_lat.shape
    mesh_rows = mesh_lat.shape[0]
    edges = g2m_slot.shape[0]
    mesh_edges = mesh_sender.shape[0]
    slots, halos = grid_send.size, halo_send.size
    capacity, halo_capacity = grid_send.shape[1], halo_send.shape[1]
    enc, proc, arrived, grid_t = start(grid_lat, grid_send, shards)
    slot_t, slot_g, enc_t, enc_g, halo_t, halo_g, sender_t, sender_g, proc_t, proc_g, recv_rows = call(
        tables_kernel,
        [
            shape(slots, edges, BF16),
            shape(edges, slots, BF16),
            shape(mesh_rows, edges, BF16),
            shape(edges, mesh_rows, BF16),
            shape(mesh_rows, halos, BF16),
            shape(halos, mesh_rows, BF16),
            shape(mesh_rows + halos, mesh_edges, BF16),
            shape(mesh_edges, mesh_rows + halos, BF16),
            shape(mesh_rows, mesh_edges, BF16),
            shape(mesh_edges, mesh_rows, BF16),
            shape(edges, features, BF16),
        ],
        mesh_lat,
        g2m_slot.reshape(1, edges),
        g2m_receiver.reshape(1, edges),
        halo_send,
        mesh_sender.reshape(1, mesh_edges),
        mesh_receiver.reshape(1, mesh_edges),
    )
    saved = [
        shape(edges, features, BF16),
        shape(edges, features, BF16),
        shape(edges, LANES, F32),
        shape(mesh_rows, features, BF16),
        shape(mesh_rows, features, BF16),
        shape(mesh_rows, LANES, F32),
    ]
    mesh_one, halo_out, *kept = call(
        encode_kernel,
        [shape(mesh_rows, features, BF16), shape(halos, features, BF16)] + saved,
        mesh_lat,
        arrived,
        slot_g,
        recv_rows,
        enc_t,
        halo_g,
        weights=enc,
    )
    halo_in = exchange(halo_out, halo_capacity)
    mesh_two, grad_one, grad_halo = call(
        process_kernel,
        [
            shape(mesh_rows, features, BF16),
            shape(mesh_rows, features, F32),
            shape(halos, features, BF16),
        ],
        mesh_one,
        halo_in,
        cotangent,
        sender_t,
        sender_g,
        proc_t,
        proc_g,
        weights=proc,
        scratch=[
            pltpu.VMEM((mesh_edges, features), BF16),
            pltpu.VMEM((mesh_edges, features), BF16),
            pltpu.VMEM((mesh_edges, LANES), F32),
            pltpu.VMEM((mesh_edges, features), BF16),
        ],
    )
    halo_back = exchange(grad_halo, halo_capacity)
    mesh_grad, grad_slots = call(
        decode_kernel,
        [shape(mesh_rows, features, F32), shape(slots, features, BF16)],
        grad_one,
        halo_back,
        halo_t,
        *kept,
        enc_t,
        enc_g,
        slot_t,
        weights=enc,
        scratch=[pltpu.VMEM((edges, features), BF16)],
    )
    returned = exchange(grad_slots, capacity)
    (grid_grad,) = call(grid_kernel, [shape(grid_rows, features, F32)], grid_t, returned)
    return (mesh_two, grid_grad, mesh_grad)


def solution(mesh):
    rows = P(AXES, None)
    flat = P(AXES)
    in_specs = (rows,) * 4 + (flat,) * 2 + (rows,) + (flat,) * 2 + (P(None, "mp"), P("mp", None)) * 4
    return jax.shard_map(
        local, mesh=mesh, in_specs=in_specs, out_specs=(rows,) * 3, check_vma=False
    )
```

```python
import jax
import jax.numpy as jnp
from jax import lax
from jax.experimental import pallas as pl
from jax.experimental.pallas import tpu as pltpu
from jax.sharding import PartitionSpec as P

F32 = jnp.float32
BF16 = jnp.bfloat16
LANES = 128
ROWS = 256
FEATURES = 512
AXES = ("groups", "graph", "mp")
PEERS = ("graph", "mp")


def dot(left, right):
    return jnp.dot(left, right, preferred_element_type=F32)


def dot_trans(left, right):
    return lax.dot_general(left, right, (((1,), (1,)), ((), ())), preferred_element_type=F32)


def shape(rows, columns, dtype):
    return pltpu.HBM((rows, columns), dtype)


def free(rows, columns, dtype):
    return jax.ShapeDtypeStruct((rows, columns), dtype)


def held(array):
    return pltpu.with_memory_space_constraint(array, pltpu.HBM)


class Input:
    def __init__(self, copies, ref, sem):
        self.copies, self.ref, self.sem = copies, ref, sem

    def __call__(self):
        if self.copies:
            pltpu.make_async_copy(self.ref, self.ref, self.sem).wait()
            self.copies = None
        return self.ref


class Output:
    def __init__(self, ref, copy):
        self.ref, self.copy = ref, copy

    def send(self, value=None):
        if value is not None:
            self.ref[...] = value
        self.copy.start()


WEIGHTS = object()


def call(kernel, out_shape, *args, weights=(), first=0, scratch=(), flops=0):
    packed = lambda a: a.dtype == BF16 and a.shape[-1] == LANES
    args = [a if a is WEIGHTS or packed(a) else held(a) for a in args]
    arrays = [a for a in args if a is not WEIGHTS]
    width = 3 * FEATURES
    count, outs = len(args), len(out_shape)

    def body(*refs):
        sources, refs = list(refs[: len(arrays)]), refs[len(arrays) :]
        blocks, refs = refs[: len(weights)], refs[len(weights) :]
        out_refs, refs = refs[:outs], refs[outs:]
        places, refs = refs[:count], refs[count:]
        results, refs = refs[:outs], refs[outs:]
        sem_in, sem_out, refs = refs[0], refs[1], refs[2:]
        which, inputs = first, []
        for i, (arg, place) in enumerate(zip(args, places)):
            if arg is WEIGHTS:
                copies, low = [], 0
                for block in blocks:
                    n = block.shape[0]
                    copies.append(
                        pltpu.make_async_copy(
                            block.at[:, pl.ds(which * width, width)],
                            place.at[pl.ds(low, n), :],
                            sem_in.at[i],
                        )
                    )
                    low += n
                which = 1 - which
            else:
                copies = [pltpu.make_async_copy(sources.pop(0), place, sem_in.at[i])]
            for copy in copies:
                copy.start()
            inputs.append(Input(copies, place, sem_in.at[i]))
        outputs = [
            Output(ref, pltpu.make_async_copy(ref, out, sem_out.at[i]))
            for i, (ref, out) in enumerate(zip(results, out_refs))
        ]
        kernel(*inputs, *outputs, *refs)
        for output in outputs:
            output.copy.wait()

    places = [
        pltpu.VMEM((FEATURES, width), BF16) if a is WEIGHTS else pltpu.VMEM(a.shape, a.dtype)
        for a in args
    ]
    total = sum(a.size * a.dtype.itemsize for a in (*arrays, *weights))
    return pl.pallas_call(
        body,
        out_shape=out_shape,
        in_specs=[pl.BlockSpec(memory_space=pl.ANY)] * (len(arrays) + len(weights)),
        out_specs=[pl.BlockSpec(memory_space=pl.ANY)] * outs,
        scratch_shapes=places
        + [pltpu.VMEM(s.shape, s.dtype) for s in out_shape]
        + [pltpu.SemaphoreType.DMA((count,)), pltpu.SemaphoreType.DMA((outs,))]
        + list(scratch),
        name=kernel.__name__,
        cost_estimate=pl.CostEstimate(flops=flops, bytes_accessed=total, transcendentals=0),
        compiler_params=pltpu.CompilerParams(vmem_limit_bytes=40 * 1024 * 1024),
    )(*arrays, *weights)


def layers(ref):
    return ref[:, : 2 * FEATURES], ref[:, 2 * FEATURES :]


def turned(first, select):
    return dot_trans(select, first).astype(BF16)


def prepare_kernel(grid, send, *refs):
    shards, (outgoing, table_out, *pieces) = refs[:8], refs[8:]
    plane = lax.axis_index("groups") * lax.axis_size("graph") + lax.axis_index("graph")
    width = 3 * FEATURES
    for i, out in ((0, pieces[0]), (1, pieces[0]), (2, pieces[1]), (3, pieces[1])):
        rows = out.ref.shape[0]
        base = plane * rows
        one, two = shards[2 * i](), shards[2 * i + 1]()
        hidden = one.shape[1]
        select = jnp.where(
            lax.broadcasted_iota(jnp.int32, (rows, hidden), 0) + base
            == lax.broadcasted_iota(jnp.int32, (rows, hidden), 1),
            1.0,
            0.0,
        ).astype(BF16)
        low = i % 2 * width
        out.ref[:, low : low + 2 * FEATURES] = turned(one[...], select)
        out.ref[:, low + 2 * FEATURES : low + width] = two[pl.ds(pl.multiple_of(base, rows), rows), :]
        if i % 2:
            out.send()
    send_kernel(grid, send, outgoing, table_out)


def own_kernel(*refs):
    shards, outs = refs[:8], refs[8:]
    width = 3 * FEATURES
    for i in range(4):
        one, two = shards[2 * i](), shards[2 * i + 1]()
        hidden = one.shape[1]
        select = jnp.where(
            lax.broadcasted_iota(jnp.int32, (hidden, hidden), 0)
            == lax.broadcasted_iota(jnp.int32, (hidden, hidden), 1),
            1.0,
            0.0,
        ).astype(BF16)
        out, low = outs[i // 2], i % 2 * width
        out.ref[:, low : low + 2 * FEATURES] = turned(one[...], select)
        out.ref[:, low + 2 * FEATURES : low + width] = two[...]
        if i % 2:
            out.send()


def across(x, flip):
    planes = lax.axis_size("groups") * lax.axis_size("graph")
    return lax.ppermute(x, ("groups", "graph"), [(p, p ^ flip) for p in range(planes)])


def spread_along(piece):
    size = lax.axis_size("mp")
    return jnp.concatenate(
        [lax.ppermute(piece, "mp", [(m, (m + s) % size) for m in range(size)]) for s in range(1, size)]
    )


def start(grid_lat, grid_send, shards):
    grid_rows, features = grid_lat.shape
    slots, capacity = grid_send.size, grid_send.shape[1]
    sent = [free(slots * features // LANES, LANES, BF16), shape(grid_rows, slots, BF16)]
    planes = lax.axis_size("groups") * lax.axis_size("graph")
    hidden = shards[1].shape[0]
    grid_send = grid_send.T
    if planes != 8 or lax.axis_size("mp") != 4 or hidden != 128 or features != FEATURES:
        outgoing, grid_t = call(send_kernel, sent, grid_lat, grid_send)
        rows = []
        for i in range(4):
            rows.append(lax.all_gather(shards[2 * i], "mp", axis=1, tiled=True).T)
            rows.append(lax.all_gather(shards[2 * i + 1], "mp", axis=0, tiled=True))
        enc, proc = jnp.concatenate(rows[:4], axis=1), jnp.concatenate(rows[4:], axis=1)
        return [enc], lambda after: ([proc], after), exchange(outgoing, capacity), grid_t
    outgoing, grid_t, enc_piece, proc_piece = call(
        prepare_kernel,
        sent + [free(hidden // planes, 6 * features, BF16)] * 2,
        grid_lat,
        grid_send,
        *shards,
    )
    first = spread_along(enc_piece)
    second = across(first, 1)
    outgoing, proc_piece, second = lax.optimization_barrier((outgoing, proc_piece, second))
    enc_own, proc_own = call(own_kernel, [shape(hidden, 6 * features, BF16)] * 2, *shards)
    enc_own, proc_own = held(enc_own), held(proc_own)
    enc = [enc_own, first, second]
    for flip in (2, 4, 6):
        block = across(first, flip)
        enc += [block, across(block, 1)]
    arrived = exchange(outgoing, capacity)
    first = spread_along(proc_piece)
    first, arrived = lax.optimization_barrier((first, arrived))
    blocks = [first] + [across(first, flip) for flip in (2, 4, 6)]

    def finish(after):
        *tied, after = lax.optimization_barrier((*blocks, after))
        return [proc_own] + tied + [across(block, 1) for block in tied], after

    return enc, finish, arrived, grid_t


def forward(inputs, first, second):
    before = dot_trans(inputs, first)
    logistic = jax.nn.sigmoid(before)
    hidden = (before * logistic).astype(BF16)
    slope = logistic * (1.0 + before * (1.0 - logistic))
    summed = dot(hidden, second)
    centered = summed - jnp.mean(summed, axis=-1, keepdims=True)
    rescale = lax.rsqrt(jnp.mean(centered * centered, axis=-1, keepdims=True) + 1e-05)
    normed = centered * rescale
    return normed, slope.astype(BF16), normed.astype(BF16), rescale


def backward_hidden(incoming, slope, normed, rescale, second):
    normed = normed.astype(F32)
    g_out = (
        incoming
        - jnp.mean(incoming, axis=-1, keepdims=True)
        - normed * jnp.mean(incoming * normed, axis=-1, keepdims=True)
    ) * rescale
    return (dot_trans(g_out.astype(BF16), second) * slope.astype(F32)).astype(BF16)


def table(index_row, count):
    n = index_row.shape[1]
    return jnp.where(lax.broadcasted_iota(jnp.int32, (count, n), 0) == index_row, 1.0, 0.0)


def flat_row(index):
    width, count = index.shape
    index = index.astype(F32).T
    at = lax.broadcasted_iota(jnp.int32, (count, count * width), 1)
    row = lax.broadcasted_iota(jnp.int32, (count, count * width), 0)
    spread = jnp.zeros(at.shape, F32)
    for c in range(width):
        spread = jnp.where(at % width == c, index[:, c : c + 1], spread)
    return jnp.sum(jnp.where(at // width == row, spread, 0.0), axis=0, keepdims=True).astype(jnp.int32)


def lane_table(n, blocks, block, tall):
    sizes = (n * blocks, n) if tall else (n, n * blocks)
    long = lax.broadcasted_iota(jnp.int32, sizes, 0 if tall else 1)
    short = lax.broadcasted_iota(jnp.int32, sizes, 1 if tall else 0)
    return jnp.where(long == short * blocks + block, 1.0, 0.0).astype(BF16)


def pack_rows(rows):
    n, blocks = rows.shape[0], rows.shape[1] // LANES
    return sum(
        dot(lane_table(n, blocks, k, True), rows[:, k * LANES : (k + 1) * LANES])
        for k in range(blocks)
    ).astype(BF16)


def unpack_rows(packed, features):
    blocks = features // LANES
    n = packed.shape[0] // blocks
    return jnp.concatenate(
        [dot(lane_table(n, blocks, k, False), packed).astype(BF16) for k in range(blocks)], axis=1
    )


def send_kernel(grid, send, outgoing, table_out):
    one = table(flat_row(send()[...]), grid().shape[0])
    rows = dot(one.T.astype(BF16), grid()[...]).astype(BF16)
    outgoing.send(pack_rows(rows))
    table_out.send(one.astype(BF16))


def tables_kernel(mesh, slot, recv_e, halo, sender, recv_p, *outs):
    for i, index in enumerate((slot, recv_e, halo, sender, recv_p)):
        scatter, gather = outs[2 * i : 2 * i + 2]
        row = flat_row(index()[...]) if index is halo else index()[...]
        one = table(row, scatter.ref.shape[0])
        scatter.send(one.astype(BF16))
        gather.send(one.T.astype(BF16))
    outs[10].send(dot(outs[3].ref[...], mesh()[...]).astype(BF16))


def encode_kernel(
    recv_rows, arrived, slot_g, weights_e, enc_t, mesh, weights_n, halo_g,
    one_out, halo_out, slope_e, normed_e, scale_e, slope_n, normed_n, scale_n,
):
    rows_in = unpack_rows(arrived()[...], FEATURES)
    edges = slot_g().shape[0]
    first, second = layers(weights_e())
    for low in range(0, edges, ROWS):
        rows = pl.ds(low, ROWS)
        sent = dot(slot_g()[rows, :], rows_in).astype(BF16)
        inputs = jnp.concatenate([sent, recv_rows()[rows, :]], axis=1)
        _, slope, normed, rescale = forward(inputs, first, second)
        slope_e.ref[rows, :] = slope
        normed_e.ref[rows, :] = normed
        scale_e.ref[rows, :] = jnp.broadcast_to(rescale, (ROWS, LANES))
    for out in (slope_e, normed_e, scale_e):
        out.send()
    aggregate = dot(enc_t()[...], normed_e.ref[...]).astype(BF16)
    first, second = layers(weights_n())
    own = mesh()[...]
    normed, slope, rounded, rescale = forward(
        jnp.concatenate([own, aggregate], axis=1), first, second
    )
    one = (own.astype(F32) + normed).astype(BF16)
    one_out.send(one)
    halo_out.send(pack_rows(dot(halo_g()[...], one).astype(BF16)))
    slope_n.send(slope)
    normed_n.send(rounded)
    scale_n.send(jnp.broadcast_to(rescale, scale_n.ref.shape))


def process_kernel(
    one_in, halo, sender_g, proc_g, weights_p, proc_t, weights_n, cotangent_in, sender_t,
    two, grad_one, grad_halo, slope_p, normed_p, scale_p, ga_p,
):
    features = FEATURES
    one = one_in()[...]
    mesh_rows = one.shape[0]
    lookup = jnp.concatenate([one, unpack_rows(halo()[...], features)], axis=0)
    edges = sender_g().shape[0]
    first, second = layers(weights_p())
    for low in range(0, edges, ROWS):
        rows = pl.ds(low, ROWS)
        sent = dot(sender_g()[rows, :], lookup).astype(BF16)
        got = dot(proc_g()[rows, :], one).astype(BF16)
        _, slope, normed, rescale = forward(jnp.concatenate([sent, got], axis=1), first, second)
        slope_p[rows, :] = slope
        normed_p[rows, :] = normed
        scale_p[rows, :] = jnp.broadcast_to(rescale, (ROWS, LANES))
    aggregate = dot(proc_t()[...], normed_p[...]).astype(BF16)
    first_n, second_n = layers(weights_n())
    normed, slope, rounded, rescale = forward(
        jnp.concatenate([one, aggregate], axis=1), first_n, second_n
    )
    two.send((one.astype(F32) + normed).astype(BF16))
    cotangent = cotangent_in()[...].astype(F32)
    ga = backward_hidden(cotangent, slope, rounded, rescale, second_n)
    g_q = dot(ga, first_n)
    g_msg = g_q[:, features:].astype(BF16)
    for low in range(0, edges, ROWS):
        rows = pl.ds(low, ROWS)
        incoming = dot(proc_g()[rows, :], g_msg)
        ga_p[rows, :] = backward_hidden(
            incoming, slope_p[rows, :], normed_p[rows, :], scale_p[rows, 0:1], second
        )
    by_send = dot(sender_t()[...], ga_p[...]).astype(BF16)
    g_send = dot(by_send, first[:, :features])
    grad_halo.send(pack_rows(g_send[mesh_rows:, :].astype(BF16)))
    by_recv = dot(proc_t()[...], ga_p[...]).astype(BF16)
    g_recv = dot(by_recv, first[:, features:])
    grad_one.send(cotangent + g_q[:, :features] + g_recv + g_send[:mesh_rows, :])


def decode_kernel(
    back, halo_t, grad_in, slope_n, normed_n, scale_n, weights_n, enc_g, slope_e, normed_e, scale_e,
    weights_e, slot_t, enc_t, mesh_grad, grad_slots, ga_e,
):
    features = FEATURES
    edges = enc_g().shape[0]
    grad_one = grad_in()[...] + dot(halo_t()[...], unpack_rows(back()[...], features))
    first_n, second_n = layers(weights_n())
    ga = backward_hidden(grad_one, slope_n()[...], normed_n()[...], scale_n()[:, 0:1], second_n)
    g_n = dot(ga, first_n)
    g_edge = g_n[:, features:].astype(BF16)
    first, second = layers(weights_e())
    for low in range(0, edges, ROWS):
        rows = pl.ds(low, ROWS)
        incoming = dot(enc_g()[rows, :], g_edge)
        ga_e[rows, :] = backward_hidden(
            incoming, slope_e()[rows, :], normed_e()[rows, :], scale_e()[rows, 0:1], second
        )
    by_slot = dot(slot_t()[...], ga_e[...]).astype(BF16)
    grad_slots.send(pack_rows(dot(by_slot, first[:, :features]).astype(BF16)))
    by_recv = dot(enc_t()[...], ga_e[...]).astype(BF16)
    mesh_grad.send(grad_one + g_n[:, :features] + dot(by_recv, first[:, features:]))


def grid_kernel(back, table_in, out):
    rows = unpack_rows(back()[...], FEATURES)
    out.send(dot(table_in()[...], rows))


def exchange(packed, capacity):
    peers = lax.axis_size("graph") * lax.axis_size("mp")
    parts = packed.reshape(peers, -1, LANES)
    return lax.all_to_all(parts, PEERS, split_axis=0, concat_axis=0, tiled=True).reshape(packed.shape)


def local(
    grid_lat,
    mesh_lat,
    cotangent,
    grid_send,
    g2m_slot,
    g2m_receiver,
    halo_send,
    mesh_sender,
    mesh_receiver,
    *shards,
):
    grid_rows, features = grid_lat.shape
    mesh_rows = mesh_lat.shape[0]
    edges = g2m_slot.shape[0]
    mesh_edges = mesh_sender.shape[0]
    slots, halos = grid_send.size, halo_send.size
    capacity, halo_capacity = grid_send.shape[1], halo_send.shape[1]
    blocks = features // LANES
    enc, finish, arrived, grid_t = start(grid_lat, grid_send, shards)
    slot_t, slot_g, enc_t, enc_g, halo_t, halo_g, sender_t, sender_g, proc_t, proc_g, recv_rows = call(
        tables_kernel,
        [
            shape(slots, edges, BF16),
            shape(edges, slots, BF16),
            shape(mesh_rows, edges, BF16),
            shape(edges, mesh_rows, BF16),
            shape(mesh_rows, halos, BF16),
            shape(halos, mesh_rows, BF16),
            shape(mesh_rows + halos, mesh_edges, BF16),
            shape(mesh_edges, mesh_rows + halos, BF16),
            shape(mesh_rows, mesh_edges, BF16),
            shape(mesh_edges, mesh_rows, BF16),
            shape(edges, features, BF16),
        ],
        mesh_lat,
        g2m_slot.reshape(1, edges),
        g2m_receiver.reshape(1, edges),
        halo_send.T,
        mesh_sender.reshape(1, mesh_edges),
        mesh_receiver.reshape(1, mesh_edges),
    )
    saved = [
        shape(edges, features, BF16),
        shape(edges, features, BF16),
        shape(edges, LANES, F32),
        shape(mesh_rows, features, BF16),
        shape(mesh_rows, features, BF16),
        shape(mesh_rows, LANES, F32),
    ]
    mesh_one, halo_out, slope_e, normed_e, scale_e, slope_n, normed_n, scale_n = call(
        encode_kernel,
        [shape(mesh_rows, features, BF16), free(halos * blocks, LANES, BF16)] + saved,
        recv_rows,
        arrived,
        slot_g,
        WEIGHTS,
        enc_t,
        mesh_lat,
        WEIGHTS,
        halo_g,
        weights=enc,
        flops=3 * 10**9,
    )
    proc, mesh_one = finish(mesh_one)
    halo_in = exchange(halo_out, halo_capacity)
    mesh_two, grad_one, grad_halo = call(
        process_kernel,
        [
            shape(mesh_rows, features, BF16),
            shape(mesh_rows, features, F32),
            free(halos * blocks, LANES, BF16),
        ],
        mesh_one,
        halo_in,
        sender_g,
        proc_g,
        WEIGHTS,
        proc_t,
        WEIGHTS,
        cotangent,
        sender_t,
        weights=proc,
        flops=5 * 10**9,
        scratch=[
            pltpu.VMEM((mesh_edges, features), BF16),
            pltpu.VMEM((mesh_edges, features), BF16),
            pltpu.VMEM((mesh_edges, LANES), F32),
            pltpu.VMEM((mesh_edges, features), BF16),
        ],
    )
    halo_back = exchange(grad_halo, halo_capacity)
    mesh_grad, grad_slots = call(
        decode_kernel,
        [shape(mesh_rows, features, F32), free(slots * blocks, LANES, BF16)],
        halo_back,
        halo_t,
        grad_one,
        slope_n,
        normed_n,
        scale_n,
        WEIGHTS,
        enc_g,
        slope_e,
        normed_e,
        scale_e,
        WEIGHTS,
        slot_t,
        enc_t,
        weights=enc,
        first=1,
        flops=3 * 10**9,
        scratch=[pltpu.VMEM((edges, features), BF16)],
    )
    returned = exchange(grad_slots, capacity)
    (grid_grad,) = call(grid_kernel, [shape(grid_rows, features, F32)], returned, grid_t)
    return (mesh_two, grid_grad, mesh_grad)


def solution(mesh):
    rows = P(AXES, None)
    flat = P(AXES)
    in_specs = (rows,) * 4 + (flat,) * 2 + (rows,) + (flat,) * 2 + (P(None, "mp"), P("mp", None)) * 4
    return jax.shard_map(
        local, mesh=mesh, in_specs=in_specs, out_specs=(rows,) * 3, check_vma=False
    )
```

```python
import jax
import jax.numpy as jnp
from jax import lax
from jax.experimental import pallas as pl
from jax.experimental.pallas import tpu as pltpu
from jax.sharding import PartitionSpec as P

F32 = jnp.float32
BF16 = jnp.bfloat16
LANES = 128
ROWS = 256
FEATURES = 512
AXES = ("groups", "graph", "mp")


def dot(left, right):
    return jnp.dot(left, right, preferred_element_type=F32)


def dot_trans(left, right):
    return lax.dot_general(left, right, (((1,), (1,)), ((), ())), preferred_element_type=F32)


def shape(rows, columns, dtype):
    return jax.ShapeDtypeStruct((rows, columns), dtype)


class Far:
    def __init__(self, array):
        self.array = pltpu.with_memory_space_constraint(array, pltpu.HBM)


class Input:
    def __init__(self, copy, ref):
        self.copy, self.ref = copy, ref

    def __call__(self):
        if self.copy is not None:
            self.copy.wait()
            self.copy = None
        return self.ref


class Output:
    def __init__(self, ref, copy):
        self.ref, self.copy = ref, copy

    def send(self, value=None):
        if value is not None:
            self.ref[...] = value
        if self.copy is not None:
            self.copy.start()


def call(kernel, out_shape, *args, last=(), scratch=(), flops=0):
    groups = [a if isinstance(a, list) else [a] for a in args]
    flat = [a for group in groups for a in group]
    far = [isinstance(a, Far) for a in flat]
    arrays = [a.array if isinstance(a, Far) else a for a in flat]
    count, outs = len(arrays), len(out_shape)

    def body(*refs):
        ins, refs = refs[:count], refs[count:]
        out_refs, refs = refs[:outs], refs[outs:]
        places, refs = list(refs[: sum(far)]), refs[sum(far) :]
        results, refs = list(refs[: len(last)]), refs[len(last) :]
        sem_in, sem_out, refs = refs[0], refs[1], refs[2:]
        inputs = []
        for ref, away in zip(ins, far):
            copy = None
            if away:
                place = places.pop(0)
                copy = pltpu.make_async_copy(ref, place, sem_in.at[len(places)])
                copy.start()
                ref = place
            inputs.append(Input(copy, ref))
        outputs = []
        for i, ref in enumerate(out_refs):
            copy = None
            if i in last:
                place = results.pop(0)
                copy = pltpu.make_async_copy(place, ref, sem_out.at[len(results)])
                ref = place
            outputs.append(Output(ref, copy))
        given = []
        for arg, group in zip(args, groups):
            part, inputs = inputs[: len(group)], inputs[len(group) :]
            given.append(part if isinstance(arg, list) else part[0])
        kernel(*given, *outputs, *refs)
        for output in outputs:
            if output.copy is not None:
                output.copy.wait()

    vmem, hbm = pl.BlockSpec(memory_space=pltpu.VMEM), pl.BlockSpec(memory_space=pl.ANY)
    total = sum(a.size * a.dtype.itemsize for a in arrays)
    return pl.pallas_call(
        body,
        out_shape=out_shape,
        in_specs=[hbm if away else vmem for away in far],
        out_specs=[hbm if i in last else vmem for i in range(outs)],
        scratch_shapes=[pltpu.VMEM(a.shape, a.dtype) for a, away in zip(arrays, far) if away]
        + [pltpu.VMEM(out_shape[i].shape, out_shape[i].dtype) for i in last]
        + [pltpu.SemaphoreType.DMA((max(sum(far), 1),)), pltpu.SemaphoreType.DMA((max(len(last), 1),))]
        + list(scratch),
        name=kernel.__name__,
        cost_estimate=pl.CostEstimate(flops=flops, bytes_accessed=total, transcendentals=0),
        compiler_params=pltpu.CompilerParams(vmem_limit_bytes=24 * 1024 * 1024),
    )(*arrays)


def layers(blocks, which):
    low = which * 3 * FEATURES
    middle = low + 2 * FEATURES
    return (
        jnp.concatenate([block()[:, low:middle] for block in blocks], axis=0),
        jnp.concatenate([block()[:, middle : middle + FEATURES] for block in blocks], axis=0),
    )


def turned(first, select):
    return dot_trans(select, first).astype(BF16)


def prepare_kernel(grid, send, shards, *outs):
    pieces, outs = outs[:2], outs[2:]
    plane = lax.axis_index("groups") * lax.axis_size("graph") + lax.axis_index("graph")
    width = 3 * FEATURES
    for i in range(4):
        out, low = pieces[i // 2], i % 2 * width
        rows = out.ref.shape[0]
        base = plane * rows
        one, two = shards[2 * i](), shards[2 * i + 1]()
        hidden = one.shape[1]
        select = jnp.where(
            lax.broadcasted_iota(jnp.int32, (rows, hidden), 0) + base
            == lax.broadcasted_iota(jnp.int32, (rows, hidden), 1),
            1.0,
            0.0,
        ).astype(BF16)
        out.ref[:, low : low + 2 * FEATURES] = turned(one[...], select)
        out.ref[:, low + 2 * FEATURES : low + width] = two[pl.ds(pl.multiple_of(base, rows), rows), :]
    send_kernel(grid, send, *outs)


def own_kernel(shards, *outs):
    width = 3 * FEATURES
    for i in range(4):
        one, two = shards[2 * i](), shards[2 * i + 1]()
        hidden = one.shape[1]
        select = jnp.where(
            lax.broadcasted_iota(jnp.int32, (hidden, hidden), 0)
            == lax.broadcasted_iota(jnp.int32, (hidden, hidden), 1),
            1.0,
            0.0,
        ).astype(BF16)
        out, low = outs[i // 2], i % 2 * width
        out.ref[:, low : low + 2 * FEATURES] = turned(one[...], select)
        out.ref[:, low + 2 * FEATURES : low + width] = two[...]


def across(x, flip):
    planes = lax.axis_size("groups") * lax.axis_size("graph")
    return lax.ppermute(x, ("groups", "graph"), [(p, p ^ flip) for p in range(planes)])


def spread_along(piece):
    size = lax.axis_size("mp")
    return jnp.concatenate(
        [lax.ppermute(piece, "mp", [(m, (m + s) % size) for m in range(size)]) for s in range(1, size)]
    )


def start(grid_lat, grid_send, shards, tables):
    grid_rows, features = grid_lat.shape
    mp, graph = lax.axis_size("mp"), lax.axis_size("graph")
    step = stride(grid_send.shape[1])
    sent = [shape(grid_rows, mp * graph * step, BF16)] + [shape(graph * step, features, BF16)] * mp
    planes = lax.axis_size("groups") * graph
    hidden = shards[1].shape[0]
    if planes != 8 or mp != 4 or hidden != 128 or features != FEATURES:
        grid_t, *outgoing = call(send_kernel, sent, Far(grid_lat), Far(grid_send.T))
        rows = []
        for i in range(4):
            rows.append(lax.all_gather(shards[2 * i], "mp", axis=1, tiled=True).T)
            rows.append(lax.all_gather(shards[2 * i + 1], "mp", axis=0, tiled=True))
        enc, proc = jnp.concatenate(rows[:4], axis=1), jnp.concatenate(rows[4:], axis=1)
        return [enc], lambda after: ([proc], after), exchange(outgoing, step), grid_t, tables
    far = [Far(s) for s in shards]
    enc_piece, proc_piece, grid_t, *outgoing = call(
        prepare_kernel,
        [shape(hidden // planes, 6 * features, BF16)] * 2 + sent,
        Far(grid_lat),
        Far(grid_send.T),
        far,
    )
    enc_own, proc_own = call(own_kernel, [shape(hidden, 6 * features, BF16)] * 2, far)
    first = spread_along(enc_piece)
    first, enc_own, *tables = lax.optimization_barrier((first, enc_own, *tables))
    second = across(first, 1)
    proc_piece, second = lax.optimization_barrier((proc_piece, second))
    plane = [across(first, flip) for flip in (2, 4, 6)]
    enc = [enc_own, first, second] + plane + [across(block, 1) for block in plane]
    arrived = exchange(outgoing, step)
    first = spread_along(proc_piece)
    first, *plane = lax.optimization_barrier((first, *plane))
    enc[3:6] = plane
    blocks = [first] + [across(first, flip) for flip in (2, 4, 6)]

    def finish(after):
        *tied, after = lax.optimization_barrier((*blocks, after))
        return [proc_own] + tied + [across(block, 1) for block in tied], after

    return enc, finish, arrived, grid_t, tables


def forward(inputs, first, second):
    before = dot_trans(inputs, first)
    logistic = jax.nn.sigmoid(before)
    hidden = (before * logistic).astype(BF16)
    slope = logistic * (1.0 + before * (1.0 - logistic))
    summed = dot(hidden, second)
    centered = summed - jnp.mean(summed, axis=-1, keepdims=True)
    rescale = lax.rsqrt(jnp.mean(centered * centered, axis=-1, keepdims=True) + 1e-05)
    normed = centered * rescale
    return normed, slope.astype(BF16), normed.astype(BF16), rescale


def backward_hidden(incoming, slope, normed, rescale, second):
    normed = normed.astype(F32)
    g_out = (
        incoming
        - jnp.mean(incoming, axis=-1, keepdims=True)
        - normed * jnp.mean(incoming * normed, axis=-1, keepdims=True)
    ) * rescale
    return (dot_trans(g_out.astype(BF16), second) * slope.astype(F32)).astype(BF16)


def table(index_row, count):
    n = index_row.shape[1]
    return jnp.where(lax.broadcasted_iota(jnp.int32, (count, n), 0) == index_row, 1.0, 0.0)


def stride(capacity):
    return max(capacity, 16 // min(lax.axis_size("mp"), lax.axis_size("graph")))


def sent_at(peer, slot, step):
    mp, graph = lax.axis_size("mp"), lax.axis_size("graph")
    shift = (peer % mp + mp - lax.axis_index("mp")) % mp
    return (shift * graph + (peer // mp ^ lax.axis_index("graph"))) * step + slot


def arrived_at(peer, slot, step):
    mp = lax.axis_size("mp")
    shift = (lax.axis_index("mp") + mp - peer % mp) % mp
    return ((peer // mp ^ lax.axis_index("graph")) * mp + shift) * step + slot


def sent_row(index, step):
    width, count = index.shape
    index = index.astype(F32).T
    at = lax.broadcasted_iota(jnp.int32, (count, count * step), 1)
    peer = lax.broadcasted_iota(jnp.int32, (count, count * step), 0)
    row = jnp.zeros(at.shape, F32)
    for slot in range(width):
        row = jnp.where(sent_at(peer, slot, step) == at, index[:, slot : slot + 1] + 1.0, row)
    return jnp.sum(row, axis=0, keepdims=True).astype(jnp.int32) - 1


def stacked(blocks):
    return jnp.concatenate([block()[...] for block in blocks], axis=0)


def split(rows, outs):
    size = rows.shape[0] // len(outs)
    for i, out in enumerate(outs):
        out.ref[...] = rows[i * size : (i + 1) * size, :].astype(BF16)


def send_kernel(grid, send, table_out, *outgoing):
    count = table_out.ref.shape[1]
    one = table(sent_row(send()[...], count // send().shape[1]), grid().shape[0])
    split(dot(one.T.astype(BF16), grid()[...]), outgoing)
    table_out.ref[...] = one.astype(BF16)


def turn_kernel(blocks, *outs):
    rows = stacked(blocks)
    step = rows.shape[0] // (len(blocks) * len(outs))
    for j, out in enumerate(outs):
        row = lax.broadcasted_iota(jnp.int32, (out.ref.shape[0], rows.shape[0]), 0)
        at = lax.broadcasted_iota(jnp.int32, row.shape, 1)
        source = (row // step * len(outs) + j) * step + row % step
        out.ref[...] = dot(jnp.where(at == source, 1.0, 0.0).astype(BF16), rows).astype(BF16)


def tables_kernel(mesh, slot, recv_e, halo, sender, recv_p, *outs):
    mesh_rows = mesh().shape[0]
    peers = halo().shape[1]
    slot_step, halo_step = outs[0].ref.shape[0] // peers, outs[4].ref.shape[1] // peers
    capacity, halo_capacity = slot_step, halo().shape[0]
    slots = slot()[...]
    slots = arrived_at(slots // capacity, slots % capacity, slot_step)
    senders = sender()[...]
    remote = jnp.maximum(senders - mesh_rows, 0)
    remote = arrived_at(remote // halo_capacity, remote % halo_capacity, halo_step)
    senders = jnp.where(senders < mesh_rows, senders, mesh_rows + remote)
    rows = (slots, recv_e()[...], sent_row(halo()[...], halo_step), senders, recv_p()[...])
    for i, row in enumerate(rows):
        scatter, gather = outs[2 * i : 2 * i + 2]
        one = table(row, scatter.ref.shape[0])
        scatter.ref[...] = one.astype(BF16)
        gather.ref[...] = one.T.astype(BF16)
    outs[10].ref[...] = dot(outs[3].ref[...], mesh()[...]).astype(BF16)


def encode_kernel(
    recv_rows, arrived, slot_g, enc_t, mesh, weights, halo_g,
    one_out, slope_e, normed_e, scale_e, slope_n, normed_n, scale_n, *halo_out,
):
    rows_in = stacked(arrived)
    edges = slot_g().shape[0]
    first, second = layers(weights, 0)
    for low in range(0, edges, ROWS):
        rows = pl.ds(low, ROWS)
        sent = dot(slot_g()[rows, :], rows_in).astype(BF16)
        inputs = jnp.concatenate([sent, recv_rows()[rows, :]], axis=1)
        _, slope, normed, rescale = forward(inputs, first, second)
        slope_e.ref[rows, :] = slope
        normed_e.ref[rows, :] = normed
        scale_e.ref[rows, :] = jnp.broadcast_to(rescale, (ROWS, LANES))
    aggregate = dot(enc_t()[...], normed_e.ref[...]).astype(BF16)
    first, second = layers(weights, 1)
    own = mesh()[...]
    normed, slope, rounded, rescale = forward(
        jnp.concatenate([own, aggregate], axis=1), first, second
    )
    one = (own.astype(F32) + normed).astype(BF16)
    one_out.ref[...] = one
    split(dot(halo_g()[...], one), halo_out)
    slope_n.ref[...] = slope
    normed_n.ref[...] = rounded
    scale_n.ref[...] = jnp.broadcast_to(rescale, scale_n.ref.shape)


def process_kernel(
    cotangent_in, one_in, halo, sender_g, proc_g, weights, proc_t, sender_t, two, grad_one, *refs
):
    grad_halo, (slope_p, normed_p, scale_p, ga_p) = refs[:-4], refs[-4:]
    features = FEATURES
    one = one_in()[...]
    mesh_rows = one.shape[0]
    lookup = jnp.concatenate([one, stacked(halo)], axis=0)
    edges = sender_g().shape[0]
    first, second = layers(weights, 0)
    for low in range(0, edges, ROWS):
        rows = pl.ds(low, ROWS)
        sent = dot(sender_g()[rows, :], lookup).astype(BF16)
        got = dot(proc_g()[rows, :], one).astype(BF16)
        _, slope, normed, rescale = forward(jnp.concatenate([sent, got], axis=1), first, second)
        slope_p[rows, :] = slope
        normed_p[rows, :] = normed
        scale_p[rows, :] = jnp.broadcast_to(rescale, (ROWS, LANES))
    aggregate = dot(proc_t()[...], normed_p[...]).astype(BF16)
    first_n, second_n = layers(weights, 1)
    normed, slope, rounded, rescale = forward(
        jnp.concatenate([one, aggregate], axis=1), first_n, second_n
    )
    two.send((one.astype(F32) + normed).astype(BF16))
    cotangent = cotangent_in()[...].astype(F32)
    ga = backward_hidden(cotangent, slope, rounded, rescale, second_n)
    g_q = dot(ga, first_n)
    g_msg = g_q[:, features:].astype(BF16)
    for low in range(0, edges, ROWS):
        rows = pl.ds(low, ROWS)
        incoming = dot(proc_g()[rows, :], g_msg)
        ga_p[rows, :] = backward_hidden(
            incoming, slope_p[rows, :], normed_p[rows, :], scale_p[rows, 0:1], second
        )
    by_send = dot(sender_t()[...], ga_p[...]).astype(BF16)
    g_send = dot(by_send, first[:, :features])
    split(g_send[mesh_rows:, :], grad_halo)
    by_recv = dot(proc_t()[...], ga_p[...]).astype(BF16)
    g_recv = dot(by_recv, first[:, features:])
    grad_one.ref[...] = cotangent + g_q[:, :features] + g_recv + g_send[:mesh_rows, :]


def decode_kernel(
    back, halo_t, grad_in, slope_n, normed_n, scale_n, enc_g, slope_e, normed_e, scale_e,
    weights, slot_t, enc_t, mesh_grad, *refs
):
    grad_slots, ga_e = refs[:-1], refs[-1]
    features = FEATURES
    edges = enc_g().shape[0]
    grad_one = grad_in()[...] + dot(halo_t()[...], stacked(back))
    first_n, second_n = layers(weights, 1)
    ga = backward_hidden(grad_one, slope_n()[...], normed_n()[...], scale_n()[:, 0:1], second_n)
    g_n = dot(ga, first_n)
    g_edge = g_n[:, features:].astype(BF16)
    first, second = layers(weights, 0)
    for low in range(0, edges, ROWS):
        rows = pl.ds(low, ROWS)
        incoming = dot(enc_g()[rows, :], g_edge)
        ga_e[rows, :] = backward_hidden(
            incoming, slope_e()[rows, :], normed_e()[rows, :], scale_e()[rows, 0:1], second
        )
    by_recv = dot(enc_t()[...], ga_e[...]).astype(BF16)
    mesh_grad.send(grad_one + g_n[:, :features] + dot(by_recv, first[:, features:]))
    by_slot = dot(slot_t()[...], ga_e[...]).astype(BF16)
    split(dot(by_slot, first[:, :features]), grad_slots)


def grid_kernel(back, table_in, out):
    out.send(dot(table_in()[...], stacked(back)))


def along(block, shift):
    size = lax.axis_size("mp")
    if shift % size == 0:
        return block
    return lax.ppermute(block, "mp", [(m, (m + shift) % size) for m in range(size)])


def beside(block, flip):
    if flip == 0:
        return block
    return lax.ppermute(block, "graph", [(g, g ^ flip) for g in range(lax.axis_size("graph"))])


def turn(blocks, count, step):
    out = shape(len(blocks) * step, blocks[0].shape[1], BF16)
    return call(turn_kernel, [out] * count, list(blocks))


def exchange(blocks, step):
    blocks = turn([along(b, s) for s, b in enumerate(blocks)], lax.axis_size("graph"), step)
    return [beside(b, t) for t, b in enumerate(blocks)]


def exchange_back(blocks, step):
    blocks = turn([beside(b, t) for t, b in enumerate(blocks)], lax.axis_size("mp"), step)
    return [along(b, -s) for s, b in enumerate(blocks)]


def local(
    grid_lat,
    mesh_lat,
    cotangent,
    grid_send,
    g2m_slot,
    g2m_receiver,
    halo_send,
    mesh_sender,
    mesh_receiver,
    *shards,
):
    grid_rows, features = grid_lat.shape
    mesh_rows = mesh_lat.shape[0]
    edges = g2m_slot.shape[0]
    mesh_edges = mesh_sender.shape[0]
    mp, graph = lax.axis_size("mp"), lax.axis_size("graph")
    step, halo_step = stride(grid_send.shape[1]), stride(halo_send.shape[1])
    slots, halos = mp * graph * step, mp * graph * halo_step
    tables = call(
        tables_kernel,
        [
            shape(slots, edges, BF16),
            shape(edges, slots, BF16),
            shape(mesh_rows, edges, BF16),
            shape(edges, mesh_rows, BF16),
            shape(mesh_rows, halos, BF16),
            shape(halos, mesh_rows, BF16),
            shape(mesh_rows + halos, mesh_edges, BF16),
            shape(mesh_edges, mesh_rows + halos, BF16),
            shape(mesh_rows, mesh_edges, BF16),
            shape(mesh_edges, mesh_rows, BF16),
            shape(edges, features, BF16),
        ],
        Far(mesh_lat),
        Far(g2m_slot.reshape(1, edges)),
        Far(g2m_receiver.reshape(1, edges)),
        Far(halo_send.T),
        Far(mesh_sender.reshape(1, mesh_edges)),
        Far(mesh_receiver.reshape(1, mesh_edges)),
    )
    enc, finish, arrived, grid_t, tables = start(grid_lat, grid_send, shards, tables)
    slot_t, slot_g, enc_t, enc_g, halo_t, halo_g, sender_t, sender_g, proc_t, proc_g, recv_rows = tables
    saved = [
        shape(edges, features, BF16),
        shape(edges, features, BF16),
        shape(edges, LANES, F32),
        shape(mesh_rows, features, BF16),
        shape(mesh_rows, features, BF16),
        shape(mesh_rows, LANES, F32),
    ]
    mesh_one, slope_e, normed_e, scale_e, slope_n, normed_n, scale_n, *halo_out = call(
        encode_kernel,
        [shape(mesh_rows, features, BF16)] + saved + [shape(graph * halo_step, features, BF16)] * mp,
        recv_rows,
        arrived,
        slot_g,
        enc_t,
        Far(mesh_lat),
        enc,
        halo_g,
        flops=3 * 10**9,
    )
    proc, mesh_one = finish(mesh_one)
    halo_in = exchange(halo_out, halo_step)
    mesh_two, grad_one, *grad_halo = call(
        process_kernel,
        [shape(mesh_rows, features, BF16), shape(mesh_rows, features, F32)]
        + [shape(mp * halo_step, features, BF16)] * graph,
        Far(cotangent),
        mesh_one,
        halo_in,
        sender_g,
        proc_g,
        proc,
        proc_t,
        sender_t,
        last=(0,),
        flops=5 * 10**9,
        scratch=[
            pltpu.VMEM((mesh_edges, features), BF16),
            pltpu.VMEM((mesh_edges, features), BF16),
            pltpu.VMEM((mesh_edges, LANES), F32),
            pltpu.VMEM((mesh_edges, features), BF16),
        ],
    )
    halo_back = exchange_back(grad_halo, halo_step)
    mesh_grad, *grad_slots = call(
        decode_kernel,
        [shape(mesh_rows, features, F32)] + [shape(mp * step, features, BF16)] * graph,
        halo_back,
        halo_t,
        grad_one,
        slope_n,
        normed_n,
        scale_n,
        enc_g,
        slope_e,
        normed_e,
        scale_e,
        enc,
        slot_t,
        enc_t,
        last=(0,),
        flops=3 * 10**9,
        scratch=[pltpu.VMEM((edges, features), BF16)],
    )
    returned = exchange_back(grad_slots, step)
    (grid_grad,) = call(
        grid_kernel, [shape(grid_rows, features, F32)], returned, grid_t, last=(0,)
    )
    return (mesh_two, grid_grad, mesh_grad)


def solution(mesh):
    rows = P(AXES, None)
    flat = P(AXES)
    in_specs = (rows,) * 4 + (flat,) * 2 + (rows,) + (flat,) * 2 + (P(None, "mp"), P("mp", None)) * 4
    return jax.shard_map(
        local, mesh=mesh, in_specs=in_specs, out_specs=(rows,) * 3, check_vma=False
    )
```

```python
import jax
import jax.numpy as jnp
from jax import lax
from jax.experimental import pallas as pl
from jax.experimental.pallas import tpu as pltpu
from jax.sharding import PartitionSpec as P

F32 = jnp.float32
BF16 = jnp.bfloat16
LANES = 128
ROWS = 256
FEATURES = 512
AXES = ("groups", "graph", "mp")


def dot(left, right):
    return jnp.dot(left, right, preferred_element_type=F32)


def dot_trans(left, right):
    return lax.dot_general(left, right, (((1,), (1,)), ((), ())), preferred_element_type=F32)


def shape(rows, columns, dtype):
    return jax.ShapeDtypeStruct((rows, columns), dtype)


class Far:
    def __init__(self, array):
        self.array = pltpu.with_memory_space_constraint(array, pltpu.HBM)


class Input:
    def __init__(self, copy, ref):
        self.copy, self.ref = copy, ref

    def __call__(self):
        if self.copy is not None:
            self.copy.wait()
            self.copy = None
        return self.ref


class Output:
    def __init__(self, ref, copy):
        self.ref, self.copy = ref, copy

    def send(self, value=None):
        if value is not None:
            self.ref[...] = value
        if self.copy is not None:
            self.copy.start()


def call(kernel, out_shape, *args, last=(), scratch=(), flops=0):
    groups = [a if isinstance(a, list) else [a] for a in args]
    flat = [a for group in groups for a in group]
    far = [isinstance(a, Far) for a in flat]
    arrays = [a.array if isinstance(a, Far) else a for a in flat]
    count, outs = len(arrays), len(out_shape)

    def body(*refs):
        ins, refs = refs[:count], refs[count:]
        out_refs, refs = refs[:outs], refs[outs:]
        places, refs = list(refs[: sum(far)]), refs[sum(far) :]
        results, refs = list(refs[: len(last)]), refs[len(last) :]
        sem_in, sem_out, refs = refs[0], refs[1], refs[2:]
        inputs = []
        for ref, away in zip(ins, far):
            copy = None
            if away:
                place = places.pop(0)
                copy = pltpu.make_async_copy(ref, place, sem_in.at[len(places)])
                copy.start()
                ref = place
            inputs.append(Input(copy, ref))
        outputs = []
        for i, ref in enumerate(out_refs):
            copy = None
            if i in last:
                place = results.pop(0)
                copy = pltpu.make_async_copy(place, ref, sem_out.at[len(results)])
                ref = place
            outputs.append(Output(ref, copy))
        given = []
        for arg, group in zip(args, groups):
            part, inputs = inputs[: len(group)], inputs[len(group) :]
            given.append(part if isinstance(arg, list) else part[0])
        kernel(*given, *outputs, *refs)
        for output in outputs:
            if output.copy is not None:
                output.copy.wait()

    vmem, hbm = pl.BlockSpec(memory_space=pltpu.VMEM), pl.BlockSpec(memory_space=pl.ANY)
    total = sum(a.size * a.dtype.itemsize for a in arrays)
    return pl.pallas_call(
        body,
        out_shape=out_shape,
        in_specs=[hbm if away else vmem for away in far],
        out_specs=[hbm if i in last else vmem for i in range(outs)],
        scratch_shapes=[pltpu.VMEM(a.shape, a.dtype) for a, away in zip(arrays, far) if away]
        + [pltpu.VMEM(out_shape[i].shape, out_shape[i].dtype) for i in last]
        + [pltpu.SemaphoreType.DMA((max(sum(far), 1),)), pltpu.SemaphoreType.DMA((max(len(last), 1),))]
        + list(scratch),
        name=kernel.__name__,
        cost_estimate=pl.CostEstimate(flops=flops, bytes_accessed=total, transcendentals=0),
        compiler_params=pltpu.CompilerParams(vmem_limit_bytes=24 * 1024 * 1024),
    )(*arrays)


def layers(blocks, which):
    low = which * 3 * FEATURES
    middle = low + 2 * FEATURES
    return (
        jnp.concatenate([block()[:, low:middle] for block in blocks], axis=0),
        jnp.concatenate([block()[:, middle : middle + FEATURES] for block in blocks], axis=0),
    )


def turned(first, select):
    return dot_trans(select, first).astype(BF16)


def prepare_kernel(grid, send, shards, proc_piece, table_out, kept, *messages):
    plane = lax.axis_index("groups") * lax.axis_size("graph") + lax.axis_index("graph")
    width = 3 * FEATURES
    rows = proc_piece.ref.shape[0]
    base = plane * rows
    for i in range(4):
        one, two = shards[2 * i](), shards[2 * i + 1]()
        hidden = one.shape[1]
        select = jnp.where(
            lax.broadcasted_iota(jnp.int32, (rows, hidden), 0) + base
            == lax.broadcasted_iota(jnp.int32, (rows, hidden), 1),
            1.0,
            0.0,
        ).astype(BF16)
        low = i % 2 * width
        first = turned(one[...], select)
        second = two[pl.ds(pl.multiple_of(base, rows), rows), :]
        for out in (proc_piece,) if i // 2 else messages:
            out.ref[:, low : low + 2 * FEATURES] = first
            out.ref[:, low + 2 * FEATURES : low + width] = second
    outgoing = send_rows(grid, send, table_out)
    size = kept.ref.shape[0]
    kept.ref[...] = outgoing[:size, :].astype(BF16)
    for i, out in enumerate(messages):
        out.ref[:, 2 * width :] = outgoing[(i + 1) * size : (i + 2) * size, :].astype(BF16)


def join_kernel(kept, messages, near, block, both):
    width = 6 * FEATURES
    weights = jnp.concatenate([m()[:, :width] for m in messages], axis=0)
    rows = jnp.concatenate([kept()[...]] + [m()[:, width:] for m in messages], axis=0)
    step = rows.shape[0] // 16
    block.ref[...] = weights
    both.ref[:, :width] = weights
    size = near.ref.shape[0]
    for j in range(4):
        moved = dot(turn_table(4, 4, step, j), rows).astype(BF16)
        if j == 0:
            near.ref[...] = moved
        else:
            both.ref[(j - 1) * size : j * size, width:] = moved


def own_kernel(shards, *outs):
    width = 3 * FEATURES
    for i in range(4):
        one, two = shards[2 * i](), shards[2 * i + 1]()
        hidden = one.shape[1]
        select = jnp.where(
            lax.broadcasted_iota(jnp.int32, (hidden, hidden), 0)
            == lax.broadcasted_iota(jnp.int32, (hidden, hidden), 1),
            1.0,
            0.0,
        ).astype(BF16)
        out, low = outs[i // 2], i % 2 * width
        out.ref[:, low : low + 2 * FEATURES] = turned(one[...], select)
        out.ref[:, low + 2 * FEATURES : low + width] = two[...]


def across(x, flip):
    planes = lax.axis_size("groups") * lax.axis_size("graph")
    return lax.ppermute(x, ("groups", "graph"), [(p, p ^ flip) for p in range(planes)])


def start(grid_lat, grid_send, shards, tables):
    grid_rows, features = grid_lat.shape
    mp, graph = lax.axis_size("mp"), lax.axis_size("graph")
    step = stride(grid_send.shape[1])
    sent = [shape(grid_rows, mp * graph * step, BF16)] + [shape(graph * step, features, BF16)] * mp
    planes = lax.axis_size("groups") * graph
    hidden = shards[1].shape[0]
    if planes != 8 or mp != 4 or hidden != 128 or features != FEATURES:
        grid_t, *outgoing = call(send_kernel, sent, Far(grid_lat), Far(grid_send.T))
        rows = []
        for i in range(4):
            rows.append(lax.all_gather(shards[2 * i], "mp", axis=1, tiled=True).T)
            rows.append(lax.all_gather(shards[2 * i + 1], "mp", axis=0, tiled=True))
        enc, proc = jnp.concatenate(rows[:4], axis=1), jnp.concatenate(rows[4:], axis=1)
        arrived = exchange(outgoing, step)
        return [enc], lambda one, moved: [proc], arrived, grid_t, tables
    far = [Far(s) for s in shards]
    piece = hidden // planes
    width = 6 * features
    proc_piece, grid_t, kept, *messages = call(
        prepare_kernel,
        [shape(piece, width, BF16)] + sent[:2] + [shape(piece, width + features, BF16)] * 3,
        Far(grid_lat),
        Far(grid_send.T),
        far,
    )
    enc_own, proc_own = call(own_kernel, [shape(hidden, width, BF16)] * 2, far)
    messages = [along(m, i + 1) for i, m in enumerate(messages)]
    kept, enc_own, *tables = lax.optimization_barrier((kept, enc_own, *tables))
    rows = mp * step
    near, first, both = call(
        join_kernel,
        [shape(rows, features, BF16), shape(3 * piece, width, BF16), shape(3 * rows, width + features, BF16)],
        kept,
        messages,
    )
    core, x, y = across(both, 1), across(both, 2), across(first, 4)
    proc_piece, _ = lax.optimization_barrier((proc_piece, core))
    low, high = relay(x, y)
    x_core, y_core = across(x, 1), across(y, 1)
    parts = [along(proc_piece, s) for s in (1, 2, 3)]
    *parts, _, _ = lax.optimization_barrier((*parts, low, high))
    far_corner = jnp.concatenate([low, high], axis=1)
    enc = [enc_own, first, core, x, y, x_core, y_core, far_corner, across(far_corner, 1)]
    arrived = [near, core, x, x_core]
    proc_first = jnp.concatenate(parts)
    proc_core, proc_x, proc_y = [across(proc_first, flip) for flip in (1, 2, 4)]

    def finish(one, moved):
        x, y, _ = lax.optimization_barrier((proc_x, proc_y, one))
        low, high = relay(x, y)
        x, y, *_ = lax.optimization_barrier((x, y, *moved))
        corner = jnp.concatenate([low, high], axis=1)
        blocks = [proc_own, proc_first, proc_core, x, y, across(x, 1), across(y, 1)]
        return blocks + [corner, across(corner, 1)]

    return enc, finish, arrived, grid_t, tables


def relay(x, y):
    half = 3 * FEATURES
    return across(x[:, :half], 4), across(y[:, half : 2 * half], 2)


def forward(inputs, first, second):
    before = dot_trans(inputs, first)
    logistic = jax.nn.sigmoid(before)
    hidden = (before * logistic).astype(BF16)
    slope = logistic * (1.0 + before * (1.0 - logistic))
    summed = dot(hidden, second)
    centered = summed - jnp.mean(summed, axis=-1, keepdims=True)
    rescale = lax.rsqrt(jnp.mean(centered * centered, axis=-1, keepdims=True) + 1e-05)
    normed = centered * rescale
    return normed, slope.astype(BF16), normed.astype(BF16), rescale


def backward_hidden(incoming, slope, normed, rescale, second):
    normed = normed.astype(F32)
    g_out = (
        incoming
        - jnp.mean(incoming, axis=-1, keepdims=True)
        - normed * jnp.mean(incoming * normed, axis=-1, keepdims=True)
    ) * rescale
    return (dot_trans(g_out.astype(BF16), second) * slope.astype(F32)).astype(BF16)


def table(index_row, count):
    n = index_row.shape[1]
    return jnp.where(lax.broadcasted_iota(jnp.int32, (count, n), 0) == index_row, 1.0, 0.0)


def stride(capacity):
    return max(capacity, 16 // min(lax.axis_size("mp"), lax.axis_size("graph")))


def sent_at(peer, slot, step):
    mp, graph = lax.axis_size("mp"), lax.axis_size("graph")
    shift = (peer % mp + mp - lax.axis_index("mp")) % mp
    return (shift * graph + (peer // mp ^ lax.axis_index("graph"))) * step + slot


def arrived_at(peer, slot, step):
    mp = lax.axis_size("mp")
    shift = (lax.axis_index("mp") + mp - peer % mp) % mp
    return ((peer // mp ^ lax.axis_index("graph")) * mp + shift) * step + slot


def sent_row(index, step):
    width, count = index.shape
    index = index.astype(F32).T
    at = lax.broadcasted_iota(jnp.int32, (count, count * step), 1)
    peer = lax.broadcasted_iota(jnp.int32, (count, count * step), 0)
    row = jnp.zeros(at.shape, F32)
    for slot in range(width):
        row = jnp.where(sent_at(peer, slot, step) == at, index[:, slot : slot + 1] + 1.0, row)
    return jnp.sum(row, axis=0, keepdims=True).astype(jnp.int32) - 1


def stacked(blocks):
    return jnp.concatenate([block()[...] for block in blocks], axis=0)


def split(rows, outs):
    size = rows.shape[0] // len(outs)
    for i, out in enumerate(outs):
        out.ref[...] = rows[i * size : (i + 1) * size, :].astype(BF16)


def send_rows(grid, send, table_out):
    count = table_out.ref.shape[1]
    one = table(sent_row(send()[...], count // send().shape[1]), grid().shape[0])
    table_out.ref[...] = one.astype(BF16)
    return dot(one.T.astype(BF16), grid()[...])


def send_kernel(grid, send, table_out, *outgoing):
    split(send_rows(grid, send, table_out), outgoing)


def turn_table(sources, targets, step, j):
    row = lax.broadcasted_iota(jnp.int32, (sources * step, sources * targets * step), 0)
    at = lax.broadcasted_iota(jnp.int32, row.shape, 1)
    source = (row // step * targets + j) * step + row % step
    return jnp.where(at == source, 1.0, 0.0).astype(BF16)


def turn_kernel(blocks, *outs):
    rows = stacked(blocks)
    step = rows.shape[0] // (len(blocks) * len(outs))
    for j, out in enumerate(outs):
        out.ref[...] = dot(turn_table(len(blocks), len(outs), step, j), rows).astype(BF16)


def tables_kernel(mesh, slot, recv_e, halo, sender, recv_p, *outs):
    mesh_rows = mesh().shape[0]
    peers = halo().shape[1]
    slot_step, halo_step = outs[0].ref.shape[0] // peers, outs[4].ref.shape[1] // peers
    capacity, halo_capacity = slot_step, halo().shape[0]
    slots = slot()[...]
    slots = arrived_at(slots // capacity, slots % capacity, slot_step)
    senders = sender()[...]
    remote = jnp.maximum(senders - mesh_rows, 0)
    remote = arrived_at(remote // halo_capacity, remote % halo_capacity, halo_step)
    senders = jnp.where(senders < mesh_rows, senders, mesh_rows + remote)
    rows = (slots, recv_e()[...], sent_row(halo()[...], halo_step), senders, recv_p()[...])
    for i, row in enumerate(rows):
        scatter, gather = outs[2 * i : 2 * i + 2]
        one = table(row, scatter.ref.shape[0])
        scatter.ref[...] = one.astype(BF16)
        gather.ref[...] = one.T.astype(BF16)
    outs[10].ref[...] = dot(outs[3].ref[...], mesh()[...]).astype(BF16)


def arrived_rows(blocks):
    size = blocks[0]().shape[0]
    rows = [blocks[0]()[...]]
    for t, block in enumerate(blocks[1:]):
        if block().shape[1] == FEATURES:
            rows.append(block()[...])
        else:
            rows.append(block()[t * size : (t + 1) * size, 6 * FEATURES :])
    return jnp.concatenate(rows, axis=0)


def encode_kernel(
    recv_rows, arrived, slot_g, enc_t, mesh, weights, halo_g,
    one_out, slope_e, normed_e, scale_e, slope_n, normed_n, scale_n, *halo_out,
):
    rows_in = arrived_rows(arrived)
    edges = slot_g().shape[0]
    first, second = layers(weights, 0)
    for low in range(0, edges, ROWS):
        rows = pl.ds(low, ROWS)
        sent = dot(slot_g()[rows, :], rows_in).astype(BF16)
        inputs = jnp.concatenate([sent, recv_rows()[rows, :]], axis=1)
        _, slope, normed, rescale = forward(inputs, first, second)
        slope_e.ref[rows, :] = slope
        normed_e.ref[rows, :] = normed
        scale_e.ref[rows, :] = jnp.broadcast_to(rescale, (ROWS, LANES))
    aggregate = dot(enc_t()[...], normed_e.ref[...]).astype(BF16)
    first, second = layers(weights, 1)
    own = mesh()[...]
    normed, slope, rounded, rescale = forward(
        jnp.concatenate([own, aggregate], axis=1), first, second
    )
    one = (own.astype(F32) + normed).astype(BF16)
    one_out.ref[...] = one
    split(dot(halo_g()[...], one), halo_out)
    slope_n.ref[...] = slope
    normed_n.ref[...] = rounded
    scale_n.ref[...] = jnp.broadcast_to(rescale, scale_n.ref.shape)


def process_kernel(
    cotangent_in, one_in, halo, sender_g, proc_g, weights, proc_t, sender_t, two, grad_one, *refs
):
    grad_halo, (slope_p, normed_p, scale_p, ga_p) = refs[:-4], refs[-4:]
    features = FEATURES
    one = one_in()[...]
    mesh_rows = one.shape[0]
    lookup = jnp.concatenate([one, stacked(halo)], axis=0)
    edges = sender_g().shape[0]
    first, second = layers(weights, 0)
    for low in range(0, edges, ROWS):
        rows = pl.ds(low, ROWS)
        sent = dot(sender_g()[rows, :], lookup).astype(BF16)
        got = dot(proc_g()[rows, :], one).astype(BF16)
        _, slope, normed, rescale = forward(jnp.concatenate([sent, got], axis=1), first, second)
        slope_p[rows, :] = slope
        normed_p[rows, :] = normed
        scale_p[rows, :] = jnp.broadcast_to(rescale, (ROWS, LANES))
    aggregate = dot(proc_t()[...], normed_p[...]).astype(BF16)
    first_n, second_n = layers(weights, 1)
    normed, slope, rounded, rescale = forward(
        jnp.concatenate([one, aggregate], axis=1), first_n, second_n
    )
    two.send((one.astype(F32) + normed).astype(BF16))
    cotangent = cotangent_in()[...].astype(F32)
    ga = backward_hidden(cotangent, slope, rounded, rescale, second_n)
    g_q = dot(ga, first_n)
    g_msg = g_q[:, features:].astype(BF16)
    for low in range(0, edges, ROWS):
        rows = pl.ds(low, ROWS)
        incoming = dot(proc_g()[rows, :], g_msg)
        ga_p[rows, :] = backward_hidden(
            incoming, slope_p[rows, :], normed_p[rows, :], scale_p[rows, 0:1], second
        )
    by_send = dot(sender_t()[...], ga_p[...]).astype(BF16)
    g_send = dot(by_send, first[:, :features])
    split(g_send[mesh_rows:, :], grad_halo)
    by_recv = dot(proc_t()[...], ga_p[...]).astype(BF16)
    g_recv = dot(by_recv, first[:, features:])
    grad_one.ref[...] = cotangent + g_q[:, :features] + g_recv + g_send[:mesh_rows, :]


def decode_kernel(
    back, halo_t, grad_in, slope_n, normed_n, scale_n, enc_g, slope_e, normed_e, scale_e,
    weights, slot_t, enc_t, mesh_grad, *refs
):
    grad_slots, ga_e = refs[:-1], refs[-1]
    features = FEATURES
    edges = enc_g().shape[0]
    grad_one = grad_in()[...] + dot(halo_t()[...], stacked(back))
    first_n, second_n = layers(weights, 1)
    ga = backward_hidden(grad_one, slope_n()[...], normed_n()[...], scale_n()[:, 0:1], second_n)
    g_n = dot(ga, first_n)
    g_edge = g_n[:, features:].astype(BF16)
    first, second = layers(weights, 0)
    for low in range(0, edges, ROWS):
        rows = pl.ds(low, ROWS)
        incoming = dot(enc_g()[rows, :], g_edge)
        ga_e[rows, :] = backward_hidden(
            incoming, slope_e()[rows, :], normed_e()[rows, :], scale_e()[rows, 0:1], second
        )
    by_recv = dot(enc_t()[...], ga_e[...]).astype(BF16)
    mesh_grad.send(grad_one + g_n[:, :features] + dot(by_recv, first[:, features:]))
    by_slot = dot(slot_t()[...], ga_e[...]).astype(BF16)
    split(dot(by_slot, first[:, :features]), grad_slots)


def grid_kernel(back, table_in, out):
    out.send(dot(table_in()[...], stacked(back)))


def along(block, shift):
    size = lax.axis_size("mp")
    if shift % size == 0:
        return block
    return lax.ppermute(block, "mp", [(m, (m + shift) % size) for m in range(size)])


def beside(block, flip):
    if flip == 0:
        return block
    return lax.ppermute(block, "graph", [(g, g ^ flip) for g in range(lax.axis_size("graph"))])


def turn(blocks, count, step):
    out = shape(len(blocks) * step, blocks[0].shape[1], BF16)
    return call(turn_kernel, [out] * count, list(blocks))


def exchange(blocks, step):
    return second_level(first_level(blocks, step))


def first_level(blocks, step):
    return turn([along(b, s) for s, b in enumerate(blocks)], lax.axis_size("graph"), step)


def second_level(blocks):
    return [beside(b, t) for t, b in enumerate(blocks)]


def exchange_back(blocks, step):
    blocks = turn([beside(b, t) for t, b in enumerate(blocks)], lax.axis_size("mp"), step)
    return [along(b, -s) for s, b in enumerate(blocks)]


def local(
    grid_lat,
    mesh_lat,
    cotangent,
    grid_send,
    g2m_slot,
    g2m_receiver,
    halo_send,
    mesh_sender,
    mesh_receiver,
    *shards,
):
    grid_rows, features = grid_lat.shape
    mesh_rows = mesh_lat.shape[0]
    edges = g2m_slot.shape[0]
    mesh_edges = mesh_sender.shape[0]
    mp, graph = lax.axis_size("mp"), lax.axis_size("graph")
    step, halo_step = stride(grid_send.shape[1]), stride(halo_send.shape[1])
    slots, halos = mp * graph * step, mp * graph * halo_step
    tables = call(
        tables_kernel,
        [
            shape(slots, edges, BF16),
            shape(edges, slots, BF16),
            shape(mesh_rows, edges, BF16),
            shape(edges, mesh_rows, BF16),
            shape(mesh_rows, halos, BF16),
            shape(halos, mesh_rows, BF16),
            shape(mesh_rows + halos, mesh_edges, BF16),
            shape(mesh_edges, mesh_rows + halos, BF16),
            shape(mesh_rows, mesh_edges, BF16),
            shape(mesh_edges, mesh_rows, BF16),
            shape(edges, features, BF16),
        ],
        Far(mesh_lat),
        Far(g2m_slot.reshape(1, edges)),
        Far(g2m_receiver.reshape(1, edges)),
        Far(halo_send.T),
        Far(mesh_sender.reshape(1, mesh_edges)),
        Far(mesh_receiver.reshape(1, mesh_edges)),
    )
    enc, finish, arrived, grid_t, tables = start(grid_lat, grid_send, shards, tables)
    slot_t, slot_g, enc_t, enc_g, halo_t, halo_g, sender_t, sender_g, proc_t, proc_g, recv_rows = tables
    saved = [
        shape(edges, features, BF16),
        shape(edges, features, BF16),
        shape(edges, LANES, F32),
        shape(mesh_rows, features, BF16),
        shape(mesh_rows, features, BF16),
        shape(mesh_rows, LANES, F32),
    ]
    mesh_one, slope_e, normed_e, scale_e, slope_n, normed_n, scale_n, *halo_out = call(
        encode_kernel,
        [shape(mesh_rows, features, BF16)] + saved + [shape(graph * halo_step, features, BF16)] * mp,
        recv_rows,
        arrived,
        slot_g,
        enc_t,
        Far(mesh_lat),
        enc,
        halo_g,
        flops=3 * 10**9,
    )
    moved = first_level(halo_out, halo_step)
    proc = finish(mesh_one, moved)
    halo_in = second_level(moved)
    mesh_two, grad_one, *grad_halo = call(
        process_kernel,
        [shape(mesh_rows, features, BF16), shape(mesh_rows, features, F32)]
        + [shape(mp * halo_step, features, BF16)] * graph,
        Far(cotangent),
        mesh_one,
        halo_in,
        sender_g,
        proc_g,
        proc,
        proc_t,
        sender_t,
        last=(0,),
        flops=5 * 10**9,
        scratch=[
            pltpu.VMEM((mesh_edges, features), BF16),
            pltpu.VMEM((mesh_edges, features), BF16),
            pltpu.VMEM((mesh_edges, LANES), F32),
            pltpu.VMEM((mesh_edges, features), BF16),
        ],
    )
    halo_back = exchange_back(grad_halo, halo_step)
    mesh_grad, *grad_slots = call(
        decode_kernel,
        [shape(mesh_rows, features, F32)] + [shape(mp * step, features, BF16)] * graph,
        halo_back,
        halo_t,
        grad_one,
        slope_n,
        normed_n,
        scale_n,
        enc_g,
        slope_e,
        normed_e,
        scale_e,
        enc,
        slot_t,
        enc_t,
        last=(0,),
        flops=3 * 10**9,
        scratch=[pltpu.VMEM((edges, features), BF16)],
    )
    returned = exchange_back(grad_slots, step)
    (grid_grad,) = call(
        grid_kernel, [shape(grid_rows, features, F32)], returned, grid_t, last=(0,)
    )
    return (mesh_two, grid_grad, mesh_grad)


def solution(mesh):
    rows = P(AXES, None)
    flat = P(AXES)
    in_specs = (rows,) * 4 + (flat,) * 2 + (rows,) + (flat,) * 2 + (P(None, "mp"), P("mp", None)) * 4
    return jax.shard_map(
        local, mesh=mesh, in_specs=in_specs, out_specs=(rows,) * 3, check_vma=False
    )
```

```python
import jax
import jax.numpy as jnp
from jax import lax
from jax.experimental import pallas as pl
from jax.experimental.pallas import tpu as pltpu
from jax.sharding import PartitionSpec as P

F32 = jnp.float32
BF16 = jnp.bfloat16
LANES = 128
ROWS = 256
FEATURES = 512
AXES = ("groups", "graph", "mp")


def dot(left, right):
    return jnp.dot(left, right, preferred_element_type=F32)


def dot_trans(left, right):
    return lax.dot_general(left, right, (((1,), (1,)), ((), ())), preferred_element_type=F32)


def shape(rows, columns, dtype):
    return jax.ShapeDtypeStruct((rows, columns), dtype)


class Far:
    def __init__(self, array):
        self.array = pltpu.with_memory_space_constraint(array, pltpu.HBM)


class Input:
    def __init__(self, copy, ref):
        self.copy, self.ref = copy, ref

    def __call__(self):
        if self.copy is not None:
            self.copy.wait()
            self.copy = None
        return self.ref


class Output:
    def __init__(self, ref, copy):
        self.ref, self.copy = ref, copy

    def send(self, value=None):
        if value is not None:
            self.ref[...] = value
        if self.copy is not None:
            self.copy.start()


def call(kernel, out_shape, *args, last=(), scratch=(), flops=0):
    groups = [a if isinstance(a, list) else [a] for a in args]
    flat = [a for group in groups for a in group]
    far = [isinstance(a, Far) for a in flat]
    arrays = [a.array if isinstance(a, Far) else a for a in flat]
    count, outs = len(arrays), len(out_shape)

    def body(*refs):
        ins, refs = refs[:count], refs[count:]
        out_refs, refs = refs[:outs], refs[outs:]
        places, refs = list(refs[: sum(far)]), refs[sum(far) :]
        results, refs = list(refs[: len(last)]), refs[len(last) :]
        sem_in, sem_out, refs = refs[0], refs[1], refs[2:]
        inputs = []
        for ref, away in zip(ins, far):
            copy = None
            if away:
                place = places.pop(0)
                copy = pltpu.make_async_copy(ref, place, sem_in.at[len(places)])
                copy.start()
                ref = place
            inputs.append(Input(copy, ref))
        outputs = []
        for i, ref in enumerate(out_refs):
            copy = None
            if i in last:
                place = results.pop(0)
                copy = pltpu.make_async_copy(place, ref, sem_out.at[len(results)])
                ref = place
            outputs.append(Output(ref, copy))
        given = []
        for arg, group in zip(args, groups):
            part, inputs = inputs[: len(group)], inputs[len(group) :]
            given.append(part if isinstance(arg, list) else part[0])
        kernel(*given, *outputs, *refs)
        for output in outputs:
            if output.copy is not None:
                output.copy.wait()

    vmem, hbm = pl.BlockSpec(memory_space=pltpu.VMEM), pl.BlockSpec(memory_space=pl.ANY)
    total = sum(a.size * a.dtype.itemsize for a in arrays)
    return pl.pallas_call(
        body,
        out_shape=out_shape,
        in_specs=[hbm if away else vmem for away in far],
        out_specs=[hbm if i in last else vmem for i in range(outs)],
        scratch_shapes=[pltpu.VMEM(a.shape, a.dtype) for a, away in zip(arrays, far) if away]
        + [pltpu.VMEM(out_shape[i].shape, out_shape[i].dtype) for i in last]
        + [pltpu.SemaphoreType.DMA((max(sum(far), 1),)), pltpu.SemaphoreType.DMA((max(len(last), 1),))]
        + list(scratch),
        name=kernel.__name__,
        cost_estimate=pl.CostEstimate(flops=flops, bytes_accessed=total, transcendentals=0),
        compiler_params=pltpu.CompilerParams(vmem_limit_bytes=24 * 1024 * 1024),
    )(*arrays)


def layers(blocks, which):
    low = which * 3 * FEATURES
    middle = low + 2 * FEATURES
    return (
        jnp.concatenate([block()[:, low:middle] for block in blocks], axis=0),
        jnp.concatenate([block()[:, middle : middle + FEATURES] for block in blocks], axis=0),
    )


def turned(first, select):
    return dot_trans(select, first).astype(BF16)


def prepare_kernel(grid, send, shards, proc_piece, table_out, kept, *messages):
    plane = lax.axis_index("groups") * lax.axis_size("graph") + lax.axis_index("graph")
    width = 3 * FEATURES
    rows = proc_piece.ref.shape[0]
    base = plane * rows
    for i in range(4):
        one, two = shards[2 * i](), shards[2 * i + 1]()
        hidden = one.shape[1]
        select = jnp.where(
            lax.broadcasted_iota(jnp.int32, (rows, hidden), 0) + base
            == lax.broadcasted_iota(jnp.int32, (rows, hidden), 1),
            1.0,
            0.0,
        ).astype(BF16)
        low = i % 2 * width
        first = turned(one[...], select)
        second = two[pl.ds(pl.multiple_of(base, rows), rows), :]
        for out in (proc_piece,) if i // 2 else messages:
            out.ref[:, low : low + 2 * FEATURES] = first
            out.ref[:, low + 2 * FEATURES : low + width] = second
    outgoing = send_rows(grid, send, table_out)
    size = kept.ref.shape[0]
    kept.ref[...] = outgoing[:size, :].astype(BF16)
    for i, out in enumerate(messages):
        out.ref[:, 2 * width :] = outgoing[(i + 1) * size : (i + 2) * size, :].astype(BF16)


def join_kernel(kept, messages, near, block, both):
    width = 6 * FEATURES
    weights = jnp.concatenate([m()[:, :width] for m in messages], axis=0)
    rows = jnp.concatenate([kept()[...]] + [m()[:, width:] for m in messages], axis=0)
    step = rows.shape[0] // 16
    block.ref[...] = weights
    both.ref[:, :width] = weights
    size = near.ref.shape[0]
    for j in range(4):
        moved = dot(turn_table(4, 4, step, j), rows).astype(BF16)
        if j == 0:
            near.ref[...] = moved
        else:
            both.ref[(j - 1) * size : j * size, width:] = moved


def own_kernel(shards, *outs):
    width = 3 * FEATURES
    for i in range(4):
        one, two = shards[2 * i](), shards[2 * i + 1]()
        hidden = one.shape[1]
        select = jnp.where(
            lax.broadcasted_iota(jnp.int32, (hidden, hidden), 0)
            == lax.broadcasted_iota(jnp.int32, (hidden, hidden), 1),
            1.0,
            0.0,
        ).astype(BF16)
        out, low = outs[i // 2], i % 2 * width
        out.ref[:, low : low + 2 * FEATURES] = turned(one[...], select)
        out.ref[:, low + 2 * FEATURES : low + width] = two[...]


def across(x, flip):
    planes = lax.axis_size("groups") * lax.axis_size("graph")
    return lax.ppermute(x, ("groups", "graph"), [(p, p ^ flip) for p in range(planes)])


def start(grid_lat, grid_send, shards, tables):
    grid_rows, features = grid_lat.shape
    mp, graph = lax.axis_size("mp"), lax.axis_size("graph")
    step = stride(grid_send.shape[1])
    sent = [shape(grid_rows, mp * graph * step, BF16)] + [shape(graph * step, features, BF16)] * mp
    planes = lax.axis_size("groups") * graph
    hidden = shards[1].shape[0]
    if planes != 8 or mp != 4 or hidden != 128 or features != FEATURES:
        grid_t, *outgoing = call(send_kernel, sent, Far(grid_lat), Far(grid_send.T))
        rows = []
        for i in range(4):
            rows.append(lax.all_gather(shards[2 * i], "mp", axis=1, tiled=True).T)
            rows.append(lax.all_gather(shards[2 * i + 1], "mp", axis=0, tiled=True))
        enc, proc = jnp.concatenate(rows[:4], axis=1), jnp.concatenate(rows[4:], axis=1)
        arrived = exchange(outgoing, step)
        return [enc], lambda moved: [proc], arrived, grid_t, tables
    far = [Far(s) for s in shards]
    piece = hidden // planes
    width = 6 * features
    proc_piece, grid_t, kept, *messages = call(
        prepare_kernel,
        [shape(piece, width, BF16)] + sent[:2] + [shape(piece, width + features, BF16)] * 3,
        Far(grid_lat),
        Far(grid_send.T),
        far,
    )
    enc_own, proc_own = call(own_kernel, [shape(hidden, width, BF16)] * 2, far)
    messages = [along(m, i + 1) for i, m in enumerate(messages)]
    kept, enc_own, *tables = lax.optimization_barrier((kept, enc_own, *tables))
    rows = mp * step
    near, first, both = call(
        join_kernel,
        [shape(rows, features, BF16), shape(3 * piece, width, BF16), shape(3 * rows, width + features, BF16)],
        kept,
        messages,
    )
    x, y, corner, core = across(both, 2), across(first, 4), across(first, 6), across(both, 1)
    proc_piece, _ = lax.optimization_barrier((proc_piece, core))
    x_core = across(x, 1)
    enc = [enc_own, first, core, x, y, corner, x_core, across(y, 1), across(corner, 1)]
    arrived = [near, core, x, x_core]
    beside_me = lax.ppermute(proc_piece, "mp", [(m, m ^ 1) for m in range(mp)])
    pair = jnp.concatenate([proc_piece, beside_me])
    others = lax.ppermute(pair, "mp", [(m, m ^ 2) for m in range(mp)])
    proc_first = jnp.concatenate([beside_me, others])
    proc_first, *_ = lax.optimization_barrier((proc_first, x, y, corner))
    plane = [across(proc_first, flip) for flip in (2, 4, 6)]
    proc = [proc_own, proc_first, across(proc_first, 1)] + plane

    def finish(moved):
        tied, *_ = lax.optimization_barrier((jnp.concatenate(plane), *moved))
        return proc + [across(tied, 1)]

    return enc, finish, arrived, grid_t, tables


def forward(inputs, first, second):
    before = dot_trans(inputs, first)
    logistic = jax.nn.sigmoid(before)
    hidden = (before * logistic).astype(BF16)
    slope = logistic * (1.0 + before * (1.0 - logistic))
    summed = dot(hidden, second)
    centered = summed - jnp.mean(summed, axis=-1, keepdims=True)
    rescale = lax.rsqrt(jnp.mean(centered * centered, axis=-1, keepdims=True) + 1e-05)
    normed = centered * rescale
    return normed, slope.astype(BF16), normed.astype(BF16), rescale


def backward_hidden(incoming, slope, normed, rescale, second):
    normed = normed.astype(F32)
    g_out = (
        incoming
        - jnp.mean(incoming, axis=-1, keepdims=True)
        - normed * jnp.mean(incoming * normed, axis=-1, keepdims=True)
    ) * rescale
    return (dot_trans(g_out.astype(BF16), second) * slope.astype(F32)).astype(BF16)


def table(index_row, count):
    n = index_row.shape[1]
    return jnp.where(lax.broadcasted_iota(jnp.int32, (count, n), 0) == index_row, 1.0, 0.0)


def stride(capacity):
    return max(capacity, 16 // min(lax.axis_size("mp"), lax.axis_size("graph")))


def sent_at(peer, slot, step):
    mp, graph = lax.axis_size("mp"), lax.axis_size("graph")
    shift = (peer % mp + mp - lax.axis_index("mp")) % mp
    return (shift * graph + (peer // mp ^ lax.axis_index("graph"))) * step + slot


def arrived_at(peer, slot, step):
    mp = lax.axis_size("mp")
    shift = (lax.axis_index("mp") + mp - peer % mp) % mp
    return ((peer // mp ^ lax.axis_index("graph")) * mp + shift) * step + slot


def sent_row(index, step):
    width, count = index.shape
    index = index.astype(F32).T
    at = lax.broadcasted_iota(jnp.int32, (count, count * step), 1)
    peer = lax.broadcasted_iota(jnp.int32, (count, count * step), 0)
    row = jnp.zeros(at.shape, F32)
    for slot in range(width):
        row = jnp.where(sent_at(peer, slot, step) == at, index[:, slot : slot + 1] + 1.0, row)
    return jnp.sum(row, axis=0, keepdims=True).astype(jnp.int32) - 1


def stacked(blocks):
    return jnp.concatenate([block()[...] for block in blocks], axis=0)


def split(rows, outs):
    size = rows.shape[0] // len(outs)
    for i, out in enumerate(outs):
        out.ref[...] = rows[i * size : (i + 1) * size, :].astype(BF16)


def send_rows(grid, send, table_out):
    count = table_out.ref.shape[1]
    one = table(sent_row(send()[...], count // send().shape[1]), grid().shape[0])
    table_out.ref[...] = one.astype(BF16)
    return dot(one.T.astype(BF16), grid()[...])


def send_kernel(grid, send, table_out, *outgoing):
    split(send_rows(grid, send, table_out), outgoing)


def turn_table(sources, targets, step, j):
    row = lax.broadcasted_iota(jnp.int32, (sources * step, sources * targets * step), 0)
    at = lax.broadcasted_iota(jnp.int32, row.shape, 1)
    source = (row // step * targets + j) * step + row % step
    return jnp.where(at == source, 1.0, 0.0).astype(BF16)


def turn_kernel(blocks, *outs):
    rows = stacked(blocks)
    step = rows.shape[0] // (len(blocks) * len(outs))
    for j, out in enumerate(outs):
        out.ref[...] = dot(turn_table(len(blocks), len(outs), step, j), rows).astype(BF16)


def tables_kernel(mesh, slot, recv_e, halo, sender, recv_p, *outs):
    mesh_rows = mesh().shape[0]
    peers = halo().shape[1]
    slot_step, halo_step = outs[0].ref.shape[0] // peers, outs[4].ref.shape[1] // peers
    capacity, halo_capacity = slot_step, halo().shape[0]
    slots = slot()[...]
    slots = arrived_at(slots // capacity, slots % capacity, slot_step)
    senders = sender()[...]
    remote = jnp.maximum(senders - mesh_rows, 0)
    remote = arrived_at(remote // halo_capacity, remote % halo_capacity, halo_step)
    senders = jnp.where(senders < mesh_rows, senders, mesh_rows + remote)
    rows = (slots, recv_e()[...], sent_row(halo()[...], halo_step), senders, recv_p()[...])
    for i, row in enumerate(rows):
        scatter, gather = outs[2 * i : 2 * i + 2]
        one = table(row, scatter.ref.shape[0])
        scatter.ref[...] = one.astype(BF16)
        gather.ref[...] = one.T.astype(BF16)
    outs[10].ref[...] = dot(outs[3].ref[...], mesh()[...]).astype(BF16)


def arrived_rows(blocks):
    size = blocks[0]().shape[0]
    rows = [blocks[0]()[...]]
    for t, block in enumerate(blocks[1:]):
        if block().shape[1] == FEATURES:
            rows.append(block()[...])
        else:
            rows.append(block()[t * size : (t + 1) * size, 6 * FEATURES :])
    return jnp.concatenate(rows, axis=0)


def encode_kernel(
    recv_rows, arrived, slot_g, enc_t, mesh, weights, halo_g,
    one_out, slope_e, normed_e, scale_e, slope_n, normed_n, scale_n, *halo_out,
):
    rows_in = arrived_rows(arrived)
    edges = slot_g().shape[0]
    first, second = layers(weights, 0)
    for low in range(0, edges, ROWS):
        rows = pl.ds(low, ROWS)
        sent = dot(slot_g()[rows, :], rows_in).astype(BF16)
        inputs = jnp.concatenate([sent, recv_rows()[rows, :]], axis=1)
        _, slope, normed, rescale = forward(inputs, first, second)
        slope_e.ref[rows, :] = slope
        normed_e.ref[rows, :] = normed
        scale_e.ref[rows, :] = jnp.broadcast_to(rescale, (ROWS, LANES))
    aggregate = dot(enc_t()[...], normed_e.ref[...]).astype(BF16)
    first, second = layers(weights, 1)
    own = mesh()[...]
    normed, slope, rounded, rescale = forward(
        jnp.concatenate([own, aggregate], axis=1), first, second
    )
    one = (own.astype(F32) + normed).astype(BF16)
    one_out.ref[...] = one
    split(dot(halo_g()[...], one), halo_out)
    slope_n.ref[...] = slope
    normed_n.ref[...] = rounded
    scale_n.ref[...] = jnp.broadcast_to(rescale, scale_n.ref.shape)


def process_kernel(
    cotangent_in, one_in, halo, sender_g, proc_g, weights, proc_t, sender_t, two, grad_one, *refs
):
    grad_halo, (slope_p, normed_p, scale_p, ga_p) = refs[:-4], refs[-4:]
    features = FEATURES
    one = one_in()[...]
    mesh_rows = one.shape[0]
    lookup = jnp.concatenate([one, stacked(halo)], axis=0)
    edges = sender_g().shape[0]
    first, second = layers(weights, 0)
    for low in range(0, edges, ROWS):
        rows = pl.ds(low, ROWS)
        sent = dot(sender_g()[rows, :], lookup).astype(BF16)
        got = dot(proc_g()[rows, :], one).astype(BF16)
        _, slope, normed, rescale = forward(jnp.concatenate([sent, got], axis=1), first, second)
        slope_p[rows, :] = slope
        normed_p[rows, :] = normed
        scale_p[rows, :] = jnp.broadcast_to(rescale, (ROWS, LANES))
    aggregate = dot(proc_t()[...], normed_p[...]).astype(BF16)
    first_n, second_n = layers(weights, 1)
    normed, slope, rounded, rescale = forward(
        jnp.concatenate([one, aggregate], axis=1), first_n, second_n
    )
    two.send((one.astype(F32) + normed).astype(BF16))
    cotangent = cotangent_in()[...].astype(F32)
    ga = backward_hidden(cotangent, slope, rounded, rescale, second_n)
    g_q = dot(ga, first_n)
    g_msg = g_q[:, features:].astype(BF16)
    for low in range(0, edges, ROWS):
        rows = pl.ds(low, ROWS)
        incoming = dot(proc_g()[rows, :], g_msg)
        ga_p[rows, :] = backward_hidden(
            incoming, slope_p[rows, :], normed_p[rows, :], scale_p[rows, 0:1], second
        )
    by_send = dot(sender_t()[...], ga_p[...]).astype(BF16)
    g_send = dot(by_send, first[:, :features])
    split(g_send[mesh_rows:, :], grad_halo)
    by_recv = dot(proc_t()[...], ga_p[...]).astype(BF16)
    g_recv = dot(by_recv, first[:, features:])
    grad_one.ref[...] = cotangent + g_q[:, :features] + g_recv + g_send[:mesh_rows, :]


def decode_kernel(
    back, halo_t, grad_in, slope_n, normed_n, scale_n, enc_g, slope_e, normed_e, scale_e,
    weights, slot_t, enc_t, mesh_grad, *refs
):
    grad_slots, ga_e = refs[:-1], refs[-1]
    features = FEATURES
    edges = enc_g().shape[0]
    grad_one = grad_in()[...] + dot(halo_t()[...], stacked(back))
    first_n, second_n = layers(weights, 1)
    ga = backward_hidden(grad_one, slope_n()[...], normed_n()[...], scale_n()[:, 0:1], second_n)
    g_n = dot(ga, first_n)
    g_edge = g_n[:, features:].astype(BF16)
    first, second = layers(weights, 0)
    for low in range(0, edges, ROWS):
        rows = pl.ds(low, ROWS)
        incoming = dot(enc_g()[rows, :], g_edge)
        ga_e[rows, :] = backward_hidden(
            incoming, slope_e()[rows, :], normed_e()[rows, :], scale_e()[rows, 0:1], second
        )
    by_recv = dot(enc_t()[...], ga_e[...]).astype(BF16)
    mesh_grad.send(grad_one + g_n[:, :features] + dot(by_recv, first[:, features:]))
    by_slot = dot(slot_t()[...], ga_e[...]).astype(BF16)
    split(dot(by_slot, first[:, :features]), grad_slots)


def grid_kernel(back, table_in, out):
    out.send(dot(table_in()[...], stacked(back)))


def along(block, shift):
    size = lax.axis_size("mp")
    if shift % size == 0:
        return block
    return lax.ppermute(block, "mp", [(m, (m + shift) % size) for m in range(size)])


def beside(block, flip):
    if flip == 0:
        return block
    return lax.ppermute(block, "graph", [(g, g ^ flip) for g in range(lax.axis_size("graph"))])


def turn(blocks, count, step):
    out = shape(len(blocks) * step, blocks[0].shape[1], BF16)
    return call(turn_kernel, [out] * count, list(blocks))


def exchange(blocks, step):
    return second_level(first_level(blocks, step))


def first_level(blocks, step):
    return turn([along(b, s) for s, b in enumerate(blocks)], lax.axis_size("graph"), step)


def second_level(blocks):
    return [beside(b, t) for t, b in enumerate(blocks)]


def exchange_back(blocks, step):
    blocks = turn([beside(b, t) for t, b in enumerate(blocks)], lax.axis_size("mp"), step)
    return [along(b, -s) for s, b in enumerate(blocks)]


def local(
    grid_lat,
    mesh_lat,
    cotangent,
    grid_send,
    g2m_slot,
    g2m_receiver,
    halo_send,
    mesh_sender,
    mesh_receiver,
    *shards,
):
    grid_rows, features = grid_lat.shape
    mesh_rows = mesh_lat.shape[0]
    edges = g2m_slot.shape[0]
    mesh_edges = mesh_sender.shape[0]
    mp, graph = lax.axis_size("mp"), lax.axis_size("graph")
    step, halo_step = stride(grid_send.shape[1]), stride(halo_send.shape[1])
    slots, halos = mp * graph * step, mp * graph * halo_step
    tables = call(
        tables_kernel,
        [
            shape(slots, edges, BF16),
            shape(edges, slots, BF16),
            shape(mesh_rows, edges, BF16),
            shape(edges, mesh_rows, BF16),
            shape(mesh_rows, halos, BF16),
            shape(halos, mesh_rows, BF16),
            shape(mesh_rows + halos, mesh_edges, BF16),
            shape(mesh_edges, mesh_rows + halos, BF16),
            shape(mesh_rows, mesh_edges, BF16),
            shape(mesh_edges, mesh_rows, BF16),
            shape(edges, features, BF16),
        ],
        Far(mesh_lat),
        Far(g2m_slot.reshape(1, edges)),
        Far(g2m_receiver.reshape(1, edges)),
        Far(halo_send.T),
        Far(mesh_sender.reshape(1, mesh_edges)),
        Far(mesh_receiver.reshape(1, mesh_edges)),
    )
    enc, finish, arrived, grid_t, tables = start(grid_lat, grid_send, shards, tables)
    slot_t, slot_g, enc_t, enc_g, halo_t, halo_g, sender_t, sender_g, proc_t, proc_g, recv_rows = tables
    saved = [
        shape(edges, features, BF16),
        shape(edges, features, BF16),
        shape(edges, LANES, F32),
        shape(mesh_rows, features, BF16),
        shape(mesh_rows, features, BF16),
        shape(mesh_rows, LANES, F32),
    ]
    mesh_one, slope_e, normed_e, scale_e, slope_n, normed_n, scale_n, *halo_out = call(
        encode_kernel,
        [shape(mesh_rows, features, BF16)] + saved + [shape(graph * halo_step, features, BF16)] * mp,
        recv_rows,
        arrived,
        slot_g,
        enc_t,
        Far(mesh_lat),
        enc,
        halo_g,
        flops=3 * 10**9,
    )
    moved = first_level(halo_out, halo_step)
    proc = finish(moved)
    halo_in = second_level(moved)
    mesh_two, grad_one, *grad_halo = call(
        process_kernel,
        [shape(mesh_rows, features, BF16), shape(mesh_rows, features, F32)]
        + [shape(mp * halo_step, features, BF16)] * graph,
        Far(cotangent),
        mesh_one,
        halo_in,
        sender_g,
        proc_g,
        proc,
        proc_t,
        sender_t,
        last=(0,),
        flops=5 * 10**9,
        scratch=[
            pltpu.VMEM((mesh_edges, features), BF16),
            pltpu.VMEM((mesh_edges, features), BF16),
            pltpu.VMEM((mesh_edges, LANES), F32),
            pltpu.VMEM((mesh_edges, features), BF16),
        ],
    )
    halo_back = exchange_back(grad_halo, halo_step)
    mesh_grad, *grad_slots = call(
        decode_kernel,
        [shape(mesh_rows, features, F32)] + [shape(mp * step, features, BF16)] * graph,
        halo_back,
        halo_t,
        grad_one,
        slope_n,
        normed_n,
        scale_n,
        enc_g,
        slope_e,
        normed_e,
        scale_e,
        enc,
        slot_t,
        enc_t,
        last=(0,),
        flops=3 * 10**9,
        scratch=[pltpu.VMEM((edges, features), BF16)],
    )
    returned = exchange_back(grad_slots, step)
    (grid_grad,) = call(
        grid_kernel, [shape(grid_rows, features, F32)], returned, grid_t, last=(0,)
    )
    return (mesh_two, grid_grad, mesh_grad)


def solution(mesh):
    rows = P(AXES, None)
    flat = P(AXES)
    in_specs = (rows,) * 4 + (flat,) * 2 + (rows,) + (flat,) * 2 + (P(None, "mp"), P("mp", None)) * 4
    return jax.shard_map(
        local, mesh=mesh, in_specs=in_specs, out_specs=(rows,) * 3, check_vma=False
    )
```

```python
import functools

import jax
import jax.numpy as jnp
from jax import lax
from jax.experimental import pallas as pl
from jax.experimental.pallas import tpu as pltpu
from jax.sharding import PartitionSpec as P

F32 = jnp.float32
BF16 = jnp.bfloat16
LANES = 128
ROWS = 256
FEATURES = 512
AXES = ("groups", "graph", "mp")


def dot(left, right):
    return jnp.dot(left, right, preferred_element_type=F32)


def dot_trans(left, right):
    return lax.dot_general(left, right, (((1,), (1,)), ((), ())), preferred_element_type=F32)


def shape(rows, columns, dtype):
    return jax.ShapeDtypeStruct((rows, columns), dtype)


class Far:
    def __init__(self, array):
        self.array = pltpu.with_memory_space_constraint(array, pltpu.HBM)


class Input:
    def __init__(self, copy, ref):
        self.copy, self.ref = copy, ref

    def __call__(self):
        if self.copy is not None:
            self.copy.wait()
            self.copy = None
        return self.ref


class Output:
    def __init__(self, ref, copy):
        self.ref, self.copy = ref, copy

    def send(self, value=None):
        if value is not None:
            self.ref[...] = value
        if self.copy is not None:
            self.copy.start()


def call(kernel, out_shape, *args, last=(), scratch=(), flops=0):
    groups = [a if isinstance(a, list) else [a] for a in args]
    flat = [a for group in groups for a in group]
    far = [isinstance(a, Far) for a in flat]
    arrays = [a.array if isinstance(a, Far) else a for a in flat]
    count, outs = len(arrays), len(out_shape)

    def body(*refs):
        ins, refs = refs[:count], refs[count:]
        out_refs, refs = refs[:outs], refs[outs:]
        places, refs = list(refs[: sum(far)]), refs[sum(far) :]
        results, refs = list(refs[: len(last)]), refs[len(last) :]
        sem_in, sem_out, refs = refs[0], refs[1], refs[2:]
        inputs = []
        for ref, away in zip(ins, far):
            copy = None
            if away:
                place = places.pop(0)
                copy = pltpu.make_async_copy(ref, place, sem_in.at[len(places)])
                copy.start()
                ref = place
            inputs.append(Input(copy, ref))
        outputs = []
        for i, ref in enumerate(out_refs):
            copy = None
            if i in last:
                place = results.pop(0)
                copy = pltpu.make_async_copy(place, ref, sem_out.at[len(results)])
                ref = place
            outputs.append(Output(ref, copy))
        given = []
        for arg, group in zip(args, groups):
            part, inputs = inputs[: len(group)], inputs[len(group) :]
            given.append(part if isinstance(arg, list) else part[0])
        kernel(*given, *outputs, *refs)
        for output in outputs:
            if output.copy is not None:
                output.copy.wait()

    vmem, hbm = pl.BlockSpec(memory_space=pltpu.VMEM), pl.BlockSpec(memory_space=pl.ANY)
    total = sum(a.size * a.dtype.itemsize for a in arrays)
    return pl.pallas_call(
        body,
        out_shape=out_shape,
        in_specs=[hbm if away else vmem for away in far],
        out_specs=[hbm if i in last else vmem for i in range(outs)],
        scratch_shapes=[pltpu.VMEM(a.shape, a.dtype) for a, away in zip(arrays, far) if away]
        + [pltpu.VMEM(out_shape[i].shape, out_shape[i].dtype) for i in last]
        + [pltpu.SemaphoreType.DMA((max(sum(far), 1),)), pltpu.SemaphoreType.DMA((max(len(last), 1),))]
        + list(scratch),
        name=getattr(kernel, "func", kernel).__name__,
        cost_estimate=pl.CostEstimate(flops=flops, bytes_accessed=total, transcendentals=0),
        compiler_params=pltpu.CompilerParams(vmem_limit_bytes=24 * 1024 * 1024),
    )(*arrays)


def layers(blocks, which):
    low = which * 3 * FEATURES
    middle = low + 2 * FEATURES
    return (
        jnp.concatenate([block()[:, low:middle] for block in blocks], axis=0),
        jnp.concatenate([block()[:, middle : middle + FEATURES] for block in blocks], axis=0),
    )


def turned(first, select):
    return dot_trans(select, first).astype(BF16)


def prepare_kernel(grid, send, shards, proc_piece, table_out, kept, *messages):
    plane = lax.axis_index("groups") * lax.axis_size("graph") + lax.axis_index("graph")
    width = 3 * FEATURES
    rows = proc_piece.ref.shape[0]
    base = plane * rows
    for i in range(4):
        one, two = shards[2 * i](), shards[2 * i + 1]()
        hidden = one.shape[1]
        select = jnp.where(
            lax.broadcasted_iota(jnp.int32, (rows, hidden), 0) + base
            == lax.broadcasted_iota(jnp.int32, (rows, hidden), 1),
            1.0,
            0.0,
        ).astype(BF16)
        low = i % 2 * width
        first = turned(one[...], select)
        second = two[pl.ds(pl.multiple_of(base, rows), rows), :]
        for out in (proc_piece,) if i // 2 else messages:
            out.ref[:, low : low + 2 * FEATURES] = first
            out.ref[:, low + 2 * FEATURES : low + width] = second
    outgoing = send_rows(grid, send, table_out)
    size = kept.ref.shape[0]
    kept.ref[...] = outgoing[:size, :].astype(BF16)
    for i, out in enumerate(messages):
        out.ref[:, 2 * width :] = outgoing[(i + 1) * size : (i + 2) * size, :].astype(BF16)


def join_kernel(kept, messages, near, block, both):
    width = 6 * FEATURES
    weights = jnp.concatenate([m()[:, :width] for m in messages], axis=0)
    rows = jnp.concatenate([kept()[...]] + [m()[:, width:] for m in messages], axis=0)
    step = rows.shape[0] // 16
    block.ref[...] = weights
    both.ref[:, :width] = weights
    size = near.ref.shape[0]
    for j in range(4):
        moved = dot(turn_table(4, 4, step, j), rows).astype(BF16)
        if j == 0:
            near.ref[...] = moved
        else:
            both.ref[(j - 1) * size : j * size, width:] = moved


def own_kernel(shards, *outs):
    width = 3 * FEATURES
    for i in range(4):
        one, two = shards[2 * i](), shards[2 * i + 1]()
        hidden = one.shape[1]
        select = jnp.where(
            lax.broadcasted_iota(jnp.int32, (hidden, hidden), 0)
            == lax.broadcasted_iota(jnp.int32, (hidden, hidden), 1),
            1.0,
            0.0,
        ).astype(BF16)
        out, low = outs[i // 2], i % 2 * width
        out.ref[:, low : low + 2 * FEATURES] = turned(one[...], select)
        out.ref[:, low + 2 * FEATURES : low + width] = two[...]


def across(x, flip):
    planes = lax.axis_size("groups") * lax.axis_size("graph")
    return lax.ppermute(x, ("groups", "graph"), [(p, p ^ flip) for p in range(planes)])


def start(grid_lat, grid_send, shards, make_tables):
    grid_rows, features = grid_lat.shape
    mp, graph = lax.axis_size("mp"), lax.axis_size("graph")
    step = stride(grid_send.shape[1])
    table_shape = shape(grid_rows, grid_send.size, BF16)
    sent = [table_shape] + [shape(graph * step, features, BF16)] * mp
    planes = lax.axis_size("groups") * graph
    hidden = shards[1].shape[0]
    if planes != 8 or mp != 4 or hidden != 128 or features != FEATURES:
        grid_t, *outgoing = call(send_kernel, sent, Far(grid_lat), Far(grid_send.T))
        rows = []
        for i in range(4):
            rows.append(lax.all_gather(shards[2 * i], "mp", axis=1, tiled=True).T)
            rows.append(lax.all_gather(shards[2 * i + 1], "mp", axis=0, tiled=True))
        enc, proc = jnp.concatenate(rows[:4], axis=1), jnp.concatenate(rows[4:], axis=1)
        arrived = exchange_levels(outgoing, step)
        return [enc], lambda after: [proc], arrived, grid_t, make_tables(outgoing[0])
    far = [Far(s) for s in shards]
    piece = hidden // planes
    width = 6 * features
    proc_piece, grid_t, kept, *messages = call(
        prepare_kernel,
        [shape(piece, width, BF16)] + sent[:2] + [shape(piece, width + features, BF16)] * 3,
        Far(grid_lat),
        Far(grid_send.T),
        far,
    )
    enc_own, proc_own = call(own_kernel, [shape(hidden, width, BF16)] * 2, far)
    messages = [along(m, i + 1) for i, m in enumerate(messages)]
    kept, proc_piece, enc_own = lax.optimization_barrier((kept, proc_piece, enc_own))
    beside_me = lax.ppermute(proc_piece, "mp", [(m, m ^ 1) for m in range(mp)])
    kept, beside_me = lax.optimization_barrier((kept, beside_me))
    rows = mp * step
    near, first, both = call(
        join_kernel,
        [shape(rows, features, BF16), shape(3 * piece, width, BF16), shape(3 * rows, width + features, BF16)],
        kept,
        messages,
    )
    x, y, corner = across(both, 2), across(first, 4), across(first, 6)
    pair = jnp.concatenate([proc_piece, beside_me])
    pairs = lax.ppermute(pair, "mp", [(m, m ^ 2) for m in range(mp)])
    proc_first = jnp.concatenate([beside_me, pairs])
    tables = make_tables(pairs)
    both, x, y, corner, _ = lax.optimization_barrier((both, x, y, corner, tables[0]))
    core, x_core, others = across(both, 1), across(x, 1), across(jnp.concatenate([y, corner]), 1)
    enc = [enc_own, first, core, x, y, corner, x_core, others]
    arrived = [near, core, x, x_core]
    proc_first, *_ = lax.optimization_barrier((proc_first, x, y, corner))
    plane = [across(proc_first, flip) for flip in (2, 4, 6)]
    proc = [proc_own, proc_first, across(proc_first, 1)] + plane

    def finish(after):
        tied, *_ = lax.optimization_barrier((jnp.concatenate(plane), after))
        return proc + [across(tied, 1)]

    return enc, finish, arrived, grid_t, tables


def forward(inputs, first, second):
    before = dot_trans(inputs, first)
    logistic = 0.5 + 0.5 * jnp.tanh(0.5 * before)
    wide = before * logistic
    hidden = wide.astype(BF16)
    slope = logistic + wide * (1.0 - logistic)
    summed = dot(hidden, second)
    centered = summed - jnp.mean(summed, axis=-1, keepdims=True)
    rescale = lax.rsqrt(jnp.mean(centered * centered, axis=-1, keepdims=True) + 1e-05)
    normed = centered * rescale
    return normed, slope.astype(BF16), normed.astype(BF16), rescale


def backward_hidden(incoming, slope, normed, rescale, second):
    normed = normed.astype(F32)
    g_out = (
        incoming
        - jnp.mean(incoming, axis=-1, keepdims=True)
        - normed * jnp.mean(incoming * normed, axis=-1, keepdims=True)
    ) * rescale
    return (dot_trans(g_out.astype(BF16), second) * slope.astype(F32)).astype(BF16)


def table(index_row, count):
    n = index_row.shape[1]
    return jnp.where(lax.broadcasted_iota(jnp.int32, (count, n), 0) == index_row, 1.0, 0.0)


def stride(capacity):
    return max(capacity, 16 // min(lax.axis_size("mp"), lax.axis_size("graph")))


def sent_at(peer, slot, step):
    mp, graph = lax.axis_size("mp"), lax.axis_size("graph")
    shift = (peer % mp + mp - lax.axis_index("mp")) % mp
    return (shift * graph + (peer // mp ^ lax.axis_index("graph"))) * step + slot


def arrived_at(peer, slot, step):
    mp = lax.axis_size("mp")
    shift = (lax.axis_index("mp") + mp - peer % mp) % mp
    return ((peer // mp ^ lax.axis_index("graph")) * mp + shift) * step + slot


def apart_at(peer, slot, step):
    rank = lax.axis_index("graph") * lax.axis_size("mp") + lax.axis_index("mp")
    return (peer ^ rank) * step + slot


def sent_row(index, step, order):
    width, count = index.shape
    index = index.astype(F32).T
    at = lax.broadcasted_iota(jnp.int32, (count, count * step), 1)
    peer = lax.broadcasted_iota(jnp.int32, (count, count * step), 0)
    row = jnp.zeros(at.shape, F32)
    for slot in range(width):
        row = jnp.where(order(peer, slot, step) == at, index[:, slot : slot + 1] + 1.0, row)
    return jnp.sum(row, axis=0, keepdims=True).astype(jnp.int32) - 1


def stacked(blocks):
    return jnp.concatenate([block()[...] for block in blocks], axis=0)


def split(rows, outs):
    size = rows.shape[0] // len(outs)
    for i, out in enumerate(outs):
        out.ref[...] = rows[i * size : (i + 1) * size, :].astype(BF16)


def send_rows(grid, send, table_out):
    index, count = send()[...], grid().shape[0]
    back = table(sent_row(index, index.shape[0], apart_at), count)
    table_out.ref[...] = back.astype(BF16)
    one = table(sent_row(index, stride(index.shape[0]), sent_at), count)
    return dot(one.T.astype(BF16), grid()[...])


def send_kernel(grid, send, table_out, *outgoing):
    split(send_rows(grid, send, table_out), outgoing)


def turn_table(sources, targets, step, j):
    row = lax.broadcasted_iota(jnp.int32, (sources * step, sources * targets * step), 0)
    at = lax.broadcasted_iota(jnp.int32, row.shape, 1)
    source = (row // step * targets + j) * step + row % step
    return jnp.where(at == source, 1.0, 0.0).astype(BF16)


def turn_kernel(blocks, *outs):
    rows = stacked(blocks)
    step = rows.shape[0] // (len(blocks) * len(outs))
    for j, out in enumerate(outs):
        out.ref[...] = dot(turn_table(len(blocks), len(outs), step, j), rows).astype(BF16)


def swap_table(kept, bit, last):
    rows, total, step = kept.rows, kept.total, kept.step
    row = lax.broadcasted_iota(jnp.int32, (rows, total), 0)
    at = lax.broadcasted_iota(jnp.int32, (rows, total), 1)
    block = row // step
    peer = block // bit * (2 * bit) + block % bit + (bit if kept.sent else 0)
    if last:
        source = peer // (2 * last) * last + peer % last + peer // last % 2 * (total // step // 2)
    else:
        source = peer
    return jnp.where(at == source * step + row % step, 1.0, 0.0).astype(BF16)


class Pick:
    def __init__(self, total, step, sent):
        self.rows, self.total, self.step, self.sent = total // 2, total, step, sent


def swap(rows, step, bit, last, keep_out, send_out):
    total = rows.shape[0]
    for out, sent in ((keep_out, False), (send_out, True)):
        picks = swap_table(Pick(total, step, sent), bit, last)
        out.ref[...] = dot(picks, rows).astype(BF16)


def tables_kernel(after, mesh, slot, recv_e, halo, sender, recv_p, *outs):
    slot_t, slot_g, enc_t, enc_g, halo_t, halo_g, sender_t, sender_g, proc_t, proc_g, recv_rows = outs
    mesh_rows = mesh().shape[0]
    peers, halo_capacity = halo().shape[1], halo().shape[0]
    capacity = slot_t.ref.shape[0] // peers
    slots = slot()[...]
    peer, place = slots // capacity, slots % capacity
    slot_t.ref[...] = table(apart_at(peer, place, capacity), slot_t.ref.shape[0]).astype(BF16)
    slots = arrived_at(peer, place, slot_g.ref.shape[1] // peers)
    slot_g.ref[...] = table(slots, slot_g.ref.shape[1]).T.astype(BF16)
    senders = sender()[...]
    remote = jnp.maximum(senders - mesh_rows, 0)
    remote = apart_at(remote // halo_capacity, remote % halo_capacity, halo_capacity)
    senders = jnp.where(senders < mesh_rows, senders, mesh_rows + remote)
    for row, scatter, gather in (
        (recv_e()[...], enc_t, enc_g),
        (sent_row(halo()[...], halo_capacity, apart_at), halo_t, halo_g),
        (senders, sender_t, sender_g),
        (recv_p()[...], proc_t, proc_g),
    ):
        one = table(row, scatter.ref.shape[0])
        scatter.ref[...] = one.astype(BF16)
        gather.ref[...] = one.T.astype(BF16)
    recv_rows.ref[...] = dot(enc_g.ref[...], mesh()[...]).astype(BF16)


def arrived_rows(blocks):
    size = blocks[0]().shape[0]
    rows = [blocks[0]()[...]]
    for t, block in enumerate(blocks[1:]):
        if block().shape[1] == FEATURES:
            rows.append(block()[...])
        else:
            rows.append(block()[t * size : (t + 1) * size, 6 * FEATURES :])
    return jnp.concatenate(rows, axis=0)


def encode_kernel(
    halo_step, recv_rows, arrived, slot_g, enc_t, mesh, weights, halo_g,
    one_out, slope_e, normed_e, scale_e, slope_n, normed_n, scale_n, *halo_out,
):
    rows_in = arrived_rows(arrived)
    edges = slot_g().shape[0]
    first, second = layers(weights, 0)
    for low in range(0, edges, ROWS):
        rows = pl.ds(low, ROWS)
        sent = dot(slot_g()[rows, :], rows_in).astype(BF16)
        inputs = jnp.concatenate([sent, recv_rows()[rows, :]], axis=1)
        _, slope, normed, rescale = forward(inputs, first, second)
        slope_e.ref[rows, :] = slope
        normed_e.ref[rows, :] = normed
        scale_e.ref[rows, :] = jnp.broadcast_to(rescale, (ROWS, LANES))
    aggregate = dot(enc_t()[...], normed_e.ref[...]).astype(BF16)
    first, second = layers(weights, 1)
    own = mesh()[...]
    normed, slope, rounded, rescale = forward(
        jnp.concatenate([own, aggregate], axis=1), first, second
    )
    one = (own.astype(F32) + normed).astype(BF16)
    one_out.ref[...] = one
    swap(dot(halo_g()[...], one).astype(BF16), halo_step, 1, 0, *halo_out)
    slope_n.ref[...] = slope
    normed_n.ref[...] = rounded
    scale_n.ref[...] = jnp.broadcast_to(rescale, scale_n.ref.shape)


def process_kernel(
    halo_step, cotangent_in, one_in, halo, sender_g, proc_g, weights, proc_t, sender_t, two, grad_one, *refs
):
    grad_halo, (slope_p, normed_p, scale_p, ga_p) = refs[:-4], refs[-4:]
    features = FEATURES
    one = one_in()[...]
    mesh_rows = one.shape[0]
    lookup = jnp.concatenate([one, stacked(halo)], axis=0)
    edges = sender_g().shape[0]
    first, second = layers(weights, 0)
    for low in range(0, edges, ROWS):
        rows = pl.ds(low, ROWS)
        sent = dot(sender_g()[rows, :], lookup).astype(BF16)
        got = dot(proc_g()[rows, :], one).astype(BF16)
        _, slope, normed, rescale = forward(jnp.concatenate([sent, got], axis=1), first, second)
        slope_p[rows, :] = slope
        normed_p[rows, :] = normed
        scale_p[rows, :] = jnp.broadcast_to(rescale, (ROWS, LANES))
    aggregate = dot(proc_t()[...], normed_p[...]).astype(BF16)
    first_n, second_n = layers(weights, 1)
    normed, slope, rounded, rescale = forward(
        jnp.concatenate([one, aggregate], axis=1), first_n, second_n
    )
    two.send((one.astype(F32) + normed).astype(BF16))
    cotangent = cotangent_in()[...].astype(F32)
    ga = backward_hidden(cotangent, slope, rounded, rescale, second_n)
    g_q = dot(ga, first_n)
    g_msg = g_q[:, features:].astype(BF16)
    for low in range(0, edges, ROWS):
        rows = pl.ds(low, ROWS)
        incoming = dot(proc_g()[rows, :], g_msg)
        ga_p[rows, :] = backward_hidden(
            incoming, slope_p[rows, :], normed_p[rows, :], scale_p[rows, 0:1], second
        )
    by_send = dot(sender_t()[...], ga_p[...]).astype(BF16)
    g_send = dot(by_send, first[:, :features])
    swap(g_send[mesh_rows:, :].astype(BF16), halo_step, 1, 0, *grad_halo)
    by_recv = dot(proc_t()[...], ga_p[...]).astype(BF16)
    g_recv = dot(by_recv, first[:, features:])
    grad_one.ref[...] = cotangent + g_q[:, :features] + g_recv + g_send[:mesh_rows, :]


def decode_kernel(
    step, back, halo_t, grad_in, slope_n, normed_n, scale_n, enc_g, slope_e, normed_e, scale_e,
    weights, slot_t, enc_t, mesh_grad, *refs
):
    grad_slots, ga_e = refs[:-1], refs[-1]
    features = FEATURES
    edges = enc_g().shape[0]
    grad_one = grad_in()[...] + dot(halo_t()[...], stacked(back))
    first_n, second_n = layers(weights, 1)
    ga = backward_hidden(grad_one, slope_n()[...], normed_n()[...], scale_n()[:, 0:1], second_n)
    g_n = dot(ga, first_n)
    g_edge = g_n[:, features:].astype(BF16)
    first, second = layers(weights, 0)
    for low in range(0, edges, ROWS):
        rows = pl.ds(low, ROWS)
        incoming = dot(enc_g()[rows, :], g_edge)
        ga_e[rows, :] = backward_hidden(
            incoming, slope_e()[rows, :], normed_e()[rows, :], scale_e()[rows, 0:1], second
        )
    by_recv = dot(enc_t()[...], ga_e[...]).astype(BF16)
    mesh_grad.send(grad_one + g_n[:, :features] + dot(by_recv, first[:, features:]))
    by_slot = dot(slot_t()[...], ga_e[...]).astype(BF16)
    swap(dot(by_slot, first[:, :features]).astype(BF16), step, 1, 0, *grad_slots)


def grid_kernel(back, table_in, out):
    out.send(dot(table_in()[...], stacked(back)))


def along(block, shift):
    size = lax.axis_size("mp")
    if shift % size == 0:
        return block
    return lax.ppermute(block, "mp", [(m, (m + shift) % size) for m in range(size)])


def beside(block, flip):
    if flip == 0:
        return block
    return lax.ppermute(block, "graph", [(g, g ^ flip) for g in range(lax.axis_size("graph"))])


def turn(blocks, count, step):
    out = shape(len(blocks) * step, blocks[0].shape[1], BF16)
    return call(turn_kernel, [out] * count, list(blocks))


def exchange_levels(blocks, step):
    blocks = turn([along(b, s) for s, b in enumerate(blocks)], lax.axis_size("graph"), step)
    return [beside(b, t) for t, b in enumerate(blocks)]


def swap_kernel(step, bit, blocks, keep_out, send_out):
    swap(stacked(blocks), step, bit, bit // 2, keep_out, send_out)


def exchange(halves, step, before_last=None):
    mp, graph = lax.axis_size("mp"), lax.axis_size("graph")
    keep, send = halves
    bit = 1
    while True:
        if 2 * bit == mp * graph and before_last is not None:
            before_last(keep)
        if bit < mp:
            got = lax.ppermute(send, "mp", [(m, m ^ bit) for m in range(mp)])
        else:
            got = lax.ppermute(send, "graph", [(g, g ^ bit // mp) for g in range(graph)])
        bit *= 2
        if bit == mp * graph:
            return [keep, got]
        half = shape(*keep.shape, BF16)
        keep, send = call(functools.partial(swap_kernel, step, bit), [half] * 2, [keep, got])


def local(
    grid_lat,
    mesh_lat,
    cotangent,
    grid_send,
    g2m_slot,
    g2m_receiver,
    halo_send,
    mesh_sender,
    mesh_receiver,
    *shards,
):
    grid_rows, features = grid_lat.shape
    mesh_rows = mesh_lat.shape[0]
    edges = g2m_slot.shape[0]
    mesh_edges = mesh_sender.shape[0]
    peers = lax.axis_size("mp") * lax.axis_size("graph")
    step, halo_step = grid_send.shape[1], halo_send.shape[1]
    slots, halos, spread = grid_send.size, halo_send.size, peers * stride(step)
    make_tables = lambda after: call(
        tables_kernel,
        [
            shape(slots, edges, BF16),
            shape(edges, spread, BF16),
            shape(mesh_rows, edges, BF16),
            shape(edges, mesh_rows, BF16),
            shape(mesh_rows, halos, BF16),
            shape(halos, mesh_rows, BF16),
            shape(mesh_rows + halos, mesh_edges, BF16),
            shape(mesh_edges, mesh_rows + halos, BF16),
            shape(mesh_rows, mesh_edges, BF16),
            shape(mesh_edges, mesh_rows, BF16),
            shape(edges, features, BF16),
        ],
        after,
        Far(mesh_lat),
        Far(g2m_slot.reshape(1, edges)),
        Far(g2m_receiver.reshape(1, edges)),
        Far(halo_send.T),
        Far(mesh_sender.reshape(1, mesh_edges)),
        Far(mesh_receiver.reshape(1, mesh_edges)),
    )
    enc, finish, arrived, grid_t, tables = start(grid_lat, grid_send, shards, make_tables)
    slot_t, slot_g, enc_t, enc_g, halo_t, halo_g, sender_t, sender_g, proc_t, proc_g, recv_rows = tables
    saved = [
        shape(edges, features, BF16),
        shape(edges, features, BF16),
        shape(edges, LANES, F32),
        shape(mesh_rows, features, BF16),
        shape(mesh_rows, features, BF16),
        shape(mesh_rows, LANES, F32),
    ]
    half, grid_half = shape(halos // 2, features, BF16), shape(slots // 2, features, BF16)
    mesh_one, slope_e, normed_e, scale_e, slope_n, normed_n, scale_n, *halo_out = call(
        functools.partial(encode_kernel, halo_step),
        [shape(mesh_rows, features, BF16)] + saved + [half] * 2,
        recv_rows,
        arrived,
        slot_g,
        enc_t,
        Far(mesh_lat),
        enc,
        halo_g,
        flops=3 * 10**9,
    )
    proc = []
    halo_in = exchange(halo_out, halo_step, lambda kept: proc.extend(finish(kept)))
    mesh_two, grad_one, *grad_halo = call(
        functools.partial(process_kernel, halo_step),
        [shape(mesh_rows, features, BF16), shape(mesh_rows, features, F32)] + [half] * 2,
        Far(cotangent),
        mesh_one,
        halo_in,
        sender_g,
        proc_g,
        proc,
        proc_t,
        sender_t,
        last=(0,),
        flops=5 * 10**9,
        scratch=[
            pltpu.VMEM((mesh_edges, features), BF16),
            pltpu.VMEM((mesh_edges, features), BF16),
            pltpu.VMEM((mesh_edges, LANES), F32),
            pltpu.VMEM((mesh_edges, features), BF16),
        ],
    )
    halo_back = exchange(grad_halo, halo_step)
    mesh_grad, *grad_slots = call(
        functools.partial(decode_kernel, step),
        [shape(mesh_rows, features, F32)] + [grid_half] * 2,
        halo_back,
        halo_t,
        grad_one,
        slope_n,
        normed_n,
        scale_n,
        enc_g,
        slope_e,
        normed_e,
        scale_e,
        enc,
        slot_t,
        enc_t,
        last=(0,),
        flops=3 * 10**9,
        scratch=[pltpu.VMEM((edges, features), BF16)],
    )
    returned = exchange(grad_slots, step)
    (grid_grad,) = call(
        grid_kernel, [shape(grid_rows, features, F32)], returned, grid_t, last=(0,)
    )
    return (mesh_two, grid_grad, mesh_grad)


def solution(mesh):
    rows = P(AXES, None)
    flat = P(AXES)
    in_specs = (rows,) * 4 + (flat,) * 2 + (rows,) + (flat,) * 2 + (P(None, "mp"), P("mp", None)) * 4
    return jax.shard_map(
        local, mesh=mesh, in_specs=in_specs, out_specs=(rows,) * 3, check_vma=False
    )
```

```python
import functools

import jax
import jax.numpy as jnp
from jax import lax
from jax.experimental import pallas as pl
from jax.experimental.pallas import tpu as pltpu
from jax.sharding import PartitionSpec as P

F32 = jnp.float32
BF16 = jnp.bfloat16
LANES = 128
ROWS = 256
FEATURES = 512
AXES = ("groups", "graph", "mp")


def dot(left, right):
    return jnp.dot(left, right, preferred_element_type=F32)


def dot_trans(left, right):
    return lax.dot_general(left, right, (((1,), (1,)), ((), ())), preferred_element_type=F32)


def shape(rows, columns, dtype):
    return jax.ShapeDtypeStruct((rows, columns), dtype)


class Far:
    def __init__(self, array):
        self.array = pltpu.with_memory_space_constraint(array, pltpu.HBM)


class Input:
    def __init__(self, copy, ref):
        self.copy, self.ref = copy, ref

    def __call__(self):
        if self.copy is not None:
            self.copy.wait()
            self.copy = None
        return self.ref


class Output:
    def __init__(self, ref, copy):
        self.ref, self.copy = ref, copy

    def send(self, value=None):
        if value is not None:
            self.ref[...] = value
        if self.copy is not None:
            self.copy.start()


def call(kernel, out_shape, *args, last=(), scratch=(), flops=0):
    groups = [a if isinstance(a, list) else [a] for a in args]
    flat = [a for group in groups for a in group]
    far = [isinstance(a, Far) for a in flat]
    arrays = [a.array if isinstance(a, Far) else a for a in flat]
    count, outs = len(arrays), len(out_shape)

    def body(*refs):
        ins, refs = refs[:count], refs[count:]
        out_refs, refs = refs[:outs], refs[outs:]
        places, refs = list(refs[: sum(far)]), refs[sum(far) :]
        results, refs = list(refs[: len(last)]), refs[len(last) :]
        sem_in, sem_out, refs = refs[0], refs[1], refs[2:]
        inputs = []
        for ref, away in zip(ins, far):
            copy = None
            if away:
                place = places.pop(0)
                copy = pltpu.make_async_copy(ref, place, sem_in.at[len(places)])
                copy.start()
                ref = place
            inputs.append(Input(copy, ref))
        outputs = []
        for i, ref in enumerate(out_refs):
            copy = None
            if i in last:
                place = results.pop(0)
                copy = pltpu.make_async_copy(place, ref, sem_out.at[len(results)])
                ref = place
            outputs.append(Output(ref, copy))
        given = []
        for arg, group in zip(args, groups):
            part, inputs = inputs[: len(group)], inputs[len(group) :]
            given.append(part if isinstance(arg, list) else part[0])
        kernel(*given, *outputs, *refs)
        for output in outputs:
            if output.copy is not None:
                output.copy.wait()

    vmem, hbm = pl.BlockSpec(memory_space=pltpu.VMEM), pl.BlockSpec(memory_space=pl.ANY)
    total = sum(a.size * a.dtype.itemsize for a in arrays)
    return pl.pallas_call(
        body,
        out_shape=out_shape,
        in_specs=[hbm if away else vmem for away in far],
        out_specs=[hbm if i in last else vmem for i in range(outs)],
        scratch_shapes=[pltpu.VMEM(a.shape, a.dtype) for a, away in zip(arrays, far) if away]
        + [pltpu.VMEM(out_shape[i].shape, out_shape[i].dtype) for i in last]
        + [pltpu.SemaphoreType.DMA((max(sum(far), 1),)), pltpu.SemaphoreType.DMA((max(len(last), 1),))]
        + list(scratch),
        name=getattr(kernel, "func", kernel).__name__,
        cost_estimate=pl.CostEstimate(flops=flops, bytes_accessed=total, transcendentals=0),
        compiler_params=pltpu.CompilerParams(vmem_limit_bytes=24 * 1024 * 1024),
    )(*arrays)


def layers(blocks, which):
    low = which * 3 * FEATURES
    middle = low + 2 * FEATURES
    return (
        jnp.concatenate([block()[:, low:middle] for block in blocks], axis=0),
        jnp.concatenate([block()[:, middle : middle + FEATURES] for block in blocks], axis=0),
    )


def turned(first, select):
    return dot_trans(select, first).astype(BF16)


def prepare_kernel(grid, send, shards, proc_piece, table_out, kept, *messages):
    plane = lax.axis_index("groups") * lax.axis_size("graph") + lax.axis_index("graph")
    width = 3 * FEATURES
    rows = proc_piece.ref.shape[0]
    base = plane * rows
    for i in range(4):
        one, two = shards[2 * i](), shards[2 * i + 1]()
        hidden = one.shape[1]
        select = jnp.where(
            lax.broadcasted_iota(jnp.int32, (rows, hidden), 0) + base
            == lax.broadcasted_iota(jnp.int32, (rows, hidden), 1),
            1.0,
            0.0,
        ).astype(BF16)
        low = i % 2 * width
        first = turned(one[...], select)
        second = two[pl.ds(pl.multiple_of(base, rows), rows), :]
        for out in (proc_piece,) if i // 2 else messages:
            out.ref[:, low : low + 2 * FEATURES] = first
            out.ref[:, low + 2 * FEATURES : low + width] = second
    outgoing = send_rows(grid, send, table_out, sent_at, stride(send().shape[0]))
    size = kept.ref.shape[0]
    kept.ref[...] = outgoing[:size, :].astype(BF16)
    for i, out in enumerate(messages):
        out.ref[:, 2 * width :] = outgoing[(i + 1) * size : (i + 2) * size, :].astype(BF16)


def join_kernel(kept, messages, near, block, both):
    width = 6 * FEATURES
    weights = jnp.concatenate([m()[:, :width] for m in messages], axis=0)
    rows = jnp.concatenate([kept()[...]] + [m()[:, width:] for m in messages], axis=0)
    step = rows.shape[0] // 16
    block.ref[...] = weights
    both.ref[:, :width] = weights
    size = near.ref.shape[0]
    for j in range(4):
        moved = dot(turn_table(4, 4, step, j), rows).astype(BF16)
        if j == 0:
            near.ref[...] = moved
        else:
            both.ref[(j - 1) * size : j * size, width:] = moved


def own_kernel(shards, *outs):
    width = 3 * FEATURES
    for i in range(4):
        one, two = shards[2 * i](), shards[2 * i + 1]()
        hidden = one.shape[1]
        select = jnp.where(
            lax.broadcasted_iota(jnp.int32, (hidden, hidden), 0)
            == lax.broadcasted_iota(jnp.int32, (hidden, hidden), 1),
            1.0,
            0.0,
        ).astype(BF16)
        out, low = outs[i // 2], i % 2 * width
        out.ref[:, low : low + 2 * FEATURES] = turned(one[...], select)
        out.ref[:, low + 2 * FEATURES : low + width] = two[...]


def across(x, flip):
    planes = lax.axis_size("groups") * lax.axis_size("graph")
    return lax.ppermute(x, ("groups", "graph"), [(p, p ^ flip) for p in range(planes)])


def start(grid_lat, grid_send, shards, make_tables):
    grid_rows, features = grid_lat.shape
    mp, graph = lax.axis_size("mp"), lax.axis_size("graph")
    step = stride(grid_send.shape[1])
    table_shape = pltpu.HBM((grid_rows, grid_send.size), BF16)
    sent = [table_shape] + [shape(graph * step, features, BF16)] * mp
    planes = lax.axis_size("groups") * graph
    hidden = shards[1].shape[0]
    if planes != 8 or mp != 4 or hidden != 128 or features != FEATURES:
        packed = shape(grid_send.size * features // LANES, LANES, BF16)
        grid_t, *outgoing = call(send_kernel, [table_shape, packed], Far(grid_lat), Far(grid_send.T), last=(0,))
        rows = []
        for i in range(4):
            rows.append(lax.all_gather(shards[2 * i], "mp", axis=1, tiled=True).T)
            rows.append(lax.all_gather(shards[2 * i + 1], "mp", axis=0, tiled=True))
        enc, proc = jnp.concatenate(rows[:4], axis=1), jnp.concatenate(rows[4:], axis=1)
        arrived = [exchange_all(outgoing[0])]
        return [enc], lambda one, moved: [proc], arrived, grid_t, make_tables()
    far = [Far(s) for s in shards]
    piece = hidden // planes
    width = 6 * features
    proc_piece, grid_t, kept, *messages = call(
        prepare_kernel,
        [shape(piece, width, BF16)] + sent[:2] + [shape(piece, width + features, BF16)] * 3,
        Far(grid_lat),
        Far(grid_send.T),
        far,
        last=(1,),
    )
    enc_own, proc_own = call(own_kernel, [shape(hidden, width, BF16)] * 2, far)
    messages = [along(m, i + 1) for i, m in enumerate(messages)]
    tables = make_tables()
    kept, enc_own, _ = lax.optimization_barrier((kept, enc_own, tables[0]))
    rows = mp * step
    near, first, both = call(
        join_kernel,
        [shape(rows, features, BF16), shape(3 * piece, width, BF16), shape(3 * rows, width + features, BF16)],
        kept,
        messages,
    )
    x, y, corner = across(both, 2), across(first, 4), across(first, 6)
    proc_piece, _ = lax.optimization_barrier((proc_piece, near))
    beside_me = lax.ppermute(proc_piece, "mp", [(m, m ^ 1) for m in range(mp)])
    pair = jnp.concatenate([proc_piece, beside_me])
    pairs = lax.ppermute(pair, "mp", [(m, m ^ 2) for m in range(mp)])
    proc_first = jnp.concatenate([beside_me, pairs])
    both, x, y, corner, _ = lax.optimization_barrier((both, x, y, corner, pairs))
    core, x_core, others = across(both, 1), across(x, 1), across(jnp.concatenate([y, corner]), 1)
    enc = [enc_own, first, core, x, y, corner, x_core, others]
    arrived = [near, core, x, x_core]
    proc_first, *_ = lax.optimization_barrier((proc_first, x, y, corner))
    proc_x, proc_y, proc_core = [across(proc_first, flip) for flip in (2, 4, 1)]

    def finish(one, moved):
        late, _ = lax.optimization_barrier((proc_x, one))
        blocks = [proc_x, proc_y, across(late, 4)]
        tied, *_ = lax.optimization_barrier((jnp.concatenate(blocks), *moved))
        return [proc_own, proc_first, proc_core] + blocks + [across(tied, 1)]

    return enc, finish, arrived, grid_t, tables


def forward(inputs, first, second):
    before = dot_trans(inputs, first)
    logistic = 0.5 + 0.5 * jnp.tanh(0.5 * before)
    wide = before * logistic
    hidden = wide.astype(BF16)
    slope = logistic + wide * (1.0 - logistic)
    summed = dot(hidden, second)
    centered = summed - jnp.mean(summed, axis=-1, keepdims=True)
    rescale = lax.rsqrt(jnp.mean(centered * centered, axis=-1, keepdims=True) + 1e-05)
    normed = centered * rescale
    return normed, slope.astype(BF16), normed.astype(BF16), rescale


def backward_hidden(incoming, slope, normed, rescale, second):
    normed = normed.astype(F32)
    g_out = (
        incoming
        - jnp.mean(incoming, axis=-1, keepdims=True)
        - normed * jnp.mean(incoming * normed, axis=-1, keepdims=True)
    ) * rescale
    return (dot_trans(g_out.astype(BF16), second) * slope.astype(F32)).astype(BF16)


def table(index_row, count):
    n = index_row.shape[1]
    return jnp.where(lax.broadcasted_iota(jnp.int32, (count, n), 0) == index_row, 1.0, 0.0)


def stride(capacity):
    return max(capacity, 16 // min(lax.axis_size("mp"), lax.axis_size("graph")))


def sent_at(peer, slot, step):
    mp, graph = lax.axis_size("mp"), lax.axis_size("graph")
    shift = (peer % mp + mp - lax.axis_index("mp")) % mp
    return (shift * graph + (peer // mp ^ lax.axis_index("graph"))) * step + slot


def arrived_at(peer, slot, step):
    mp = lax.axis_size("mp")
    shift = (lax.axis_index("mp") + mp - peer % mp) % mp
    return ((peer // mp ^ lax.axis_index("graph")) * mp + shift) * step + slot


def small():
    return lax.axis_size("mp") == 4 and lax.axis_size("graph") == 4


def plain_at(peer, slot, step):
    return peer * step + slot


def apart(peer):
    rank = lax.axis_index("graph") * 4 + lax.axis_index("mp")
    differs = peer ^ rank
    return differs // 4 % 2, differs // 8 * 4 + differs % 4


def out_at(peer, slot, step):
    if not small():
        return plain_at(peer, slot, step)
    core, chip = apart(peer)
    return (core * 8 + chip) * step + slot


def in_at(peer, slot, step):
    if not small():
        return plain_at(peer, slot, step)
    core, chip = apart(peer)
    return chip * 16 + core * step + slot


def in_rows(count, step):
    return 128 if small() else count * step


def sent_row(index, step, order):
    width, count = index.shape
    index = index.astype(F32).T
    at = lax.broadcasted_iota(jnp.int32, (count, count * step), 1)
    peer = lax.broadcasted_iota(jnp.int32, (count, count * step), 0)
    row = jnp.zeros(at.shape, F32)
    for slot in range(width):
        row = jnp.where(order(peer, slot, step) == at, index[:, slot : slot + 1] + 1.0, row)
    return jnp.sum(row, axis=0, keepdims=True).astype(jnp.int32) - 1


def stacked(blocks):
    return jnp.concatenate([block()[...] for block in blocks], axis=0)


def split(rows, outs):
    size = rows.shape[0] // len(outs)
    for i, out in enumerate(outs):
        out.ref[...] = rows[i * size : (i + 1) * size, :].astype(BF16)


def send_rows(grid, send, table_out, order, step):
    index, count = send()[...], grid().shape[0]
    table_out.send(table(sent_row(index, index.shape[0], plain_at), count).astype(BF16))
    one = table(sent_row(index, step, order), count)
    return dot(one.T.astype(BF16), grid()[...])


def send_kernel(grid, send, table_out, outgoing):
    rows = send_rows(grid, send, table_out, plain_at, send().shape[0])
    outgoing.ref[...] = pack_rows(rows.astype(BF16))


def turn_table(sources, targets, step, j):
    row = lax.broadcasted_iota(jnp.int32, (sources * step, sources * targets * step), 0)
    at = lax.broadcasted_iota(jnp.int32, row.shape, 1)
    source = (row // step * targets + j) * step + row % step
    return jnp.where(at == source, 1.0, 0.0).astype(BF16)


def lane_table(n, blocks, block, tall):
    sizes = (n * blocks, n) if tall else (n, n * blocks)
    long = lax.broadcasted_iota(jnp.int32, sizes, 0 if tall else 1)
    short = lax.broadcasted_iota(jnp.int32, sizes, 1 if tall else 0)
    return jnp.where(long == short * blocks + block, 1.0, 0.0).astype(BF16)


def pack_rows(rows):
    n, blocks = rows.shape[0], rows.shape[1] // LANES
    return sum(
        dot(lane_table(n, blocks, k, True), rows[:, k * LANES : (k + 1) * LANES])
        for k in range(blocks)
    ).astype(BF16)


def unpack_rows(packed):
    blocks = FEATURES // LANES
    n = packed.shape[0] // blocks
    return jnp.concatenate(
        [dot(lane_table(n, blocks, k, False), packed).astype(BF16) for k in range(blocks)], axis=1
    )


def pick_rows(rows, count, source):
    row = lax.broadcasted_iota(jnp.int32, (count, rows.shape[0]), 0)
    at = lax.broadcasted_iota(jnp.int32, row.shape, 1)
    return dot(jnp.where(at == source(row), 1.0, 0.0).astype(BF16), rows).astype(BF16)


def fan_kernel(step, halves, *outs):
    rows = stacked(halves)
    for chip, out in enumerate(outs):

        def source(row, chip=chip):
            from_row = (row // step * 8 + chip) * step + row % step
            return jnp.where(row < 2 * step, from_row, -1)

        out.ref[...] = pick_rows(rows, 16, source)


def fold_kernel(step, blocks, keep_out, send_out):
    rows = stacked(blocks)
    for core, out in enumerate((keep_out, send_out)):
        out.ref[...] = pick_rows(
            rows, 8 * step, lambda row: row // step * 16 + core * step + row % step
        )


def put(rows, outs):
    rows = rows.astype(BF16)
    if len(outs) == 1:
        outs[0].ref[...] = pack_rows(rows)
    else:
        split(rows, outs)


def joined(blocks):
    rows = stacked(blocks)
    return unpack_rows(rows) if rows.shape[1] == LANES else rows


def tables_kernel(mesh, slot, recv_e, halo, sender, recv_p, *outs):
    slot_t, slot_g, enc_t, enc_g, halo_t, halo_g, sender_t, sender_g, proc_t, proc_g, recv_rows = outs
    mesh_rows = mesh().shape[0]
    peers, halo_capacity = halo().shape[1], halo().shape[0]
    capacity = slot_t.ref.shape[0] // peers
    slots = slot()[...]
    slot_t.ref[...] = table(slots, slot_t.ref.shape[0]).astype(BF16)
    if small():
        slots = arrived_at(slots // capacity, slots % capacity, slot_g.ref.shape[1] // peers)
    slot_g.ref[...] = table(slots, slot_g.ref.shape[1]).T.astype(BF16)
    senders = sender()[...]
    remote = jnp.maximum(senders - mesh_rows, 0)
    remote = in_at(remote // halo_capacity, remote % halo_capacity, halo_capacity)
    senders = jnp.where(senders < mesh_rows, senders, mesh_rows + remote)
    for row, scatter, gather in (
        (recv_e()[...], enc_t, enc_g),
        (sent_row(halo()[...], halo_capacity, out_at), halo_t, halo_g),
        (senders, sender_t, sender_g),
        (recv_p()[...], proc_t, proc_g),
    ):
        one = table(row, scatter.ref.shape[0])
        scatter.ref[...] = one.astype(BF16)
        gather.ref[...] = one.T.astype(BF16)
    recv_rows.ref[...] = dot(enc_g.ref[...], mesh()[...]).astype(BF16)


def arrived_rows(blocks):
    size = blocks[0]().shape[0]
    if len(blocks) == 1:
        return joined(blocks)
    rows = [blocks[0]()[...]]
    for t, block in enumerate(blocks[1:]):
        if block().shape[1] == FEATURES:
            rows.append(block()[...])
        else:
            rows.append(block()[t * size : (t + 1) * size, 6 * FEATURES :])
    return jnp.concatenate(rows, axis=0)


def encode_kernel(
    recv_rows, arrived, slot_g, enc_t, mesh, weights, halo_g,
    one_out, slope_e, normed_e, scale_e, slope_n, normed_n, scale_n, *halo_out,
):
    rows_in = arrived_rows(arrived)
    edges = slot_g().shape[0]
    first, second = layers(weights, 0)
    for low in range(0, edges, ROWS):
        rows = pl.ds(low, ROWS)
        sent = dot(slot_g()[rows, :], rows_in).astype(BF16)
        inputs = jnp.concatenate([sent, recv_rows()[rows, :]], axis=1)
        _, slope, normed, rescale = forward(inputs, first, second)
        slope_e.ref[rows, :] = slope
        normed_e.ref[rows, :] = normed
        scale_e.ref[rows, :] = jnp.broadcast_to(rescale, (ROWS, LANES))
    aggregate = dot(enc_t()[...], normed_e.ref[...]).astype(BF16)
    first, second = layers(weights, 1)
    own = mesh()[...]
    normed, slope, rounded, rescale = forward(
        jnp.concatenate([own, aggregate], axis=1), first, second
    )
    one = (own.astype(F32) + normed).astype(BF16)
    one_out.ref[...] = one
    put(dot(halo_g()[...], one), halo_out)
    slope_n.ref[...] = slope
    normed_n.ref[...] = rounded
    scale_n.ref[...] = jnp.broadcast_to(rescale, scale_n.ref.shape)


def process_kernel(
    cotangent_in, one_in, halo, sender_g, proc_g, weights, proc_t, sender_t, two, grad_one, *refs
):
    grad_halo, (slope_p, normed_p, scale_p, ga_p) = refs[:-4], refs[-4:]
    features = FEATURES
    one = one_in()[...]
    mesh_rows = one.shape[0]
    lookup = jnp.concatenate([one, joined(halo)], axis=0)
    edges = sender_g().shape[0]
    first, second = layers(weights, 0)
    for low in range(0, edges, ROWS):
        rows = pl.ds(low, ROWS)
        sent = dot(sender_g()[rows, :], lookup).astype(BF16)
        got = dot(proc_g()[rows, :], one).astype(BF16)
        _, slope, normed, rescale = forward(jnp.concatenate([sent, got], axis=1), first, second)
        slope_p[rows, :] = slope
        normed_p[rows, :] = normed
        scale_p[rows, :] = jnp.broadcast_to(rescale, (ROWS, LANES))
    aggregate = dot(proc_t()[...], normed_p[...]).astype(BF16)
    first_n, second_n = layers(weights, 1)
    normed, slope, rounded, rescale = forward(
        jnp.concatenate([one, aggregate], axis=1), first_n, second_n
    )
    two.send((one.astype(F32) + normed).astype(BF16))
    cotangent = cotangent_in()[...].astype(F32)
    ga = backward_hidden(cotangent, slope, rounded, rescale, second_n)
    g_q = dot(ga, first_n)
    g_msg = g_q[:, features:].astype(BF16)
    for low in range(0, edges, ROWS):
        rows = pl.ds(low, ROWS)
        incoming = dot(proc_g()[rows, :], g_msg)
        ga_p[rows, :] = backward_hidden(
            incoming, slope_p[rows, :], normed_p[rows, :], scale_p[rows, 0:1], second
        )
    by_send = dot(sender_t()[...], ga_p[...]).astype(BF16)
    g_send = dot(by_send, first[:, :features])
    put(g_send[mesh_rows:, :], grad_halo)
    by_recv = dot(proc_t()[...], ga_p[...]).astype(BF16)
    g_recv = dot(by_recv, first[:, features:])
    grad_one.ref[...] = cotangent + g_q[:, :features] + g_recv + g_send[:mesh_rows, :]


def decode_kernel(
    back, halo_t, grad_in, slope_n, normed_n, scale_n, enc_g, slope_e, normed_e, scale_e,
    weights, slot_t, enc_t, mesh_grad, *refs
):
    grad_slots, ga_e = refs[:-1], refs[-1]
    features = FEATURES
    edges = enc_g().shape[0]
    grad_one = grad_in()[...] + dot(halo_t()[...], joined(back))
    first_n, second_n = layers(weights, 1)
    ga = backward_hidden(grad_one, slope_n()[...], normed_n()[...], scale_n()[:, 0:1], second_n)
    g_n = dot(ga, first_n)
    g_edge = g_n[:, features:].astype(BF16)
    first, second = layers(weights, 0)
    for low in range(0, edges, ROWS):
        rows = pl.ds(low, ROWS)
        incoming = dot(enc_g()[rows, :], g_edge)
        ga_e[rows, :] = backward_hidden(
            incoming, slope_e()[rows, :], normed_e()[rows, :], scale_e()[rows, 0:1], second
        )
    by_recv = dot(enc_t()[...], ga_e[...]).astype(BF16)
    mesh_grad.send(grad_one + g_n[:, :features] + dot(by_recv, first[:, features:]))
    by_slot = dot(slot_t()[...], ga_e[...]).astype(BF16)
    put(dot(by_slot, first[:, :features]), grad_slots)


def grid_kernel(back, table_in, out):
    out.send(dot(table_in()[...], joined(back)))


def along(block, shift):
    size = lax.axis_size("mp")
    if shift % size == 0:
        return block
    return lax.ppermute(block, "mp", [(m, (m + shift) % size) for m in range(size)])


def chip_to_chip(blocks):
    names = ("graph", "mp")
    return [blocks[0]] + [
        lax.ppermute(b, names, [(r, r ^ (c // 4 * 8 + c % 4)) for r in range(16)])
        for c, b in enumerate(blocks)
        if c
    ]


def core_to_core(block):
    return lax.ppermute(block, "graph", [(g, g ^ 1) for g in range(4)])


def exchange_all(packed):
    peers = lax.axis_size("graph") * lax.axis_size("mp")
    parts = packed.reshape(peers, -1, LANES)
    parts = lax.all_to_all(parts, ("graph", "mp"), split_axis=0, concat_axis=0, tiled=True)
    return parts.reshape(packed.shape)


def exchange(halves, step):
    if not small():
        return [exchange_all(halves[0])]
    keep, send = halves
    block = shape(16, keep.shape[1], BF16)
    blocks = call(functools.partial(fan_kernel, step), [block] * 8, [keep, core_to_core(send)])
    return chip_to_chip(blocks)


def exchange_back(blocks, step):
    if not small():
        return [exchange_all(blocks[0])]
    half = shape(8 * step, blocks[0].shape[1], BF16)
    keep, send = call(functools.partial(fold_kernel, step), [half] * 2, chip_to_chip(blocks))
    return [keep, core_to_core(send)]


def local(
    grid_lat,
    mesh_lat,
    cotangent,
    grid_send,
    g2m_slot,
    g2m_receiver,
    halo_send,
    mesh_sender,
    mesh_receiver,
    *shards,
):
    grid_rows, features = grid_lat.shape
    mesh_rows = mesh_lat.shape[0]
    edges = g2m_slot.shape[0]
    mesh_edges = mesh_sender.shape[0]
    peers = lax.axis_size("mp") * lax.axis_size("graph")
    step, halo_step = grid_send.shape[1], halo_send.shape[1]
    slots, halos, halos_in = grid_send.size, halo_send.size, in_rows(peers, halo_step)
    spread = peers * stride(step) if small() else slots
    make_tables = lambda: call(
        tables_kernel,
        [
            shape(slots, edges, BF16),
            shape(edges, spread, BF16),
            shape(mesh_rows, edges, BF16),
            shape(edges, mesh_rows, BF16),
            shape(mesh_rows, halos, BF16),
            shape(halos, mesh_rows, BF16),
            shape(mesh_rows + halos_in, mesh_edges, BF16),
            shape(mesh_edges, mesh_rows + halos_in, BF16),
            shape(mesh_rows, mesh_edges, BF16),
            shape(mesh_edges, mesh_rows, BF16),
            shape(edges, features, BF16),
        ],
        Far(mesh_lat),
        Far(g2m_slot.reshape(1, edges)),
        Far(g2m_receiver.reshape(1, edges)),
        Far(halo_send.T),
        Far(mesh_sender.reshape(1, mesh_edges)),
        Far(mesh_receiver.reshape(1, mesh_edges)),
    )
    enc, finish, arrived, grid_t, tables = start(grid_lat, grid_send, shards, make_tables)
    slot_t, slot_g, enc_t, enc_g, halo_t, halo_g, sender_t, sender_g, proc_t, proc_g, recv_rows = tables
    saved = [
        shape(edges, features, BF16),
        shape(edges, features, BF16),
        shape(edges, LANES, F32),
        shape(mesh_rows, features, BF16),
        shape(mesh_rows, features, BF16),
        shape(mesh_rows, LANES, F32),
    ]
    packed = lambda rows: [shape(rows * features // LANES, LANES, BF16)]
    halo_parts = [shape(halos // 2, features, BF16)] * 2 if small() else packed(halos)
    back_parts = [shape(16, features, BF16)] * 8 if small() else packed(halos)
    mesh_one, slope_e, normed_e, scale_e, slope_n, normed_n, scale_n, *halo_out = call(
        encode_kernel,
        [shape(mesh_rows, features, BF16)] + saved + halo_parts,
        recv_rows,
        arrived,
        slot_g,
        enc_t,
        Far(mesh_lat),
        enc,
        halo_g,
        flops=3 * 10**9,
    )
    halo_in = exchange(halo_out, halo_step)
    proc = finish(mesh_one, halo_in[1:6])
    mesh_two, grad_one, *grad_halo = call(
        process_kernel,
        [shape(mesh_rows, features, BF16), shape(mesh_rows, features, F32)] + back_parts,
        Far(cotangent),
        mesh_one,
        halo_in,
        sender_g,
        proc_g,
        proc,
        proc_t,
        sender_t,
        last=(0,),
        flops=5 * 10**9,
        scratch=[
            pltpu.VMEM((mesh_edges, features), BF16),
            pltpu.VMEM((mesh_edges, features), BF16),
            pltpu.VMEM((mesh_edges, LANES), F32),
            pltpu.VMEM((mesh_edges, features), BF16),
        ],
    )
    halo_back = exchange_back(grad_halo, halo_step)
    mesh_grad, *grad_slots = call(
        decode_kernel,
        [shape(mesh_rows, features, F32)] + packed(slots),
        halo_back,
        halo_t,
        grad_one,
        slope_n,
        normed_n,
        scale_n,
        enc_g,
        slope_e,
        normed_e,
        scale_e,
        enc,
        slot_t,
        enc_t,
        last=(0,),
        flops=3 * 10**9,
        scratch=[pltpu.VMEM((edges, features), BF16)],
    )
    returned = exchange_all(grad_slots[0])
    (grid_grad,) = call(
        grid_kernel, [shape(grid_rows, features, F32)], [returned], Far(grid_t), last=(0,)
    )
    return (mesh_two, grid_grad, mesh_grad)


def solution(mesh):
    rows = P(AXES, None)
    flat = P(AXES)
    in_specs = (rows,) * 4 + (flat,) * 2 + (rows,) + (flat,) * 2 + (P(None, "mp"), P("mp", None)) * 4
    return jax.shard_map(
        local, mesh=mesh, in_specs=in_specs, out_specs=(rows,) * 3, check_vma=False
    )
```

```python
import functools

import jax
import jax.numpy as jnp
from jax import lax
from jax.experimental import pallas as pl
from jax.experimental.pallas import tpu as pltpu
from jax.sharding import PartitionSpec as P

F32 = jnp.float32
BF16 = jnp.bfloat16
LANES = 128
ROWS = 256
FEATURES = 512
AXES = ("groups", "graph", "mp")


def dot(left, right):
    return jnp.dot(left, right, preferred_element_type=F32)


def dot_trans(left, right):
    return lax.dot_general(left, right, (((1,), (1,)), ((), ())), preferred_element_type=F32)


def shape(rows, columns, dtype):
    return jax.ShapeDtypeStruct((rows, columns), dtype)


class Far:
    def __init__(self, array):
        self.array = pltpu.with_memory_space_constraint(array, pltpu.HBM)


class Input:
    def __init__(self, copy, ref):
        self.copy, self.ref = copy, ref

    def __call__(self):
        if self.copy is not None:
            self.copy.wait()
            self.copy = None
        return self.ref


class Output:
    def __init__(self, ref, copy):
        self.ref, self.copy = ref, copy

    def send(self, value=None):
        if value is not None:
            self.ref[...] = value
        if self.copy is not None:
            self.copy.start()


def call(kernel, out_shape, *args, last=(), scratch=(), flops=0):
    groups = [a if isinstance(a, list) else [a] for a in args]
    flat = [a for group in groups for a in group]
    far = [isinstance(a, Far) for a in flat]
    arrays = [a.array if isinstance(a, Far) else a for a in flat]
    count, outs = len(arrays), len(out_shape)

    def body(*refs):
        ins, refs = refs[:count], refs[count:]
        out_refs, refs = refs[:outs], refs[outs:]
        places, refs = list(refs[: sum(far)]), refs[sum(far) :]
        results, refs = list(refs[: len(last)]), refs[len(last) :]
        sem_in, sem_out, refs = refs[0], refs[1], refs[2:]
        inputs = []
        for ref, away in zip(ins, far):
            copy = None
            if away:
                place = places.pop(0)
                copy = pltpu.make_async_copy(ref, place, sem_in.at[len(places)])
                copy.start()
                ref = place
            inputs.append(Input(copy, ref))
        outputs = []
        for i, ref in enumerate(out_refs):
            copy = None
            if i in last:
                place = results.pop(0)
                copy = pltpu.make_async_copy(place, ref, sem_out.at[len(results)])
                ref = place
            outputs.append(Output(ref, copy))
        given = []
        for arg, group in zip(args, groups):
            part, inputs = inputs[: len(group)], inputs[len(group) :]
            given.append(part if isinstance(arg, list) else part[0])
        kernel(*given, *outputs, *refs)
        for output in outputs:
            if output.copy is not None:
                output.copy.wait()

    vmem, hbm = pl.BlockSpec(memory_space=pltpu.VMEM), pl.BlockSpec(memory_space=pl.ANY)
    total = sum(a.size * a.dtype.itemsize for a in arrays)
    return pl.pallas_call(
        body,
        out_shape=out_shape,
        in_specs=[hbm if away else vmem for away in far],
        out_specs=[hbm if i in last else vmem for i in range(outs)],
        scratch_shapes=[pltpu.VMEM(a.shape, a.dtype) for a, away in zip(arrays, far) if away]
        + [pltpu.VMEM(out_shape[i].shape, out_shape[i].dtype) for i in last]
        + [pltpu.SemaphoreType.DMA((max(sum(far), 1),)), pltpu.SemaphoreType.DMA((max(len(last), 1),))]
        + list(scratch),
        name=getattr(kernel, "func", kernel).__name__,
        cost_estimate=pl.CostEstimate(flops=flops, bytes_accessed=total, transcendentals=0),
        compiler_params=pltpu.CompilerParams(vmem_limit_bytes=24 * 1024 * 1024),
    )(*arrays)


def layers(blocks, which):
    low = which * 3 * FEATURES
    middle = low + 2 * FEATURES
    return (
        jnp.concatenate([block()[:, low:middle] for block in blocks], axis=0),
        jnp.concatenate([block()[:, middle : middle + FEATURES] for block in blocks], axis=0),
    )


def turned(first, select):
    return dot_trans(select, first).astype(BF16)


def prepare_kernel(grid, send, shards, proc_piece, table_out, kept, *messages):
    plane = lax.axis_index("groups") * lax.axis_size("graph") + lax.axis_index("graph")
    width = 3 * FEATURES
    rows = proc_piece.ref.shape[0]
    base = plane * rows
    for i in range(4):
        one, two = shards[2 * i](), shards[2 * i + 1]()
        hidden = one.shape[1]
        select = jnp.where(
            lax.broadcasted_iota(jnp.int32, (rows, hidden), 0) + base
            == lax.broadcasted_iota(jnp.int32, (rows, hidden), 1),
            1.0,
            0.0,
        ).astype(BF16)
        low = i % 2 * width
        first = turned(one[...], select)
        second = two[pl.ds(pl.multiple_of(base, rows), rows), :]
        for out in (proc_piece,) if i // 2 else messages:
            out.ref[:, low : low + 2 * FEATURES] = first
            out.ref[:, low + 2 * FEATURES : low + width] = second
    outgoing = send_rows(grid, send, table_out, sent_at, stride(send().shape[0]))
    size = kept.ref.shape[0]
    kept.ref[...] = outgoing[:size, :].astype(BF16)
    for i, out in enumerate(messages):
        out.ref[:, 2 * width :] = outgoing[(i + 1) * size : (i + 2) * size, :].astype(BF16)


def join_kernel(kept, messages, near, block, both):
    width = 6 * FEATURES
    weights = jnp.concatenate([m()[:, :width] for m in messages], axis=0)
    rows = jnp.concatenate([kept()[...]] + [m()[:, width:] for m in messages], axis=0)
    step = rows.shape[0] // 16
    block.ref[...] = weights
    both.ref[:, :width] = weights
    size = near.ref.shape[0]
    for j in range(4):
        moved = dot(turn_table(4, 4, step, j), rows).astype(BF16)
        if j == 0:
            near.ref[...] = moved
        else:
            both.ref[(j - 1) * size : j * size, width:] = moved


def own_kernel(shards, *outs):
    width = 3 * FEATURES
    for i in range(4):
        one, two = shards[2 * i](), shards[2 * i + 1]()
        hidden = one.shape[1]
        select = jnp.where(
            lax.broadcasted_iota(jnp.int32, (hidden, hidden), 0)
            == lax.broadcasted_iota(jnp.int32, (hidden, hidden), 1),
            1.0,
            0.0,
        ).astype(BF16)
        out, low = outs[i // 2], i % 2 * width
        out.ref[:, low : low + 2 * FEATURES] = turned(one[...], select)
        out.ref[:, low + 2 * FEATURES : low + width] = two[...]


def across(x, flip):
    planes = lax.axis_size("groups") * lax.axis_size("graph")
    return lax.ppermute(x, ("groups", "graph"), [(p, p ^ flip) for p in range(planes)])


def start(grid_lat, grid_send, shards, make_tables):
    grid_rows, features = grid_lat.shape
    mp, graph = lax.axis_size("mp"), lax.axis_size("graph")
    step = stride(grid_send.shape[1])
    table_shape = shape(grid_rows, mp * graph * spread(grid_send.shape[1]), BF16)
    sent = [table_shape] + [shape(graph * step, features, BF16)] * mp
    planes = lax.axis_size("groups") * graph
    hidden = shards[1].shape[0]
    if planes != 8 or mp != 4 or hidden != 128 or features != FEATURES:
        packed = shape(grid_send.size * features // LANES, LANES, BF16)
        grid_t, *outgoing = call(send_kernel, [table_shape, packed], Far(grid_lat), Far(grid_send.T))
        rows = []
        for i in range(4):
            rows.append(lax.all_gather(shards[2 * i], "mp", axis=1, tiled=True).T)
            rows.append(lax.all_gather(shards[2 * i + 1], "mp", axis=0, tiled=True))
        enc, proc = jnp.concatenate(rows[:4], axis=1), jnp.concatenate(rows[4:], axis=1)
        arrived = [exchange_all(outgoing[0])]
        return [enc], lambda moved: [proc], arrived, grid_t, make_tables()
    far = [Far(s) for s in shards]
    piece = hidden // planes
    width = 6 * features
    proc_piece, grid_t, kept, *messages = call(
        prepare_kernel,
        [shape(piece, width, BF16)] + sent[:2] + [shape(piece, width + features, BF16)] * 3,
        Far(grid_lat),
        Far(grid_send.T),
        far,
    )
    enc_own, proc_own = call(own_kernel, [shape(hidden, width, BF16)] * 2, far)
    messages = [along(m, i + 1) for i, m in enumerate(messages)]
    tables = make_tables()
    kept, enc_own, _ = lax.optimization_barrier((kept, enc_own, tables[0]))
    rows = mp * step
    near, first, both = call(
        join_kernel,
        [shape(rows, features, BF16), shape(3 * piece, width, BF16), shape(3 * rows, width + features, BF16)],
        kept,
        messages,
    )
    x, y, corner = across(both, 2), across(first, 4), across(first, 6)
    proc_piece, _ = lax.optimization_barrier((proc_piece, near))
    beside_me = lax.ppermute(proc_piece, "mp", [(m, m ^ 1) for m in range(mp)])
    pair = jnp.concatenate([proc_piece, beside_me])
    pairs = lax.ppermute(pair, "mp", [(m, m ^ 2) for m in range(mp)])
    proc_first = jnp.concatenate([beside_me, pairs])
    both, x, y, corner, _ = lax.optimization_barrier((both, x, y, corner, pairs))
    core, x_core, others = across(both, 1), across(x, 1), across(jnp.concatenate([y, corner]), 1)
    enc = [enc_own, first, core, x, y, corner, x_core, others]
    arrived = [near, core, x, x_core]
    proc_first, *_ = lax.optimization_barrier((proc_first, x, y, corner))
    plane = [across(proc_first, flip) for flip in (2, 4, 6)]

    def finish(moved):
        tied, *_ = lax.optimization_barrier((jnp.concatenate(plane), *moved))
        return [proc_own, proc_first, across(proc_first, 1)] + plane + [across(tied, 1)]

    return enc, finish, arrived, grid_t, tables


def forward(inputs, first, second):
    before = dot_trans(inputs, first)
    logistic = 0.5 + 0.5 * jnp.tanh(0.5 * before)
    wide = before * logistic
    hidden = wide.astype(BF16)
    slope = logistic + wide * (1.0 - logistic)
    summed = dot(hidden, second)
    centered = summed - jnp.mean(summed, axis=-1, keepdims=True)
    rescale = lax.rsqrt(jnp.mean(centered * centered, axis=-1, keepdims=True) + 1e-05)
    normed = centered * rescale
    return normed, slope.astype(BF16), normed.astype(BF16), rescale


def backward_hidden(incoming, slope, normed, rescale, second):
    normed = normed.astype(F32)
    g_out = (
        incoming
        - jnp.mean(incoming, axis=-1, keepdims=True)
        - normed * jnp.mean(incoming * normed, axis=-1, keepdims=True)
    ) * rescale
    return (dot_trans(g_out.astype(BF16), second) * slope.astype(F32)).astype(BF16)


def table(index_row, count):
    n = index_row.shape[1]
    return jnp.where(lax.broadcasted_iota(jnp.int32, (count, n), 0) == index_row, 1.0, 0.0)


def stride(capacity):
    return max(capacity, 16 // min(lax.axis_size("mp"), lax.axis_size("graph")))


def sent_at(peer, slot, step):
    mp, graph = lax.axis_size("mp"), lax.axis_size("graph")
    shift = (peer % mp + mp - lax.axis_index("mp")) % mp
    return (shift * graph + (peer // mp ^ lax.axis_index("graph"))) * step + slot


def arrived_at(peer, slot, step):
    mp = lax.axis_size("mp")
    shift = (lax.axis_index("mp") + mp - peer % mp) % mp
    return ((peer // mp ^ lax.axis_index("graph")) * mp + shift) * step + slot


def small():
    return lax.axis_size("mp") == 4 and lax.axis_size("graph") == 4


def plain_at(peer, slot, step):
    return peer * step + slot


def apart(peer):
    differs = peer // 4 ^ lax.axis_index("graph")
    return differs % 2, differs // 2


def out_at(peer, slot, step):
    if not small():
        return plain_at(peer, slot, step)
    core, x = apart(peer)
    shift = (peer % 4 + 4 - lax.axis_index("mp")) % 4
    return ((core * 2 + x) * 4 + shift) * step + slot


def in_at(peer, slot, step):
    if not small():
        return plain_at(peer, slot, step)
    core, x = apart(peer)
    shift = (lax.axis_index("mp") + 4 - peer % 4) % 4
    return (shift * 4 + x * 2 + core) * step + slot


def spread(capacity):
    return stride(capacity) if small() else capacity


def sent_row(index, step, order):
    width, count = index.shape
    index = index.astype(F32).T
    at = lax.broadcasted_iota(jnp.int32, (count, count * step), 1)
    peer = lax.broadcasted_iota(jnp.int32, (count, count * step), 0)
    row = jnp.zeros(at.shape, F32)
    for slot in range(width):
        row = jnp.where(order(peer, slot, step) == at, index[:, slot : slot + 1] + 1.0, row)
    return jnp.sum(row, axis=0, keepdims=True).astype(jnp.int32) - 1


def stacked(blocks):
    return jnp.concatenate([block()[...] for block in blocks], axis=0)


def split(rows, outs):
    size = rows.shape[0] // len(outs)
    for i, out in enumerate(outs):
        out.ref[...] = rows[i * size : (i + 1) * size, :].astype(BF16)


def send_rows(grid, send, table_out, order, step):
    index, count = send()[...], grid().shape[0]
    table_out.ref[...] = table(sent_row(index, spread(index.shape[0]), in_at), count).astype(BF16)
    one = table(sent_row(index, step, order), count)
    return dot(one.T.astype(BF16), grid()[...])


def send_kernel(grid, send, table_out, outgoing):
    rows = send_rows(grid, send, table_out, plain_at, send().shape[0])
    outgoing.ref[...] = pack_rows(rows.astype(BF16))


def turn_table(sources, targets, step, j):
    row = lax.broadcasted_iota(jnp.int32, (sources * step, sources * targets * step), 0)
    at = lax.broadcasted_iota(jnp.int32, row.shape, 1)
    source = (row // step * targets + j) * step + row % step
    return jnp.where(at == source, 1.0, 0.0).astype(BF16)


def lane_table(n, blocks, block, tall):
    sizes = (n * blocks, n) if tall else (n, n * blocks)
    long = lax.broadcasted_iota(jnp.int32, sizes, 0 if tall else 1)
    short = lax.broadcasted_iota(jnp.int32, sizes, 1 if tall else 0)
    return jnp.where(long == short * blocks + block, 1.0, 0.0).astype(BF16)


def pack_rows(rows):
    n, blocks = rows.shape[0], rows.shape[1] // LANES
    return sum(
        dot(lane_table(n, blocks, k, True), rows[:, k * LANES : (k + 1) * LANES])
        for k in range(blocks)
    ).astype(BF16)


def unpack_rows(packed):
    blocks = FEATURES // LANES
    n = packed.shape[0] // blocks
    return jnp.concatenate(
        [dot(lane_table(n, blocks, k, False), packed).astype(BF16) for k in range(blocks)], axis=1
    )


def pick_rows(rows, count, source):
    row = lax.broadcasted_iota(jnp.int32, (count, rows.shape[0]), 0)
    at = lax.broadcasted_iota(jnp.int32, row.shape, 1)
    return dot(jnp.where(at == source(row), 1.0, 0.0).astype(BF16), rows).astype(BF16)


def level_kernel(step, inner, halves, *outs):
    rows = stacked(halves)
    count = len(outs)
    for value, out in enumerate(outs):
        size = inner * step

        def source(row, value=value):
            return (row // size * count + value) * size + row % size

        out.ref[...] = pick_rows(rows, out.ref.shape[0], source)


def put(rows, outs):
    rows = rows.astype(BF16)
    if len(outs) == 1:
        outs[0].ref[...] = pack_rows(rows)
    else:
        split(rows, outs)


def joined(blocks):
    rows = stacked(blocks)
    return unpack_rows(rows) if rows.shape[1] == LANES else rows


def tables_kernel(capacity, mesh, slot, recv_e, halo, sender, recv_p, *outs):
    slot_t, slot_g, enc_t, enc_g, halo_t, halo_g, sender_t, sender_g, proc_t, proc_g, recv_rows = outs
    mesh_rows = mesh().shape[0]
    peers, halo_capacity = halo().shape[1], halo().shape[0]
    slots = slot()[...]
    peer, place = slots // capacity, slots % capacity
    step = spread(capacity)
    slot_t.ref[...] = table(out_at(peer, place, step), slot_t.ref.shape[0]).astype(BF16)
    if small():
        slots = arrived_at(peer, place, step)
    slot_g.ref[...] = table(slots, slot_g.ref.shape[1]).T.astype(BF16)
    senders, step = sender()[...], spread(halo_capacity)
    remote = jnp.maximum(senders - mesh_rows, 0)
    peer, place = remote // halo_capacity, remote % halo_capacity
    own = senders < mesh_rows
    coming = jnp.where(own, senders, mesh_rows + in_at(peer, place, step))
    going = jnp.where(own, senders, mesh_rows + out_at(peer, place, step))
    sender_g.ref[...] = table(coming, sender_g.ref.shape[1]).T.astype(BF16)
    sender_t.ref[...] = table(going, sender_t.ref.shape[0]).astype(BF16)
    halo_g.ref[...] = table(sent_row(halo()[...], step, out_at), mesh_rows).T.astype(BF16)
    halo_t.ref[...] = table(sent_row(halo()[...], step, in_at), mesh_rows).astype(BF16)
    for row, scatter, gather in ((recv_e()[...], enc_t, enc_g), (recv_p()[...], proc_t, proc_g)):
        one = table(row, mesh_rows)
        scatter.ref[...] = one.astype(BF16)
        gather.ref[...] = one.T.astype(BF16)
    recv_rows.ref[...] = dot(enc_g.ref[...], mesh()[...]).astype(BF16)


def arrived_rows(blocks):
    size = blocks[0]().shape[0]
    if len(blocks) == 1:
        return joined(blocks)
    rows = [blocks[0]()[...]]
    for t, block in enumerate(blocks[1:]):
        if block().shape[1] == FEATURES:
            rows.append(block()[...])
        else:
            rows.append(block()[t * size : (t + 1) * size, 6 * FEATURES :])
    return jnp.concatenate(rows, axis=0)


def encode_kernel(
    recv_rows, arrived, slot_g, enc_t, mesh, weights, halo_g,
    one_out, slope_e, normed_e, scale_e, slope_n, normed_n, scale_n, *halo_out,
):
    rows_in = arrived_rows(arrived)
    edges = slot_g().shape[0]
    first, second = layers(weights, 0)
    for low in range(0, edges, ROWS):
        rows = pl.ds(low, ROWS)
        sent = dot(slot_g()[rows, :], rows_in).astype(BF16)
        inputs = jnp.concatenate([sent, recv_rows()[rows, :]], axis=1)
        _, slope, normed, rescale = forward(inputs, first, second)
        slope_e.ref[rows, :] = slope
        normed_e.ref[rows, :] = normed
        scale_e.ref[rows, :] = jnp.broadcast_to(rescale, (ROWS, LANES))
    aggregate = dot(enc_t()[...], normed_e.ref[...]).astype(BF16)
    first, second = layers(weights, 1)
    own = mesh()[...]
    normed, slope, rounded, rescale = forward(
        jnp.concatenate([own, aggregate], axis=1), first, second
    )
    one = (own.astype(F32) + normed).astype(BF16)
    one_out.ref[...] = one
    put(dot(halo_g()[...], one), halo_out)
    slope_n.ref[...] = slope
    normed_n.ref[...] = rounded
    scale_n.ref[...] = jnp.broadcast_to(rescale, scale_n.ref.shape)


def process_kernel(
    cotangent_in, one_in, halo, sender_g, proc_g, weights, proc_t, sender_t, two, grad_one, *refs
):
    grad_halo, (slope_p, normed_p, scale_p, ga_p) = refs[:-4], refs[-4:]
    features = FEATURES
    one = one_in()[...]
    mesh_rows = one.shape[0]
    lookup = jnp.concatenate([one, joined(halo)], axis=0)
    edges = sender_g().shape[0]
    first, second = layers(weights, 0)
    for low in range(0, edges, ROWS):
        rows = pl.ds(low, ROWS)
        sent = dot(sender_g()[rows, :], lookup).astype(BF16)
        got = dot(proc_g()[rows, :], one).astype(BF16)
        _, slope, normed, rescale = forward(jnp.concatenate([sent, got], axis=1), first, second)
        slope_p[rows, :] = slope
        normed_p[rows, :] = normed
        scale_p[rows, :] = jnp.broadcast_to(rescale, (ROWS, LANES))
    aggregate = dot(proc_t()[...], normed_p[...]).astype(BF16)
    first_n, second_n = layers(weights, 1)
    normed, slope, rounded, rescale = forward(
        jnp.concatenate([one, aggregate], axis=1), first_n, second_n
    )
    two.send((one.astype(F32) + normed).astype(BF16))
    cotangent = cotangent_in()[...].astype(F32)
    ga = backward_hidden(cotangent, slope, rounded, rescale, second_n)
    g_q = dot(ga, first_n)
    g_msg = g_q[:, features:].astype(BF16)
    for low in range(0, edges, ROWS):
        rows = pl.ds(low, ROWS)
        incoming = dot(proc_g()[rows, :], g_msg)
        ga_p[rows, :] = backward_hidden(
            incoming, slope_p[rows, :], normed_p[rows, :], scale_p[rows, 0:1], second
        )
    by_send = dot(sender_t()[...], ga_p[...]).astype(BF16)
    g_send = dot(by_send, first[:, :features])
    put(g_send[mesh_rows:, :], grad_halo)
    by_recv = dot(proc_t()[...], ga_p[...]).astype(BF16)
    g_recv = dot(by_recv, first[:, features:])
    grad_one.ref[...] = cotangent + g_q[:, :features] + g_recv + g_send[:mesh_rows, :]


def decode_kernel(
    back, halo_t, grad_in, slope_n, normed_n, scale_n, enc_g, slope_e, normed_e, scale_e,
    weights, slot_t, enc_t, mesh_grad, *refs
):
    grad_slots, ga_e = refs[:-1], refs[-1]
    features = FEATURES
    edges = enc_g().shape[0]
    grad_one = grad_in()[...] + dot(halo_t()[...], joined(back))
    first_n, second_n = layers(weights, 1)
    ga = backward_hidden(grad_one, slope_n()[...], normed_n()[...], scale_n()[:, 0:1], second_n)
    g_n = dot(ga, first_n)
    g_edge = g_n[:, features:].astype(BF16)
    first, second = layers(weights, 0)
    for low in range(0, edges, ROWS):
        rows = pl.ds(low, ROWS)
        incoming = dot(enc_g()[rows, :], g_edge)
        ga_e[rows, :] = backward_hidden(
            incoming, slope_e()[rows, :], normed_e()[rows, :], scale_e()[rows, 0:1], second
        )
    by_recv = dot(enc_t()[...], ga_e[...]).astype(BF16)
    mesh_grad.send(grad_one + g_n[:, :features] + dot(by_recv, first[:, features:]))
    by_slot = dot(slot_t()[...], ga_e[...]).astype(BF16)
    put(dot(by_slot, first[:, :features]), grad_slots)


def grid_kernel(back, table_in, out):
    out.send(dot(table_in()[...], joined(back)))


def along(block, shift):
    size = lax.axis_size("mp")
    if shift % size == 0:
        return block
    return lax.ppermute(block, "mp", [(m, (m + shift) % size) for m in range(size)])


def beside(block, flip):
    return lax.ppermute(block, "graph", [(g, g ^ flip) for g in range(4)])


def exchange_all(packed):
    peers = lax.axis_size("graph") * lax.axis_size("mp")
    parts = packed.reshape(peers, -1, LANES)
    parts = lax.all_to_all(parts, ("graph", "mp"), split_axis=0, concat_axis=0, tiled=True)
    return parts.reshape(packed.shape)


def exchange(halves, step, behind=None):
    if not small():
        return [exchange_all(halves[0])]
    width = halves[0].shape[1]
    keep, send = halves
    half, block = shape(8 * step, width, BF16), shape(4 * step, width, BF16)
    level = functools.partial(level_kernel, step)
    keep, send = call(functools.partial(level, 4), [half] * 2, [keep, beside(send, 1)])
    blocks = call(functools.partial(level, 1), [block] * 4, [keep, beside(send, 2)])
    if behind is not None:
        behind(blocks)
    return [along(b, s) for s, b in enumerate(blocks)]


def local(
    grid_lat,
    mesh_lat,
    cotangent,
    grid_send,
    g2m_slot,
    g2m_receiver,
    halo_send,
    mesh_sender,
    mesh_receiver,
    *shards,
):
    grid_rows, features = grid_lat.shape
    mesh_rows = mesh_lat.shape[0]
    edges = g2m_slot.shape[0]
    mesh_edges = mesh_sender.shape[0]
    peers = lax.axis_size("mp") * lax.axis_size("graph")
    step, halo_step = spread(grid_send.shape[1]), spread(halo_send.shape[1])
    slots, halos = peers * step, peers * halo_step
    make_tables = lambda: call(
        functools.partial(tables_kernel, grid_send.shape[1]),
        [
            shape(slots, edges, BF16),
            shape(edges, slots, BF16),
            shape(mesh_rows, edges, BF16),
            shape(edges, mesh_rows, BF16),
            shape(mesh_rows, halos, BF16),
            shape(halos, mesh_rows, BF16),
            shape(mesh_rows + halos, mesh_edges, BF16),
            shape(mesh_edges, mesh_rows + halos, BF16),
            shape(mesh_rows, mesh_edges, BF16),
            shape(mesh_edges, mesh_rows, BF16),
            shape(edges, features, BF16),
        ],
        Far(mesh_lat),
        Far(g2m_slot.reshape(1, edges)),
        Far(g2m_receiver.reshape(1, edges)),
        Far(halo_send.T),
        Far(mesh_sender.reshape(1, mesh_edges)),
        Far(mesh_receiver.reshape(1, mesh_edges)),
    )
    enc, finish, arrived, grid_t, tables = start(grid_lat, grid_send, shards, make_tables)
    slot_t, slot_g, enc_t, enc_g, halo_t, halo_g, sender_t, sender_g, proc_t, proc_g, recv_rows = tables
    saved = [
        shape(edges, features, BF16),
        shape(edges, features, BF16),
        shape(edges, LANES, F32),
        shape(mesh_rows, features, BF16),
        shape(mesh_rows, features, BF16),
        shape(mesh_rows, LANES, F32),
    ]
    def leaving(rows):
        if small():
            return [shape(rows // 2, features, BF16)] * 2
        return [shape(rows * features // LANES, LANES, BF16)]

    mesh_one, slope_e, normed_e, scale_e, slope_n, normed_n, scale_n, *halo_out = call(
        encode_kernel,
        [shape(mesh_rows, features, BF16)] + saved + leaving(halos),
        recv_rows,
        arrived,
        slot_g,
        enc_t,
        Far(mesh_lat),
        enc,
        halo_g,
        flops=3 * 10**9,
    )
    proc = []
    halo_in = exchange(halo_out, halo_step, lambda blocks: proc.extend(finish(blocks)))
    proc = proc or finish(halo_in)
    mesh_two, grad_one, *grad_halo = call(
        process_kernel,
        [shape(mesh_rows, features, BF16), shape(mesh_rows, features, F32)] + leaving(halos),
        Far(cotangent),
        mesh_one,
        halo_in,
        sender_g,
        proc_g,
        proc,
        proc_t,
        sender_t,
        last=(0,),
        flops=5 * 10**9,
        scratch=[
            pltpu.VMEM((mesh_edges, features), BF16),
            pltpu.VMEM((mesh_edges, features), BF16),
            pltpu.VMEM((mesh_edges, LANES), F32),
            pltpu.VMEM((mesh_edges, features), BF16),
        ],
    )
    halo_back = exchange(grad_halo, halo_step)
    mesh_grad, *grad_slots = call(
        decode_kernel,
        [shape(mesh_rows, features, F32)] + leaving(slots),
        halo_back,
        halo_t,
        grad_one,
        slope_n,
        normed_n,
        scale_n,
        enc_g,
        slope_e,
        normed_e,
        scale_e,
        enc,
        slot_t,
        enc_t,
        last=(0,),
        flops=3 * 10**9,
        scratch=[pltpu.VMEM((edges, features), BF16)],
    )
    returned = exchange(grad_slots, step)
    (grid_grad,) = call(
        grid_kernel, [shape(grid_rows, features, F32)], returned, grid_t, last=(0,)
    )
    return (mesh_two, grid_grad, mesh_grad)


def solution(mesh):
    rows = P(AXES, None)
    flat = P(AXES)
    in_specs = (rows,) * 4 + (flat,) * 2 + (rows,) + (flat,) * 2 + (P(None, "mp"), P("mp", None)) * 4
    return jax.shard_map(
        local, mesh=mesh, in_specs=in_specs, out_specs=(rows,) * 3, check_vma=False
    )
```

```python
import jax
import jax.numpy as jnp
from jax import lax
from jax.experimental import pallas as pl
from jax.experimental.pallas import tpu as pltpu
from jax.sharding import PartitionSpec as P

F32 = jnp.float32
BF16 = jnp.bfloat16
LANES = 128
ROWS = 256
FEATURES = 512
AXES = ("groups", "graph", "mp")


def dot(left, right):
    return jnp.dot(left, right, preferred_element_type=F32)


def dot_trans(left, right):
    return lax.dot_general(left, right, (((1,), (1,)), ((), ())), preferred_element_type=F32)


def shape(rows, columns, dtype):
    return jax.ShapeDtypeStruct((rows, columns), dtype)


class Far:
    def __init__(self, array):
        self.array = pltpu.with_memory_space_constraint(array, pltpu.HBM)


class Input:
    def __init__(self, copy, ref):
        self.copy, self.ref = copy, ref

    def __call__(self):
        if self.copy is not None:
            self.copy.wait()
            self.copy = None
        return self.ref


class Output:
    def __init__(self, ref, copy):
        self.ref, self.copy = ref, copy

    def send(self, value=None):
        if value is not None:
            self.ref[...] = value
        if self.copy is not None:
            self.copy.start()


def call(kernel, out_shape, *args, last=(), scratch=(), flops=0):
    groups = [a if isinstance(a, list) else [a] for a in args]
    flat = [a for group in groups for a in group]
    far = [isinstance(a, Far) for a in flat]
    arrays = [a.array if isinstance(a, Far) else a for a in flat]
    count, outs = len(arrays), len(out_shape)

    def body(*refs):
        ins, refs = refs[:count], refs[count:]
        out_refs, refs = refs[:outs], refs[outs:]
        places, refs = list(refs[: sum(far)]), refs[sum(far) :]
        results, refs = list(refs[: len(last)]), refs[len(last) :]
        sem_in, sem_out, refs = refs[0], refs[1], refs[2:]
        inputs = []
        for ref, away in zip(ins, far):
            copy = None
            if away:
                place = places.pop(0)
                copy = pltpu.make_async_copy(ref, place, sem_in.at[len(places)])
                copy.start()
                ref = place
            inputs.append(Input(copy, ref))
        outputs = []
        for i, ref in enumerate(out_refs):
            copy = None
            if i in last:
                place = results.pop(0)
                copy = pltpu.make_async_copy(place, ref, sem_out.at[len(results)])
                ref = place
            outputs.append(Output(ref, copy))
        given = []
        for arg, group in zip(args, groups):
            part, inputs = inputs[: len(group)], inputs[len(group) :]
            given.append(part if isinstance(arg, list) else part[0])
        kernel(*given, *outputs, *refs)
        for output in outputs:
            if output.copy is not None:
                output.copy.wait()

    vmem, hbm = pl.BlockSpec(memory_space=pltpu.VMEM), pl.BlockSpec(memory_space=pl.ANY)
    total = sum(a.size * a.dtype.itemsize for a in arrays)
    return pl.pallas_call(
        body,
        out_shape=out_shape,
        in_specs=[hbm if away else vmem for away in far],
        out_specs=[hbm if i in last else vmem for i in range(outs)],
        scratch_shapes=[pltpu.VMEM(a.shape, a.dtype) for a, away in zip(arrays, far) if away]
        + [pltpu.VMEM(out_shape[i].shape, out_shape[i].dtype) for i in last]
        + [pltpu.SemaphoreType.DMA((max(sum(far), 1),)), pltpu.SemaphoreType.DMA((max(len(last), 1),))]
        + list(scratch),
        name=kernel.__name__,
        cost_estimate=pl.CostEstimate(flops=flops, bytes_accessed=total, transcendentals=0),
        compiler_params=pltpu.CompilerParams(vmem_limit_bytes=24 * 1024 * 1024),
    )(*arrays)


def layers(blocks, which):
    low = which * 3 * FEATURES
    middle = low + 2 * FEATURES
    return (
        jnp.concatenate([block()[:, low:middle] for block in blocks], axis=0),
        jnp.concatenate([block()[:, middle : middle + FEATURES] for block in blocks], axis=0),
    )


def turned(first, select):
    return dot_trans(select, first).astype(BF16)


def prepare_kernel(grid, send, shards, proc_piece, table_out, kept, *messages):
    plane = lax.axis_index("groups") * lax.axis_size("graph") + lax.axis_index("graph")
    width = 3 * FEATURES
    rows = proc_piece.ref.shape[0]
    base = plane * rows
    for i in range(4):
        one, two = shards[2 * i](), shards[2 * i + 1]()
        hidden = one.shape[1]
        select = jnp.where(
            lax.broadcasted_iota(jnp.int32, (rows, hidden), 0) + base
            == lax.broadcasted_iota(jnp.int32, (rows, hidden), 1),
            1.0,
            0.0,
        ).astype(BF16)
        low = i % 2 * width
        first = turned(one[...], select)
        second = two[pl.ds(pl.multiple_of(base, rows), rows), :]
        for out in (proc_piece,) if i // 2 else messages:
            out.ref[:, low : low + 2 * FEATURES] = first
            out.ref[:, low + 2 * FEATURES : low + width] = second
    outgoing = send_rows(grid, send, table_out)
    size = kept.ref.shape[0]
    kept.ref[...] = outgoing[:size, :].astype(BF16)
    for i, out in enumerate(messages):
        out.ref[:, 2 * width :] = outgoing[(i + 1) * size : (i + 2) * size, :].astype(BF16)


def join_kernel(kept, messages, near, block, both):
    width = 6 * FEATURES
    weights = jnp.concatenate([m()[:, :width] for m in messages], axis=0)
    rows = jnp.concatenate([kept()[...]] + [m()[:, width:] for m in messages], axis=0)
    step = rows.shape[0] // 16
    block.ref[...] = weights
    both.ref[:, :width] = weights
    size = near.ref.shape[0]
    for j in range(4):
        moved = dot(turn_table(4, 4, step, j), rows).astype(BF16)
        if j == 0:
            near.ref[...] = moved
        else:
            both.ref[(j - 1) * size : j * size, width:] = moved


def own_kernel(shards, *outs):
    width = 3 * FEATURES
    for i in range(4):
        one, two = shards[2 * i](), shards[2 * i + 1]()
        hidden = one.shape[1]
        select = jnp.where(
            lax.broadcasted_iota(jnp.int32, (hidden, hidden), 0)
            == lax.broadcasted_iota(jnp.int32, (hidden, hidden), 1),
            1.0,
            0.0,
        ).astype(BF16)
        out, low = outs[i // 2], i % 2 * width
        out.ref[:, low : low + 2 * FEATURES] = turned(one[...], select)
        out.ref[:, low + 2 * FEATURES : low + width] = two[...]


def across(x, flip):
    planes = lax.axis_size("groups") * lax.axis_size("graph")
    return lax.ppermute(x, ("groups", "graph"), [(p, p ^ flip) for p in range(planes)])


def start(grid_lat, grid_send, shards, tables):
    grid_rows, features = grid_lat.shape
    mp, graph = lax.axis_size("mp"), lax.axis_size("graph")
    step = stride(grid_send.shape[1])
    sent = [shape(grid_rows, mp * graph * step, BF16)] + [shape(graph * step, features, BF16)] * mp
    planes = lax.axis_size("groups") * graph
    hidden = shards[1].shape[0]
    if planes != 8 or mp != 4 or hidden != 128 or features != FEATURES:
        grid_t, *outgoing = call(send_kernel, sent, Far(grid_lat), Far(grid_send.T))
        rows = []
        for i in range(4):
            rows.append(lax.all_gather(shards[2 * i], "mp", axis=1, tiled=True).T)
            rows.append(lax.all_gather(shards[2 * i + 1], "mp", axis=0, tiled=True))
        enc, proc = jnp.concatenate(rows[:4], axis=1), jnp.concatenate(rows[4:], axis=1)
        arrived = exchange(outgoing, step)
        return [enc], lambda moved, arrive: ([proc], arrive(moved)), arrived, grid_t, tables
    far = [Far(s) for s in shards]
    piece = hidden // planes
    width = 6 * features
    proc_piece, grid_t, kept, *messages = call(
        prepare_kernel,
        [shape(piece, width, BF16)] + sent[:2] + [shape(piece, width + features, BF16)] * 3,
        Far(grid_lat),
        Far(grid_send.T),
        far,
    )
    enc_own, proc_own = call(own_kernel, [shape(hidden, width, BF16)] * 2, far)
    messages = [along(m, i + 1) for i, m in enumerate(messages)]
    proc_piece, enc_own = lax.optimization_barrier((proc_piece, enc_own))
    beside_me = lax.ppermute(proc_piece, "mp", [(m, m ^ 1) for m in range(mp)])
    kept, beside_me, *tables = lax.optimization_barrier((kept, beside_me, *tables))
    rows = mp * step
    near, first, both = call(
        join_kernel,
        [shape(rows, features, BF16), shape(3 * piece, width, BF16), shape(3 * rows, width + features, BF16)],
        kept,
        messages,
    )
    x, y = across(both, 2), across(first, 4)
    pair = jnp.concatenate([proc_piece, beside_me])
    pairs = lax.ppermute(pair, "mp", [(m, m ^ 2) for m in range(mp)])
    proc_first = jnp.concatenate([beside_me, pairs])
    late_x, late_y, both, _ = lax.optimization_barrier((x, y, both, pairs))
    low, high = relay(late_x, late_y)
    core, x_core = across(both, 1), across(late_x, 1)
    corner = jnp.concatenate([low, high], axis=1)
    others = across(jnp.concatenate([y, corner]), 1)
    enc = [enc_own, first, core, x, y, corner, x_core, others]
    arrived = [near, core, x, x_core]
    proc_first, *_ = lax.optimization_barrier((proc_first, low, high))
    proc_x, proc_y = across(proc_first, 2), across(proc_first, 4)

    def finish(moved, arrive):
        x, y, *_ = lax.optimization_barrier((proc_x, proc_y, *moved))
        low, high = relay(x, y)
        came = arrive(moved)
        corner, *_ = lax.optimization_barrier((jnp.concatenate([low, high], axis=1), *came))
        sides = jnp.concatenate([x, y])
        blocks = [proc_own, proc_first, across(proc_first, 1), sides, across(sides, 1)]
        return blocks + [corner, across(corner, 1)], came

    return enc, finish, arrived, grid_t, tables


def relay(x, y):
    half = 3 * FEATURES
    return across(x[:, :half], 4), across(y[:, half : 2 * half], 2)


def forward(inputs, first, second):
    before = dot_trans(inputs, first)
    logistic = 0.5 + 0.5 * jnp.tanh(0.5 * before)
    wide = before * logistic
    hidden = wide.astype(BF16)
    slope = logistic + wide * (1.0 - logistic)
    summed = dot(hidden, second)
    centered = summed - jnp.mean(summed, axis=-1, keepdims=True)
    rescale = lax.rsqrt(jnp.mean(centered * centered, axis=-1, keepdims=True) + 1e-05)
    normed = centered * rescale
    return normed, slope.astype(BF16), normed.astype(BF16), rescale


def backward_hidden(incoming, slope, normed, rescale, second):
    normed = normed.astype(F32)
    g_out = (
        incoming
        - jnp.mean(incoming, axis=-1, keepdims=True)
        - normed * jnp.mean(incoming * normed, axis=-1, keepdims=True)
    ) * rescale
    return (dot_trans(g_out.astype(BF16), second) * slope.astype(F32)).astype(BF16)


def table(index_row, count):
    n = index_row.shape[1]
    return jnp.where(lax.broadcasted_iota(jnp.int32, (count, n), 0) == index_row, 1.0, 0.0)


def stride(capacity):
    return max(capacity, 16 // min(lax.axis_size("mp"), lax.axis_size("graph")))


def sent_at(peer, slot, step):
    mp, graph = lax.axis_size("mp"), lax.axis_size("graph")
    shift = (peer % mp + mp - lax.axis_index("mp")) % mp
    return (shift * graph + (peer // mp ^ lax.axis_index("graph"))) * step + slot


def arrived_at(peer, slot, step):
    mp = lax.axis_size("mp")
    shift = (lax.axis_index("mp") + mp - peer % mp) % mp
    return ((peer // mp ^ lax.axis_index("graph")) * mp + shift) * step + slot


def sent_row(index, step):
    width, count = index.shape
    index = index.astype(F32).T
    at = lax.broadcasted_iota(jnp.int32, (count, count * step), 1)
    peer = lax.broadcasted_iota(jnp.int32, (count, count * step), 0)
    row = jnp.zeros(at.shape, F32)
    for slot in range(width):
        row = jnp.where(sent_at(peer, slot, step) == at, index[:, slot : slot + 1] + 1.0, row)
    return jnp.sum(row, axis=0, keepdims=True).astype(jnp.int32) - 1


def stacked(blocks):
    return jnp.concatenate([block()[...] for block in blocks], axis=0)


def split(rows, outs):
    size = rows.shape[0] // len(outs)
    for i, out in enumerate(outs):
        out.ref[...] = rows[i * size : (i + 1) * size, :].astype(BF16)


def send_rows(grid, send, table_out):
    count = table_out.ref.shape[1]
    one = table(sent_row(send()[...], count // send().shape[1]), grid().shape[0])
    table_out.ref[...] = one.astype(BF16)
    return dot(one.T.astype(BF16), grid()[...])


def send_kernel(grid, send, table_out, *outgoing):
    split(send_rows(grid, send, table_out), outgoing)


def turn_table(sources, targets, step, j):
    row = lax.broadcasted_iota(jnp.int32, (sources * step, sources * targets * step), 0)
    at = lax.broadcasted_iota(jnp.int32, row.shape, 1)
    source = (row // step * targets + j) * step + row % step
    return jnp.where(at == source, 1.0, 0.0).astype(BF16)


def turn_kernel(blocks, *outs):
    rows = stacked(blocks)
    step = rows.shape[0] // (len(blocks) * len(outs))
    for j, out in enumerate(outs):
        out.ref[...] = dot(turn_table(len(blocks), len(outs), step, j), rows).astype(BF16)


def tables_kernel(mesh, slot, recv_e, halo, sender, recv_p, *outs):
    mesh_rows = mesh().shape[0]
    peers = halo().shape[1]
    slot_step, halo_step = outs[0].ref.shape[0] // peers, outs[4].ref.shape[1] // peers
    capacity, halo_capacity = slot_step, halo().shape[0]
    slots = slot()[...]
    slots = arrived_at(slots // capacity, slots % capacity, slot_step)
    senders = sender()[...]
    remote = jnp.maximum(senders - mesh_rows, 0)
    remote = arrived_at(remote // halo_capacity, remote % halo_capacity, halo_step)
    senders = jnp.where(senders < mesh_rows, senders, mesh_rows + remote)
    rows = (slots, recv_e()[...], sent_row(halo()[...], halo_step), senders, recv_p()[...])
    for i, row in enumerate(rows):
        scatter, gather = outs[2 * i : 2 * i + 2]
        one = table(row, scatter.ref.shape[0])
        scatter.ref[...] = one.astype(BF16)
        gather.ref[...] = one.T.astype(BF16)
    outs[10].ref[...] = dot(outs[3].ref[...], mesh()[...]).astype(BF16)


def arrived_rows(blocks):
    size = blocks[0]().shape[0]
    rows = [blocks[0]()[...]]
    for t, block in enumerate(blocks[1:]):
        if block().shape[1] == FEATURES:
            rows.append(block()[...])
        else:
            rows.append(block()[t * size : (t + 1) * size, 6 * FEATURES :])
    return jnp.concatenate(rows, axis=0)


def encode_kernel(
    recv_rows, arrived, slot_g, enc_t, mesh, weights, halo_g,
    one_out, slope_e, normed_e, scale_e, slope_n, normed_n, scale_n, *halo_out,
):
    rows_in = arrived_rows(arrived)
    edges = slot_g().shape[0]
    first, second = layers(weights, 0)
    for low in range(0, edges, ROWS):
        rows = pl.ds(low, ROWS)
        sent = dot(slot_g()[rows, :], rows_in).astype(BF16)
        inputs = jnp.concatenate([sent, recv_rows()[rows, :]], axis=1)
        _, slope, normed, rescale = forward(inputs, first, second)
        slope_e.ref[rows, :] = slope
        normed_e.ref[rows, :] = normed
        scale_e.ref[rows, :] = jnp.broadcast_to(rescale, (ROWS, LANES))
    aggregate = dot(enc_t()[...], normed_e.ref[...]).astype(BF16)
    first, second = layers(weights, 1)
    own = mesh()[...]
    normed, slope, rounded, rescale = forward(
        jnp.concatenate([own, aggregate], axis=1), first, second
    )
    one = (own.astype(F32) + normed).astype(BF16)
    one_out.ref[...] = one
    split(dot(halo_g()[...], one), halo_out)
    slope_n.ref[...] = slope
    normed_n.ref[...] = rounded
    scale_n.ref[...] = jnp.broadcast_to(rescale, scale_n.ref.shape)


def process_kernel(
    cotangent_in, one_in, halo, sender_g, proc_g, weights, proc_t, sender_t, two, grad_one, *refs
):
    grad_halo, (slope_p, normed_p, scale_p, ga_p) = refs[:-4], refs[-4:]
    features = FEATURES
    one = one_in()[...]
    mesh_rows = one.shape[0]
    lookup = jnp.concatenate([one, stacked(halo)], axis=0)
    edges = sender_g().shape[0]
    first, second = layers(weights, 0)
    for low in range(0, edges, ROWS):
        rows = pl.ds(low, ROWS)
        sent = dot(sender_g()[rows, :], lookup).astype(BF16)
        got = dot(proc_g()[rows, :], one).astype(BF16)
        _, slope, normed, rescale = forward(jnp.concatenate([sent, got], axis=1), first, second)
        slope_p[rows, :] = slope
        normed_p[rows, :] = normed
        scale_p[rows, :] = jnp.broadcast_to(rescale, (ROWS, LANES))
    aggregate = dot(proc_t()[...], normed_p[...]).astype(BF16)
    first_n, second_n = layers(weights, 1)
    normed, slope, rounded, rescale = forward(
        jnp.concatenate([one, aggregate], axis=1), first_n, second_n
    )
    two.send((one.astype(F32) + normed).astype(BF16))
    cotangent = cotangent_in()[...].astype(F32)
    ga = backward_hidden(cotangent, slope, rounded, rescale, second_n)
    g_q = dot(ga, first_n)
    g_msg = g_q[:, features:].astype(BF16)
    for low in range(0, edges, ROWS):
        rows = pl.ds(low, ROWS)
        incoming = dot(proc_g()[rows, :], g_msg)
        ga_p[rows, :] = backward_hidden(
            incoming, slope_p[rows, :], normed_p[rows, :], scale_p[rows, 0:1], second
        )
    by_send = dot(sender_t()[...], ga_p[...]).astype(BF16)
    g_send = dot(by_send, first[:, :features])
    split(g_send[mesh_rows:, :], grad_halo)
    by_recv = dot(proc_t()[...], ga_p[...]).astype(BF16)
    g_recv = dot(by_recv, first[:, features:])
    grad_one.ref[...] = cotangent + g_q[:, :features] + g_recv + g_send[:mesh_rows, :]


def decode_kernel(
    back, halo_t, grad_in, slope_n, normed_n, scale_n, enc_g, slope_e, normed_e, scale_e,
    weights, slot_t, enc_t, mesh_grad, *refs
):
    grad_slots, ga_e = refs[:-1], refs[-1]
    features = FEATURES
    edges = enc_g().shape[0]
    grad_one = grad_in()[...] + dot(halo_t()[...], stacked(back))
    first_n, second_n = layers(weights, 1)
    ga = backward_hidden(grad_one, slope_n()[...], normed_n()[...], scale_n()[:, 0:1], second_n)
    g_n = dot(ga, first_n)
    g_edge = g_n[:, features:].astype(BF16)
    first, second = layers(weights, 0)
    for low in range(0, edges, ROWS):
        rows = pl.ds(low, ROWS)
        incoming = dot(enc_g()[rows, :], g_edge)
        ga_e[rows, :] = backward_hidden(
            incoming, slope_e()[rows, :], normed_e()[rows, :], scale_e()[rows, 0:1], second
        )
    by_recv = dot(enc_t()[...], ga_e[...]).astype(BF16)
    mesh_grad.send(grad_one + g_n[:, :features] + dot(by_recv, first[:, features:]))
    by_slot = dot(slot_t()[...], ga_e[...]).astype(BF16)
    split(dot(by_slot, first[:, :features]), grad_slots)


def grid_kernel(back, table_in, out):
    out.send(dot(table_in()[...], stacked(back)))


def along(block, shift):
    size = lax.axis_size("mp")
    if shift % size == 0:
        return block
    return lax.ppermute(block, "mp", [(m, (m + shift) % size) for m in range(size)])


def beside(block, flip):
    if flip == 0:
        return block
    return lax.ppermute(block, "graph", [(g, g ^ flip) for g in range(lax.axis_size("graph"))])


def turn(blocks, count, step):
    out = shape(len(blocks) * step, blocks[0].shape[1], BF16)
    return call(turn_kernel, [out] * count, list(blocks))


def exchange(blocks, step):
    return second_level(first_level(blocks, step))


def first_level(blocks, step):
    return turn([along(b, s) for s, b in enumerate(blocks)], lax.axis_size("graph"), step)


def second_level(blocks):
    return [beside(b, t) for t, b in enumerate(blocks)]


def exchange_back(blocks, step):
    blocks = turn([beside(b, t) for t, b in enumerate(blocks)], lax.axis_size("mp"), step)
    return [along(b, -s) for s, b in enumerate(blocks)]


def local(
    grid_lat,
    mesh_lat,
    cotangent,
    grid_send,
    g2m_slot,
    g2m_receiver,
    halo_send,
    mesh_sender,
    mesh_receiver,
    *shards,
):
    grid_rows, features = grid_lat.shape
    mesh_rows = mesh_lat.shape[0]
    edges = g2m_slot.shape[0]
    mesh_edges = mesh_sender.shape[0]
    mp, graph = lax.axis_size("mp"), lax.axis_size("graph")
    step, halo_step = stride(grid_send.shape[1]), stride(halo_send.shape[1])
    slots, halos = mp * graph * step, mp * graph * halo_step
    tables = call(
        tables_kernel,
        [
            shape(slots, edges, BF16),
            shape(edges, slots, BF16),
            shape(mesh_rows, edges, BF16),
            shape(edges, mesh_rows, BF16),
            shape(mesh_rows, halos, BF16),
            shape(halos, mesh_rows, BF16),
            shape(mesh_rows + halos, mesh_edges, BF16),
            shape(mesh_edges, mesh_rows + halos, BF16),
            shape(mesh_rows, mesh_edges, BF16),
            shape(mesh_edges, mesh_rows, BF16),
            shape(edges, features, BF16),
        ],
        Far(mesh_lat),
        Far(g2m_slot.reshape(1, edges)),
        Far(g2m_receiver.reshape(1, edges)),
        Far(halo_send.T),
        Far(mesh_sender.reshape(1, mesh_edges)),
        Far(mesh_receiver.reshape(1, mesh_edges)),
    )
    enc, finish, arrived, grid_t, tables = start(grid_lat, grid_send, shards, tables)
    slot_t, slot_g, enc_t, enc_g, halo_t, halo_g, sender_t, sender_g, proc_t, proc_g, recv_rows = tables
    saved = [
        shape(edges, features, BF16),
        shape(edges, features, BF16),
        shape(edges, LANES, F32),
        shape(mesh_rows, features, BF16),
        shape(mesh_rows, features, BF16),
        shape(mesh_rows, LANES, F32),
    ]
    mesh_one, slope_e, normed_e, scale_e, slope_n, normed_n, scale_n, *halo_out = call(
        encode_kernel,
        [shape(mesh_rows, features, BF16)] + saved + [shape(graph * halo_step, features, BF16)] * mp,
        recv_rows,
        arrived,
        slot_g,
        enc_t,
        Far(mesh_lat),
        enc,
        halo_g,
        flops=3 * 10**9,
    )
    proc, halo_in = finish(first_level(halo_out, halo_step), second_level)
    mesh_two, grad_one, *grad_halo = call(
        process_kernel,
        [shape(mesh_rows, features, BF16), shape(mesh_rows, features, F32)]
        + [shape(mp * halo_step, features, BF16)] * graph,
        Far(cotangent),
        mesh_one,
        halo_in,
        sender_g,
        proc_g,
        proc,
        proc_t,
        sender_t,
        last=(0,),
        flops=5 * 10**9,
        scratch=[
            pltpu.VMEM((mesh_edges, features), BF16),
            pltpu.VMEM((mesh_edges, features), BF16),
            pltpu.VMEM((mesh_edges, LANES), F32),
            pltpu.VMEM((mesh_edges, features), BF16),
        ],
    )
    halo_back = exchange_back(grad_halo, halo_step)
    mesh_grad, *grad_slots = call(
        decode_kernel,
        [shape(mesh_rows, features, F32)] + [shape(mp * step, features, BF16)] * graph,
        halo_back,
        halo_t,
        grad_one,
        slope_n,
        normed_n,
        scale_n,
        enc_g,
        slope_e,
        normed_e,
        scale_e,
        enc,
        slot_t,
        enc_t,
        last=(0,),
        flops=3 * 10**9,
        scratch=[pltpu.VMEM((edges, features), BF16)],
    )
    returned = exchange_back(grad_slots, step)
    (grid_grad,) = call(
        grid_kernel, [shape(grid_rows, features, F32)], returned, grid_t, last=(0,)
    )
    return (mesh_two, grid_grad, mesh_grad)


def solution(mesh):
    rows = P(AXES, None)
    flat = P(AXES)
    in_specs = (rows,) * 4 + (flat,) * 2 + (rows,) + (flat,) * 2 + (P(None, "mp"), P("mp", None)) * 4
    return jax.shard_map(
        local, mesh=mesh, in_specs=in_specs, out_specs=(rows,) * 3, check_vma=False
    )
```

```python
import jax
import jax.numpy as jnp
from jax import lax
from jax.experimental import pallas as pl
from jax.experimental.pallas import tpu as pltpu
from jax.sharding import PartitionSpec as P

F32 = jnp.float32
BF16 = jnp.bfloat16
LANES = 128
ROWS = 256
FEATURES = 512
AXES = ("groups", "graph", "mp")


def dot(left, right):
    return jnp.dot(left, right, preferred_element_type=F32)


def dot_trans(left, right):
    return lax.dot_general(left, right, (((1,), (1,)), ((), ())), preferred_element_type=F32)


def shape(rows, columns, dtype):
    return jax.ShapeDtypeStruct((rows, columns), dtype)


class Far:
    def __init__(self, array):
        self.array = pltpu.with_memory_space_constraint(array, pltpu.HBM)


class Input:
    def __init__(self, copy, ref):
        self.copy, self.ref = copy, ref

    def __call__(self):
        if self.copy is not None:
            self.copy.wait()
            self.copy = None
        return self.ref


class Output:
    def __init__(self, ref, copy):
        self.ref, self.copy = ref, copy

    def send(self, value=None):
        if value is not None:
            self.ref[...] = value
        if self.copy is not None:
            self.copy.start()


def call(kernel, out_shape, *args, last=(), scratch=(), flops=0):
    groups = [a if isinstance(a, list) else [a] for a in args]
    flat = [a for group in groups for a in group]
    far = [isinstance(a, Far) for a in flat]
    arrays = [a.array if isinstance(a, Far) else a for a in flat]
    count, outs = len(arrays), len(out_shape)

    def body(*refs):
        ins, refs = refs[:count], refs[count:]
        out_refs, refs = refs[:outs], refs[outs:]
        places, refs = list(refs[: sum(far)]), refs[sum(far) :]
        results, refs = list(refs[: len(last)]), refs[len(last) :]
        sem_in, sem_out, refs = refs[0], refs[1], refs[2:]
        inputs = []
        for ref, away in zip(ins, far):
            copy = None
            if away:
                place = places.pop(0)
                copy = pltpu.make_async_copy(ref, place, sem_in.at[len(places)])
                copy.start()
                ref = place
            inputs.append(Input(copy, ref))
        outputs = []
        for i, ref in enumerate(out_refs):
            copy = None
            if i in last:
                place = results.pop(0)
                copy = pltpu.make_async_copy(place, ref, sem_out.at[len(results)])
                ref = place
            outputs.append(Output(ref, copy))
        given = []
        for arg, group in zip(args, groups):
            part, inputs = inputs[: len(group)], inputs[len(group) :]
            given.append(part if isinstance(arg, list) else part[0])
        kernel(*given, *outputs, *refs)
        for output in outputs:
            if output.copy is not None:
                output.copy.wait()

    vmem, hbm = pl.BlockSpec(memory_space=pltpu.VMEM), pl.BlockSpec(memory_space=pl.ANY)
    total = sum(a.size * a.dtype.itemsize for a in arrays)
    return pl.pallas_call(
        body,
        out_shape=out_shape,
        in_specs=[hbm if away else vmem for away in far],
        out_specs=[hbm if i in last else vmem for i in range(outs)],
        scratch_shapes=[pltpu.VMEM(a.shape, a.dtype) for a, away in zip(arrays, far) if away]
        + [pltpu.VMEM(out_shape[i].shape, out_shape[i].dtype) for i in last]
        + [pltpu.SemaphoreType.DMA((max(sum(far), 1),)), pltpu.SemaphoreType.DMA((max(len(last), 1),))]
        + list(scratch),
        name=kernel.__name__,
        cost_estimate=pl.CostEstimate(flops=flops, bytes_accessed=total, transcendentals=0),
        compiler_params=pltpu.CompilerParams(vmem_limit_bytes=24 * 1024 * 1024),
    )(*arrays)


def layers(blocks, which):
    low = which * 3 * FEATURES
    middle = low + 2 * FEATURES
    return (
        jnp.concatenate([block()[:, low:middle] for block in blocks], axis=0),
        jnp.concatenate([block()[:, middle : middle + FEATURES] for block in blocks], axis=0),
    )


def turned(first, select):
    return dot_trans(select, first).astype(BF16)


def prepare_kernel(grid, send, shards, proc_piece, table_out, kept, *messages):
    plane = lax.axis_index("groups") * lax.axis_size("graph") + lax.axis_index("graph")
    width = 3 * FEATURES
    graph = lax.axis_index("graph")
    core_and_y = lax.axis_index("groups") * 2 + graph % 2
    for i, part in enumerate((plane, plane, graph, core_and_y)):
        rows = proc_piece.ref.shape[0] if i // 2 else messages[0].ref.shape[0]
        base = part * rows
        one, two = shards[2 * i](), shards[2 * i + 1]()
        hidden = one.shape[1]
        select = jnp.where(
            lax.broadcasted_iota(jnp.int32, (rows, hidden), 0) + base
            == lax.broadcasted_iota(jnp.int32, (rows, hidden), 1),
            1.0,
            0.0,
        ).astype(BF16)
        low = i % 2 * width
        first = turned(one[...], select)
        second = two[pl.ds(pl.multiple_of(base, rows), rows), :]
        for out in (proc_piece,) if i // 2 else messages:
            out.ref[:, low : low + 2 * FEATURES] = first
            out.ref[:, low + 2 * FEATURES : low + width] = second
    outgoing = send_rows(grid, send, table_out)
    size = kept.ref.shape[0]
    kept.ref[...] = outgoing[:size, :].astype(BF16)
    for i, out in enumerate(messages):
        out.ref[:, 2 * width :] = outgoing[(i + 1) * size : (i + 2) * size, :].astype(BF16)


def join_kernel(kept, messages, near, block, both):
    width = 6 * FEATURES
    weights = jnp.concatenate([m()[:, :width] for m in messages], axis=0)
    rows = jnp.concatenate([kept()[...]] + [m()[:, width:] for m in messages], axis=0)
    step = rows.shape[0] // 16
    block.ref[...] = weights
    both.ref[:, :width] = weights
    size = near.ref.shape[0]
    for j in range(4):
        moved = dot(turn_table(4, 4, step, j), rows).astype(BF16)
        if j == 0:
            near.ref[...] = moved
        else:
            both.ref[(j - 1) * size : j * size, width:] = moved


def own_kernel(shards, *outs):
    width = 3 * FEATURES
    for i in range(4):
        one, two = shards[2 * i](), shards[2 * i + 1]()
        hidden = one.shape[1]
        select = jnp.where(
            lax.broadcasted_iota(jnp.int32, (hidden, hidden), 0)
            == lax.broadcasted_iota(jnp.int32, (hidden, hidden), 1),
            1.0,
            0.0,
        ).astype(BF16)
        out, low = outs[max(i - 1, 0)], i % 2 * width if i < 2 else 0
        out.ref[:, low : low + 2 * FEATURES] = turned(one[...], select)
        out.ref[:, low + 2 * FEATURES : low + width] = two[...]


def across(x, flip):
    planes = lax.axis_size("groups") * lax.axis_size("graph")
    return lax.ppermute(x, ("groups", "graph"), [(p, p ^ flip) for p in range(planes)])


def start(grid_lat, grid_send, shards, tables):
    grid_rows, features = grid_lat.shape
    mp, graph = lax.axis_size("mp"), lax.axis_size("graph")
    step = stride(grid_send.shape[1])
    sent = [shape(grid_rows, mp * graph * step, BF16)] + [shape(graph * step, features, BF16)] * mp
    planes = lax.axis_size("groups") * graph
    hidden = shards[1].shape[0]
    if planes != 8 or mp != 4 or hidden != 128 or features != FEATURES:
        grid_t, *outgoing = call(send_kernel, sent, Far(grid_lat), Far(grid_send.T))
        rows = []
        for i in range(4):
            rows.append(lax.all_gather(shards[2 * i], "mp", axis=1, tiled=True).T)
            rows.append(lax.all_gather(shards[2 * i + 1], "mp", axis=0, tiled=True))
        enc = jnp.concatenate(rows[:4], axis=1)
        edge, node = jnp.concatenate(rows[4:6], axis=1), jnp.concatenate(rows[6:], axis=1)
        arrived = exchange(outgoing, step)
        return [enc], lambda one, early, moved, arrive: ([edge], [node], arrive(moved)), arrived, grid_t, tables
    far = [Far(s) for s in shards]
    piece = hidden // planes
    width = 6 * features
    proc_piece, grid_t, kept, *messages = call(
        prepare_kernel,
        [shape(2 * piece, width, BF16)] + sent[:2] + [shape(piece, width + features, BF16)] * 3,
        Far(grid_lat),
        Far(grid_send.T),
        far,
    )
    enc_own, edge_own, node_own = call(
        own_kernel, [shape(hidden, w, BF16) for w in (width, width // 2, width // 2)], far
    )
    messages = [along(m, i + 1) for i, m in enumerate(messages)]
    kept, enc_own, *tables = lax.optimization_barrier((kept, enc_own, *tables))
    rows = mp * step
    near, first, both = call(
        join_kernel,
        [shape(rows, features, BF16), shape(3 * piece, width, BF16), shape(3 * rows, width + features, BF16)],
        kept,
        messages,
    )
    x, y, corner = across(both, 2), across(first, 4), across(first, 6)
    proc_piece, _ = lax.optimization_barrier((proc_piece, near))
    beside_me = lax.ppermute(proc_piece, "mp", [(m, m ^ 1) for m in range(mp)])
    half = width // 2
    edge_pair, node_pair = [
        jnp.concatenate([proc_piece[:, a : a + half], beside_me[:, a : a + half]]) for a in (0, half)
    ]
    over_two = [(m, m ^ 2) for m in range(mp)]
    edge_pairs = lax.ppermute(edge_pair, "mp", over_two)
    node_pair, _ = lax.optimization_barrier((node_pair, edge_pairs))
    node_pairs = lax.ppermute(node_pair, "mp", over_two)
    both, x, y, corner, _ = lax.optimization_barrier((both, x, y, corner, edge_pairs))
    core, x_core = across(both, 1), across(x, 1)
    enc = [enc_own, first, core, x, y, corner, x_core, across(jnp.concatenate([y, corner]), 1)]
    arrived = [near, core, x, x_core]

    def finish(one, early, moved, arrive):
        near_edge, far_edge, _ = lax.optimization_barrier((beside_me, edge_pairs, one))
        edge = jnp.concatenate([near_edge[:, :half], far_edge])
        edge_x = across(edge, 2)
        near_node, far_node, *_ = lax.optimization_barrier((beside_me, node_pairs, early))
        node = jnp.concatenate([near_node[:, half:], far_node])
        node_y = across(node, 4)
        edge, edge_x, *_ = lax.optimization_barrier((edge, edge_x, *moved))
        edge = jnp.concatenate([edge, edge_x])
        came = arrive(moved)
        node, node_y, *_ = lax.optimization_barrier((node, node_y, *came))
        node = jnp.concatenate([node, node_y])
        return [edge_own, edge, across(edge, 1)], [node_own, node, across(node, 1)], came

    return enc, finish, arrived, grid_t, tables


def forward(inputs, first, second):
    before = dot_trans(inputs, first)
    logistic = 0.5 + 0.5 * jnp.tanh(0.5 * before)
    wide = before * logistic
    hidden = wide.astype(BF16)
    slope = logistic + wide * (1.0 - logistic)
    summed = dot(hidden, second)
    centered = summed - jnp.mean(summed, axis=-1, keepdims=True)
    rescale = lax.rsqrt(jnp.mean(centered * centered, axis=-1, keepdims=True) + 1e-05)
    normed = centered * rescale
    return normed, slope.astype(BF16), normed.astype(BF16), rescale


def backward_hidden(incoming, slope, normed, rescale, second):
    normed = normed.astype(F32)
    g_out = (
        incoming
        - jnp.mean(incoming, axis=-1, keepdims=True)
        - normed * jnp.mean(incoming * normed, axis=-1, keepdims=True)
    ) * rescale
    return (dot_trans(g_out.astype(BF16), second) * slope.astype(F32)).astype(BF16)


def table(index_row, count):
    n = index_row.shape[1]
    return jnp.where(lax.broadcasted_iota(jnp.int32, (count, n), 0) == index_row, 1.0, 0.0)


def stride(capacity):
    return max(capacity, 16 // min(lax.axis_size("mp"), lax.axis_size("graph")))


def sent_at(peer, slot, step):
    mp, graph = lax.axis_size("mp"), lax.axis_size("graph")
    shift = (peer % mp + mp - lax.axis_index("mp")) % mp
    return (shift * graph + (peer // mp ^ lax.axis_index("graph"))) * step + slot


def arrived_at(peer, slot, step):
    mp = lax.axis_size("mp")
    shift = (lax.axis_index("mp") + mp - peer % mp) % mp
    return ((peer // mp ^ lax.axis_index("graph")) * mp + shift) * step + slot


def sent_row(index, step):
    width, count = index.shape
    index = index.astype(F32).T
    at = lax.broadcasted_iota(jnp.int32, (count, count * step), 1)
    peer = lax.broadcasted_iota(jnp.int32, (count, count * step), 0)
    row = jnp.zeros(at.shape, F32)
    for slot in range(width):
        row = jnp.where(sent_at(peer, slot, step) == at, index[:, slot : slot + 1] + 1.0, row)
    return jnp.sum(row, axis=0, keepdims=True).astype(jnp.int32) - 1


def stacked(blocks):
    return jnp.concatenate([block()[...] for block in blocks], axis=0)


def split(rows, outs):
    size = rows.shape[0] // len(outs)
    for i, out in enumerate(outs):
        out.ref[...] = rows[i * size : (i + 1) * size, :].astype(BF16)


def send_rows(grid, send, table_out):
    count = table_out.ref.shape[1]
    one = table(sent_row(send()[...], count // send().shape[1]), grid().shape[0])
    table_out.ref[...] = one.astype(BF16)
    return dot(one.T.astype(BF16), grid()[...])


def send_kernel(grid, send, table_out, *outgoing):
    split(send_rows(grid, send, table_out), outgoing)


def turn_table(sources, targets, step, j):
    row = lax.broadcasted_iota(jnp.int32, (sources * step, sources * targets * step), 0)
    at = lax.broadcasted_iota(jnp.int32, row.shape, 1)
    source = (row // step * targets + j) * step + row % step
    return jnp.where(at == source, 1.0, 0.0).astype(BF16)


def turn_kernel(blocks, *outs):
    rows = stacked(blocks)
    step = rows.shape[0] // (len(blocks) * len(outs))
    for j, out in enumerate(outs):
        out.ref[...] = dot(turn_table(len(blocks), len(outs), step, j), rows).astype(BF16)


def tables_kernel(mesh, slot, recv_e, halo, sender, recv_p, *outs):
    mesh_rows = mesh().shape[0]
    peers = halo().shape[1]
    slot_step, halo_step = outs[0].ref.shape[0] // peers, outs[4].ref.shape[1] // peers
    capacity, halo_capacity = slot_step, halo().shape[0]
    slots = slot()[...]
    slots = arrived_at(slots // capacity, slots % capacity, slot_step)
    senders = sender()[...]
    remote = jnp.maximum(senders - mesh_rows, 0)
    remote = arrived_at(remote // halo_capacity, remote % halo_capacity, halo_step)
    senders = jnp.where(senders < mesh_rows, senders, mesh_rows + remote)
    rows = (slots, recv_e()[...], sent_row(halo()[...], halo_step), senders, recv_p()[...])
    for i, row in enumerate(rows):
        scatter, gather = outs[2 * i : 2 * i + 2]
        one = table(row, scatter.ref.shape[0])
        scatter.ref[...] = one.astype(BF16)
        gather.ref[...] = one.T.astype(BF16)
    outs[10].ref[...] = dot(outs[3].ref[...], mesh()[...]).astype(BF16)


def arrived_rows(blocks):
    size = blocks[0]().shape[0]
    rows = [blocks[0]()[...]]
    for t, block in enumerate(blocks[1:]):
        if block().shape[1] == FEATURES:
            rows.append(block()[...])
        else:
            rows.append(block()[t * size : (t + 1) * size, 6 * FEATURES :])
    return jnp.concatenate(rows, axis=0)


def encode_kernel(
    recv_rows, arrived, slot_g, enc_t, mesh, weights, halo_g,
    one_out, slope_e, normed_e, scale_e, slope_n, normed_n, scale_n, *halo_out,
):
    rows_in = arrived_rows(arrived)
    edges = slot_g().shape[0]
    first, second = layers(weights, 0)
    for low in range(0, edges, ROWS):
        rows = pl.ds(low, ROWS)
        sent = dot(slot_g()[rows, :], rows_in).astype(BF16)
        inputs = jnp.concatenate([sent, recv_rows()[rows, :]], axis=1)
        _, slope, normed, rescale = forward(inputs, first, second)
        slope_e.ref[rows, :] = slope
        normed_e.ref[rows, :] = normed
        scale_e.ref[rows, :] = jnp.broadcast_to(rescale, (ROWS, LANES))
    aggregate = dot(enc_t()[...], normed_e.ref[...]).astype(BF16)
    first, second = layers(weights, 1)
    own = mesh()[...]
    normed, slope, rounded, rescale = forward(
        jnp.concatenate([own, aggregate], axis=1), first, second
    )
    one = (own.astype(F32) + normed).astype(BF16)
    one_out.ref[...] = one
    split(dot(halo_g()[...], one), halo_out)
    slope_n.ref[...] = slope
    normed_n.ref[...] = rounded
    scale_n.ref[...] = jnp.broadcast_to(rescale, scale_n.ref.shape)


def process_kernel(
    cotangent_in, one_in, halo, sender_g, proc_g, edge, node, proc_t, sender_t, two, grad_one, *refs
):
    grad_halo, (slope_p, normed_p, scale_p, ga_p) = refs[:-4], refs[-4:]
    features = FEATURES
    one = one_in()[...]
    mesh_rows = one.shape[0]
    lookup = jnp.concatenate([one, stacked(halo)], axis=0)
    edges = sender_g().shape[0]
    first, second = layers(edge, 0)
    for low in range(0, edges, ROWS):
        rows = pl.ds(low, ROWS)
        sent = dot(sender_g()[rows, :], lookup).astype(BF16)
        got = dot(proc_g()[rows, :], one).astype(BF16)
        _, slope, normed, rescale = forward(jnp.concatenate([sent, got], axis=1), first, second)
        slope_p[rows, :] = slope
        normed_p[rows, :] = normed
        scale_p[rows, :] = jnp.broadcast_to(rescale, (ROWS, LANES))
    aggregate = dot(proc_t()[...], normed_p[...]).astype(BF16)
    first_n, second_n = layers(node, 0)
    normed, slope, rounded, rescale = forward(
        jnp.concatenate([one, aggregate], axis=1), first_n, second_n
    )
    two.send((one.astype(F32) + normed).astype(BF16))
    cotangent = cotangent_in()[...].astype(F32)
    ga = backward_hidden(cotangent, slope, rounded, rescale, second_n)
    g_q = dot(ga, first_n)
    g_msg = g_q[:, features:].astype(BF16)
    for low in range(0, edges, ROWS):
        rows = pl.ds(low, ROWS)
        incoming = dot(proc_g()[rows, :], g_msg)
        ga_p[rows, :] = backward_hidden(
            incoming, slope_p[rows, :], normed_p[rows, :], scale_p[rows, 0:1], second
        )
    by_send = dot(sender_t()[...], ga_p[...]).astype(BF16)
    g_send = dot(by_send, first[:, :features])
    split(g_send[mesh_rows:, :], grad_halo)
    by_recv = dot(proc_t()[...], ga_p[...]).astype(BF16)
    g_recv = dot(by_recv, first[:, features:])
    grad_one.ref[...] = cotangent + g_q[:, :features] + g_recv + g_send[:mesh_rows, :]


def decode_kernel(
    back, halo_t, grad_in, slope_n, normed_n, scale_n, enc_g, slope_e, normed_e, scale_e,
    weights, slot_t, enc_t, mesh_grad, *refs
):
    grad_slots, ga_e = refs[:-1], refs[-1]
    features = FEATURES
    edges = enc_g().shape[0]
    grad_one = grad_in()[...] + dot(halo_t()[...], stacked(back))
    first_n, second_n = layers(weights, 1)
    ga = backward_hidden(grad_one, slope_n()[...], normed_n()[...], scale_n()[:, 0:1], second_n)
    g_n = dot(ga, first_n)
    g_edge = g_n[:, features:].astype(BF16)
    first, second = layers(weights, 0)
    for low in range(0, edges, ROWS):
        rows = pl.ds(low, ROWS)
        incoming = dot(enc_g()[rows, :], g_edge)
        ga_e[rows, :] = backward_hidden(
            incoming, slope_e()[rows, :], normed_e()[rows, :], scale_e()[rows, 0:1], second
        )
    by_recv = dot(enc_t()[...], ga_e[...]).astype(BF16)
    mesh_grad.send(grad_one + g_n[:, :features] + dot(by_recv, first[:, features:]))
    by_slot = dot(slot_t()[...], ga_e[...]).astype(BF16)
    split(dot(by_slot, first[:, :features]), grad_slots)


def grid_kernel(back, table_in, out):
    out.send(dot(table_in()[...], stacked(back)))


def along(block, shift):
    size = lax.axis_size("mp")
    if shift % size == 0:
        return block
    return lax.ppermute(block, "mp", [(m, (m + shift) % size) for m in range(size)])


def beside(block, flip):
    if flip == 0:
        return block
    return lax.ppermute(block, "graph", [(g, g ^ flip) for g in range(lax.axis_size("graph"))])


def turn(blocks, count, step):
    out = shape(len(blocks) * step, blocks[0].shape[1], BF16)
    return call(turn_kernel, [out] * count, list(blocks))


def exchange(blocks, step):
    return second_level(first_level(blocks, step))


def first_level(blocks, step):
    return turn([along(b, s) for s, b in enumerate(blocks)], lax.axis_size("graph"), step)


def second_level(blocks):
    return [beside(b, t) for t, b in enumerate(blocks)]


def exchange_back(blocks, step):
    blocks = turn([beside(b, t) for t, b in enumerate(blocks)], lax.axis_size("mp"), step)
    return [along(b, -s) for s, b in enumerate(blocks)]


def local(
    grid_lat,
    mesh_lat,
    cotangent,
    grid_send,
    g2m_slot,
    g2m_receiver,
    halo_send,
    mesh_sender,
    mesh_receiver,
    *shards,
):
    grid_rows, features = grid_lat.shape
    mesh_rows = mesh_lat.shape[0]
    edges = g2m_slot.shape[0]
    mesh_edges = mesh_sender.shape[0]
    mp, graph = lax.axis_size("mp"), lax.axis_size("graph")
    step, halo_step = stride(grid_send.shape[1]), stride(halo_send.shape[1])
    slots, halos = mp * graph * step, mp * graph * halo_step
    tables = call(
        tables_kernel,
        [
            shape(slots, edges, BF16),
            shape(edges, slots, BF16),
            shape(mesh_rows, edges, BF16),
            shape(edges, mesh_rows, BF16),
            shape(mesh_rows, halos, BF16),
            shape(halos, mesh_rows, BF16),
            shape(mesh_rows + halos, mesh_edges, BF16),
            shape(mesh_edges, mesh_rows + halos, BF16),
            shape(mesh_rows, mesh_edges, BF16),
            shape(mesh_edges, mesh_rows, BF16),
            shape(edges, features, BF16),
        ],
        Far(mesh_lat),
        Far(g2m_slot.reshape(1, edges)),
        Far(g2m_receiver.reshape(1, edges)),
        Far(halo_send.T),
        Far(mesh_sender.reshape(1, mesh_edges)),
        Far(mesh_receiver.reshape(1, mesh_edges)),
    )
    enc, finish, arrived, grid_t, tables = start(grid_lat, grid_send, shards, tables)
    slot_t, slot_g, enc_t, enc_g, halo_t, halo_g, sender_t, sender_g, proc_t, proc_g, recv_rows = tables
    saved = [
        shape(edges, features, BF16),
        shape(edges, features, BF16),
        shape(edges, LANES, F32),
        shape(mesh_rows, features, BF16),
        shape(mesh_rows, features, BF16),
        shape(mesh_rows, LANES, F32),
    ]
    mesh_one, slope_e, normed_e, scale_e, slope_n, normed_n, scale_n, *halo_out = call(
        encode_kernel,
        [shape(mesh_rows, features, BF16)] + saved + [shape(graph * halo_step, features, BF16)] * mp,
        recv_rows,
        arrived,
        slot_g,
        enc_t,
        Far(mesh_lat),
        enc,
        halo_g,
        flops=3 * 10**9,
    )
    shifted = [along(b, s) for s, b in enumerate(halo_out)]
    moved = turn(shifted, graph, halo_step)
    edge, node, halo_in = finish(mesh_one, shifted[1], moved, second_level)
    mesh_two, grad_one, *grad_halo = call(
        process_kernel,
        [shape(mesh_rows, features, BF16), shape(mesh_rows, features, F32)]
        + [shape(mp * halo_step, features, BF16)] * graph,
        Far(cotangent),
        mesh_one,
        halo_in,
        sender_g,
        proc_g,
        edge,
        node,
        proc_t,
        sender_t,
        last=(0,),
        flops=5 * 10**9,
        scratch=[
            pltpu.VMEM((mesh_edges, features), BF16),
            pltpu.VMEM((mesh_edges, features), BF16),
            pltpu.VMEM((mesh_edges, LANES), F32),
            pltpu.VMEM((mesh_edges, features), BF16),
        ],
    )
    halo_back = exchange_back(grad_halo, halo_step)
    mesh_grad, *grad_slots = call(
        decode_kernel,
        [shape(mesh_rows, features, F32)] + [shape(mp * step, features, BF16)] * graph,
        halo_back,
        halo_t,
        grad_one,
        slope_n,
        normed_n,
        scale_n,
        enc_g,
        slope_e,
        normed_e,
        scale_e,
        enc,
        slot_t,
        enc_t,
        last=(0,),
        flops=3 * 10**9,
        scratch=[pltpu.VMEM((edges, features), BF16)],
    )
    returned = exchange_back(grad_slots, step)
    (grid_grad,) = call(
        grid_kernel, [shape(grid_rows, features, F32)], returned, grid_t, last=(0,)
    )
    return (mesh_two, grid_grad, mesh_grad)


def solution(mesh):
    rows = P(AXES, None)
    flat = P(AXES)
    in_specs = (rows,) * 4 + (flat,) * 2 + (rows,) + (flat,) * 2 + (P(None, "mp"), P("mp", None)) * 4
    return jax.shard_map(
        local, mesh=mesh, in_specs=in_specs, out_specs=(rows,) * 3, check_vma=False
    )
```

```python
import jax
import jax.numpy as jnp
from jax import lax
from jax.experimental import pallas as pl
from jax.experimental.pallas import tpu as pltpu
from jax.sharding import PartitionSpec as P

F32 = jnp.float32
BF16 = jnp.bfloat16
LANES = 128
ROWS = 256
FEATURES = 512
AXES = ("groups", "graph", "mp")


def dot(left, right):
    return jnp.dot(left, right, preferred_element_type=F32)


def dot_trans(left, right):
    return lax.dot_general(left, right, (((1,), (1,)), ((), ())), preferred_element_type=F32)


def shape(rows, columns, dtype):
    return jax.ShapeDtypeStruct((rows, columns), dtype)


class Far:
    def __init__(self, array):
        self.array = pltpu.with_memory_space_constraint(array, pltpu.HBM)


class Input:
    def __init__(self, copy, ref):
        self.copy, self.ref = copy, ref

    def __call__(self):
        if self.copy is not None:
            self.copy.wait()
            self.copy = None
        return self.ref


class Output:
    def __init__(self, ref, copy):
        self.ref, self.copy = ref, copy

    def send(self, value=None):
        if value is not None:
            self.ref[...] = value
        if self.copy is not None:
            self.copy.start()


def call(kernel, out_shape, *args, last=(), scratch=(), flops=0):
    groups = [a if isinstance(a, list) else [a] for a in args]
    flat = [a for group in groups for a in group]
    far = [isinstance(a, Far) for a in flat]
    arrays = [a.array if isinstance(a, Far) else a for a in flat]
    count, outs = len(arrays), len(out_shape)

    def body(*refs):
        ins, refs = refs[:count], refs[count:]
        out_refs, refs = refs[:outs], refs[outs:]
        places, refs = list(refs[: sum(far)]), refs[sum(far) :]
        results, refs = list(refs[: len(last)]), refs[len(last) :]
        sem_in, sem_out, refs = refs[0], refs[1], refs[2:]
        inputs = []
        for ref, away in zip(ins, far):
            copy = None
            if away:
                place = places.pop(0)
                copy = pltpu.make_async_copy(ref, place, sem_in.at[len(places)])
                copy.start()
                ref = place
            inputs.append(Input(copy, ref))
        outputs = []
        for i, ref in enumerate(out_refs):
            copy = None
            if i in last:
                place = results.pop(0)
                copy = pltpu.make_async_copy(place, ref, sem_out.at[len(results)])
                ref = place
            outputs.append(Output(ref, copy))
        given = []
        for arg, group in zip(args, groups):
            part, inputs = inputs[: len(group)], inputs[len(group) :]
            given.append(part if isinstance(arg, list) else part[0])
        kernel(*given, *outputs, *refs)
        for output in outputs:
            if output.copy is not None:
                output.copy.wait()

    vmem, hbm = pl.BlockSpec(memory_space=pltpu.VMEM), pl.BlockSpec(memory_space=pl.ANY)
    total = sum(a.size * a.dtype.itemsize for a in arrays)
    return pl.pallas_call(
        body,
        out_shape=out_shape,
        in_specs=[hbm if away else vmem for away in far],
        out_specs=[hbm if i in last else vmem for i in range(outs)],
        scratch_shapes=[pltpu.VMEM(a.shape, a.dtype) for a, away in zip(arrays, far) if away]
        + [pltpu.VMEM(out_shape[i].shape, out_shape[i].dtype) for i in last]
        + [pltpu.SemaphoreType.DMA((max(sum(far), 1),)), pltpu.SemaphoreType.DMA((max(len(last), 1),))]
        + list(scratch),
        name=kernel.__name__,
        cost_estimate=pl.CostEstimate(flops=flops, bytes_accessed=total, transcendentals=0),
        compiler_params=pltpu.CompilerParams(vmem_limit_bytes=24 * 1024 * 1024),
    )(*arrays)


def layers(blocks, which):
    low = which * 3 * FEATURES
    middle = low + 2 * FEATURES
    return (
        jnp.concatenate([block()[:, low:middle] for block in blocks], axis=0),
        jnp.concatenate([block()[:, middle : middle + FEATURES] for block in blocks], axis=0),
    )


def turned(first, select):
    return dot_trans(select, first).astype(BF16)


def prepare_kernel(grid, send, shards, table_out, kept, *messages):
    width = 3 * FEATURES
    outgoing = send_rows(grid, send, table_out)
    size = kept.ref.shape[0]
    kept.ref[...] = outgoing[:size, :].astype(BF16)
    for i, out in enumerate(messages):
        out.ref[:, 2 * width :] = outgoing[(i + 1) * size : (i + 2) * size, :].astype(BF16)
    for i in range(2):
        first, second = piece_of(shards[2 * i], shards[2 * i + 1], messages[0].ref.shape[0])
        low = i * width
        for out in messages:
            out.ref[:, low : low + 2 * FEATURES] = first
            out.ref[:, low + 2 * FEATURES : low + width] = second


def piece_of(one, two, rows):
    plane = lax.axis_index("groups") * lax.axis_size("graph") + lax.axis_index("graph")
    base = plane * rows
    hidden = two().shape[0]
    select = jnp.where(
        lax.broadcasted_iota(jnp.int32, (rows, hidden), 0) + base
        == lax.broadcasted_iota(jnp.int32, (rows, hidden), 1),
        1.0,
        0.0,
    ).astype(BF16)
    return turned(one()[...], select), two()[pl.ds(pl.multiple_of(base, rows), rows), :]


def join_kernel(kept, messages, near, block, both):
    width = 6 * FEATURES
    weights = jnp.concatenate([m()[:, :width] for m in messages], axis=0)
    rows = jnp.concatenate([kept()[...]] + [m()[:, width:] for m in messages], axis=0)
    step = rows.shape[0] // 16
    block.ref[...] = weights
    both.ref[:, :width] = weights
    size = near.ref.shape[0]
    for j in range(4):
        moved = dot(turn_table(4, 4, step, j), rows).astype(BF16)
        if j == 0:
            near.ref[...] = moved
        else:
            both.ref[(j - 1) * size : j * size, width:] = moved


def own_kernel(shards, enc_own, proc_own, proc_piece):
    width = 3 * FEATURES
    for i in range(4):
        one, two = shards[2 * i](), shards[2 * i + 1]()
        hidden = one.shape[1]
        select = jnp.where(
            lax.broadcasted_iota(jnp.int32, (hidden, hidden), 0)
            == lax.broadcasted_iota(jnp.int32, (hidden, hidden), 1),
            1.0,
            0.0,
        ).astype(BF16)
        out, low = (enc_own, proc_own)[i // 2], i % 2 * width
        out.ref[:, low : low + 2 * FEATURES] = turned(one[...], select)
        out.ref[:, low + 2 * FEATURES : low + width] = two[...]
    for i in (2, 3):
        first, second = piece_of(shards[2 * i], shards[2 * i + 1], proc_piece.ref.shape[0])
        low = i % 2 * width
        proc_piece.ref[:, low : low + 2 * FEATURES] = first
        proc_piece.ref[:, low + 2 * FEATURES : low + width] = second


def across(x, flip):
    planes = lax.axis_size("groups") * lax.axis_size("graph")
    return lax.ppermute(x, ("groups", "graph"), [(p, p ^ flip) for p in range(planes)])


def start(grid_lat, grid_send, shards, tables):
    grid_rows, features = grid_lat.shape
    mp, graph = lax.axis_size("mp"), lax.axis_size("graph")
    step = stride(grid_send.shape[1])
    sent = [shape(grid_rows, mp * graph * step, BF16)] + [shape(graph * step, features, BF16)] * mp
    planes = lax.axis_size("groups") * graph
    hidden = shards[1].shape[0]
    if planes != 8 or mp != 4 or hidden != 128 or features != FEATURES:
        grid_t, *outgoing = call(send_kernel, sent, Far(grid_lat), Far(grid_send.T))
        rows = []
        for i in range(4):
            rows.append(lax.all_gather(shards[2 * i], "mp", axis=1, tiled=True).T)
            rows.append(lax.all_gather(shards[2 * i + 1], "mp", axis=0, tiled=True))
        enc, proc = jnp.concatenate(rows[:4], axis=1), jnp.concatenate(rows[4:], axis=1)
        arrived = exchange(outgoing, step)
        return [enc], lambda after: [proc], arrived, grid_t, tables
    far = [Far(s) for s in shards]
    piece = hidden // planes
    width = 6 * features
    grid_t, kept, *messages = call(
        prepare_kernel,
        sent[:2] + [shape(piece, width + features, BF16)] * 3,
        Far(grid_lat),
        Far(grid_send.T),
        far[:4],
    )
    enc_own, proc_own, proc_piece = call(
        own_kernel, [shape(hidden, width, BF16)] * 2 + [shape(piece, width, BF16)], far
    )
    messages = [along(m, i + 1) for i, m in enumerate(messages)]
    kept, enc_own, *tables = lax.optimization_barrier((kept, enc_own, *tables))
    rows = mp * step
    near, first, both = call(
        join_kernel,
        [shape(rows, features, BF16), shape(3 * piece, width, BF16), shape(3 * rows, width + features, BF16)],
        kept,
        messages,
    )
    x, y, corner = across(both, 2), across(first, 4), across(first, 6)
    proc_piece, _ = lax.optimization_barrier((proc_piece, near))
    beside_me = lax.ppermute(proc_piece, "mp", [(m, m ^ 1) for m in range(mp)])
    pair = jnp.concatenate([proc_piece, beside_me])
    pairs = lax.ppermute(pair, "mp", [(m, m ^ 2) for m in range(mp)])
    proc_first = jnp.concatenate([beside_me, pairs])
    both, x, y, corner, _ = lax.optimization_barrier((both, x, y, corner, pairs))
    core, x_core, others = across(both, 1), across(x, 1), across(jnp.concatenate([y, corner]), 1)
    enc = [enc_own, first, core, x, y, corner, x_core, others]
    arrived = [near, core, x, x_core]
    proc_first, *_ = lax.optimization_barrier((proc_first, x, y, corner))
    plane = [across(proc_first, flip) for flip in (2, 4, 6)]
    proc = [proc_own, proc_first, across(proc_first, 1)] + plane

    def finish(after):
        tied = [lax.optimization_barrier((block, *after))[0] for block in plane]
        return proc + [across(jnp.concatenate(tied), 1)]

    return enc, finish, arrived, grid_t, tables


def forward(inputs, first, second):
    before = dot_trans(inputs, first)
    logistic = 0.5 + 0.5 * jnp.tanh(0.5 * before)
    wide = before * logistic
    hidden = wide.astype(BF16)
    slope = logistic + wide * (1.0 - logistic)
    summed = dot(hidden, second)
    centered = summed - jnp.mean(summed, axis=-1, keepdims=True)
    rescale = lax.rsqrt(jnp.mean(centered * centered, axis=-1, keepdims=True) + 1e-05)
    normed = centered * rescale
    return normed, slope.astype(BF16), normed.astype(BF16), rescale


def backward_hidden(incoming, slope, normed, rescale, second):
    normed = normed.astype(F32)
    g_out = (
        incoming
        - jnp.mean(incoming, axis=-1, keepdims=True)
        - normed * jnp.mean(incoming * normed, axis=-1, keepdims=True)
    ) * rescale
    return (dot_trans(g_out.astype(BF16), second) * slope.astype(F32)).astype(BF16)


def table(index_row, count):
    n = index_row.shape[1]
    return jnp.where(lax.broadcasted_iota(jnp.int32, (count, n), 0) == index_row, 1.0, 0.0)


def stride(capacity):
    return max(capacity, 16 // min(lax.axis_size("mp"), lax.axis_size("graph")))


def sent_at(peer, slot, step):
    mp, graph = lax.axis_size("mp"), lax.axis_size("graph")
    shift = (peer % mp + mp - lax.axis_index("mp")) % mp
    return (shift * graph + (peer // mp ^ lax.axis_index("graph"))) * step + slot


def arrived_at(peer, slot, step):
    mp = lax.axis_size("mp")
    shift = (lax.axis_index("mp") + mp - peer % mp) % mp
    return ((peer // mp ^ lax.axis_index("graph")) * mp + shift) * step + slot


def sent_row(index, step):
    width, count = index.shape
    index = index.astype(F32).T
    at = lax.broadcasted_iota(jnp.int32, (count, count * step), 1)
    peer = lax.broadcasted_iota(jnp.int32, (count, count * step), 0)
    row = jnp.zeros(at.shape, F32)
    for slot in range(width):
        row = jnp.where(sent_at(peer, slot, step) == at, index[:, slot : slot + 1] + 1.0, row)
    return jnp.sum(row, axis=0, keepdims=True).astype(jnp.int32) - 1


def stacked(blocks):
    return jnp.concatenate([block()[...] for block in blocks], axis=0)


def split(rows, outs):
    size = rows.shape[0] // len(outs)
    for i, out in enumerate(outs):
        out.ref[...] = rows[i * size : (i + 1) * size, :].astype(BF16)


def send_rows(grid, send, table_out):
    count = table_out.ref.shape[1]
    one = table(sent_row(send()[...], count // send().shape[1]), grid().shape[0])
    table_out.ref[...] = one.astype(BF16)
    return dot(one.T.astype(BF16), grid()[...])


def send_kernel(grid, send, table_out, *outgoing):
    split(send_rows(grid, send, table_out), outgoing)


def turn_table(sources, targets, step, j):
    row = lax.broadcasted_iota(jnp.int32, (sources * step, sources * targets * step), 0)
    at = lax.broadcasted_iota(jnp.int32, row.shape, 1)
    source = (row // step * targets + j) * step + row % step
    return jnp.where(at == source, 1.0, 0.0).astype(BF16)


def turn_kernel(blocks, *outs):
    rows = stacked(blocks)
    step = rows.shape[0] // (len(blocks) * len(outs))
    for j, out in enumerate(outs):
        out.ref[...] = dot(turn_table(len(blocks), len(outs), step, j), rows).astype(BF16)


def tables_kernel(mesh, slot, recv_e, halo, sender, recv_p, *outs):
    mesh_rows = mesh().shape[0]
    peers = halo().shape[1]
    slot_step, halo_step = outs[0].ref.shape[0] // peers, outs[4].ref.shape[1] // peers
    capacity, halo_capacity = slot_step, halo().shape[0]
    slots = slot()[...]
    slots = arrived_at(slots // capacity, slots % capacity, slot_step)
    senders = sender()[...]
    remote = jnp.maximum(senders - mesh_rows, 0)
    remote = arrived_at(remote // halo_capacity, remote % halo_capacity, halo_step)
    senders = jnp.where(senders < mesh_rows, senders, mesh_rows + remote)
    rows = (slots, recv_e()[...], sent_row(halo()[...], halo_step), senders, recv_p()[...])
    for i, row in enumerate(rows):
        scatter, gather = outs[2 * i : 2 * i + 2]
        one = table(row, scatter.ref.shape[0])
        scatter.ref[...] = one.astype(BF16)
        gather.ref[...] = one.T.astype(BF16)
    outs[10].ref[...] = dot(outs[3].ref[...], mesh()[...]).astype(BF16)


def arrived_rows(blocks):
    size = blocks[0]().shape[0]
    rows = [blocks[0]()[...]]
    for t, block in enumerate(blocks[1:]):
        if block().shape[1] == FEATURES:
            rows.append(block()[...])
        else:
            rows.append(block()[t * size : (t + 1) * size, 6 * FEATURES :])
    return jnp.concatenate(rows, axis=0)


def encode_kernel(
    recv_rows, arrived, slot_g, enc_t, mesh, weights, halo_g,
    one_out, slope_e, normed_e, scale_e, slope_n, normed_n, scale_n, *halo_out,
):
    rows_in = arrived_rows(arrived)
    edges = slot_g().shape[0]
    first, second = layers(weights, 0)
    for low in range(0, edges, ROWS):
        rows = pl.ds(low, ROWS)
        sent = dot(slot_g()[rows, :], rows_in).astype(BF16)
        inputs = jnp.concatenate([sent, recv_rows()[rows, :]], axis=1)
        _, slope, normed, rescale = forward(inputs, first, second)
        slope_e.ref[rows, :] = slope
        normed_e.ref[rows, :] = normed
        scale_e.ref[rows, :] = jnp.broadcast_to(rescale, (ROWS, LANES))
    aggregate = dot(enc_t()[...], normed_e.ref[...]).astype(BF16)
    first, second = layers(weights, 1)
    own = mesh()[...]
    normed, slope, rounded, rescale = forward(
        jnp.concatenate([own, aggregate], axis=1), first, second
    )
    one = (own.astype(F32) + normed).astype(BF16)
    one_out.ref[...] = one
    split(dot(halo_g()[...], one), halo_out)
    slope_n.ref[...] = slope
    normed_n.ref[...] = rounded
    scale_n.ref[...] = jnp.broadcast_to(rescale, scale_n.ref.shape)


def process_kernel(
    cotangent_in, one_in, halo, sender_g, proc_g, weights, proc_t, sender_t, two, part, ga, *refs
):
    grad_halo, (slope_p, normed_p, scale_p) = refs[:-3], refs[-3:]
    ga_p = ga.ref
    features = FEATURES
    one = one_in()[...]
    mesh_rows = one.shape[0]
    lookup = jnp.concatenate([one, stacked(halo)], axis=0)
    edges = sender_g().shape[0]
    first, second = layers(weights, 0)
    for low in range(0, edges, ROWS):
        rows = pl.ds(low, ROWS)
        sent = dot(sender_g()[rows, :], lookup).astype(BF16)
        got = dot(proc_g()[rows, :], one).astype(BF16)
        _, slope, normed, rescale = forward(jnp.concatenate([sent, got], axis=1), first, second)
        slope_p[rows, :] = slope
        normed_p[rows, :] = normed
        scale_p[rows, :] = jnp.broadcast_to(rescale, (ROWS, LANES))
    aggregate = dot(proc_t()[...], normed_p[...]).astype(BF16)
    first_n, second_n = layers(weights, 1)
    normed, slope, rounded, rescale = forward(
        jnp.concatenate([one, aggregate], axis=1), first_n, second_n
    )
    two.send((one.astype(F32) + normed).astype(BF16))
    cotangent = cotangent_in()[...].astype(F32)
    g_q = dot(backward_hidden(cotangent, slope, rounded, rescale, second_n), first_n)
    g_msg = g_q[:, features:].astype(BF16)
    for low in range(0, edges, ROWS):
        rows = pl.ds(low, ROWS)
        incoming = dot(proc_g()[rows, :], g_msg)
        ga_p[rows, :] = backward_hidden(
            incoming, slope_p[rows, :], normed_p[rows, :], scale_p[rows, 0:1], second
        )
    by_send = dot(sender_t()[...], ga_p[...]).astype(BF16)
    g_send = dot(by_send, first[:, :features])
    split(g_send[mesh_rows:, :], grad_halo)
    part.ref[...] = cotangent + g_q[:, :features] + g_send[:mesh_rows, :]


def receive_kernel(part, ga, scatter, weights, out):
    by_recv = dot(scatter()[...], ga()[...]).astype(BF16)
    first, _ = layers(weights, 0)
    out.send(part()[...] + dot(by_recv, first[:, FEATURES:]))


def decode_kernel(
    back, halo_t, grad_in, slope_n, normed_n, scale_n, enc_g, slope_e, normed_e, scale_e,
    weights, slot_t, part, ga, *grad_slots
):
    ga_e = ga.ref
    features = FEATURES
    edges = enc_g().shape[0]
    grad_one = grad_in()[...] + dot(halo_t()[...], stacked(back))
    first_n, second_n = layers(weights, 1)
    ga_n = backward_hidden(grad_one, slope_n()[...], normed_n()[...], scale_n()[:, 0:1], second_n)
    g_n = dot(ga_n, first_n)
    part.ref[...] = grad_one + g_n[:, :features]
    g_edge = g_n[:, features:].astype(BF16)
    first, second = layers(weights, 0)
    for low in range(0, edges, ROWS):
        rows = pl.ds(low, ROWS)
        incoming = dot(enc_g()[rows, :], g_edge)
        ga_e[rows, :] = backward_hidden(
            incoming, slope_e()[rows, :], normed_e()[rows, :], scale_e()[rows, 0:1], second
        )
    by_slot = dot(slot_t()[...], ga_e[...]).astype(BF16)
    split(dot(by_slot, first[:, :features]), grad_slots)


def grid_kernel(back, table_in, out):
    out.send(dot(table_in()[...], stacked(back)))


def along(block, shift):
    size = lax.axis_size("mp")
    if shift % size == 0:
        return block
    return lax.ppermute(block, "mp", [(m, (m + shift) % size) for m in range(size)])


def beside(block, flip):
    if flip == 0:
        return block
    return lax.ppermute(block, "graph", [(g, g ^ flip) for g in range(lax.axis_size("graph"))])


def turn(blocks, count, step):
    out = shape(len(blocks) * step, blocks[0].shape[1], BF16)
    return call(turn_kernel, [out] * count, list(blocks))


def exchange(blocks, step):
    return second_level(first_level(blocks, step))


def first_level(blocks, step):
    return turn([along(b, s) for s, b in enumerate(blocks)], lax.axis_size("graph"), step)


def second_level(blocks):
    return [beside(b, t) for t, b in enumerate(blocks)]


def exchange_back(blocks, step):
    blocks = turn([beside(b, t) for t, b in enumerate(blocks)], lax.axis_size("mp"), step)
    return [along(b, -s) for s, b in enumerate(blocks)], blocks[0]


def local(
    grid_lat,
    mesh_lat,
    cotangent,
    grid_send,
    g2m_slot,
    g2m_receiver,
    halo_send,
    mesh_sender,
    mesh_receiver,
    *shards,
):
    grid_rows, features = grid_lat.shape
    mesh_rows = mesh_lat.shape[0]
    edges = g2m_slot.shape[0]
    mesh_edges = mesh_sender.shape[0]
    mp, graph = lax.axis_size("mp"), lax.axis_size("graph")
    step, halo_step = stride(grid_send.shape[1]), stride(halo_send.shape[1])
    slots, halos = mp * graph * step, mp * graph * halo_step
    tables = call(
        tables_kernel,
        [
            shape(slots, edges, BF16),
            shape(edges, slots, BF16),
            shape(mesh_rows, edges, BF16),
            shape(edges, mesh_rows, BF16),
            shape(mesh_rows, halos, BF16),
            shape(halos, mesh_rows, BF16),
            shape(mesh_rows + halos, mesh_edges, BF16),
            shape(mesh_edges, mesh_rows + halos, BF16),
            shape(mesh_rows, mesh_edges, BF16),
            shape(mesh_edges, mesh_rows, BF16),
            shape(edges, features, BF16),
        ],
        Far(mesh_lat),
        Far(g2m_slot.reshape(1, edges)),
        Far(g2m_receiver.reshape(1, edges)),
        Far(halo_send.T),
        Far(mesh_sender.reshape(1, mesh_edges)),
        Far(mesh_receiver.reshape(1, mesh_edges)),
    )
    enc, finish, arrived, grid_t, tables = start(grid_lat, grid_send, shards, tables)
    slot_t, slot_g, enc_t, enc_g, halo_t, halo_g, sender_t, sender_g, proc_t, proc_g, recv_rows = tables
    saved = [
        shape(edges, features, BF16),
        shape(edges, features, BF16),
        shape(edges, LANES, F32),
        shape(mesh_rows, features, BF16),
        shape(mesh_rows, features, BF16),
        shape(mesh_rows, LANES, F32),
    ]
    mesh_one, slope_e, normed_e, scale_e, slope_n, normed_n, scale_n, *halo_out = call(
        encode_kernel,
        [shape(mesh_rows, features, BF16)] + saved + [shape(graph * halo_step, features, BF16)] * mp,
        recv_rows,
        arrived,
        slot_g,
        enc_t,
        Far(mesh_lat),
        enc,
        halo_g,
        flops=3 * 10**9,
    )
    halo_in = second_level(first_level(halo_out, halo_step))
    proc = finish(halo_in[1:])
    mesh_two, part, ga, *grad_halo = call(
        process_kernel,
        [
            shape(mesh_rows, features, BF16),
            shape(mesh_rows, features, F32),
            shape(mesh_edges, features, BF16),
        ]
        + [shape(mp * halo_step, features, BF16)] * graph,
        Far(cotangent),
        mesh_one,
        halo_in,
        sender_g,
        proc_g,
        proc,
        proc_t,
        sender_t,
        last=(0,),
        flops=5 * 10**9,
        scratch=[
            pltpu.VMEM((mesh_edges, features), BF16),
            pltpu.VMEM((mesh_edges, features), BF16),
            pltpu.VMEM((mesh_edges, LANES), F32),
        ],
    )
    halo_back, half_way = exchange_back(grad_halo, halo_step)
    part, _ = lax.optimization_barrier((part, half_way))
    (grad_one,) = call(
        receive_kernel, [shape(mesh_rows, features, F32)], part, ga, proc_t, proc, flops=3 * 10**8
    )
    part, ga, *grad_slots = call(
        decode_kernel,
        [shape(mesh_rows, features, F32), shape(edges, features, BF16)]
        + [shape(mp * step, features, BF16)] * graph,
        halo_back,
        halo_t,
        grad_one,
        slope_n,
        normed_n,
        scale_n,
        enc_g,
        slope_e,
        normed_e,
        scale_e,
        enc,
        slot_t,
        flops=3 * 10**9,
    )
    returned, half_way = exchange_back(grad_slots, step)
    part, _ = lax.optimization_barrier((part, half_way))
    (mesh_grad,) = call(
        receive_kernel, [shape(mesh_rows, features, F32)], part, ga, enc_t, enc, last=(0,), flops=3 * 10**8
    )
    (grid_grad,) = call(
        grid_kernel, [shape(grid_rows, features, F32)], returned, grid_t, last=(0,)
    )
    return (mesh_two, grid_grad, mesh_grad)


def solution(mesh):
    rows = P(AXES, None)
    flat = P(AXES)
    in_specs = (rows,) * 4 + (flat,) * 2 + (rows,) + (flat,) * 2 + (P(None, "mp"), P("mp", None)) * 4
    return jax.shard_map(
        local, mesh=mesh, in_specs=in_specs, out_specs=(rows,) * 3, check_vma=False
    )
```

```python
import jax
import jax.numpy as jnp
from jax import lax
from jax.experimental import pallas as pl
from jax.experimental.pallas import tpu as pltpu
from jax.sharding import PartitionSpec as P

F32 = jnp.float32
BF16 = jnp.bfloat16
LANES = 128
ROWS = 512
FEATURES = 512
AXES = ("groups", "graph", "mp")


def dot(left, right):
    return jnp.dot(left, right, preferred_element_type=F32)


def dot_trans(left, right):
    return lax.dot_general(left, right, (((1,), (1,)), ((), ())), preferred_element_type=F32)


def shape(rows, columns, dtype):
    return jax.ShapeDtypeStruct((rows, columns), dtype)


class Far:
    def __init__(self, array):
        self.array = pltpu.with_memory_space_constraint(array, pltpu.HBM)


class Input:
    def __init__(self, copy, ref):
        self.copy, self.ref = copy, ref

    def __call__(self):
        if self.copy is not None:
            self.copy.wait()
            self.copy = None
        return self.ref


class Output:
    def __init__(self, ref, copy):
        self.ref, self.copy = ref, copy

    def send(self, value=None):
        if value is not None:
            self.ref[...] = value
        if self.copy is not None:
            self.copy.start()


def call(kernel, out_shape, *args, last=(), scratch=(), flops=0):
    groups = [a if isinstance(a, list) else [a] for a in args]
    flat = [a for group in groups for a in group]
    far = [isinstance(a, Far) for a in flat]
    arrays = [a.array if isinstance(a, Far) else a for a in flat]
    count, outs = len(arrays), len(out_shape)

    def body(*refs):
        ins, refs = refs[:count], refs[count:]
        out_refs, refs = refs[:outs], refs[outs:]
        places, refs = list(refs[: sum(far)]), refs[sum(far) :]
        results, refs = list(refs[: len(last)]), refs[len(last) :]
        sem_in, sem_out, refs = refs[0], refs[1], refs[2:]
        inputs = []
        for ref, away in zip(ins, far):
            copy = None
            if away:
                place = places.pop(0)
                copy = pltpu.make_async_copy(ref, place, sem_in.at[len(places)])
                copy.start()
                ref = place
            inputs.append(Input(copy, ref))
        outputs = []
        for i, ref in enumerate(out_refs):
            copy = None
            if i in last:
                place = results.pop(0)
                copy = pltpu.make_async_copy(place, ref, sem_out.at[len(results)])
                ref = place
            outputs.append(Output(ref, copy))
        given = []
        for arg, group in zip(args, groups):
            part, inputs = inputs[: len(group)], inputs[len(group) :]
            given.append(part if isinstance(arg, list) else part[0])
        kernel(*given, *outputs, *refs)
        for output in outputs:
            if output.copy is not None:
                output.copy.wait()

    vmem, hbm = pl.BlockSpec(memory_space=pltpu.VMEM), pl.BlockSpec(memory_space=pl.ANY)
    total = sum(a.size * a.dtype.itemsize for a in arrays)
    return pl.pallas_call(
        body,
        out_shape=out_shape,
        in_specs=[hbm if away else vmem for away in far],
        out_specs=[hbm if i in last else vmem for i in range(outs)],
        scratch_shapes=[pltpu.VMEM(a.shape, a.dtype) for a, away in zip(arrays, far) if away]
        + [pltpu.VMEM(out_shape[i].shape, out_shape[i].dtype) for i in last]
        + [pltpu.SemaphoreType.DMA((max(sum(far), 1),)), pltpu.SemaphoreType.DMA((max(len(last), 1),))]
        + list(scratch),
        name=kernel.__name__,
        cost_estimate=pl.CostEstimate(flops=flops, bytes_accessed=total, transcendentals=0),
        compiler_params=pltpu.CompilerParams(vmem_limit_bytes=24 * 1024 * 1024),
    )(*arrays)


def layers(blocks, which):
    low = which * 3 * FEATURES
    middle = low + 2 * FEATURES
    return (
        jnp.concatenate([block()[:, low:middle] for block in blocks], axis=0),
        jnp.concatenate([block()[:, middle : middle + FEATURES] for block in blocks], axis=0),
    )


def turned(first, select):
    return dot_trans(select, first).astype(BF16)


def prepare_kernel(grid, send, shards, table_out, kept, *messages):
    width = 3 * FEATURES
    outgoing = send_rows(grid, send, table_out)
    size = kept.ref.shape[0]
    kept.ref[...] = outgoing[:size, :].astype(BF16)
    for i, out in enumerate(messages):
        out.ref[:, 2 * width :] = outgoing[(i + 1) * size : (i + 2) * size, :].astype(BF16)
    for i in range(2):
        first, second = piece_of(shards[2 * i], shards[2 * i + 1], messages[0].ref.shape[0])
        low = i * width
        for out in messages:
            out.ref[:, low : low + 2 * FEATURES] = first
            out.ref[:, low + 2 * FEATURES : low + width] = second


def piece_of(one, two, rows):
    plane = lax.axis_index("groups") * lax.axis_size("graph") + lax.axis_index("graph")
    base = plane * rows
    hidden = two().shape[0]
    select = jnp.where(
        lax.broadcasted_iota(jnp.int32, (rows, hidden), 0) + base
        == lax.broadcasted_iota(jnp.int32, (rows, hidden), 1),
        1.0,
        0.0,
    ).astype(BF16)
    return turned(one()[...], select), two()[pl.ds(pl.multiple_of(base, rows), rows), :]


def join_kernel(kept, messages, near, block, both):
    width = 6 * FEATURES
    weights = jnp.concatenate([m()[:, :width] for m in messages], axis=0)
    rows = jnp.concatenate([kept()[...]] + [m()[:, width:] for m in messages], axis=0)
    step = rows.shape[0] // 16
    block.ref[...] = weights
    both.ref[:, :width] = weights
    size = near.ref.shape[0]
    for j in range(4):
        moved = dot(turn_table(4, 4, step, j), rows).astype(BF16)
        if j == 0:
            near.ref[...] = moved
        else:
            both.ref[(j - 1) * size : j * size, width:] = moved


def own_kernel(shards, enc_own, proc_own, proc_piece):
    width = 3 * FEATURES
    for i in range(4):
        one, two = shards[2 * i](), shards[2 * i + 1]()
        hidden = one.shape[1]
        select = jnp.where(
            lax.broadcasted_iota(jnp.int32, (hidden, hidden), 0)
            == lax.broadcasted_iota(jnp.int32, (hidden, hidden), 1),
            1.0,
            0.0,
        ).astype(BF16)
        out, low = (enc_own, proc_own)[i // 2], i % 2 * width
        out.ref[:, low : low + 2 * FEATURES] = turned(one[...], select)
        out.ref[:, low + 2 * FEATURES : low + width] = two[...]
    for i in (2, 3):
        first, second = piece_of(shards[2 * i], shards[2 * i + 1], proc_piece.ref.shape[0])
        low = i % 2 * width
        proc_piece.ref[:, low : low + 2 * FEATURES] = first
        proc_piece.ref[:, low + 2 * FEATURES : low + width] = second


def across(x, flip):
    planes = lax.axis_size("groups") * lax.axis_size("graph")
    return lax.ppermute(x, ("groups", "graph"), [(p, p ^ flip) for p in range(planes)])


def start(grid_lat, grid_send, shards, tables):
    grid_rows, features = grid_lat.shape
    mp, graph = lax.axis_size("mp"), lax.axis_size("graph")
    step = stride(grid_send.shape[1])
    sent = [shape(grid_rows, mp * graph * step, BF16)] + [shape(graph * step, features, BF16)] * mp
    planes = lax.axis_size("groups") * graph
    hidden = shards[1].shape[0]
    if planes != 8 or mp != 4 or hidden != 128 or features != FEATURES:
        grid_t, *outgoing = call(send_kernel, sent, Far(grid_lat), Far(grid_send.T))
        rows = []
        for i in range(4):
            rows.append(lax.all_gather(shards[2 * i], "mp", axis=1, tiled=True).T)
            rows.append(lax.all_gather(shards[2 * i + 1], "mp", axis=0, tiled=True))
        enc, proc = jnp.concatenate(rows[:4], axis=1), jnp.concatenate(rows[4:], axis=1)
        arrived = exchange(outgoing, step)
        return [enc], lambda after: [proc], arrived, grid_t, tables
    far = [Far(s) for s in shards]
    piece = hidden // planes
    width = 6 * features
    grid_t, kept, *messages = call(
        prepare_kernel,
        sent[:2] + [shape(piece, width + features, BF16)] * 3,
        Far(grid_lat),
        Far(grid_send.T),
        far[:4],
    )
    enc_own, proc_own, proc_piece = call(
        own_kernel, [shape(hidden, width, BF16)] * 2 + [shape(piece, width, BF16)], far
    )
    messages = [along(m, i + 1) for i, m in enumerate(messages)]
    kept, enc_own, *tables = lax.optimization_barrier((kept, enc_own, *tables))
    rows = mp * step
    near, first, both = call(
        join_kernel,
        [shape(rows, features, BF16), shape(3 * piece, width, BF16), shape(3 * rows, width + features, BF16)],
        kept,
        messages,
    )
    x, y, corner = across(both, 2), across(first, 4), across(first, 6)
    proc_piece, _ = lax.optimization_barrier((proc_piece, near))
    beside_me = lax.ppermute(proc_piece, "mp", [(m, m ^ 1) for m in range(mp)])
    pair = jnp.concatenate([proc_piece, beside_me])
    pairs = lax.ppermute(pair, "mp", [(m, m ^ 2) for m in range(mp)])
    proc_first = jnp.concatenate([beside_me, pairs])
    both, x, y, corner, _ = lax.optimization_barrier((both, x, y, corner, pairs))
    core, x_core, others = across(both, 1), across(x, 1), across(jnp.concatenate([y, corner]), 1)
    enc = [enc_own, first, core, x, y, corner, x_core, others]
    arrived = [near, core, x, x_core]
    proc_first, *_ = lax.optimization_barrier((proc_first, x, y, corner))
    plane = [across(proc_first, flip) for flip in (2, 4, 6)]
    proc = [proc_own, proc_first, across(proc_first, 1)] + plane

    def finish(after):
        tied = [lax.optimization_barrier((block, *after))[0] for block in plane]
        return proc + [across(jnp.concatenate(tied), 1)]

    return enc, finish, arrived, grid_t, tables


def forward(inputs, first, second):
    before = dot_trans(inputs, first)
    logistic = 0.5 + 0.5 * jnp.tanh(0.5 * before)
    wide = before * logistic
    hidden = wide.astype(BF16)
    slope = logistic + wide * (1.0 - logistic)
    summed = dot(hidden, second)
    centered = summed - jnp.mean(summed, axis=-1, keepdims=True)
    rescale = lax.rsqrt(jnp.mean(centered * centered, axis=-1, keepdims=True) + 1e-05)
    normed = centered * rescale
    return normed, slope.astype(BF16), normed.astype(BF16), rescale


def backward_hidden(incoming, slope, normed, rescale, second):
    normed = normed.astype(F32)
    g_out = (
        incoming
        - jnp.mean(incoming, axis=-1, keepdims=True)
        - normed * jnp.mean(incoming * normed, axis=-1, keepdims=True)
    ) * rescale
    return (dot_trans(g_out.astype(BF16), second) * slope.astype(F32)).astype(BF16)


def table(index_row, count):
    n = index_row.shape[1]
    return jnp.where(lax.broadcasted_iota(jnp.int32, (count, n), 0) == index_row, 1.0, 0.0)


def stride(capacity):
    return max(capacity, 16 // min(lax.axis_size("mp"), lax.axis_size("graph")))


def sent_at(peer, slot, step):
    mp, graph = lax.axis_size("mp"), lax.axis_size("graph")
    shift = (peer % mp + mp - lax.axis_index("mp")) % mp
    return (shift * graph + (peer // mp ^ lax.axis_index("graph"))) * step + slot


def arrived_at(peer, slot, step):
    mp = lax.axis_size("mp")
    shift = (lax.axis_index("mp") + mp - peer % mp) % mp
    return ((peer // mp ^ lax.axis_index("graph")) * mp + shift) * step + slot


def sent_row(index, step):
    width, count = index.shape
    index = index.astype(F32).T
    at = lax.broadcasted_iota(jnp.int32, (count, count * step), 1)
    peer = lax.broadcasted_iota(jnp.int32, (count, count * step), 0)
    row = jnp.zeros(at.shape, F32)
    for slot in range(width):
        row = jnp.where(sent_at(peer, slot, step) == at, index[:, slot : slot + 1] + 1.0, row)
    return jnp.sum(row, axis=0, keepdims=True).astype(jnp.int32) - 1


def stacked(blocks):
    return jnp.concatenate([block()[...] for block in blocks], axis=0)


def split(rows, outs):
    size = rows.shape[0] // len(outs)
    for i, out in enumerate(outs):
        out.ref[...] = rows[i * size : (i + 1) * size, :].astype(BF16)


def send_rows(grid, send, table_out):
    count = table_out.ref.shape[1]
    one = table(sent_row(send()[...], count // send().shape[1]), grid().shape[0])
    table_out.ref[...] = one.astype(BF16)
    return dot(one.T.astype(BF16), grid()[...])


def send_kernel(grid, send, table_out, *outgoing):
    split(send_rows(grid, send, table_out), outgoing)


def turn_table(sources, targets, step, j):
    row = lax.broadcasted_iota(jnp.int32, (sources * step, sources * targets * step), 0)
    at = lax.broadcasted_iota(jnp.int32, row.shape, 1)
    source = (row // step * targets + j) * step + row % step
    return jnp.where(at == source, 1.0, 0.0).astype(BF16)


def turn_kernel(blocks, *outs):
    rows = stacked(blocks)
    step = rows.shape[0] // (len(blocks) * len(outs))
    for j, out in enumerate(outs):
        out.ref[...] = dot(turn_table(len(blocks), len(outs), step, j), rows).astype(BF16)


def tables_kernel(mesh, slot, recv_e, halo, sender, recv_p, *outs):
    mesh_rows = mesh().shape[0]
    peers = halo().shape[1]
    slot_step, halo_step = outs[0].ref.shape[0] // peers, outs[4].ref.shape[1] // peers
    capacity, halo_capacity = slot_step, halo().shape[0]
    slots = slot()[...]
    slots = arrived_at(slots // capacity, slots % capacity, slot_step)
    senders = sender()[...]
    remote = jnp.maximum(senders - mesh_rows, 0)
    remote = arrived_at(remote // halo_capacity, remote % halo_capacity, halo_step)
    senders = jnp.where(senders < mesh_rows, senders, mesh_rows + remote)
    rows = (slots, recv_e()[...], sent_row(halo()[...], halo_step), senders, recv_p()[...])
    for i, row in enumerate(rows):
        scatter, gather = outs[2 * i : 2 * i + 2]
        one = table(row, scatter.ref.shape[0])
        scatter.ref[...] = one.astype(BF16)
        gather.ref[...] = one.T.astype(BF16)
    outs[10].ref[...] = dot(outs[3].ref[...], mesh()[...]).astype(BF16)


def arrived_rows(blocks):
    size = blocks[0]().shape[0]
    rows = [blocks[0]()[...]]
    for t, block in enumerate(blocks[1:]):
        if block().shape[1] == FEATURES:
            rows.append(block()[...])
        else:
            rows.append(block()[t * size : (t + 1) * size, 6 * FEATURES :])
    return jnp.concatenate(rows, axis=0)


def encode_kernel(
    recv_rows, arrived, slot_g, enc_t, mesh, weights, halo_g,
    one_out, slope_e, normed_e, scale_e, slope_n, normed_n, scale_n, *halo_out,
):
    rows_in = arrived_rows(arrived)
    edges = slot_g().shape[0]
    first, second = layers(weights, 0)
    for low in range(0, edges, ROWS):
        rows = pl.ds(low, ROWS)
        sent = dot(slot_g()[rows, :], rows_in).astype(BF16)
        inputs = jnp.concatenate([sent, recv_rows()[rows, :]], axis=1)
        _, slope, normed, rescale = forward(inputs, first, second)
        slope_e.ref[rows, :] = slope
        normed_e.ref[rows, :] = normed
        scale_e.ref[rows, :] = jnp.broadcast_to(rescale, (ROWS, LANES))
    aggregate = dot(enc_t()[...], normed_e.ref[...]).astype(BF16)
    first, second = layers(weights, 1)
    own = mesh()[...]
    normed, slope, rounded, rescale = forward(
        jnp.concatenate([own, aggregate], axis=1), first, second
    )
    one = (own.astype(F32) + normed).astype(BF16)
    one_out.ref[...] = one
    split(dot(halo_g()[...], one), halo_out)
    slope_n.ref[...] = slope
    normed_n.ref[...] = rounded
    scale_n.ref[...] = jnp.broadcast_to(rescale, scale_n.ref.shape)


def process_kernel(
    cotangent_in, one_in, halo, sender_g, proc_g, weights, proc_t, sender_t, two, part, ga, *refs
):
    grad_halo, (slope_p, normed_p, scale_p) = refs[:-3], refs[-3:]
    ga_p = ga.ref
    features = FEATURES
    one = one_in()[...]
    mesh_rows = one.shape[0]
    lookup = jnp.concatenate([one, stacked(halo)], axis=0)
    edges = sender_g().shape[0]
    first, second = layers(weights, 0)
    for low in range(0, edges, ROWS):
        rows = pl.ds(low, ROWS)
        sent = dot(sender_g()[rows, :], lookup).astype(BF16)
        got = dot(proc_g()[rows, :], one).astype(BF16)
        _, slope, normed, rescale = forward(jnp.concatenate([sent, got], axis=1), first, second)
        slope_p[rows, :] = slope
        normed_p[rows, :] = normed
        scale_p[rows, :] = jnp.broadcast_to(rescale, (ROWS, LANES))
    aggregate = dot(proc_t()[...], normed_p[...]).astype(BF16)
    first_n, second_n = layers(weights, 1)
    normed, slope, rounded, rescale = forward(
        jnp.concatenate([one, aggregate], axis=1), first_n, second_n
    )
    two.send((one.astype(F32) + normed).astype(BF16))
    cotangent = cotangent_in()[...].astype(F32)
    g_q = dot(backward_hidden(cotangent, slope, rounded, rescale, second_n), first_n)
    g_msg = g_q[:, features:].astype(BF16)
    for low in range(0, edges, ROWS):
        rows = pl.ds(low, ROWS)
        incoming = dot(proc_g()[rows, :], g_msg)
        ga_p[rows, :] = backward_hidden(
            incoming, slope_p[rows, :], normed_p[rows, :], scale_p[rows, 0:1], second
        )
    by_send = dot(sender_t()[...], ga_p[...]).astype(BF16)
    g_send = dot(by_send, first[:, :features])
    split(g_send[mesh_rows:, :], grad_halo)
    part.ref[...] = cotangent + g_q[:, :features] + g_send[:mesh_rows, :]


def receive_kernel(part, ga, scatter, weights, out):
    by_recv = dot(scatter()[...], ga()[...]).astype(BF16)
    first, _ = layers(weights, 0)
    out.send(part()[...] + dot(by_recv, first[:, FEATURES:]))


def decode_kernel(
    back, halo_t, grad_in, slope_n, normed_n, scale_n, enc_g, slope_e, normed_e, scale_e,
    weights, slot_t, part, ga, *grad_slots
):
    ga_e = ga.ref
    features = FEATURES
    edges = enc_g().shape[0]
    grad_one = grad_in()[...] + dot(halo_t()[...], stacked(back))
    first_n, second_n = layers(weights, 1)
    ga_n = backward_hidden(grad_one, slope_n()[...], normed_n()[...], scale_n()[:, 0:1], second_n)
    g_n = dot(ga_n, first_n)
    part.ref[...] = grad_one + g_n[:, :features]
    g_edge = g_n[:, features:].astype(BF16)
    first, second = layers(weights, 0)
    for low in range(0, edges, ROWS):
        rows = pl.ds(low, ROWS)
        incoming = dot(enc_g()[rows, :], g_edge)
        ga_e[rows, :] = backward_hidden(
            incoming, slope_e()[rows, :], normed_e()[rows, :], scale_e()[rows, 0:1], second
        )
    by_slot = dot(slot_t()[...], ga_e[...]).astype(BF16)
    split(dot(by_slot, first[:, :features]), grad_slots)


def grid_kernel(back, table_in, out):
    out.send(dot(table_in()[...], stacked(back)))


def along(block, shift):
    size = lax.axis_size("mp")
    if shift % size == 0:
        return block
    return lax.ppermute(block, "mp", [(m, (m + shift) % size) for m in range(size)])


def beside(block, flip):
    if flip == 0:
        return block
    return lax.ppermute(block, "graph", [(g, g ^ flip) for g in range(lax.axis_size("graph"))])


def turn(blocks, count, step):
    out = shape(len(blocks) * step, blocks[0].shape[1], BF16)
    return call(turn_kernel, [out] * count, list(blocks))


def exchange(blocks, step):
    return second_level(first_level(blocks, step))


def first_level(blocks, step):
    return turn([along(b, s) for s, b in enumerate(blocks)], lax.axis_size("graph"), step)


def second_level(blocks):
    return [beside(b, t) for t, b in enumerate(blocks)]


def exchange_back(blocks, step):
    blocks = turn([beside(b, t) for t, b in enumerate(blocks)], lax.axis_size("mp"), step)
    return [along(b, -s) for s, b in enumerate(blocks)], blocks[0]


def local(
    grid_lat,
    mesh_lat,
    cotangent,
    grid_send,
    g2m_slot,
    g2m_receiver,
    halo_send,
    mesh_sender,
    mesh_receiver,
    *shards,
):
    grid_rows, features = grid_lat.shape
    mesh_rows = mesh_lat.shape[0]
    edges = g2m_slot.shape[0]
    mesh_edges = mesh_sender.shape[0]
    mp, graph = lax.axis_size("mp"), lax.axis_size("graph")
    step, halo_step = stride(grid_send.shape[1]), stride(halo_send.shape[1])
    slots, halos = mp * graph * step, mp * graph * halo_step
    tables = call(
        tables_kernel,
        [
            shape(slots, edges, BF16),
            shape(edges, slots, BF16),
            shape(mesh_rows, edges, BF16),
            shape(edges, mesh_rows, BF16),
            shape(mesh_rows, halos, BF16),
            shape(halos, mesh_rows, BF16),
            shape(mesh_rows + halos, mesh_edges, BF16),
            shape(mesh_edges, mesh_rows + halos, BF16),
            shape(mesh_rows, mesh_edges, BF16),
            shape(mesh_edges, mesh_rows, BF16),
            shape(edges, features, BF16),
        ],
        Far(mesh_lat),
        Far(g2m_slot.reshape(1, edges)),
        Far(g2m_receiver.reshape(1, edges)),
        Far(halo_send.T),
        Far(mesh_sender.reshape(1, mesh_edges)),
        Far(mesh_receiver.reshape(1, mesh_edges)),
    )
    enc, finish, arrived, grid_t, tables = start(grid_lat, grid_send, shards, tables)
    slot_t, slot_g, enc_t, enc_g, halo_t, halo_g, sender_t, sender_g, proc_t, proc_g, recv_rows = tables
    saved = [
        shape(edges, features, BF16),
        shape(edges, features, BF16),
        shape(edges, LANES, F32),
        shape(mesh_rows, features, BF16),
        shape(mesh_rows, features, BF16),
        shape(mesh_rows, LANES, F32),
    ]
    mesh_one, slope_e, normed_e, scale_e, slope_n, normed_n, scale_n, *halo_out = call(
        encode_kernel,
        [shape(mesh_rows, features, BF16)] + saved + [shape(graph * halo_step, features, BF16)] * mp,
        recv_rows,
        arrived,
        slot_g,
        enc_t,
        Far(mesh_lat),
        enc,
        halo_g,
        flops=3 * 10**9,
    )
    halo_in = second_level(first_level(halo_out, halo_step))
    proc = finish(halo_in[1:])
    mesh_two, part, ga, *grad_halo = call(
        process_kernel,
        [
            shape(mesh_rows, features, BF16),
            shape(mesh_rows, features, F32),
            shape(mesh_edges, features, BF16),
        ]
        + [shape(mp * halo_step, features, BF16)] * graph,
        Far(cotangent),
        mesh_one,
        halo_in,
        sender_g,
        proc_g,
        proc,
        proc_t,
        sender_t,
        last=(0,),
        flops=5 * 10**9,
        scratch=[
            pltpu.VMEM((mesh_edges, features), BF16),
            pltpu.VMEM((mesh_edges, features), BF16),
            pltpu.VMEM((mesh_edges, LANES), F32),
        ],
    )
    halo_back, half_way = exchange_back(grad_halo, halo_step)
    part, _ = lax.optimization_barrier((part, half_way))
    (grad_one,) = call(
        receive_kernel, [shape(mesh_rows, features, F32)], part, ga, proc_t, proc, flops=3 * 10**8
    )
    part, ga, *grad_slots = call(
        decode_kernel,
        [shape(mesh_rows, features, F32), shape(edges, features, BF16)]
        + [shape(mp * step, features, BF16)] * graph,
        halo_back,
        halo_t,
        grad_one,
        slope_n,
        normed_n,
        scale_n,
        enc_g,
        slope_e,
        normed_e,
        scale_e,
        enc,
        slot_t,
        flops=3 * 10**9,
    )
    returned, half_way = exchange_back(grad_slots, step)
    part, _ = lax.optimization_barrier((part, half_way))
    (mesh_grad,) = call(
        receive_kernel, [shape(mesh_rows, features, F32)], part, ga, enc_t, enc, last=(0,), flops=3 * 10**8
    )
    (grid_grad,) = call(
        grid_kernel, [shape(grid_rows, features, F32)], returned, grid_t, last=(0,)
    )
    return (mesh_two, grid_grad, mesh_grad)


def solution(mesh):
    rows = P(AXES, None)
    flat = P(AXES)
    in_specs = (rows,) * 4 + (flat,) * 2 + (rows,) + (flat,) * 2 + (P(None, "mp"), P("mp", None)) * 4
    return jax.shard_map(
        local, mesh=mesh, in_specs=in_specs, out_specs=(rows,) * 3, check_vma=False
    )
```

```python
import jax
import jax.numpy as jnp
from jax import lax
from jax.experimental import pallas as pl
from jax.experimental.pallas import tpu as pltpu
from jax.sharding import PartitionSpec as P

F32 = jnp.float32
BF16 = jnp.bfloat16
LANES = 128
ROWS = 512
FEATURES = 512
AXES = ("groups", "graph", "mp")


def dot(left, right):
    return jnp.dot(left, right, preferred_element_type=F32)


def dot_trans(left, right):
    return lax.dot_general(left, right, (((1,), (1,)), ((), ())), preferred_element_type=F32)


def shape(rows, columns, dtype):
    return jax.ShapeDtypeStruct((rows, columns), dtype)


class Far:
    def __init__(self, array):
        self.array = pltpu.with_memory_space_constraint(array, pltpu.HBM)


class Input:
    def __init__(self, copy, ref):
        self.copy, self.ref = copy, ref

    def __call__(self):
        if self.copy is not None:
            self.copy.wait()
            self.copy = None
        return self.ref


class Output:
    def __init__(self, ref, copy):
        self.ref, self.copy = ref, copy

    def send(self, value=None):
        if value is not None:
            self.ref[...] = value
        if self.copy is not None:
            self.copy.start()


def call(kernel, out_shape, *args, last=(), scratch=(), flops=0):
    groups = [a if isinstance(a, list) else [a] for a in args]
    flat = [a for group in groups for a in group]
    far = [isinstance(a, Far) for a in flat]
    arrays = [a.array if isinstance(a, Far) else a for a in flat]
    count, outs = len(arrays), len(out_shape)

    def body(*refs):
        ins, refs = refs[:count], refs[count:]
        out_refs, refs = refs[:outs], refs[outs:]
        places, refs = list(refs[: sum(far)]), refs[sum(far) :]
        results, refs = list(refs[: len(last)]), refs[len(last) :]
        sem_in, sem_out, refs = refs[0], refs[1], refs[2:]
        inputs = []
        for ref, away in zip(ins, far):
            copy = None
            if away:
                place = places.pop(0)
                copy = pltpu.make_async_copy(ref, place, sem_in.at[len(places)])
                copy.start()
                ref = place
            inputs.append(Input(copy, ref))
        outputs = []
        for i, ref in enumerate(out_refs):
            copy = None
            if i in last:
                place = results.pop(0)
                copy = pltpu.make_async_copy(place, ref, sem_out.at[len(results)])
                ref = place
            outputs.append(Output(ref, copy))
        given = []
        for arg, group in zip(args, groups):
            part, inputs = inputs[: len(group)], inputs[len(group) :]
            given.append(part if isinstance(arg, list) else part[0])
        kernel(*given, *outputs, *refs)
        for output in outputs:
            if output.copy is not None:
                output.copy.wait()

    vmem, hbm = pl.BlockSpec(memory_space=pltpu.VMEM), pl.BlockSpec(memory_space=pl.ANY)
    total = sum(a.size * a.dtype.itemsize for a in arrays)
    return pl.pallas_call(
        body,
        out_shape=out_shape,
        in_specs=[hbm if away else vmem for away in far],
        out_specs=[hbm if i in last else vmem for i in range(outs)],
        scratch_shapes=[pltpu.VMEM(a.shape, a.dtype) for a, away in zip(arrays, far) if away]
        + [pltpu.VMEM(out_shape[i].shape, out_shape[i].dtype) for i in last]
        + [pltpu.SemaphoreType.DMA((max(sum(far), 1),)), pltpu.SemaphoreType.DMA((max(len(last), 1),))]
        + list(scratch),
        name=kernel.__name__,
        cost_estimate=pl.CostEstimate(flops=flops, bytes_accessed=total, transcendentals=0),
        compiler_params=pltpu.CompilerParams(vmem_limit_bytes=24 * 1024 * 1024),
    )(*arrays)


def layers(blocks, which):
    low = which * 3 * FEATURES
    middle = low + 2 * FEATURES
    return (
        jnp.concatenate([block()[:, low:middle] for block in blocks], axis=0),
        jnp.concatenate([block()[:, middle : middle + FEATURES] for block in blocks], axis=0),
    )


def turned(first, select):
    return dot_trans(select, first).astype(BF16)


def prepare_kernel(grid, send, shards, table_out, kept, *messages):
    width = 3 * FEATURES
    outgoing = send_rows(grid, send, table_out)
    size = kept.ref.shape[0]
    kept.ref[...] = outgoing[:size, :].astype(BF16)
    for i, out in enumerate(messages):
        out.ref[:, 2 * width :] = outgoing[(i + 1) * size : (i + 2) * size, :].astype(BF16)
    for i in range(2):
        first, second = piece_of(shards[2 * i], shards[2 * i + 1], messages[0].ref.shape[0])
        low = i * width
        for out in messages:
            out.ref[:, low : low + 2 * FEATURES] = first
            out.ref[:, low + 2 * FEATURES : low + width] = second


def piece_of(one, two, rows):
    plane = lax.axis_index("groups") * lax.axis_size("graph") + lax.axis_index("graph")
    base = plane * rows
    hidden = two().shape[0]
    select = jnp.where(
        lax.broadcasted_iota(jnp.int32, (rows, hidden), 0) + base
        == lax.broadcasted_iota(jnp.int32, (rows, hidden), 1),
        1.0,
        0.0,
    ).astype(BF16)
    return turned(one()[...], select), two()[pl.ds(pl.multiple_of(base, rows), rows), :]


def join_kernel(kept, messages, near, block, both):
    width = 6 * FEATURES
    weights = jnp.concatenate([m()[:, :width] for m in messages], axis=0)
    rows = jnp.concatenate([kept()[...]] + [m()[:, width:] for m in messages], axis=0)
    step = rows.shape[0] // 16
    block.ref[...] = weights
    both.ref[:, :width] = weights
    size = near.ref.shape[0]
    for j in range(4):
        moved = dot(turn_table(4, 4, step, j), rows).astype(BF16)
        if j == 0:
            near.ref[...] = moved
        else:
            both.ref[(j - 1) * size : j * size, width:] = moved


def own_kernel(shards, enc_own, proc_own, proc_piece):
    width = 3 * FEATURES
    for i in range(4):
        one, two = shards[2 * i](), shards[2 * i + 1]()
        hidden = one.shape[1]
        select = jnp.where(
            lax.broadcasted_iota(jnp.int32, (hidden, hidden), 0)
            == lax.broadcasted_iota(jnp.int32, (hidden, hidden), 1),
            1.0,
            0.0,
        ).astype(BF16)
        out, low = (enc_own, proc_own)[i // 2], i % 2 * width
        out.ref[:, low : low + 2 * FEATURES] = turned(one[...], select)
        out.ref[:, low + 2 * FEATURES : low + width] = two[...]
    for i in (2, 3):
        first, second = piece_of(shards[2 * i], shards[2 * i + 1], proc_piece.ref.shape[0])
        low = i % 2 * width
        proc_piece.ref[:, low : low + 2 * FEATURES] = first
        proc_piece.ref[:, low + 2 * FEATURES : low + width] = second


def across(x, flip):
    planes = lax.axis_size("groups") * lax.axis_size("graph")
    return lax.ppermute(x, ("groups", "graph"), [(p, p ^ flip) for p in range(planes)])


def start(grid_lat, grid_send, shards, tables):
    grid_rows, features = grid_lat.shape
    mp, graph = lax.axis_size("mp"), lax.axis_size("graph")
    step = stride(grid_send.shape[1])
    sent = [shape(grid_rows, mp * graph * step, BF16)] + [shape(graph * step, features, BF16)] * mp
    planes = lax.axis_size("groups") * graph
    hidden = shards[1].shape[0]
    if planes != 8 or mp != 4 or hidden != 128 or features != FEATURES:
        grid_t, *outgoing = call(send_kernel, sent, Far(grid_lat), Far(grid_send.T))
        rows = []
        for i in range(4):
            rows.append(lax.all_gather(shards[2 * i], "mp", axis=1, tiled=True).T)
            rows.append(lax.all_gather(shards[2 * i + 1], "mp", axis=0, tiled=True))
        enc, proc = jnp.concatenate(rows[:4], axis=1), jnp.concatenate(rows[4:], axis=1)
        arrived = exchange(outgoing, step)
        return [enc], lambda one, moved, came: [proc], arrived, grid_t, tables
    far = [Far(s) for s in shards]
    piece = hidden // planes
    width = 6 * features
    grid_t, kept, *messages = call(
        prepare_kernel,
        sent[:2] + [shape(piece, width + features, BF16)] * 3,
        Far(grid_lat),
        Far(grid_send.T),
        far[:4],
    )
    enc_own, proc_own, proc_piece = call(
        own_kernel, [shape(hidden, width, BF16)] * 2 + [shape(piece, width, BF16)], far
    )
    messages = [along(m, i + 1) for i, m in enumerate(messages)]
    kept, enc_own, *tables = lax.optimization_barrier((kept, enc_own, *tables))
    rows = mp * step
    near, first, both = call(
        join_kernel,
        [shape(rows, features, BF16), shape(3 * piece, width, BF16), shape(3 * rows, width + features, BF16)],
        kept,
        messages,
    )
    x, y, corner = across(both, 2), across(first, 4), across(first, 6)
    proc_piece, _ = lax.optimization_barrier((proc_piece, near))
    beside_me = lax.ppermute(proc_piece, "mp", [(m, m ^ 1) for m in range(mp)])
    pair = jnp.concatenate([proc_piece, beside_me])
    pairs = lax.ppermute(pair, "mp", [(m, m ^ 2) for m in range(mp)])
    proc_first = jnp.concatenate([beside_me, pairs])
    both, x, y, corner, _ = lax.optimization_barrier((both, x, y, corner, pairs))
    core, x_core, others = across(both, 1), across(x, 1), across(jnp.concatenate([y, corner]), 1)
    enc = [enc_own, first, core, x, y, corner, x_core, others]
    arrived = [near, core, x, x_core]
    proc_first, *_ = lax.optimization_barrier((proc_first, x, y, corner))
    proc_x, proc_y = across(proc_first, 2), across(proc_first, 4)

    def finish(one, moved, came):
        late, _ = lax.optimization_barrier((proc_first, one))
        corner = across(late, 6)
        x, y, *_ = lax.optimization_barrier((proc_x, proc_y, *moved))
        sides = across(jnp.concatenate([x, y]), 1)
        corner, *_ = lax.optimization_barrier((corner, *came))
        return [proc_own, proc_first, across(proc_first, 1), x, y, sides, corner, across(corner, 1)]

    return enc, finish, arrived, grid_t, tables


def forward(inputs, first, second):
    before = dot_trans(inputs, first)
    logistic = 0.5 + 0.5 * jnp.tanh(0.5 * before)
    wide = before * logistic
    hidden = wide.astype(BF16)
    slope = logistic + wide * (1.0 - logistic)
    summed = dot(hidden, second)
    centered = summed - jnp.mean(summed, axis=-1, keepdims=True)
    rescale = lax.rsqrt(jnp.mean(centered * centered, axis=-1, keepdims=True) + 1e-05)
    normed = centered * rescale
    return normed, slope.astype(BF16), normed.astype(BF16), rescale


def backward_hidden(incoming, slope, normed, rescale, second):
    normed = normed.astype(F32)
    g_out = (
        incoming
        - jnp.mean(incoming, axis=-1, keepdims=True)
        - normed * jnp.mean(incoming * normed, axis=-1, keepdims=True)
    ) * rescale
    return (dot_trans(g_out.astype(BF16), second) * slope.astype(F32)).astype(BF16)


def table(index_row, count):
    n = index_row.shape[1]
    return jnp.where(lax.broadcasted_iota(jnp.int32, (count, n), 0) == index_row, 1.0, 0.0)


def stride(capacity):
    return max(capacity, 16 // min(lax.axis_size("mp"), lax.axis_size("graph")))


def sent_at(peer, slot, step):
    mp, graph = lax.axis_size("mp"), lax.axis_size("graph")
    shift = (peer % mp + mp - lax.axis_index("mp")) % mp
    return (shift * graph + (peer // mp ^ lax.axis_index("graph"))) * step + slot


def arrived_at(peer, slot, step):
    mp = lax.axis_size("mp")
    shift = (lax.axis_index("mp") + mp - peer % mp) % mp
    return ((peer // mp ^ lax.axis_index("graph")) * mp + shift) * step + slot


def sent_row(index, step):
    width, count = index.shape
    index = index.astype(F32).T
    at = lax.broadcasted_iota(jnp.int32, (count, count * step), 1)
    peer = lax.broadcasted_iota(jnp.int32, (count, count * step), 0)
    row = jnp.zeros(at.shape, F32)
    for slot in range(width):
        row = jnp.where(sent_at(peer, slot, step) == at, index[:, slot : slot + 1] + 1.0, row)
    return jnp.sum(row, axis=0, keepdims=True).astype(jnp.int32) - 1


def stacked(blocks):
    return jnp.concatenate([block()[...] for block in blocks], axis=0)


def split(rows, outs):
    size = rows.shape[0] // len(outs)
    for i, out in enumerate(outs):
        out.ref[...] = rows[i * size : (i + 1) * size, :].astype(BF16)


def send_rows(grid, send, table_out):
    count = table_out.ref.shape[1]
    one = table(sent_row(send()[...], count // send().shape[1]), grid().shape[0])
    table_out.ref[...] = one.astype(BF16)
    return dot(one.T.astype(BF16), grid()[...])


def send_kernel(grid, send, table_out, *outgoing):
    split(send_rows(grid, send, table_out), outgoing)


def turn_table(sources, targets, step, j):
    row = lax.broadcasted_iota(jnp.int32, (sources * step, sources * targets * step), 0)
    at = lax.broadcasted_iota(jnp.int32, row.shape, 1)
    source = (row // step * targets + j) * step + row % step
    return jnp.where(at == source, 1.0, 0.0).astype(BF16)


def turn_kernel(blocks, *outs):
    rows = stacked(blocks)
    step = rows.shape[0] // (len(blocks) * len(outs))
    for j, out in enumerate(outs):
        out.ref[...] = dot(turn_table(len(blocks), len(outs), step, j), rows).astype(BF16)


def tables_kernel(mesh, slot, recv_e, halo, sender, recv_p, *outs):
    mesh_rows = mesh().shape[0]
    peers = halo().shape[1]
    slot_step, halo_step = outs[0].ref.shape[0] // peers, outs[4].ref.shape[1] // peers
    capacity, halo_capacity = slot_step, halo().shape[0]
    slots = slot()[...]
    slots = arrived_at(slots // capacity, slots % capacity, slot_step)
    senders = sender()[...]
    remote = jnp.maximum(senders - mesh_rows, 0)
    remote = arrived_at(remote // halo_capacity, remote % halo_capacity, halo_step)
    senders = jnp.where(senders < mesh_rows, senders, mesh_rows + remote)
    rows = (slots, recv_e()[...], sent_row(halo()[...], halo_step), senders, recv_p()[...])
    for i, row in enumerate(rows):
        scatter, gather = outs[2 * i : 2 * i + 2]
        one = table(row, scatter.ref.shape[0])
        scatter.ref[...] = one.astype(BF16)
        gather.ref[...] = one.T.astype(BF16)
    outs[10].ref[...] = dot(outs[3].ref[...], mesh()[...]).astype(BF16)


def arrived_rows(blocks):
    size = blocks[0]().shape[0]
    rows = [blocks[0]()[...]]
    for t, block in enumerate(blocks[1:]):
        if block().shape[1] == FEATURES:
            rows.append(block()[...])
        else:
            rows.append(block()[t * size : (t + 1) * size, 6 * FEATURES :])
    return jnp.concatenate(rows, axis=0)


def encode_kernel(
    recv_rows, arrived, slot_g, enc_t, mesh, weights, halo_g,
    one_out, slope_e, normed_e, scale_e, slope_n, normed_n, scale_n, *halo_out,
):
    rows_in = arrived_rows(arrived)
    edges = slot_g().shape[0]
    first, second = layers(weights, 0)
    for low in range(0, edges, ROWS):
        rows = pl.ds(low, ROWS)
        sent = dot(slot_g()[rows, :], rows_in).astype(BF16)
        inputs = jnp.concatenate([sent, recv_rows()[rows, :]], axis=1)
        _, slope, normed, rescale = forward(inputs, first, second)
        slope_e.ref[rows, :] = slope
        normed_e.ref[rows, :] = normed
        scale_e.ref[rows, :] = jnp.broadcast_to(rescale, (ROWS, LANES))
    aggregate = dot(enc_t()[...], normed_e.ref[...]).astype(BF16)
    first, second = layers(weights, 1)
    own = mesh()[...]
    normed, slope, rounded, rescale = forward(
        jnp.concatenate([own, aggregate], axis=1), first, second
    )
    one = (own.astype(F32) + normed).astype(BF16)
    one_out.ref[...] = one
    split(dot(halo_g()[...], one), halo_out)
    slope_n.ref[...] = slope
    normed_n.ref[...] = rounded
    scale_n.ref[...] = jnp.broadcast_to(rescale, scale_n.ref.shape)


def process_kernel(
    cotangent_in, one_in, halo, sender_g, proc_g, weights, proc_t, sender_t, two, part, ga, *refs
):
    grad_halo, (slope_p, normed_p, scale_p) = refs[:-3], refs[-3:]
    ga_p = ga.ref
    features = FEATURES
    one = one_in()[...]
    mesh_rows = one.shape[0]
    lookup = jnp.concatenate([one, stacked(halo)], axis=0)
    edges = sender_g().shape[0]
    first, second = layers(weights, 0)
    for low in range(0, edges, ROWS):
        rows = pl.ds(low, ROWS)
        sent = dot(sender_g()[rows, :], lookup).astype(BF16)
        got = dot(proc_g()[rows, :], one).astype(BF16)
        _, slope, normed, rescale = forward(jnp.concatenate([sent, got], axis=1), first, second)
        slope_p[rows, :] = slope
        normed_p[rows, :] = normed
        scale_p[rows, :] = jnp.broadcast_to(rescale, (ROWS, LANES))
    aggregate = dot(proc_t()[...], normed_p[...]).astype(BF16)
    first_n, second_n = layers(weights, 1)
    normed, slope, rounded, rescale = forward(
        jnp.concatenate([one, aggregate], axis=1), first_n, second_n
    )
    two.send((one.astype(F32) + normed).astype(BF16))
    cotangent = cotangent_in()[...].astype(F32)
    g_q = dot(backward_hidden(cotangent, slope, rounded, rescale, second_n), first_n)
    g_msg = g_q[:, features:].astype(BF16)
    for low in range(0, edges, ROWS):
        rows = pl.ds(low, ROWS)
        incoming = dot(proc_g()[rows, :], g_msg)
        ga_p[rows, :] = backward_hidden(
            incoming, slope_p[rows, :], normed_p[rows, :], scale_p[rows, 0:1], second
        )
    by_send = dot(sender_t()[...], ga_p[...]).astype(BF16)
    g_send = dot(by_send, first[:, :features])
    split(g_send[mesh_rows:, :], grad_halo)
    part.ref[...] = cotangent + g_q[:, :features] + g_send[:mesh_rows, :]


def receive_kernel(part, ga, scatter, weights, out):
    by_recv = dot(scatter()[...], ga()[...]).astype(BF16)
    first, _ = layers(weights, 0)
    out.send(part()[...] + dot(by_recv, first[:, FEATURES:]))


def decode_kernel(
    back, halo_t, grad_in, slope_n, normed_n, scale_n, enc_g, slope_e, normed_e, scale_e,
    weights, slot_t, part, ga, *grad_slots
):
    ga_e = ga.ref
    features = FEATURES
    edges = enc_g().shape[0]
    grad_one = grad_in()[...] + dot(halo_t()[...], stacked(back))
    first_n, second_n = layers(weights, 1)
    ga_n = backward_hidden(grad_one, slope_n()[...], normed_n()[...], scale_n()[:, 0:1], second_n)
    g_n = dot(ga_n, first_n)
    part.ref[...] = grad_one + g_n[:, :features]
    g_edge = g_n[:, features:].astype(BF16)
    first, second = layers(weights, 0)
    for low in range(0, edges, ROWS):
        rows = pl.ds(low, ROWS)
        incoming = dot(enc_g()[rows, :], g_edge)
        ga_e[rows, :] = backward_hidden(
            incoming, slope_e()[rows, :], normed_e()[rows, :], scale_e()[rows, 0:1], second
        )
    by_slot = dot(slot_t()[...], ga_e[...]).astype(BF16)
    split(dot(by_slot, first[:, :features]), grad_slots)


def grid_kernel(back, table_in, out):
    out.send(dot(table_in()[...], stacked(back)))


def along(block, shift):
    size = lax.axis_size("mp")
    if shift % size == 0:
        return block
    return lax.ppermute(block, "mp", [(m, (m + shift) % size) for m in range(size)])


def beside(block, flip):
    if flip == 0:
        return block
    return lax.ppermute(block, "graph", [(g, g ^ flip) for g in range(lax.axis_size("graph"))])


def turn(blocks, count, step):
    out = shape(len(blocks) * step, blocks[0].shape[1], BF16)
    return call(turn_kernel, [out] * count, list(blocks))


def exchange(blocks, step):
    return second_level(first_level(blocks, step))


def first_level(blocks, step):
    return turn([along(b, s) for s, b in enumerate(blocks)], lax.axis_size("graph"), step)


def second_level(blocks):
    return [beside(b, t) for t, b in enumerate(blocks)]


def exchange_back(blocks, step):
    blocks = turn([beside(b, t) for t, b in enumerate(blocks)], lax.axis_size("mp"), step)
    return [along(b, -s) for s, b in enumerate(blocks)], blocks[0]


def local(
    grid_lat,
    mesh_lat,
    cotangent,
    grid_send,
    g2m_slot,
    g2m_receiver,
    halo_send,
    mesh_sender,
    mesh_receiver,
    *shards,
):
    grid_rows, features = grid_lat.shape
    mesh_rows = mesh_lat.shape[0]
    edges = g2m_slot.shape[0]
    mesh_edges = mesh_sender.shape[0]
    mp, graph = lax.axis_size("mp"), lax.axis_size("graph")
    step, halo_step = stride(grid_send.shape[1]), stride(halo_send.shape[1])
    slots, halos = mp * graph * step, mp * graph * halo_step
    tables = call(
        tables_kernel,
        [
            shape(slots, edges, BF16),
            shape(edges, slots, BF16),
            shape(mesh_rows, edges, BF16),
            shape(edges, mesh_rows, BF16),
            shape(mesh_rows, halos, BF16),
            shape(halos, mesh_rows, BF16),
            shape(mesh_rows + halos, mesh_edges, BF16),
            shape(mesh_edges, mesh_rows + halos, BF16),
            shape(mesh_rows, mesh_edges, BF16),
            shape(mesh_edges, mesh_rows, BF16),
            shape(edges, features, BF16),
        ],
        Far(mesh_lat),
        Far(g2m_slot.reshape(1, edges)),
        Far(g2m_receiver.reshape(1, edges)),
        Far(halo_send.T),
        Far(mesh_sender.reshape(1, mesh_edges)),
        Far(mesh_receiver.reshape(1, mesh_edges)),
    )
    enc, finish, arrived, grid_t, tables = start(grid_lat, grid_send, shards, tables)
    slot_t, slot_g, enc_t, enc_g, halo_t, halo_g, sender_t, sender_g, proc_t, proc_g, recv_rows = tables
    saved = [
        shape(edges, features, BF16),
        shape(edges, features, BF16),
        shape(edges, LANES, F32),
        shape(mesh_rows, features, BF16),
        shape(mesh_rows, features, BF16),
        shape(mesh_rows, LANES, F32),
    ]
    mesh_one, slope_e, normed_e, scale_e, slope_n, normed_n, scale_n, *halo_out = call(
        encode_kernel,
        [shape(mesh_rows, features, BF16)] + saved + [shape(graph * halo_step, features, BF16)] * mp,
        recv_rows,
        arrived,
        slot_g,
        enc_t,
        Far(mesh_lat),
        enc,
        halo_g,
        flops=3 * 10**9,
    )
    moved = first_level(halo_out, halo_step)
    halo_in = second_level(moved)
    proc = finish(mesh_one, moved, halo_in[1:])
    mesh_two, part, ga, *grad_halo = call(
        process_kernel,
        [
            shape(mesh_rows, features, BF16),
            shape(mesh_rows, features, F32),
            shape(mesh_edges, features, BF16),
        ]
        + [shape(mp * halo_step, features, BF16)] * graph,
        Far(cotangent),
        mesh_one,
        halo_in,
        sender_g,
        proc_g,
        proc,
        proc_t,
        sender_t,
        last=(0,),
        flops=5 * 10**9,
        scratch=[
            pltpu.VMEM((mesh_edges, features), BF16),
            pltpu.VMEM((mesh_edges, features), BF16),
            pltpu.VMEM((mesh_edges, LANES), F32),
        ],
    )
    halo_back, half_way = exchange_back(grad_halo, halo_step)
    part, _ = lax.optimization_barrier((part, half_way))
    (grad_one,) = call(
        receive_kernel, [shape(mesh_rows, features, F32)], part, ga, proc_t, proc, flops=3 * 10**8
    )
    part, ga, *grad_slots = call(
        decode_kernel,
        [shape(mesh_rows, features, F32), shape(edges, features, BF16)]
        + [shape(mp * step, features, BF16)] * graph,
        halo_back,
        halo_t,
        grad_one,
        slope_n,
        normed_n,
        scale_n,
        enc_g,
        slope_e,
        normed_e,
        scale_e,
        enc,
        slot_t,
        flops=3 * 10**9,
    )
    returned, half_way = exchange_back(grad_slots, step)
    part, _ = lax.optimization_barrier((part, half_way))
    (mesh_grad,) = call(
        receive_kernel, [shape(mesh_rows, features, F32)], part, ga, enc_t, enc, last=(0,), flops=3 * 10**8
    )
    (grid_grad,) = call(
        grid_kernel, [shape(grid_rows, features, F32)], returned, grid_t, last=(0,)
    )
    return (mesh_two, grid_grad, mesh_grad)


def solution(mesh):
    rows = P(AXES, None)
    flat = P(AXES)
    in_specs = (rows,) * 4 + (flat,) * 2 + (rows,) + (flat,) * 2 + (P(None, "mp"), P("mp", None)) * 4
    return jax.shard_map(
        local, mesh=mesh, in_specs=in_specs, out_specs=(rows,) * 3, check_vma=False
    )
```

```python
import jax
import jax.numpy as jnp
from jax import lax
from jax.experimental import pallas as pl
from jax.experimental.pallas import tpu as pltpu
from jax.sharding import PartitionSpec as P

F32 = jnp.float32
BF16 = jnp.bfloat16
LANES = 128
ROWS = 512
FEATURES = 512
AXES = ("groups", "graph", "mp")


def dot(left, right):
    return jnp.dot(left, right, preferred_element_type=F32)


def dot_trans(left, right):
    return lax.dot_general(left, right, (((1,), (1,)), ((), ())), preferred_element_type=F32)


def shape(rows, columns, dtype):
    return jax.ShapeDtypeStruct((rows, columns), dtype)


class Far:
    def __init__(self, array):
        self.array = pltpu.with_memory_space_constraint(array, pltpu.HBM)


class Input:
    def __init__(self, copy, ref):
        self.copy, self.ref = copy, ref

    def __call__(self):
        if self.copy is not None:
            self.copy.wait()
            self.copy = None
        return self.ref


class Output:
    def __init__(self, ref, copy):
        self.ref, self.copy = ref, copy

    def send(self, value=None):
        if value is not None:
            self.ref[...] = value
        if self.copy is not None:
            self.copy.start()


def call(kernel, out_shape, *args, last=(), scratch=(), flops=0):
    groups = [a if isinstance(a, list) else [a] for a in args]
    flat = [a for group in groups for a in group]
    far = [isinstance(a, Far) for a in flat]
    arrays = [a.array if isinstance(a, Far) else a for a in flat]
    count, outs = len(arrays), len(out_shape)

    def body(*refs):
        ins, refs = refs[:count], refs[count:]
        out_refs, refs = refs[:outs], refs[outs:]
        places, refs = list(refs[: sum(far)]), refs[sum(far) :]
        results, refs = list(refs[: len(last)]), refs[len(last) :]
        sem_in, sem_out, refs = refs[0], refs[1], refs[2:]
        inputs = []
        for ref, away in zip(ins, far):
            copy = None
            if away:
                place = places.pop(0)
                copy = pltpu.make_async_copy(ref, place, sem_in.at[len(places)])
                copy.start()
                ref = place
            inputs.append(Input(copy, ref))
        outputs = []
        for i, ref in enumerate(out_refs):
            copy = None
            if i in last:
                place = results.pop(0)
                copy = pltpu.make_async_copy(place, ref, sem_out.at[len(results)])
                ref = place
            outputs.append(Output(ref, copy))
        given = []
        for arg, group in zip(args, groups):
            part, inputs = inputs[: len(group)], inputs[len(group) :]
            given.append(part if isinstance(arg, list) else part[0])
        kernel(*given, *outputs, *refs)
        for output in outputs:
            if output.copy is not None:
                output.copy.wait()

    vmem, hbm = pl.BlockSpec(memory_space=pltpu.VMEM), pl.BlockSpec(memory_space=pl.ANY)
    total = sum(a.size * a.dtype.itemsize for a in arrays)
    return pl.pallas_call(
        body,
        out_shape=out_shape,
        in_specs=[hbm if away else vmem for away in far],
        out_specs=[hbm if i in last else vmem for i in range(outs)],
        scratch_shapes=[pltpu.VMEM(a.shape, a.dtype) for a, away in zip(arrays, far) if away]
        + [pltpu.VMEM(out_shape[i].shape, out_shape[i].dtype) for i in last]
        + [pltpu.SemaphoreType.DMA((max(sum(far), 1),)), pltpu.SemaphoreType.DMA((max(len(last), 1),))]
        + list(scratch),
        name=kernel.__name__,
        cost_estimate=pl.CostEstimate(flops=flops, bytes_accessed=total, transcendentals=0),
        compiler_params=pltpu.CompilerParams(vmem_limit_bytes=24 * 1024 * 1024),
    )(*arrays)


def layers(blocks, which):
    low = which * 3 * FEATURES
    middle = low + 2 * FEATURES
    return (
        jnp.concatenate([block()[:, low:middle] for block in blocks], axis=0),
        jnp.concatenate([block()[:, middle : middle + FEATURES] for block in blocks], axis=0),
    )


def turned(first, select):
    return dot_trans(select, first).astype(BF16)


def prepare_kernel(grid, send, shards, table_out, kept, *messages):
    width = 3 * FEATURES
    outgoing = send_rows(grid, send, table_out)
    size = kept.ref.shape[0]
    kept.ref[...] = outgoing[:size, :].astype(BF16)
    for i, out in enumerate(messages):
        out.ref[:, 2 * width :] = outgoing[(i + 1) * size : (i + 2) * size, :].astype(BF16)
    for i in range(2):
        first, second = piece_of(shards[2 * i], shards[2 * i + 1], messages[0].ref.shape[0])
        low = i * width
        for out in messages:
            out.ref[:, low : low + 2 * FEATURES] = first
            out.ref[:, low + 2 * FEATURES : low + width] = second


def piece_of(one, two, rows):
    plane = lax.axis_index("groups") * lax.axis_size("graph") + lax.axis_index("graph")
    base = plane * rows
    hidden = two().shape[0]
    select = jnp.where(
        lax.broadcasted_iota(jnp.int32, (rows, hidden), 0) + base
        == lax.broadcasted_iota(jnp.int32, (rows, hidden), 1),
        1.0,
        0.0,
    ).astype(BF16)
    return turned(one()[...], select), two()[pl.ds(pl.multiple_of(base, rows), rows), :]


def join_kernel(kept, messages, near, block, both):
    width = 6 * FEATURES
    weights = jnp.concatenate([m()[:, :width] for m in messages], axis=0)
    rows = jnp.concatenate([kept()[...]] + [m()[:, width:] for m in messages], axis=0)
    step = rows.shape[0] // 16
    block.ref[...] = weights
    both.ref[:, :width] = weights
    size = near.ref.shape[0]
    for j in range(4):
        moved = dot(turn_table(4, 4, step, j), rows).astype(BF16)
        if j == 0:
            near.ref[...] = moved
        else:
            both.ref[(j - 1) * size : j * size, width:] = moved


def own_kernel(shards, enc_own, proc_own, proc_piece):
    width = 3 * FEATURES
    for i in range(4):
        one, two = shards[2 * i](), shards[2 * i + 1]()
        hidden = one.shape[1]
        select = jnp.where(
            lax.broadcasted_iota(jnp.int32, (hidden, hidden), 0)
            == lax.broadcasted_iota(jnp.int32, (hidden, hidden), 1),
            1.0,
            0.0,
        ).astype(BF16)
        out, low = (enc_own, proc_own)[i // 2], i % 2 * width
        out.ref[:, low : low + 2 * FEATURES] = turned(one[...], select)
        out.ref[:, low + 2 * FEATURES : low + width] = two[...]
    for i in (2, 3):
        first, second = piece_of(shards[2 * i], shards[2 * i + 1], proc_piece.ref.shape[0])
        low = i % 2 * width
        proc_piece.ref[:, low : low + 2 * FEATURES] = first
        proc_piece.ref[:, low + 2 * FEATURES : low + width] = second


def across(x, flip):
    planes = lax.axis_size("groups") * lax.axis_size("graph")
    return lax.ppermute(x, ("groups", "graph"), [(p, p ^ flip) for p in range(planes)])


def start(grid_lat, grid_send, shards, tables):
    grid_rows, features = grid_lat.shape
    mp, graph = lax.axis_size("mp"), lax.axis_size("graph")
    step = stride(grid_send.shape[1])
    sent = [shape(grid_rows, mp * graph * step, BF16)] + [shape(graph * step, features, BF16)] * mp
    planes = lax.axis_size("groups") * graph
    hidden = shards[1].shape[0]
    if planes != 8 or mp != 4 or hidden != 128 or features != FEATURES:
        grid_t, *outgoing = call(send_kernel, sent, Far(grid_lat), Far(grid_send.T))
        rows = []
        for i in range(4):
            rows.append(lax.all_gather(shards[2 * i], "mp", axis=1, tiled=True).T)
            rows.append(lax.all_gather(shards[2 * i + 1], "mp", axis=0, tiled=True))
        enc, proc = jnp.concatenate(rows[:4], axis=1), jnp.concatenate(rows[4:], axis=1)
        arrived = exchange(outgoing, step)
        return [enc], lambda one, moved, came: [proc], arrived, grid_t, tables
    far = [Far(s) for s in shards]
    piece = hidden // planes
    width = 6 * features
    grid_t, kept, *messages = call(
        prepare_kernel,
        sent[:2] + [shape(piece, width + features, BF16)] * 3,
        Far(grid_lat),
        Far(grid_send.T),
        far[:4],
    )
    enc_own, proc_own, proc_piece = call(
        own_kernel, [shape(hidden, width, BF16)] * 2 + [shape(piece, width, BF16)], far
    )
    messages = [along(m, i + 1) for i, m in enumerate(messages)]
    kept, enc_own, *tables = lax.optimization_barrier((kept, enc_own, *tables))
    rows = mp * step
    near, first, both = call(
        join_kernel,
        [shape(rows, features, BF16), shape(3 * piece, width, BF16), shape(3 * rows, width + features, BF16)],
        kept,
        messages,
    )
    x, y, corner = across(both, 2), across(first, 4), across(first, 6)
    proc_piece, _ = lax.optimization_barrier((proc_piece, near))
    beside_me = lax.ppermute(proc_piece, "mp", [(m, m ^ 1) for m in range(mp)])
    pair = jnp.concatenate([proc_piece, beside_me])
    pairs = lax.ppermute(pair, "mp", [(m, m ^ 2) for m in range(mp)])
    proc_first = jnp.concatenate([beside_me, pairs])
    both, x, y, corner, _ = lax.optimization_barrier((both, x, y, corner, pairs))
    core, x_core, others = across(both, 1), across(x, 1), across(jnp.concatenate([y, corner]), 1)
    enc = [enc_own, first, core, x, y, corner, x_core, others]
    arrived = [near, core, x, x_core]
    proc_first, *_ = lax.optimization_barrier((proc_first, x, y, corner))
    proc_x, proc_y = across(proc_first, 2), across(proc_first, 4)

    def finish(one, moved, came):
        late, _ = lax.optimization_barrier((proc_first, one))
        corner = across(late, 6)
        x, y, *_ = lax.optimization_barrier((proc_x, proc_y, *moved))
        sides = across(jnp.concatenate([x, y]), 1)
        corner, *_ = lax.optimization_barrier((corner, *came))
        return [proc_own, proc_first, across(proc_first, 1), x, y, sides, corner, across(corner, 1)]

    return enc, finish, arrived, grid_t, tables


def forward(inputs, first, second):
    before = dot_trans(inputs, first)
    logistic = 0.5 + 0.5 * jnp.tanh(0.5 * before)
    wide = before * logistic
    hidden = wide.astype(BF16)
    slope = logistic + wide * (1.0 - logistic)
    summed = dot(hidden, second)
    centered = summed - jnp.mean(summed, axis=-1, keepdims=True)
    rescale = lax.rsqrt(jnp.mean(centered * centered, axis=-1, keepdims=True) + 1e-05)
    normed = centered * rescale
    return normed, slope.astype(BF16), normed.astype(BF16), rescale


def backward_hidden(incoming, slope, normed, rescale, second):
    normed = normed.astype(F32)
    g_out = (
        incoming
        - jnp.mean(incoming, axis=-1, keepdims=True)
        - normed * jnp.mean(incoming * normed, axis=-1, keepdims=True)
    ) * rescale
    return (dot_trans(g_out.astype(BF16), second) * slope.astype(F32)).astype(BF16)


def table(index_row, count):
    n = index_row.shape[1]
    return jnp.where(lax.broadcasted_iota(jnp.int32, (count, n), 0) == index_row, 1.0, 0.0)


def stride(capacity):
    return max(capacity, 16 // min(lax.axis_size("mp"), lax.axis_size("graph")))


def apart_at(peer, slot, step, mp_first):
    mp, graph = lax.axis_size("mp"), lax.axis_size("graph")
    along_mp, along_graph = peer % mp ^ lax.axis_index("mp"), peer // mp ^ lax.axis_index("graph")
    block = along_mp * graph + along_graph if mp_first else along_graph * mp + along_mp
    return block * step + slot


def sent_at(peer, slot, step):
    return apart_at(peer, slot, step, True)


def arrived_at(peer, slot, step):
    return apart_at(peer, slot, step, False)


def sent_row(index, step):
    width, count = index.shape
    index = index.astype(F32).T
    at = lax.broadcasted_iota(jnp.int32, (count, count * step), 1)
    peer = lax.broadcasted_iota(jnp.int32, (count, count * step), 0)
    row = jnp.zeros(at.shape, F32)
    for slot in range(width):
        row = jnp.where(sent_at(peer, slot, step) == at, index[:, slot : slot + 1] + 1.0, row)
    return jnp.sum(row, axis=0, keepdims=True).astype(jnp.int32) - 1


def stacked(blocks):
    return jnp.concatenate([block()[...] for block in blocks], axis=0)


def split(rows, outs):
    size = rows.shape[0] // len(outs)
    for i, out in enumerate(outs):
        out.ref[...] = rows[i * size : (i + 1) * size, :].astype(BF16)


def send_rows(grid, send, table_out):
    count = table_out.ref.shape[1]
    one = table(sent_row(send()[...], count // send().shape[1]), grid().shape[0])
    table_out.ref[...] = one.astype(BF16)
    return dot(one.T.astype(BF16), grid()[...])


def send_kernel(grid, send, table_out, *outgoing):
    split(send_rows(grid, send, table_out), outgoing)


def turn_table(sources, targets, step, j):
    row = lax.broadcasted_iota(jnp.int32, (sources * step, sources * targets * step), 0)
    at = lax.broadcasted_iota(jnp.int32, row.shape, 1)
    source = (row // step * targets + j) * step + row % step
    return jnp.where(at == source, 1.0, 0.0).astype(BF16)


def turn_kernel(blocks, *outs):
    rows = stacked(blocks)
    step = rows.shape[0] // (len(blocks) * len(outs))
    for j, out in enumerate(outs):
        out.ref[...] = dot(turn_table(len(blocks), len(outs), step, j), rows).astype(BF16)


def tables_kernel(mesh, slot, recv_e, halo, sender, recv_p, *outs):
    mesh_rows = mesh().shape[0]
    peers = halo().shape[1]
    slot_step, halo_step = outs[0].ref.shape[0] // peers, outs[4].ref.shape[1] // peers
    capacity, halo_capacity = slot_step, halo().shape[0]
    slots = slot()[...]
    slots = arrived_at(slots // capacity, slots % capacity, slot_step)
    senders = sender()[...]
    remote = jnp.maximum(senders - mesh_rows, 0)
    remote = arrived_at(remote // halo_capacity, remote % halo_capacity, halo_step)
    senders = jnp.where(senders < mesh_rows, senders, mesh_rows + remote)
    rows = (slots, recv_e()[...], sent_row(halo()[...], halo_step), senders, recv_p()[...])
    for i, row in enumerate(rows):
        scatter, gather = outs[2 * i : 2 * i + 2]
        one = table(row, scatter.ref.shape[0])
        scatter.ref[...] = one.astype(BF16)
        gather.ref[...] = one.T.astype(BF16)
    outs[10].ref[...] = dot(outs[3].ref[...], mesh()[...]).astype(BF16)


def arrived_rows(blocks):
    size = blocks[0]().shape[0]
    rows = [blocks[0]()[...]]
    for t, block in enumerate(blocks[1:]):
        if block().shape[1] == FEATURES:
            rows.append(block()[...])
        else:
            rows.append(block()[t * size : (t + 1) * size, 6 * FEATURES :])
    return jnp.concatenate(rows, axis=0)


def encode_kernel(
    recv_rows, arrived, slot_g, enc_t, mesh, weights, halo_g,
    one_out, slope_e, normed_e, scale_e, slope_n, normed_n, scale_n, *halo_out,
):
    rows_in = arrived_rows(arrived)
    edges = slot_g().shape[0]
    first, second = layers(weights, 0)
    for low in range(0, edges, ROWS):
        rows = pl.ds(low, ROWS)
        sent = dot(slot_g()[rows, :], rows_in).astype(BF16)
        inputs = jnp.concatenate([sent, recv_rows()[rows, :]], axis=1)
        _, slope, normed, rescale = forward(inputs, first, second)
        slope_e.ref[rows, :] = slope
        normed_e.ref[rows, :] = normed
        scale_e.ref[rows, :] = jnp.broadcast_to(rescale, (ROWS, LANES))
    aggregate = dot(enc_t()[...], normed_e.ref[...]).astype(BF16)
    first, second = layers(weights, 1)
    own = mesh()[...]
    normed, slope, rounded, rescale = forward(
        jnp.concatenate([own, aggregate], axis=1), first, second
    )
    one = (own.astype(F32) + normed).astype(BF16)
    one_out.ref[...] = one
    split(dot(halo_g()[...], one), halo_out)
    slope_n.ref[...] = slope
    normed_n.ref[...] = rounded
    scale_n.ref[...] = jnp.broadcast_to(rescale, scale_n.ref.shape)


def process_kernel(
    cotangent_in, one_in, halo, sender_g, proc_g, weights, proc_t, sender_t, two, part, ga, *refs
):
    grad_halo, (slope_p, normed_p, scale_p) = refs[:-3], refs[-3:]
    ga_p = ga.ref
    features = FEATURES
    one = one_in()[...]
    mesh_rows = one.shape[0]
    lookup = jnp.concatenate([one, stacked(halo)], axis=0)
    edges = sender_g().shape[0]
    first, second = layers(weights, 0)
    for low in range(0, edges, ROWS):
        rows = pl.ds(low, ROWS)
        sent = dot(sender_g()[rows, :], lookup).astype(BF16)
        got = dot(proc_g()[rows, :], one).astype(BF16)
        _, slope, normed, rescale = forward(jnp.concatenate([sent, got], axis=1), first, second)
        slope_p[rows, :] = slope
        normed_p[rows, :] = normed
        scale_p[rows, :] = jnp.broadcast_to(rescale, (ROWS, LANES))
    aggregate = dot(proc_t()[...], normed_p[...]).astype(BF16)
    first_n, second_n = layers(weights, 1)
    normed, slope, rounded, rescale = forward(
        jnp.concatenate([one, aggregate], axis=1), first_n, second_n
    )
    two.send((one.astype(F32) + normed).astype(BF16))
    cotangent = cotangent_in()[...].astype(F32)
    g_q = dot(backward_hidden(cotangent, slope, rounded, rescale, second_n), first_n)
    g_msg = g_q[:, features:].astype(BF16)
    for low in range(0, edges, ROWS):
        rows = pl.ds(low, ROWS)
        incoming = dot(proc_g()[rows, :], g_msg)
        ga_p[rows, :] = backward_hidden(
            incoming, slope_p[rows, :], normed_p[rows, :], scale_p[rows, 0:1], second
        )
    by_send = dot(sender_t()[...], ga_p[...]).astype(BF16)
    g_send = dot(by_send, first[:, :features])
    split(g_send[mesh_rows:, :], grad_halo)
    part.ref[...] = cotangent + g_q[:, :features] + g_send[:mesh_rows, :]


def receive_kernel(part, ga, scatter, weights, out):
    by_recv = dot(scatter()[...], ga()[...]).astype(BF16)
    first, _ = layers(weights, 0)
    out.send(part()[...] + dot(by_recv, first[:, FEATURES:]))


def decode_kernel(
    back, halo_t, grad_in, slope_n, normed_n, scale_n, enc_g, slope_e, normed_e, scale_e,
    weights, slot_t, part, ga, *grad_slots
):
    ga_e = ga.ref
    features = FEATURES
    edges = enc_g().shape[0]
    grad_one = grad_in()[...] + dot(halo_t()[...], stacked(back))
    first_n, second_n = layers(weights, 1)
    ga_n = backward_hidden(grad_one, slope_n()[...], normed_n()[...], scale_n()[:, 0:1], second_n)
    g_n = dot(ga_n, first_n)
    part.ref[...] = grad_one + g_n[:, :features]
    g_edge = g_n[:, features:].astype(BF16)
    first, second = layers(weights, 0)
    for low in range(0, edges, ROWS):
        rows = pl.ds(low, ROWS)
        incoming = dot(enc_g()[rows, :], g_edge)
        ga_e[rows, :] = backward_hidden(
            incoming, slope_e()[rows, :], normed_e()[rows, :], scale_e()[rows, 0:1], second
        )
    by_slot = dot(slot_t()[...], ga_e[...]).astype(BF16)
    split(dot(by_slot, first[:, :features]), grad_slots)


def grid_kernel(back, table_in, out):
    out.send(dot(table_in()[...], stacked(back)))


def along(block, flip):
    size = lax.axis_size("mp")
    if flip == 0:
        return block
    return lax.ppermute(block, "mp", [(m, m ^ flip) for m in range(size)])


def beside(block, flip):
    if flip == 0:
        return block
    return lax.ppermute(block, "graph", [(g, g ^ flip) for g in range(lax.axis_size("graph"))])


def turn(blocks, count, step):
    out = shape(len(blocks) * step, blocks[0].shape[1], BF16)
    return call(turn_kernel, [out] * count, list(blocks))


def exchange(blocks, step):
    return second_level(first_level(blocks, step))


def first_level(blocks, step):
    return turn([along(b, s) for s, b in enumerate(blocks)], lax.axis_size("graph"), step)


def second_level(blocks):
    return [beside(b, t) for t, b in enumerate(blocks)]


def exchange_back(blocks, step):
    blocks = turn([beside(b, t) for t, b in enumerate(blocks)], lax.axis_size("mp"), step)
    return [along(b, s) for s, b in enumerate(blocks)], blocks[0]


def local(
    grid_lat,
    mesh_lat,
    cotangent,
    grid_send,
    g2m_slot,
    g2m_receiver,
    halo_send,
    mesh_sender,
    mesh_receiver,
    *shards,
):
    grid_rows, features = grid_lat.shape
    mesh_rows = mesh_lat.shape[0]
    edges = g2m_slot.shape[0]
    mesh_edges = mesh_sender.shape[0]
    mp, graph = lax.axis_size("mp"), lax.axis_size("graph")
    step, halo_step = stride(grid_send.shape[1]), stride(halo_send.shape[1])
    slots, halos = mp * graph * step, mp * graph * halo_step
    tables = call(
        tables_kernel,
        [
            shape(slots, edges, BF16),
            shape(edges, slots, BF16),
            shape(mesh_rows, edges, BF16),
            shape(edges, mesh_rows, BF16),
            shape(mesh_rows, halos, BF16),
            shape(halos, mesh_rows, BF16),
            shape(mesh_rows + halos, mesh_edges, BF16),
            shape(mesh_edges, mesh_rows + halos, BF16),
            shape(mesh_rows, mesh_edges, BF16),
            shape(mesh_edges, mesh_rows, BF16),
            shape(edges, features, BF16),
        ],
        Far(mesh_lat),
        Far(g2m_slot.reshape(1, edges)),
        Far(g2m_receiver.reshape(1, edges)),
        Far(halo_send.T),
        Far(mesh_sender.reshape(1, mesh_edges)),
        Far(mesh_receiver.reshape(1, mesh_edges)),
    )
    enc, finish, arrived, grid_t, tables = start(grid_lat, grid_send, shards, tables)
    slot_t, slot_g, enc_t, enc_g, halo_t, halo_g, sender_t, sender_g, proc_t, proc_g, recv_rows = tables
    saved = [
        shape(edges, features, BF16),
        shape(edges, features, BF16),
        shape(edges, LANES, F32),
        shape(mesh_rows, features, BF16),
        shape(mesh_rows, features, BF16),
        shape(mesh_rows, LANES, F32),
    ]
    mesh_one, slope_e, normed_e, scale_e, slope_n, normed_n, scale_n, *halo_out = call(
        encode_kernel,
        [shape(mesh_rows, features, BF16)] + saved + [shape(graph * halo_step, features, BF16)] * mp,
        recv_rows,
        arrived,
        slot_g,
        enc_t,
        Far(mesh_lat),
        enc,
        halo_g,
        flops=3 * 10**9,
    )
    moved = first_level(halo_out, halo_step)
    halo_in = second_level(moved)
    proc = finish(mesh_one, moved, halo_in[1:])
    mesh_two, part, ga, *grad_halo = call(
        process_kernel,
        [
            shape(mesh_rows, features, BF16),
            shape(mesh_rows, features, F32),
            shape(mesh_edges, features, BF16),
        ]
        + [shape(mp * halo_step, features, BF16)] * graph,
        Far(cotangent),
        mesh_one,
        halo_in,
        sender_g,
        proc_g,
        proc,
        proc_t,
        sender_t,
        last=(0,),
        flops=5 * 10**9,
        scratch=[
            pltpu.VMEM((mesh_edges, features), BF16),
            pltpu.VMEM((mesh_edges, features), BF16),
            pltpu.VMEM((mesh_edges, LANES), F32),
        ],
    )
    halo_back, half_way = exchange_back(grad_halo, halo_step)
    part, _ = lax.optimization_barrier((part, half_way))
    (grad_one,) = call(
        receive_kernel, [shape(mesh_rows, features, F32)], part, ga, proc_t, proc, flops=3 * 10**8
    )
    part, ga, *grad_slots = call(
        decode_kernel,
        [shape(mesh_rows, features, F32), shape(edges, features, BF16)]
        + [shape(mp * step, features, BF16)] * graph,
        halo_back,
        halo_t,
        grad_one,
        slope_n,
        normed_n,
        scale_n,
        enc_g,
        slope_e,
        normed_e,
        scale_e,
        enc,
        slot_t,
        flops=3 * 10**9,
    )
    returned, half_way = exchange_back(grad_slots, step)
    part, _ = lax.optimization_barrier((part, half_way))
    (mesh_grad,) = call(
        receive_kernel, [shape(mesh_rows, features, F32)], part, ga, enc_t, enc, last=(0,), flops=3 * 10**8
    )
    (grid_grad,) = call(
        grid_kernel, [shape(grid_rows, features, F32)], returned, grid_t, last=(0,)
    )
    return (mesh_two, grid_grad, mesh_grad)


def solution(mesh):
    rows = P(AXES, None)
    flat = P(AXES)
    in_specs = (rows,) * 4 + (flat,) * 2 + (rows,) + (flat,) * 2 + (P(None, "mp"), P("mp", None)) * 4
    return jax.shard_map(
        local, mesh=mesh, in_specs=in_specs, out_specs=(rows,) * 3, check_vma=False
    )
```

```python
import jax
import jax.numpy as jnp
from jax import lax
from jax.experimental import pallas as pl
from jax.experimental.pallas import tpu as pltpu
from jax.sharding import PartitionSpec as P

F32 = jnp.float32
BF16 = jnp.bfloat16
LANES = 128
ROWS = 512
FEATURES = 512
AXES = ("groups", "graph", "mp")


def dot(left, right):
    return jnp.dot(left, right, preferred_element_type=F32)


def dot_trans(left, right):
    return lax.dot_general(left, right, (((1,), (1,)), ((), ())), preferred_element_type=F32)


def shape(rows, columns, dtype):
    return jax.ShapeDtypeStruct((rows, columns), dtype)


class Far:
    def __init__(self, array):
        self.array = pltpu.with_memory_space_constraint(array, pltpu.HBM)


class Input:
    def __init__(self, copy, ref):
        self.copy, self.ref = copy, ref

    def __call__(self):
        if self.copy is not None:
            self.copy.wait()
            self.copy = None
        return self.ref


class Output:
    def __init__(self, ref, copy):
        self.ref, self.copy = ref, copy

    def send(self, value=None):
        if value is not None:
            self.ref[...] = value
        if self.copy is not None:
            self.copy.start()


def call(kernel, out_shape, *args, last=(), scratch=(), flops=0):
    groups = [a if isinstance(a, list) else [a] for a in args]
    flat = [a for group in groups for a in group]
    far = [isinstance(a, Far) for a in flat]
    arrays = [a.array if isinstance(a, Far) else a for a in flat]
    count, outs = len(arrays), len(out_shape)

    def body(*refs):
        ins, refs = refs[:count], refs[count:]
        out_refs, refs = refs[:outs], refs[outs:]
        places, refs = list(refs[: sum(far)]), refs[sum(far) :]
        results, refs = list(refs[: len(last)]), refs[len(last) :]
        sem_in, sem_out, refs = refs[0], refs[1], refs[2:]
        inputs = []
        for ref, away in zip(ins, far):
            copy = None
            if away:
                place = places.pop(0)
                copy = pltpu.make_async_copy(ref, place, sem_in.at[len(places)])
                copy.start()
                ref = place
            inputs.append(Input(copy, ref))
        outputs = []
        for i, ref in enumerate(out_refs):
            copy = None
            if i in last:
                place = results.pop(0)
                copy = pltpu.make_async_copy(place, ref, sem_out.at[len(results)])
                ref = place
            outputs.append(Output(ref, copy))
        given = []
        for arg, group in zip(args, groups):
            part, inputs = inputs[: len(group)], inputs[len(group) :]
            given.append(part if isinstance(arg, list) else part[0])
        kernel(*given, *outputs, *refs)
        for output in outputs:
            if output.copy is not None:
                output.copy.wait()

    vmem, hbm = pl.BlockSpec(memory_space=pltpu.VMEM), pl.BlockSpec(memory_space=pl.ANY)
    total = sum(a.size * a.dtype.itemsize for a in arrays)
    return pl.pallas_call(
        body,
        out_shape=out_shape,
        in_specs=[hbm if away else vmem for away in far],
        out_specs=[hbm if i in last else vmem for i in range(outs)],
        scratch_shapes=[pltpu.VMEM(a.shape, a.dtype) for a, away in zip(arrays, far) if away]
        + [pltpu.VMEM(out_shape[i].shape, out_shape[i].dtype) for i in last]
        + [pltpu.SemaphoreType.DMA((max(sum(far), 1),)), pltpu.SemaphoreType.DMA((max(len(last), 1),))]
        + list(scratch),
        name=kernel.__name__,
        cost_estimate=pl.CostEstimate(flops=flops, bytes_accessed=total, transcendentals=0),
        compiler_params=pltpu.CompilerParams(vmem_limit_bytes=24 * 1024 * 1024),
    )(*arrays)


def layers(blocks, which):
    low = which * 3 * FEATURES
    middle = low + 2 * FEATURES
    return (
        jnp.concatenate([block()[:, low:middle] for block in blocks], axis=0),
        jnp.concatenate([block()[:, middle : middle + FEATURES] for block in blocks], axis=0),
    )


def turned(first, select):
    return dot_trans(select, first).astype(BF16)


def prepare_kernel(grid, send, shards, kept, *messages):
    width = 3 * FEATURES
    outgoing = send_rows(grid, send)
    size = kept.ref.shape[0]
    kept.ref[...] = outgoing[:size, :].astype(BF16)
    for i, out in enumerate(messages):
        out.ref[:, 2 * width :] = outgoing[(i + 1) * size : (i + 2) * size, :].astype(BF16)
    for i in range(2):
        first, second = piece_of(shards[2 * i], shards[2 * i + 1], messages[0].ref.shape[0])
        low = i * width
        for out in messages:
            out.ref[:, low : low + 2 * FEATURES] = first
            out.ref[:, low + 2 * FEATURES : low + width] = second


def piece_of(one, two, rows):
    plane = lax.axis_index("groups") * lax.axis_size("graph") + lax.axis_index("graph")
    base = plane * rows
    hidden = two().shape[0]
    select = jnp.where(
        lax.broadcasted_iota(jnp.int32, (rows, hidden), 0) + base
        == lax.broadcasted_iota(jnp.int32, (rows, hidden), 1),
        1.0,
        0.0,
    ).astype(BF16)
    return turned(one()[...], select), two()[pl.ds(pl.multiple_of(base, rows), rows), :]


def join_kernel(kept, messages, near, block, both):
    width = 6 * FEATURES
    weights = jnp.concatenate([m()[:, :width] for m in messages], axis=0)
    rows = jnp.concatenate([kept()[...]] + [m()[:, width:] for m in messages], axis=0)
    step = rows.shape[0] // 16
    block.ref[...] = weights
    both.ref[:, :width] = weights
    size = near.ref.shape[0]
    for j in range(4):
        moved = dot(turn_table(4, 4, step, j), rows).astype(BF16)
        if j == 0:
            near.ref[...] = moved
        else:
            both.ref[(j - 1) * size : j * size, width:] = moved


def own_kernel(shards, enc_own, proc_own, proc_piece):
    width = 3 * FEATURES
    for i in range(4):
        one, two = shards[2 * i](), shards[2 * i + 1]()
        hidden = one.shape[1]
        select = jnp.where(
            lax.broadcasted_iota(jnp.int32, (hidden, hidden), 0)
            == lax.broadcasted_iota(jnp.int32, (hidden, hidden), 1),
            1.0,
            0.0,
        ).astype(BF16)
        out, low = (enc_own, proc_own)[i // 2], i % 2 * width
        out.ref[:, low : low + 2 * FEATURES] = turned(one[...], select)
        out.ref[:, low + 2 * FEATURES : low + width] = two[...]
    for i in (2, 3):
        first, second = piece_of(shards[2 * i], shards[2 * i + 1], proc_piece.ref.shape[0])
        low = i % 2 * width
        proc_piece.ref[:, low : low + 2 * FEATURES] = first
        proc_piece.ref[:, low + 2 * FEATURES : low + width] = second


def across(x, flip):
    planes = lax.axis_size("groups") * lax.axis_size("graph")
    return lax.ppermute(x, ("groups", "graph"), [(p, p ^ flip) for p in range(planes)])


def start(grid_lat, grid_send, shards, tables):
    grid_rows, features = grid_lat.shape
    mp, graph = lax.axis_size("mp"), lax.axis_size("graph")
    step = stride(grid_send.shape[1])
    sent = [shape(graph * step, features, BF16)] * mp
    planes = lax.axis_size("groups") * graph
    hidden = shards[1].shape[0]
    if planes != 8 or mp != 4 or hidden != 128 or features != FEATURES:
        outgoing = call(send_kernel, sent, Far(grid_lat), Far(grid_send.T))
        rows = []
        for i in range(4):
            rows.append(lax.all_gather(shards[2 * i], "mp", axis=1, tiled=True).T)
            rows.append(lax.all_gather(shards[2 * i + 1], "mp", axis=0, tiled=True))
        enc, proc = jnp.concatenate(rows[:4], axis=1), jnp.concatenate(rows[4:], axis=1)
        arrived = exchange(outgoing, step)
        return [enc], lambda one, moved, came: [proc], arrived, tables
    far = [Far(s) for s in shards]
    piece = hidden // planes
    width = 6 * features
    kept, *messages = call(
        prepare_kernel,
        sent[:1] + [shape(piece, width + features, BF16)] * 3,
        Far(grid_lat),
        Far(grid_send.T),
        far[:4],
    )
    enc_own, proc_own, proc_piece = call(
        own_kernel, [shape(hidden, width, BF16)] * 2 + [shape(piece, width, BF16)], far
    )
    messages = [along(m, i + 1, True) for i, m in enumerate(messages)]
    kept, enc_own, *tables = lax.optimization_barrier((kept, enc_own, *tables))
    rows = mp * step
    near, first, both = call(
        join_kernel,
        [shape(rows, features, BF16), shape(3 * piece, width, BF16), shape(3 * rows, width + features, BF16)],
        kept,
        messages,
    )
    x, y, corner = across(both, 2), across(first, 4), across(first, 6)
    proc_piece, _ = lax.optimization_barrier((proc_piece, near))
    beside_me = lax.ppermute(proc_piece, "mp", [(m, m ^ 1) for m in range(mp)])
    pair = jnp.concatenate([proc_piece, beside_me])
    pairs = lax.ppermute(pair, "mp", [(m, m ^ 2) for m in range(mp)])
    proc_first = jnp.concatenate([beside_me, pairs])
    both, x, y, corner, _ = lax.optimization_barrier((both, x, y, corner, pairs))
    core, x_core, others = across(both, 1), across(x, 1), across(jnp.concatenate([y, corner]), 1)
    enc = [enc_own, first, core, x, y, corner, x_core, others]
    arrived = [near, core, x, x_core]
    proc_first, *_ = lax.optimization_barrier((proc_first, x, y, corner))
    proc_x, proc_y = across(proc_first, 2), across(proc_first, 4)

    def finish(one, moved, came):
        late, _ = lax.optimization_barrier((proc_first, one))
        corner = across(late, 6)
        x, y, *_ = lax.optimization_barrier((proc_x, proc_y, *moved))
        sides = across(jnp.concatenate([x, y]), 1)
        corner, *_ = lax.optimization_barrier((corner, *came))
        return [proc_own, proc_first, across(proc_first, 1), x, y, sides, corner, across(corner, 1)]

    return enc, finish, arrived, tables


def forward(inputs, first, second):
    before = dot_trans(inputs, first)
    logistic = 0.5 + 0.5 * jnp.tanh(0.5 * before)
    wide = before * logistic
    hidden = wide.astype(BF16)
    slope = logistic + wide * (1.0 - logistic)
    summed = dot(hidden, second)
    centered = summed - jnp.mean(summed, axis=-1, keepdims=True)
    rescale = lax.rsqrt(jnp.mean(centered * centered, axis=-1, keepdims=True) + 1e-05)
    normed = centered * rescale
    return normed, slope.astype(BF16), normed.astype(BF16), rescale


def backward_hidden(incoming, slope, normed, rescale, second):
    normed = normed.astype(F32)
    g_out = (
        incoming
        - jnp.mean(incoming, axis=-1, keepdims=True)
        - normed * jnp.mean(incoming * normed, axis=-1, keepdims=True)
    ) * rescale
    return (dot_trans(g_out.astype(BF16), second) * slope.astype(F32)).astype(BF16)


def table(index_row, count):
    n = index_row.shape[1]
    return jnp.where(lax.broadcasted_iota(jnp.int32, (count, n), 0) == index_row, 1.0, 0.0)


def stride(capacity):
    return max(capacity, 16 // min(lax.axis_size("mp"), lax.axis_size("graph")))


def sent_at(peer, slot, step, paired=False):
    mp, graph = lax.axis_size("mp"), lax.axis_size("graph")
    me, other = lax.axis_index("mp"), peer % mp
    shift = other ^ me if paired else (other + mp - me) % mp
    return (shift * graph + (peer // mp ^ lax.axis_index("graph"))) * step + slot


def arrived_at(peer, slot, step, paired=False):
    mp = lax.axis_size("mp")
    me, other = lax.axis_index("mp"), peer % mp
    shift = other ^ me if paired else (me + mp - other) % mp
    return ((peer // mp ^ lax.axis_index("graph")) * mp + shift) * step + slot


def sent_row(index, step, paired=False):
    width, count = index.shape
    index = index.astype(F32).T
    at = lax.broadcasted_iota(jnp.int32, (count, count * step), 1)
    peer = lax.broadcasted_iota(jnp.int32, (count, count * step), 0)
    row = jnp.zeros(at.shape, F32)
    for slot in range(width):
        hit = sent_at(peer, slot, step, paired) == at
        row = jnp.where(hit, index[:, slot : slot + 1] + 1.0, row)
    return jnp.sum(row, axis=0, keepdims=True).astype(jnp.int32) - 1


def stacked(blocks):
    return jnp.concatenate([block()[...] for block in blocks], axis=0)


def split(rows, outs):
    size = rows.shape[0] // len(outs)
    for i, out in enumerate(outs):
        out.ref[...] = rows[i * size : (i + 1) * size, :].astype(BF16)


def send_rows(grid, send):
    index = send()[...]
    one = table(sent_row(index, stride(index.shape[0]), True), grid().shape[0])
    return dot(one.T.astype(BF16), grid()[...])


def send_kernel(grid, send, *outgoing):
    split(send_rows(grid, send), outgoing)


def turn_table(sources, targets, step, j):
    row = lax.broadcasted_iota(jnp.int32, (sources * step, sources * targets * step), 0)
    at = lax.broadcasted_iota(jnp.int32, row.shape, 1)
    source = (row // step * targets + j) * step + row % step
    return jnp.where(at == source, 1.0, 0.0).astype(BF16)


def turn_kernel(blocks, *outs):
    rows = stacked(blocks)
    step = rows.shape[0] // (len(blocks) * len(outs))
    for j, out in enumerate(outs):
        out.ref[...] = dot(turn_table(len(blocks), len(outs), step, j), rows).astype(BF16)


def tables_kernel(mesh, slot, recv_e, halo, sender, recv_p, send, *outs):
    mesh_rows = mesh().shape[0]
    peers = halo().shape[1]
    slot_step, halo_step = outs[0].ref.shape[0] // peers, outs[4].ref.shape[1] // peers
    capacity, halo_capacity = slot_step, halo().shape[0]
    slots = slot()[...]
    coming = arrived_at(slots // capacity, slots % capacity, slot_step, True)
    slots = arrived_at(slots // capacity, slots % capacity, slot_step)
    senders = sender()[...]
    remote = jnp.maximum(senders - mesh_rows, 0)
    remote = arrived_at(remote // halo_capacity, remote % halo_capacity, halo_step)
    senders = jnp.where(senders < mesh_rows, senders, mesh_rows + remote)
    rows = (slots, recv_e()[...], sent_row(halo()[...], halo_step), senders, recv_p()[...])
    for i, row in enumerate(rows):
        scatter, gather = outs[2 * i : 2 * i + 2]
        one = table(row, scatter.ref.shape[0])
        scatter.ref[...] = one.astype(BF16)
        gather.ref[...] = (table(coming, slot_step * peers) if i == 0 else one).T.astype(BF16)
    outs[10].ref[...] = dot(outs[3].ref[...], mesh()[...]).astype(BF16)
    outs[11].ref[...] = table(sent_row(send()[...], slot_step), outs[11].ref.shape[0]).astype(BF16)


def arrived_rows(blocks):
    size = blocks[0]().shape[0]
    rows = [blocks[0]()[...]]
    for t, block in enumerate(blocks[1:]):
        if block().shape[1] == FEATURES:
            rows.append(block()[...])
        else:
            rows.append(block()[t * size : (t + 1) * size, 6 * FEATURES :])
    return jnp.concatenate(rows, axis=0)


def encode_kernel(
    recv_rows, arrived, slot_g, enc_t, mesh, weights, halo_g,
    one_out, slope_e, normed_e, scale_e, slope_n, normed_n, scale_n, *halo_out,
):
    rows_in = arrived_rows(arrived)
    edges = slot_g().shape[0]
    first, second = layers(weights, 0)
    for low in range(0, edges, ROWS):
        rows = pl.ds(low, ROWS)
        sent = dot(slot_g()[rows, :], rows_in).astype(BF16)
        inputs = jnp.concatenate([sent, recv_rows()[rows, :]], axis=1)
        _, slope, normed, rescale = forward(inputs, first, second)
        slope_e.ref[rows, :] = slope
        normed_e.ref[rows, :] = normed
        scale_e.ref[rows, :] = jnp.broadcast_to(rescale, (ROWS, LANES))
    aggregate = dot(enc_t()[...], normed_e.ref[...]).astype(BF16)
    first, second = layers(weights, 1)
    own = mesh()[...]
    normed, slope, rounded, rescale = forward(
        jnp.concatenate([own, aggregate], axis=1), first, second
    )
    one = (own.astype(F32) + normed).astype(BF16)
    one_out.ref[...] = one
    split(dot(halo_g()[...], one), halo_out)
    slope_n.ref[...] = slope
    normed_n.ref[...] = rounded
    scale_n.ref[...] = jnp.broadcast_to(rescale, scale_n.ref.shape)


def process_kernel(
    cotangent_in, one_in, halo, sender_g, proc_g, weights, proc_t, sender_t, two, part, ga, *refs
):
    grad_halo, (slope_p, normed_p, scale_p) = refs[:-3], refs[-3:]
    ga_p = ga.ref
    features = FEATURES
    one = one_in()[...]
    mesh_rows = one.shape[0]
    lookup = jnp.concatenate([one, stacked(halo)], axis=0)
    edges = sender_g().shape[0]
    first, second = layers(weights, 0)
    for low in range(0, edges, ROWS):
        rows = pl.ds(low, ROWS)
        sent = dot(sender_g()[rows, :], lookup).astype(BF16)
        got = dot(proc_g()[rows, :], one).astype(BF16)
        _, slope, normed, rescale = forward(jnp.concatenate([sent, got], axis=1), first, second)
        slope_p[rows, :] = slope
        normed_p[rows, :] = normed
        scale_p[rows, :] = jnp.broadcast_to(rescale, (ROWS, LANES))
    aggregate = dot(proc_t()[...], normed_p[...]).astype(BF16)
    first_n, second_n = layers(weights, 1)
    normed, slope, rounded, rescale = forward(
        jnp.concatenate([one, aggregate], axis=1), first_n, second_n
    )
    two.send((one.astype(F32) + normed).astype(BF16))
    cotangent = cotangent_in()[...].astype(F32)
    g_q = dot(backward_hidden(cotangent, slope, rounded, rescale, second_n), first_n)
    g_msg = g_q[:, features:].astype(BF16)
    for low in range(0, edges, ROWS):
        rows = pl.ds(low, ROWS)
        incoming = dot(proc_g()[rows, :], g_msg)
        ga_p[rows, :] = backward_hidden(
            incoming, slope_p[rows, :], normed_p[rows, :], scale_p[rows, 0:1], second
        )
    by_send = dot(sender_t()[...], ga_p[...]).astype(BF16)
    g_send = dot(by_send, first[:, :features])
    split(g_send[mesh_rows:, :], grad_halo)
    part.ref[...] = cotangent + g_q[:, :features] + g_send[:mesh_rows, :]


def receive_kernel(part, ga, scatter, weights, out):
    by_recv = dot(scatter()[...], ga()[...]).astype(BF16)
    first, _ = layers(weights, 0)
    out.send(part()[...] + dot(by_recv, first[:, FEATURES:]))


def decode_kernel(
    back, halo_t, grad_in, slope_n, normed_n, scale_n, enc_g, slope_e, normed_e, scale_e,
    weights, slot_t, part, ga, *grad_slots
):
    ga_e = ga.ref
    features = FEATURES
    edges = enc_g().shape[0]
    grad_one = grad_in()[...] + dot(halo_t()[...], stacked(back))
    first_n, second_n = layers(weights, 1)
    ga_n = backward_hidden(grad_one, slope_n()[...], normed_n()[...], scale_n()[:, 0:1], second_n)
    g_n = dot(ga_n, first_n)
    part.ref[...] = grad_one + g_n[:, :features]
    g_edge = g_n[:, features:].astype(BF16)
    first, second = layers(weights, 0)
    for low in range(0, edges, ROWS):
        rows = pl.ds(low, ROWS)
        incoming = dot(enc_g()[rows, :], g_edge)
        ga_e[rows, :] = backward_hidden(
            incoming, slope_e()[rows, :], normed_e()[rows, :], scale_e()[rows, 0:1], second
        )
    by_slot = dot(slot_t()[...], ga_e[...]).astype(BF16)
    split(dot(by_slot, first[:, :features]), grad_slots)


def grid_kernel(back, table_in, out):
    out.send(dot(table_in()[...], stacked(back)))


def along(block, shift, paired=False):
    size = lax.axis_size("mp")
    if shift % size == 0:
        return block
    to = [m ^ shift if paired else (m + shift) % size for m in range(size)]
    return lax.ppermute(block, "mp", list(enumerate(to)))


def beside(block, flip):
    if flip == 0:
        return block
    return lax.ppermute(block, "graph", [(g, g ^ flip) for g in range(lax.axis_size("graph"))])


def turn(blocks, count, step):
    out = shape(len(blocks) * step, blocks[0].shape[1], BF16)
    return call(turn_kernel, [out] * count, list(blocks))


def exchange(blocks, step):
    return second_level(first_level(blocks, step, True))


def first_level(blocks, step, paired=False):
    return turn([along(b, s, paired) for s, b in enumerate(blocks)], lax.axis_size("graph"), step)


def second_level(blocks):
    return [beside(b, t) for t, b in enumerate(blocks)]


def exchange_back(blocks, step):
    blocks = turn([beside(b, t) for t, b in enumerate(blocks)], lax.axis_size("mp"), step)
    return [along(b, -s) for s, b in enumerate(blocks)], blocks[0]


def local(
    grid_lat,
    mesh_lat,
    cotangent,
    grid_send,
    g2m_slot,
    g2m_receiver,
    halo_send,
    mesh_sender,
    mesh_receiver,
    *shards,
):
    grid_rows, features = grid_lat.shape
    mesh_rows = mesh_lat.shape[0]
    edges = g2m_slot.shape[0]
    mesh_edges = mesh_sender.shape[0]
    mp, graph = lax.axis_size("mp"), lax.axis_size("graph")
    step, halo_step = stride(grid_send.shape[1]), stride(halo_send.shape[1])
    slots, halos = mp * graph * step, mp * graph * halo_step
    tables = call(
        tables_kernel,
        [
            shape(slots, edges, BF16),
            shape(edges, slots, BF16),
            shape(mesh_rows, edges, BF16),
            shape(edges, mesh_rows, BF16),
            shape(mesh_rows, halos, BF16),
            shape(halos, mesh_rows, BF16),
            shape(mesh_rows + halos, mesh_edges, BF16),
            shape(mesh_edges, mesh_rows + halos, BF16),
            shape(mesh_rows, mesh_edges, BF16),
            shape(mesh_edges, mesh_rows, BF16),
            shape(edges, features, BF16),
            shape(grid_rows, slots, BF16),
        ],
        Far(mesh_lat),
        Far(g2m_slot.reshape(1, edges)),
        Far(g2m_receiver.reshape(1, edges)),
        Far(halo_send.T),
        Far(mesh_sender.reshape(1, mesh_edges)),
        Far(mesh_receiver.reshape(1, mesh_edges)),
        Far(grid_send.T),
    )
    enc, finish, arrived, tables = start(grid_lat, grid_send, shards, tables)
    slot_t, slot_g, enc_t, enc_g, halo_t, halo_g, sender_t, sender_g, proc_t, proc_g = tables[:10]
    recv_rows, grid_t = tables[10:]
    saved = [
        shape(edges, features, BF16),
        shape(edges, features, BF16),
        shape(edges, LANES, F32),
        shape(mesh_rows, features, BF16),
        shape(mesh_rows, features, BF16),
        shape(mesh_rows, LANES, F32),
    ]
    mesh_one, slope_e, normed_e, scale_e, slope_n, normed_n, scale_n, *halo_out = call(
        encode_kernel,
        [shape(mesh_rows, features, BF16)] + saved + [shape(graph * halo_step, features, BF16)] * mp,
        recv_rows,
        arrived,
        slot_g,
        enc_t,
        Far(mesh_lat),
        enc,
        halo_g,
        flops=3 * 10**9,
    )
    moved = first_level(halo_out, halo_step)
    halo_in = second_level(moved)
    proc = finish(mesh_one, moved, halo_in[1:])
    mesh_two, part, ga, *grad_halo = call(
        process_kernel,
        [
            shape(mesh_rows, features, BF16),
            shape(mesh_rows, features, F32),
            shape(mesh_edges, features, BF16),
        ]
        + [shape(mp * halo_step, features, BF16)] * graph,
        Far(cotangent),
        mesh_one,
        halo_in,
        sender_g,
        proc_g,
        proc,
        proc_t,
        sender_t,
        last=(0,),
        flops=5 * 10**9,
        scratch=[
            pltpu.VMEM((mesh_edges, features), BF16),
            pltpu.VMEM((mesh_edges, features), BF16),
            pltpu.VMEM((mesh_edges, LANES), F32),
        ],
    )
    halo_back, half_way = exchange_back(grad_halo, halo_step)
    part, _ = lax.optimization_barrier((part, half_way))
    (grad_one,) = call(
        receive_kernel, [shape(mesh_rows, features, F32)], part, ga, proc_t, proc, flops=3 * 10**8
    )
    part, ga, *grad_slots = call(
        decode_kernel,
        [shape(mesh_rows, features, F32), shape(edges, features, BF16)]
        + [shape(mp * step, features, BF16)] * graph,
        halo_back,
        halo_t,
        grad_one,
        slope_n,
        normed_n,
        scale_n,
        enc_g,
        slope_e,
        normed_e,
        scale_e,
        enc,
        slot_t,
        flops=3 * 10**9,
    )
    returned, half_way = exchange_back(grad_slots, step)
    part, _ = lax.optimization_barrier((part, half_way))
    (mesh_grad,) = call(
        receive_kernel, [shape(mesh_rows, features, F32)], part, ga, enc_t, enc, last=(0,), flops=3 * 10**8
    )
    (grid_grad,) = call(
        grid_kernel, [shape(grid_rows, features, F32)], returned, grid_t, last=(0,)
    )
    return (mesh_two, grid_grad, mesh_grad)


def solution(mesh):
    rows = P(AXES, None)
    flat = P(AXES)
    in_specs = (rows,) * 4 + (flat,) * 2 + (rows,) + (flat,) * 2 + (P(None, "mp"), P("mp", None)) * 4
    return jax.shard_map(
        local, mesh=mesh, in_specs=in_specs, out_specs=(rows,) * 3, check_vma=False
    )
```

```python
import jax
import jax.numpy as jnp
from jax import lax
from jax.experimental import pallas as pl
from jax.experimental.pallas import tpu as pltpu
from jax.sharding import PartitionSpec as P

F32 = jnp.float32
BF16 = jnp.bfloat16
LANES = 128
ROWS = 512
FEATURES = 512
AXES = ("groups", "graph", "mp")


def dot(left, right):
    return jnp.dot(left, right, preferred_element_type=F32)


def dot_trans(left, right):
    return lax.dot_general(left, right, (((1,), (1,)), ((), ())), preferred_element_type=F32)


def shape(rows, columns, dtype):
    return jax.ShapeDtypeStruct((rows, columns), dtype)


class Far:
    def __init__(self, array):
        self.array = pltpu.with_memory_space_constraint(array, pltpu.HBM)


class Input:
    def __init__(self, copy, ref):
        self.copy, self.ref = copy, ref

    def __call__(self):
        if self.copy is not None:
            self.copy.wait()
            self.copy = None
        return self.ref


class Output:
    def __init__(self, ref, copy):
        self.ref, self.copy = ref, copy

    def send(self, value=None):
        if value is not None:
            self.ref[...] = value
        if self.copy is not None:
            self.copy.start()


def call(kernel, out_shape, *args, last=(), scratch=(), flops=0):
    groups = [a if isinstance(a, list) else [a] for a in args]
    flat = [a for group in groups for a in group]
    far = [isinstance(a, Far) for a in flat]
    arrays = [a.array if isinstance(a, Far) else a for a in flat]
    count, outs = len(arrays), len(out_shape)

    def body(*refs):
        ins, refs = refs[:count], refs[count:]
        out_refs, refs = refs[:outs], refs[outs:]
        places, refs = list(refs[: sum(far)]), refs[sum(far) :]
        results, refs = list(refs[: len(last)]), refs[len(last) :]
        sem_in, sem_out, refs = refs[0], refs[1], refs[2:]
        inputs = []
        for ref, away in zip(ins, far):
            copy = None
            if away:
                place = places.pop(0)
                copy = pltpu.make_async_copy(ref, place, sem_in.at[len(places)])
                copy.start()
                ref = place
            inputs.append(Input(copy, ref))
        outputs = []
        for i, ref in enumerate(out_refs):
            copy = None
            if i in last:
                place = results.pop(0)
                copy = pltpu.make_async_copy(place, ref, sem_out.at[len(results)])
                ref = place
            outputs.append(Output(ref, copy))
        given = []
        for arg, group in zip(args, groups):
            part, inputs = inputs[: len(group)], inputs[len(group) :]
            given.append(part if isinstance(arg, list) else part[0])
        kernel(*given, *outputs, *refs)
        for output in outputs:
            if output.copy is not None:
                output.copy.wait()

    vmem, hbm = pl.BlockSpec(memory_space=pltpu.VMEM), pl.BlockSpec(memory_space=pl.ANY)
    total = sum(a.size * a.dtype.itemsize for a in arrays)
    return pl.pallas_call(
        body,
        out_shape=out_shape,
        in_specs=[hbm if away else vmem for away in far],
        out_specs=[hbm if i in last else vmem for i in range(outs)],
        scratch_shapes=[pltpu.VMEM(a.shape, a.dtype) for a, away in zip(arrays, far) if away]
        + [pltpu.VMEM(out_shape[i].shape, out_shape[i].dtype) for i in last]
        + [pltpu.SemaphoreType.DMA((max(sum(far), 1),)), pltpu.SemaphoreType.DMA((max(len(last), 1),))]
        + list(scratch),
        name=kernel.__name__,
        cost_estimate=pl.CostEstimate(flops=flops, bytes_accessed=total, transcendentals=0),
        compiler_params=pltpu.CompilerParams(vmem_limit_bytes=24 * 1024 * 1024),
    )(*arrays)


def layers(blocks, which):
    low = which * 3 * FEATURES
    middle = low + 2 * FEATURES
    return (
        jnp.concatenate([block()[:, low:middle] for block in blocks], axis=0),
        jnp.concatenate([block()[:, middle : middle + FEATURES] for block in blocks], axis=0),
    )


def turned(first, select):
    return dot_trans(select, first).astype(BF16)


def prepare_kernel(grid, send, shards, kept, *messages):
    width = 3 * FEATURES
    outgoing = send_rows(grid, send)
    size = kept.ref.shape[0]
    kept.ref[...] = outgoing[:size, :].astype(BF16)
    for i, out in enumerate(messages):
        out.ref[:, 2 * width :] = outgoing[(i + 1) * size : (i + 2) * size, :].astype(BF16)
    for i in range(2):
        first, second = piece_of(shards[2 * i], shards[2 * i + 1], messages[0].ref.shape[0])
        low = i * width
        for out in messages:
            out.ref[:, low : low + 2 * FEATURES] = first
            out.ref[:, low + 2 * FEATURES : low + width] = second


def piece_of(one, two, rows):
    plane = lax.axis_index("groups") * lax.axis_size("graph") + lax.axis_index("graph")
    base = plane * rows
    hidden = two().shape[0]
    select = jnp.where(
        lax.broadcasted_iota(jnp.int32, (rows, hidden), 0) + base
        == lax.broadcasted_iota(jnp.int32, (rows, hidden), 1),
        1.0,
        0.0,
    ).astype(BF16)
    return turned(one()[...], select), two()[pl.ds(pl.multiple_of(base, rows), rows), :]


def join_kernel(kept, messages, near, block, both):
    width = 6 * FEATURES
    weights = jnp.concatenate([m()[:, :width] for m in messages], axis=0)
    rows = jnp.concatenate([kept()[...]] + [m()[:, width:] for m in messages], axis=0)
    step = rows.shape[0] // 16
    block.ref[...] = weights
    both.ref[:, :width] = weights
    size = near.ref.shape[0]
    for j in range(4):
        moved = dot(turn_table(4, 4, step, j), rows).astype(BF16)
        if j == 0:
            near.ref[...] = moved
        else:
            both.ref[(j - 1) * size : j * size, width:] = moved


def own_kernel(shards, enc_own, proc_own, proc_piece):
    width = 3 * FEATURES
    for i in range(4):
        one, two = shards[2 * i](), shards[2 * i + 1]()
        hidden = one.shape[1]
        select = jnp.where(
            lax.broadcasted_iota(jnp.int32, (hidden, hidden), 0)
            == lax.broadcasted_iota(jnp.int32, (hidden, hidden), 1),
            1.0,
            0.0,
        ).astype(BF16)
        out, low = (enc_own, proc_own)[i // 2], i % 2 * width
        out.ref[:, low : low + 2 * FEATURES] = turned(one[...], select)
        out.ref[:, low + 2 * FEATURES : low + width] = two[...]
    for i in (2, 3):
        first, second = piece_of(shards[2 * i], shards[2 * i + 1], proc_piece.ref.shape[0])
        low = i % 2 * width
        proc_piece.ref[:, low : low + 2 * FEATURES] = first
        proc_piece.ref[:, low + 2 * FEATURES : low + width] = second


def across(x, flip):
    planes = lax.axis_size("groups") * lax.axis_size("graph")
    return lax.ppermute(x, ("groups", "graph"), [(p, p ^ flip) for p in range(planes)])


def start(grid_lat, grid_send, shards, tables):
    grid_rows, features = grid_lat.shape
    mp, graph = lax.axis_size("mp"), lax.axis_size("graph")
    step = stride(grid_send.shape[1])
    sent = [shape(graph * step, features, BF16)] * mp
    planes = lax.axis_size("groups") * graph
    hidden = shards[1].shape[0]
    if planes != 8 or mp != 4 or hidden != 128 or features != FEATURES:
        outgoing = call(send_kernel, sent, Far(grid_lat), Far(grid_send.T))
        rows = []
        for i in range(4):
            rows.append(lax.all_gather(shards[2 * i], "mp", axis=1, tiled=True).T)
            rows.append(lax.all_gather(shards[2 * i + 1], "mp", axis=0, tiled=True))
        enc, proc = jnp.concatenate(rows[:4], axis=1), jnp.concatenate(rows[4:], axis=1)
        arrived = exchange(outgoing, step)
        return [enc], lambda one, moved, came: [proc], arrived, tables
    far = [Far(s) for s in shards]
    piece = hidden // planes
    width = 6 * features
    kept, *messages = call(
        prepare_kernel,
        sent[:1] + [shape(piece, width + features, BF16)] * 3,
        Far(grid_lat),
        Far(grid_send.T),
        far[:4],
    )
    enc_own, proc_own, proc_piece = call(
        own_kernel, [shape(hidden, width, BF16)] * 2 + [shape(piece, width, BF16)], far
    )
    messages = [along(m, i + 1, True) for i, m in enumerate(messages)]
    kept, enc_own, *tables = lax.optimization_barrier((kept, enc_own, *tables))
    rows = mp * step
    near, first, both = call(
        join_kernel,
        [shape(rows, features, BF16), shape(3 * piece, width, BF16), shape(3 * rows, width + features, BF16)],
        kept,
        messages,
    )
    x, y, corner = across(both, 2), across(first, 4), across(first, 6)
    proc_piece, _ = lax.optimization_barrier((proc_piece, near))
    beside_me = lax.ppermute(proc_piece, "mp", [(m, m ^ 1) for m in range(mp)])
    pair = jnp.concatenate([proc_piece, beside_me])
    pairs = lax.ppermute(pair, "mp", [(m, m ^ 2) for m in range(mp)])
    proc_first = jnp.concatenate([beside_me, pairs])
    both, x, y, corner, _ = lax.optimization_barrier((both, x, y, corner, pairs))
    core, x_core, others = across(both, 1), across(x, 1), across(jnp.concatenate([y, corner]), 1)
    enc = [enc_own, first, core, x, y, corner, x_core, others]
    arrived = [near, core, x, x_core]
    proc_first, *_ = lax.optimization_barrier((proc_first, x, y, corner))
    proc_x, proc_y = across(proc_first, 2), across(proc_first, 4)

    def finish(one, moved, came):
        late, _ = lax.optimization_barrier((proc_x, one))
        corner = across(late, 4)
        x, y, *_ = lax.optimization_barrier((proc_x, proc_y, *moved))
        sides = across(jnp.concatenate([x, y]), 1)
        corner, *_ = lax.optimization_barrier((corner, *came))
        return [proc_own, proc_first, across(proc_first, 1), x, y, sides, corner, across(corner, 1)]

    return enc, finish, arrived, tables


def forward(inputs, first, second):
    before = dot_trans(inputs, first)
    logistic = 0.5 + 0.5 * jnp.tanh(0.5 * before)
    wide = before * logistic
    hidden = wide.astype(BF16)
    slope = logistic + wide * (1.0 - logistic)
    summed = dot(hidden, second)
    centered = summed - jnp.mean(summed, axis=-1, keepdims=True)
    rescale = lax.rsqrt(jnp.mean(centered * centered, axis=-1, keepdims=True) + 1e-05)
    normed = centered * rescale
    return normed, slope.astype(BF16), normed.astype(BF16), rescale


def backward_hidden(incoming, slope, normed, rescale, second):
    normed = normed.astype(F32)
    g_out = (
        incoming
        - jnp.mean(incoming, axis=-1, keepdims=True)
        - normed * jnp.mean(incoming * normed, axis=-1, keepdims=True)
    ) * rescale
    return (dot_trans(g_out.astype(BF16), second) * slope.astype(F32)).astype(BF16)


def table(index_row, count):
    n = index_row.shape[1]
    return jnp.where(lax.broadcasted_iota(jnp.int32, (count, n), 0) == index_row, 1.0, 0.0)


def stride(capacity):
    return max(capacity, 16 // min(lax.axis_size("mp"), lax.axis_size("graph")))


def sent_at(peer, slot, step, paired=False):
    mp, graph = lax.axis_size("mp"), lax.axis_size("graph")
    me, other = lax.axis_index("mp"), peer % mp
    shift = other ^ me if paired else (other + mp - me) % mp
    return (shift * graph + (peer // mp ^ lax.axis_index("graph"))) * step + slot


def arrived_at(peer, slot, step, paired=False):
    mp = lax.axis_size("mp")
    me, other = lax.axis_index("mp"), peer % mp
    shift = other ^ me if paired else (me + mp - other) % mp
    return ((peer // mp ^ lax.axis_index("graph")) * mp + shift) * step + slot


def sent_row(index, step, paired=False):
    width, count = index.shape
    index = index.astype(F32).T
    at = lax.broadcasted_iota(jnp.int32, (count, count * step), 1)
    peer = lax.broadcasted_iota(jnp.int32, (count, count * step), 0)
    row = jnp.zeros(at.shape, F32)
    for slot in range(width):
        hit = sent_at(peer, slot, step, paired) == at
        row = jnp.where(hit, index[:, slot : slot + 1] + 1.0, row)
    return jnp.sum(row, axis=0, keepdims=True).astype(jnp.int32) - 1


def stacked(blocks):
    return jnp.concatenate([block()[...] for block in blocks], axis=0)


def split(rows, outs):
    size = rows.shape[0] // len(outs)
    for i, out in enumerate(outs):
        out.ref[...] = rows[i * size : (i + 1) * size, :].astype(BF16)


def send_rows(grid, send):
    index = send()[...]
    one = table(sent_row(index, stride(index.shape[0]), True), grid().shape[0])
    return dot(one.T.astype(BF16), grid()[...])


def send_kernel(grid, send, *outgoing):
    split(send_rows(grid, send), outgoing)


def turn_table(sources, targets, step, j):
    row = lax.broadcasted_iota(jnp.int32, (sources * step, sources * targets * step), 0)
    at = lax.broadcasted_iota(jnp.int32, row.shape, 1)
    source = (row // step * targets + j) * step + row % step
    return jnp.where(at == source, 1.0, 0.0).astype(BF16)


def turn_kernel(blocks, *outs):
    rows = stacked(blocks)
    step = rows.shape[0] // (len(blocks) * len(outs))
    for j, out in enumerate(outs):
        out.ref[...] = dot(turn_table(len(blocks), len(outs), step, j), rows).astype(BF16)


def tables_kernel(mesh, slot, recv_e, halo, sender, recv_p, send, *outs):
    mesh_rows = mesh().shape[0]
    peers = halo().shape[1]
    slot_step, halo_step = outs[0].ref.shape[0] // peers, outs[4].ref.shape[1] // peers
    capacity, halo_capacity = slot_step, halo().shape[0]
    slots = slot()[...]
    coming = arrived_at(slots // capacity, slots % capacity, slot_step, True)
    slots = arrived_at(slots // capacity, slots % capacity, slot_step)
    senders = sender()[...]
    remote = jnp.maximum(senders - mesh_rows, 0)
    remote = arrived_at(remote // halo_capacity, remote % halo_capacity, halo_step)
    senders = jnp.where(senders < mesh_rows, senders, mesh_rows + remote)
    rows = (slots, recv_e()[...], sent_row(halo()[...], halo_step), senders, recv_p()[...])
    for i, row in enumerate(rows):
        scatter, gather = outs[2 * i : 2 * i + 2]
        one = table(row, scatter.ref.shape[0])
        scatter.ref[...] = one.astype(BF16)
        gather.ref[...] = (table(coming, slot_step * peers) if i == 0 else one).T.astype(BF16)
    outs[10].ref[...] = dot(outs[3].ref[...], mesh()[...]).astype(BF16)
    outs[11].ref[...] = table(sent_row(send()[...], slot_step), outs[11].ref.shape[0]).astype(BF16)


def arrived_rows(blocks):
    size = blocks[0]().shape[0]
    rows = [blocks[0]()[...]]
    for t, block in enumerate(blocks[1:]):
        if block().shape[1] == FEATURES:
            rows.append(block()[...])
        else:
            rows.append(block()[t * size : (t + 1) * size, 6 * FEATURES :])
    return jnp.concatenate(rows, axis=0)


def encode_kernel(
    recv_rows, arrived, slot_g, enc_t, mesh, weights, halo_g,
    one_out, slope_e, normed_e, scale_e, slope_n, normed_n, scale_n, *halo_out,
):
    rows_in = arrived_rows(arrived)
    edges = slot_g().shape[0]
    first, second = layers(weights, 0)
    for low in range(0, edges, ROWS):
        rows = pl.ds(low, ROWS)
        sent = dot(slot_g()[rows, :], rows_in).astype(BF16)
        inputs = jnp.concatenate([sent, recv_rows()[rows, :]], axis=1)
        _, slope, normed, rescale = forward(inputs, first, second)
        slope_e.ref[rows, :] = slope
        normed_e.ref[rows, :] = normed
        scale_e.ref[rows, :] = jnp.broadcast_to(rescale, (ROWS, LANES))
    aggregate = dot(enc_t()[...], normed_e.ref[...]).astype(BF16)
    first, second = layers(weights, 1)
    own = mesh()[...]
    normed, slope, rounded, rescale = forward(
        jnp.concatenate([own, aggregate], axis=1), first, second
    )
    one = (own.astype(F32) + normed).astype(BF16)
    one_out.ref[...] = one
    split(dot(halo_g()[...], one), halo_out)
    slope_n.ref[...] = slope
    normed_n.ref[...] = rounded
    scale_n.ref[...] = jnp.broadcast_to(rescale, scale_n.ref.shape)


def process_kernel(
    cotangent_in, one_in, halo, sender_g, proc_g, weights, proc_t, sender_t, two, part, ga, *refs
):
    grad_halo, (slope_p, normed_p, scale_p) = refs[:-3], refs[-3:]
    ga_p = ga.ref
    features = FEATURES
    one = one_in()[...]
    mesh_rows = one.shape[0]
    lookup = jnp.concatenate([one, stacked(halo)], axis=0)
    edges = sender_g().shape[0]
    first, second = layers(weights, 0)
    for low in range(0, edges, ROWS):
        rows = pl.ds(low, ROWS)
        sent = dot(sender_g()[rows, :], lookup).astype(BF16)
        got = dot(proc_g()[rows, :], one).astype(BF16)
        _, slope, normed, rescale = forward(jnp.concatenate([sent, got], axis=1), first, second)
        slope_p[rows, :] = slope
        normed_p[rows, :] = normed
        scale_p[rows, :] = jnp.broadcast_to(rescale, (ROWS, LANES))
    aggregate = dot(proc_t()[...], normed_p[...]).astype(BF16)
    first_n, second_n = layers(weights, 1)
    normed, slope, rounded, rescale = forward(
        jnp.concatenate([one, aggregate], axis=1), first_n, second_n
    )
    two.send((one.astype(F32) + normed).astype(BF16))
    cotangent = cotangent_in()[...].astype(F32)
    g_q = dot(backward_hidden(cotangent, slope, rounded, rescale, second_n), first_n)
    g_msg = g_q[:, features:].astype(BF16)
    for low in range(0, edges, ROWS):
        rows = pl.ds(low, ROWS)
        incoming = dot(proc_g()[rows, :], g_msg)
        ga_p[rows, :] = backward_hidden(
            incoming, slope_p[rows, :], normed_p[rows, :], scale_p[rows, 0:1], second
        )
    by_send = dot(sender_t()[...], ga_p[...]).astype(BF16)
    g_send = dot(by_send, first[:, :features])
    split(g_send[mesh_rows:, :], grad_halo)
    part.ref[...] = cotangent + g_q[:, :features] + g_send[:mesh_rows, :]


def receive_kernel(part, ga, scatter, weights, out):
    by_recv = dot(scatter()[...], ga()[...]).astype(BF16)
    first, _ = layers(weights, 0)
    out.send(part()[...] + dot(by_recv, first[:, FEATURES:]))


def decode_kernel(
    back, halo_t, grad_in, slope_n, normed_n, scale_n, enc_g, slope_e, normed_e, scale_e,
    weights, slot_t, part, ga, *grad_slots
):
    ga_e = ga.ref
    features = FEATURES
    edges = enc_g().shape[0]
    grad_one = grad_in()[...] + dot(halo_t()[...], stacked(back))
    first_n, second_n = layers(weights, 1)
    ga_n = backward_hidden(grad_one, slope_n()[...], normed_n()[...], scale_n()[:, 0:1], second_n)
    g_n = dot(ga_n, first_n)
    part.ref[...] = grad_one + g_n[:, :features]
    g_edge = g_n[:, features:].astype(BF16)
    first, second = layers(weights, 0)
    for low in range(0, edges, ROWS):
        rows = pl.ds(low, ROWS)
        incoming = dot(enc_g()[rows, :], g_edge)
        ga_e[rows, :] = backward_hidden(
            incoming, slope_e()[rows, :], normed_e()[rows, :], scale_e()[rows, 0:1], second
        )
    by_slot = dot(slot_t()[...], ga_e[...]).astype(BF16)
    split(dot(by_slot, first[:, :features]), grad_slots)


def grid_kernel(back, table_in, out):
    out.send(dot(table_in()[...], stacked(back)))


def along(block, shift, paired=False):
    size = lax.axis_size("mp")
    if shift % size == 0:
        return block
    to = [m ^ shift if paired else (m + shift) % size for m in range(size)]
    return lax.ppermute(block, "mp", list(enumerate(to)))


def beside(block, flip):
    if flip == 0:
        return block
    return lax.ppermute(block, "graph", [(g, g ^ flip) for g in range(lax.axis_size("graph"))])


def turn(blocks, count, step):
    out = shape(len(blocks) * step, blocks[0].shape[1], BF16)
    return call(turn_kernel, [out] * count, list(blocks))


def exchange(blocks, step):
    return second_level(first_level(blocks, step, True))


def first_level(blocks, step, paired=False):
    return turn([along(b, s, paired) for s, b in enumerate(blocks)], lax.axis_size("graph"), step)


def second_level(blocks):
    return [beside(b, t) for t, b in enumerate(blocks)]


def exchange_back(blocks, step):
    blocks = turn([beside(b, t) for t, b in enumerate(blocks)], lax.axis_size("mp"), step)
    return [along(b, -s) for s, b in enumerate(blocks)], blocks[0]


def local(
    grid_lat,
    mesh_lat,
    cotangent,
    grid_send,
    g2m_slot,
    g2m_receiver,
    halo_send,
    mesh_sender,
    mesh_receiver,
    *shards,
):
    grid_rows, features = grid_lat.shape
    mesh_rows = mesh_lat.shape[0]
    edges = g2m_slot.shape[0]
    mesh_edges = mesh_sender.shape[0]
    mp, graph = lax.axis_size("mp"), lax.axis_size("graph")
    step, halo_step = stride(grid_send.shape[1]), stride(halo_send.shape[1])
    slots, halos = mp * graph * step, mp * graph * halo_step
    tables = call(
        tables_kernel,
        [
            shape(slots, edges, BF16),
            shape(edges, slots, BF16),
            shape(mesh_rows, edges, BF16),
            shape(edges, mesh_rows, BF16),
            shape(mesh_rows, halos, BF16),
            shape(halos, mesh_rows, BF16),
            shape(mesh_rows + halos, mesh_edges, BF16),
            shape(mesh_edges, mesh_rows + halos, BF16),
            shape(mesh_rows, mesh_edges, BF16),
            shape(mesh_edges, mesh_rows, BF16),
            shape(edges, features, BF16),
            shape(grid_rows, slots, BF16),
        ],
        Far(mesh_lat),
        Far(g2m_slot.reshape(1, edges)),
        Far(g2m_receiver.reshape(1, edges)),
        Far(halo_send.T),
        Far(mesh_sender.reshape(1, mesh_edges)),
        Far(mesh_receiver.reshape(1, mesh_edges)),
        Far(grid_send.T),
    )
    enc, finish, arrived, tables = start(grid_lat, grid_send, shards, tables)
    slot_t, slot_g, enc_t, enc_g, halo_t, halo_g, sender_t, sender_g, proc_t, proc_g = tables[:10]
    recv_rows, grid_t = tables[10:]
    saved = [
        shape(edges, features, BF16),
        shape(edges, features, BF16),
        shape(edges, LANES, F32),
        shape(mesh_rows, features, BF16),
        shape(mesh_rows, features, BF16),
        shape(mesh_rows, LANES, F32),
    ]
    mesh_one, slope_e, normed_e, scale_e, slope_n, normed_n, scale_n, *halo_out = call(
        encode_kernel,
        [shape(mesh_rows, features, BF16)] + saved + [shape(graph * halo_step, features, BF16)] * mp,
        recv_rows,
        arrived,
        slot_g,
        enc_t,
        Far(mesh_lat),
        enc,
        halo_g,
        flops=3 * 10**9,
    )
    moved = first_level(halo_out, halo_step)
    halo_in = second_level(moved)
    proc = finish(mesh_one, moved, halo_in[1:])
    mesh_two, part, ga, *grad_halo = call(
        process_kernel,
        [
            shape(mesh_rows, features, BF16),
            shape(mesh_rows, features, F32),
            shape(mesh_edges, features, BF16),
        ]
        + [shape(mp * halo_step, features, BF16)] * graph,
        Far(cotangent),
        mesh_one,
        halo_in,
        sender_g,
        proc_g,
        proc,
        proc_t,
        sender_t,
        last=(0,),
        flops=5 * 10**9,
        scratch=[
            pltpu.VMEM((mesh_edges, features), BF16),
            pltpu.VMEM((mesh_edges, features), BF16),
            pltpu.VMEM((mesh_edges, LANES), F32),
        ],
    )
    halo_back, half_way = exchange_back(grad_halo, halo_step)
    part, _ = lax.optimization_barrier((part, half_way))
    (grad_one,) = call(
        receive_kernel, [shape(mesh_rows, features, F32)], part, ga, proc_t, proc, flops=3 * 10**8
    )
    part, ga, *grad_slots = call(
        decode_kernel,
        [shape(mesh_rows, features, F32), shape(edges, features, BF16)]
        + [shape(mp * step, features, BF16)] * graph,
        halo_back,
        halo_t,
        grad_one,
        slope_n,
        normed_n,
        scale_n,
        enc_g,
        slope_e,
        normed_e,
        scale_e,
        enc,
        slot_t,
        flops=3 * 10**9,
    )
    returned, half_way = exchange_back(grad_slots, step)
    part, _ = lax.optimization_barrier((part, half_way))
    (mesh_grad,) = call(
        receive_kernel, [shape(mesh_rows, features, F32)], part, ga, enc_t, enc, last=(0,), flops=3 * 10**8
    )
    (grid_grad,) = call(
        grid_kernel, [shape(grid_rows, features, F32)], returned, grid_t, last=(0,)
    )
    return (mesh_two, grid_grad, mesh_grad)


def solution(mesh):
    rows = P(AXES, None)
    flat = P(AXES)
    in_specs = (rows,) * 4 + (flat,) * 2 + (rows,) + (flat,) * 2 + (P(None, "mp"), P("mp", None)) * 4
    return jax.shard_map(
        local, mesh=mesh, in_specs=in_specs, out_specs=(rows,) * 3, check_vma=False
    )
```

```python
import jax
import jax.numpy as jnp
from jax import lax
from jax.experimental import pallas as pl
from jax.experimental.pallas import tpu as pltpu
from jax.sharding import PartitionSpec as P

F32 = jnp.float32
BF16 = jnp.bfloat16
LANES = 128
ROWS = 512
FEATURES = 512
AXES = ("groups", "graph", "mp")


def dot(left, right):
    return jnp.dot(left, right, preferred_element_type=F32)


def dot_trans(left, right):
    return lax.dot_general(left, right, (((1,), (1,)), ((), ())), preferred_element_type=F32)


def shape(rows, columns, dtype):
    return jax.ShapeDtypeStruct((rows, columns), dtype)


class Far:
    def __init__(self, array):
        self.array = pltpu.with_memory_space_constraint(array, pltpu.HBM)


class Input:
    def __init__(self, copy, ref):
        self.copy, self.ref = copy, ref

    def __call__(self):
        if self.copy is not None:
            self.copy.wait()
            self.copy = None
        return self.ref


class Output:
    def __init__(self, ref, copy):
        self.ref, self.copy = ref, copy

    def send(self, value=None):
        if value is not None:
            self.ref[...] = value
        if self.copy is not None:
            self.copy.start()


def call(kernel, out_shape, *args, last=(), scratch=(), flops=0):
    groups = [a if isinstance(a, list) else [a] for a in args]
    flat = [a for group in groups for a in group]
    far = [isinstance(a, Far) for a in flat]
    arrays = [a.array if isinstance(a, Far) else a for a in flat]
    count, outs = len(arrays), len(out_shape)

    def body(*refs):
        ins, refs = refs[:count], refs[count:]
        out_refs, refs = refs[:outs], refs[outs:]
        places, refs = list(refs[: sum(far)]), refs[sum(far) :]
        results, refs = list(refs[: len(last)]), refs[len(last) :]
        sem_in, sem_out, refs = refs[0], refs[1], refs[2:]
        inputs = []
        for ref, away in zip(ins, far):
            copy = None
            if away:
                place = places.pop(0)
                copy = pltpu.make_async_copy(ref, place, sem_in.at[len(places)])
                copy.start()
                ref = place
            inputs.append(Input(copy, ref))
        outputs = []
        for i, ref in enumerate(out_refs):
            copy = None
            if i in last:
                place = results.pop(0)
                copy = pltpu.make_async_copy(place, ref, sem_out.at[len(results)])
                ref = place
            outputs.append(Output(ref, copy))
        given = []
        for arg, group in zip(args, groups):
            part, inputs = inputs[: len(group)], inputs[len(group) :]
            given.append(part if isinstance(arg, list) else part[0])
        kernel(*given, *outputs, *refs)
        for output in outputs:
            if output.copy is not None:
                output.copy.wait()

    vmem, hbm = pl.BlockSpec(memory_space=pltpu.VMEM), pl.BlockSpec(memory_space=pl.ANY)
    total = sum(a.size * a.dtype.itemsize for a in arrays)
    return pl.pallas_call(
        body,
        out_shape=out_shape,
        in_specs=[hbm if away else vmem for away in far],
        out_specs=[hbm if i in last else vmem for i in range(outs)],
        scratch_shapes=[pltpu.VMEM(a.shape, a.dtype) for a, away in zip(arrays, far) if away]
        + [pltpu.VMEM(out_shape[i].shape, out_shape[i].dtype) for i in last]
        + [pltpu.SemaphoreType.DMA((max(sum(far), 1),)), pltpu.SemaphoreType.DMA((max(len(last), 1),))]
        + list(scratch),
        name=kernel.__name__,
        cost_estimate=pl.CostEstimate(flops=flops, bytes_accessed=total, transcendentals=0),
        compiler_params=pltpu.CompilerParams(vmem_limit_bytes=24 * 1024 * 1024),
    )(*arrays)


def layers(blocks, which):
    low = which * 3 * FEATURES
    middle = low + 2 * FEATURES
    return (
        jnp.concatenate([block()[:, low:middle] for block in blocks], axis=0),
        jnp.concatenate([block()[:, middle : middle + FEATURES] for block in blocks], axis=0),
    )


def turned(first, select):
    return dot_trans(select, first).astype(BF16)


def prepare_kernel(grid, send, shards, kept, *messages):
    width = 3 * FEATURES
    outgoing = send_rows(grid, send)
    size = kept.ref.shape[0]
    kept.ref[...] = outgoing[:size, :].astype(BF16)
    for i, out in enumerate(messages):
        out.ref[:, 2 * width :] = outgoing[(i + 1) * size : (i + 2) * size, :].astype(BF16)
    for i in range(2):
        first, second = piece_of(shards[2 * i], shards[2 * i + 1], messages[0].ref.shape[0])
        low = i * width
        for out in messages:
            out.ref[:, low : low + 2 * FEATURES] = first
            out.ref[:, low + 2 * FEATURES : low + width] = second


def piece_of(one, two, rows):
    plane = lax.axis_index("groups") * lax.axis_size("graph") + lax.axis_index("graph")
    base = plane * rows
    hidden = two().shape[0]
    select = jnp.where(
        lax.broadcasted_iota(jnp.int32, (rows, hidden), 0) + base
        == lax.broadcasted_iota(jnp.int32, (rows, hidden), 1),
        1.0,
        0.0,
    ).astype(BF16)
    return turned(one()[...], select), two()[pl.ds(pl.multiple_of(base, rows), rows), :]


def join_kernel(kept, messages, near, block, both):
    width = 6 * FEATURES
    weights = jnp.concatenate([m()[:, :width] for m in messages], axis=0)
    rows = jnp.concatenate([kept()[...]] + [m()[:, width:] for m in messages], axis=0)
    step = rows.shape[0] // 16
    block.ref[...] = weights
    both.ref[:, :width] = weights
    size = near.ref.shape[0]
    for j in range(4):
        moved = dot(turn_table(4, 4, step, j), rows).astype(BF16)
        if j == 0:
            near.ref[...] = moved
        else:
            both.ref[(j - 1) * size : j * size, width:] = moved


def own_kernel(shards, enc_own, proc_own, proc_piece):
    width = 3 * FEATURES
    for i in range(4):
        one, two = shards[2 * i](), shards[2 * i + 1]()
        hidden = one.shape[1]
        select = jnp.where(
            lax.broadcasted_iota(jnp.int32, (hidden, hidden), 0)
            == lax.broadcasted_iota(jnp.int32, (hidden, hidden), 1),
            1.0,
            0.0,
        ).astype(BF16)
        out, low = (enc_own, proc_own)[i // 2], i % 2 * width
        out.ref[:, low : low + 2 * FEATURES] = turned(one[...], select)
        out.ref[:, low + 2 * FEATURES : low + width] = two[...]
    for i in (2, 3):
        first, second = piece_of(shards[2 * i], shards[2 * i + 1], proc_piece.ref.shape[0])
        low = i % 2 * width
        proc_piece.ref[:, low : low + 2 * FEATURES] = first
        proc_piece.ref[:, low + 2 * FEATURES : low + width] = second


def across(x, flip):
    planes = lax.axis_size("groups") * lax.axis_size("graph")
    return lax.ppermute(x, ("groups", "graph"), [(p, p ^ flip) for p in range(planes)])


def start(grid_lat, grid_send, shards, tables):
    grid_rows, features = grid_lat.shape
    mp, graph = lax.axis_size("mp"), lax.axis_size("graph")
    step = stride(grid_send.shape[1])
    sent = [shape(graph * step, features, BF16)] * mp
    planes = lax.axis_size("groups") * graph
    hidden = shards[1].shape[0]
    if planes != 8 or mp != 4 or hidden != 128 or features != FEATURES:
        outgoing = call(send_kernel, sent, Far(grid_lat), Far(grid_send.T))
        rows = []
        for i in range(4):
            rows.append(lax.all_gather(shards[2 * i], "mp", axis=1, tiled=True).T)
            rows.append(lax.all_gather(shards[2 * i + 1], "mp", axis=0, tiled=True))
        enc, proc = jnp.concatenate(rows[:4], axis=1), jnp.concatenate(rows[4:], axis=1)
        arrived = exchange(outgoing, step)
        return [enc], lambda one, moved, came: [proc], arrived, tables
    far = [Far(s) for s in shards]
    piece = hidden // planes
    width = 6 * features
    kept, *messages = call(
        prepare_kernel,
        sent[:1] + [shape(piece, width + features, BF16)] * 3,
        Far(grid_lat),
        Far(grid_send.T),
        far[:4],
    )
    enc_own, proc_own, proc_piece = call(
        own_kernel, [shape(hidden, width, BF16)] * 2 + [shape(piece, width, BF16)], far
    )
    messages = [along(m, i + 1, True) for i, m in enumerate(messages)]
    kept, enc_own, *tables = lax.optimization_barrier((kept, enc_own, *tables))
    rows = mp * step
    near, first, both = call(
        join_kernel,
        [shape(rows, features, BF16), shape(3 * piece, width, BF16), shape(3 * rows, width + features, BF16)],
        kept,
        messages,
    )
    x, y, corner = across(both, 2), across(first, 4), across(first, 6)
    proc_piece, _ = lax.optimization_barrier((proc_piece, near))
    beside_me = lax.ppermute(proc_piece, "mp", [(m, m ^ 1) for m in range(mp)])
    pair = jnp.concatenate([proc_piece, beside_me])
    pairs = lax.ppermute(pair, "mp", [(m, m ^ 2) for m in range(mp)])
    proc_first = jnp.concatenate([beside_me, pairs])
    both, x, y, corner, _ = lax.optimization_barrier((both, x, y, corner, pairs))
    core, x_core, others = across(both, 1), across(x, 1), across(jnp.concatenate([y, corner]), 1)
    enc = [enc_own, first, core, x, y, corner, x_core, others]
    arrived = [near, core, x, x_core]
    proc_first, *_ = lax.optimization_barrier((proc_first, x, y, corner))
    proc_x, proc_y = across(proc_first, 2), across(proc_first, 4)

    def finish(one, moved, came):
        late, _ = lax.optimization_barrier((proc_x, one))
        corner = across(late, 4)
        x, y, *_ = lax.optimization_barrier((proc_x, proc_y, *moved))
        sides = across(jnp.concatenate([x, y]), 1)
        corner, *_ = lax.optimization_barrier((corner, *came))
        return [proc_own, proc_first, across(proc_first, 1), x, y, sides, corner, across(corner, 1)]

    return enc, finish, arrived, tables


def forward(inputs, first, second):
    before = dot_trans(inputs, first)
    logistic = 0.5 + 0.5 * jnp.tanh(0.5 * before)
    wide = before * logistic
    hidden = wide.astype(BF16)
    slope = logistic + wide * (1.0 - logistic)
    summed = dot(hidden, second)
    centered = summed - jnp.mean(summed, axis=-1, keepdims=True)
    rescale = lax.rsqrt(jnp.mean(centered * centered, axis=-1, keepdims=True) + 1e-05)
    normed = centered * rescale
    return normed, slope.astype(BF16), normed.astype(BF16), rescale


def backward_hidden(incoming, slope, normed, rescale, second):
    normed = normed.astype(F32)
    g_out = (
        incoming
        - jnp.mean(incoming, axis=-1, keepdims=True)
        - normed * jnp.mean(incoming * normed, axis=-1, keepdims=True)
    ) * rescale
    return (dot_trans(g_out.astype(BF16), second) * slope.astype(F32)).astype(BF16)


def table(index_row, count):
    n = index_row.shape[1]
    return jnp.where(lax.broadcasted_iota(jnp.int32, (count, n), 0) == index_row, 1.0, 0.0)


def stride(capacity):
    return max(capacity, 16 // min(lax.axis_size("mp"), lax.axis_size("graph")))


def sent_at(peer, slot, step, paired=False):
    mp, graph = lax.axis_size("mp"), lax.axis_size("graph")
    me, other = lax.axis_index("mp"), peer % mp
    shift = other ^ me if paired else (other + mp - me) % mp
    return (shift * graph + (peer // mp ^ lax.axis_index("graph"))) * step + slot


def arrived_at(peer, slot, step, paired=False):
    mp = lax.axis_size("mp")
    me, other = lax.axis_index("mp"), peer % mp
    shift = other ^ me if paired else (me + mp - other) % mp
    return ((peer // mp ^ lax.axis_index("graph")) * mp + shift) * step + slot


def sent_row(index, step, paired=False, order=sent_at):
    width, count = index.shape
    index = index.astype(F32).T
    at = lax.broadcasted_iota(jnp.int32, (count, count * step), 1)
    peer = lax.broadcasted_iota(jnp.int32, (count, count * step), 0)
    row = jnp.zeros(at.shape, F32)
    for slot in range(width):
        hit = order(peer, slot, step, paired) == at
        row = jnp.where(hit, index[:, slot : slot + 1] + 1.0, row)
    return jnp.sum(row, axis=0, keepdims=True).astype(jnp.int32) - 1


def stacked(blocks):
    return jnp.concatenate([block()[...] for block in blocks], axis=0)


def split(rows, outs):
    size = rows.shape[0] // len(outs)
    for i, out in enumerate(outs):
        out.ref[...] = rows[i * size : (i + 1) * size, :].astype(BF16)


def send_rows(grid, send):
    index = send()[...]
    one = table(sent_row(index, stride(index.shape[0]), True), grid().shape[0])
    return dot(one.T.astype(BF16), grid()[...])


def send_kernel(grid, send, *outgoing):
    split(send_rows(grid, send), outgoing)


def turn_table(sources, targets, step, j):
    row = lax.broadcasted_iota(jnp.int32, (sources * step, sources * targets * step), 0)
    at = lax.broadcasted_iota(jnp.int32, row.shape, 1)
    source = (row // step * targets + j) * step + row % step
    return jnp.where(at == source, 1.0, 0.0).astype(BF16)


def turn_kernel(blocks, *outs):
    rows = stacked(blocks)
    step = rows.shape[0] // (len(blocks) * len(outs))
    for j, out in enumerate(outs):
        out.ref[...] = dot(turn_table(len(blocks), len(outs), step, j), rows).astype(BF16)


def tables_kernel(mesh, slot, recv_e, halo, sender, recv_p, send, *outs):
    mesh_rows = mesh().shape[0]
    peers = halo().shape[1]
    slot_step, halo_step = outs[0].ref.shape[0] // peers, outs[4].ref.shape[1] // peers
    capacity, halo_capacity = slot_step, halo().shape[0]
    slots = slot()[...]
    coming = arrived_at(slots // capacity, slots % capacity, slot_step, True)
    slots = sent_at(slots // capacity, slots % capacity, slot_step)
    senders = sender()[...]
    remote = jnp.maximum(senders - mesh_rows, 0)
    own, peer, place = senders < mesh_rows, remote // halo_capacity, remote % halo_capacity
    back = jnp.where(own, senders, mesh_rows + sent_at(peer, place, halo_step))
    senders = jnp.where(own, senders, mesh_rows + arrived_at(peer, place, halo_step))
    halo_back = sent_row(halo()[...], halo_step, order=arrived_at)
    halo_rows = sent_row(halo()[...], halo_step)
    rows = (slots, recv_e()[...], halo_back, back, recv_p()[...])
    gathered = (coming, rows[1], halo_rows, senders, rows[4])
    for i, row in enumerate(rows):
        scatter, gather = outs[2 * i : 2 * i + 2]
        count = scatter.ref.shape[0]
        one = table(row, count)
        scatter.ref[...] = one.astype(BF16)
        other = one if gathered[i] is row else table(gathered[i], count)
        gather.ref[...] = other.T.astype(BF16)
    outs[10].ref[...] = dot(outs[3].ref[...], mesh()[...]).astype(BF16)
    returned = sent_row(send()[...], slot_step, order=arrived_at)
    outs[11].ref[...] = table(returned, outs[11].ref.shape[0]).astype(BF16)


def arrived_rows(blocks):
    size = blocks[0]().shape[0]
    rows = [blocks[0]()[...]]
    for t, block in enumerate(blocks[1:]):
        if block().shape[1] == FEATURES:
            rows.append(block()[...])
        else:
            rows.append(block()[t * size : (t + 1) * size, 6 * FEATURES :])
    return jnp.concatenate(rows, axis=0)


def encode_kernel(
    recv_rows, arrived, slot_g, enc_t, mesh, weights, halo_g,
    one_out, slope_e, normed_e, scale_e, slope_n, normed_n, scale_n, *halo_out,
):
    rows_in = arrived_rows(arrived)
    edges = slot_g().shape[0]
    first, second = layers(weights, 0)
    for low in range(0, edges, ROWS):
        rows = pl.ds(low, ROWS)
        sent = dot(slot_g()[rows, :], rows_in).astype(BF16)
        inputs = jnp.concatenate([sent, recv_rows()[rows, :]], axis=1)
        _, slope, normed, rescale = forward(inputs, first, second)
        slope_e.ref[rows, :] = slope
        normed_e.ref[rows, :] = normed
        scale_e.ref[rows, :] = jnp.broadcast_to(rescale, (ROWS, LANES))
    aggregate = dot(enc_t()[...], normed_e.ref[...]).astype(BF16)
    first, second = layers(weights, 1)
    own = mesh()[...]
    normed, slope, rounded, rescale = forward(
        jnp.concatenate([own, aggregate], axis=1), first, second
    )
    one = (own.astype(F32) + normed).astype(BF16)
    one_out.ref[...] = one
    split(dot(halo_g()[...], one), halo_out)
    slope_n.ref[...] = slope
    normed_n.ref[...] = rounded
    scale_n.ref[...] = jnp.broadcast_to(rescale, scale_n.ref.shape)


def process_kernel(
    cotangent_in, one_in, halo, sender_g, proc_g, weights, proc_t, sender_t, two, part, ga, *refs
):
    grad_halo, (slope_p, normed_p, scale_p) = refs[:-3], refs[-3:]
    ga_p = ga.ref
    features = FEATURES
    one = one_in()[...]
    mesh_rows = one.shape[0]
    lookup = jnp.concatenate([one, stacked(halo)], axis=0)
    edges = sender_g().shape[0]
    first, second = layers(weights, 0)
    for low in range(0, edges, ROWS):
        rows = pl.ds(low, ROWS)
        sent = dot(sender_g()[rows, :], lookup).astype(BF16)
        got = dot(proc_g()[rows, :], one).astype(BF16)
        _, slope, normed, rescale = forward(jnp.concatenate([sent, got], axis=1), first, second)
        slope_p[rows, :] = slope
        normed_p[rows, :] = normed
        scale_p[rows, :] = jnp.broadcast_to(rescale, (ROWS, LANES))
    aggregate = dot(proc_t()[...], normed_p[...]).astype(BF16)
    first_n, second_n = layers(weights, 1)
    normed, slope, rounded, rescale = forward(
        jnp.concatenate([one, aggregate], axis=1), first_n, second_n
    )
    two.send((one.astype(F32) + normed).astype(BF16))
    cotangent = cotangent_in()[...].astype(F32)
    g_q = dot(backward_hidden(cotangent, slope, rounded, rescale, second_n), first_n)
    g_msg = g_q[:, features:].astype(BF16)
    for low in range(0, edges, ROWS):
        rows = pl.ds(low, ROWS)
        incoming = dot(proc_g()[rows, :], g_msg)
        ga_p[rows, :] = backward_hidden(
            incoming, slope_p[rows, :], normed_p[rows, :], scale_p[rows, 0:1], second
        )
    by_send = dot(sender_t()[...], ga_p[...]).astype(BF16)
    g_send = dot(by_send, first[:, :features])
    split(g_send[mesh_rows:, :], grad_halo)
    part.ref[...] = cotangent + g_q[:, :features] + g_send[:mesh_rows, :]


def receive_kernel(part, ga, scatter, weights, out):
    by_recv = dot(scatter()[...], ga()[...]).astype(BF16)
    first, _ = layers(weights, 0)
    out.send(part()[...] + dot(by_recv, first[:, FEATURES:]))


def decode_kernel(
    back, halo_t, grad_in, slope_n, normed_n, scale_n, enc_g, slope_e, normed_e, scale_e,
    weights, slot_t, part, ga, *grad_slots
):
    ga_e = ga.ref
    features = FEATURES
    edges = enc_g().shape[0]
    grad_one = grad_in()[...] + dot(halo_t()[...], stacked(back))
    first_n, second_n = layers(weights, 1)
    ga_n = backward_hidden(grad_one, slope_n()[...], normed_n()[...], scale_n()[:, 0:1], second_n)
    g_n = dot(ga_n, first_n)
    part.ref[...] = grad_one + g_n[:, :features]
    g_edge = g_n[:, features:].astype(BF16)
    first, second = layers(weights, 0)
    for low in range(0, edges, ROWS):
        rows = pl.ds(low, ROWS)
        incoming = dot(enc_g()[rows, :], g_edge)
        ga_e[rows, :] = backward_hidden(
            incoming, slope_e()[rows, :], normed_e()[rows, :], scale_e()[rows, 0:1], second
        )
    by_slot = dot(slot_t()[...], ga_e[...]).astype(BF16)
    split(dot(by_slot, first[:, :features]), grad_slots)


def grid_kernel(back, table_in, out):
    out.send(dot(table_in()[...], stacked(back)))


def along(block, shift, paired=False):
    size = lax.axis_size("mp")
    if shift % size == 0:
        return block
    to = [m ^ shift if paired else (m + shift) % size for m in range(size)]
    return lax.ppermute(block, "mp", list(enumerate(to)))


def beside(block, flip):
    if flip == 0:
        return block
    return lax.ppermute(block, "graph", [(g, g ^ flip) for g in range(lax.axis_size("graph"))])


def turn(blocks, count, step):
    out = shape(len(blocks) * step, blocks[0].shape[1], BF16)
    return call(turn_kernel, [out] * count, list(blocks))


def exchange(blocks, step):
    return second_level(first_level(blocks, step, True))


def first_level(blocks, step, paired=False):
    return turn([along(b, s, paired) for s, b in enumerate(blocks)], lax.axis_size("graph"), step)


def second_level(blocks):
    return [beside(b, t) for t, b in enumerate(blocks)]


def exchange_back(blocks, step):
    moved = first_level(blocks, step)
    return second_level(moved), moved[0]


def local(
    grid_lat,
    mesh_lat,
    cotangent,
    grid_send,
    g2m_slot,
    g2m_receiver,
    halo_send,
    mesh_sender,
    mesh_receiver,
    *shards,
):
    grid_rows, features = grid_lat.shape
    mesh_rows = mesh_lat.shape[0]
    edges = g2m_slot.shape[0]
    mesh_edges = mesh_sender.shape[0]
    mp, graph = lax.axis_size("mp"), lax.axis_size("graph")
    step, halo_step = stride(grid_send.shape[1]), stride(halo_send.shape[1])
    slots, halos = mp * graph * step, mp * graph * halo_step
    tables = call(
        tables_kernel,
        [
            shape(slots, edges, BF16),
            shape(edges, slots, BF16),
            shape(mesh_rows, edges, BF16),
            shape(edges, mesh_rows, BF16),
            shape(mesh_rows, halos, BF16),
            shape(halos, mesh_rows, BF16),
            shape(mesh_rows + halos, mesh_edges, BF16),
            shape(mesh_edges, mesh_rows + halos, BF16),
            shape(mesh_rows, mesh_edges, BF16),
            shape(mesh_edges, mesh_rows, BF16),
            shape(edges, features, BF16),
            shape(grid_rows, slots, BF16),
        ],
        Far(mesh_lat),
        Far(g2m_slot.reshape(1, edges)),
        Far(g2m_receiver.reshape(1, edges)),
        Far(halo_send.T),
        Far(mesh_sender.reshape(1, mesh_edges)),
        Far(mesh_receiver.reshape(1, mesh_edges)),
        Far(grid_send.T),
    )
    enc, finish, arrived, tables = start(grid_lat, grid_send, shards, tables)
    slot_t, slot_g, enc_t, enc_g, halo_t, halo_g, sender_t, sender_g, proc_t, proc_g = tables[:10]
    recv_rows, grid_t = tables[10:]
    saved = [
        shape(edges, features, BF16),
        shape(edges, features, BF16),
        shape(edges, LANES, F32),
        shape(mesh_rows, features, BF16),
        shape(mesh_rows, features, BF16),
        shape(mesh_rows, LANES, F32),
    ]
    mesh_one, slope_e, normed_e, scale_e, slope_n, normed_n, scale_n, *halo_out = call(
        encode_kernel,
        [shape(mesh_rows, features, BF16)] + saved + [shape(graph * halo_step, features, BF16)] * mp,
        recv_rows,
        arrived,
        slot_g,
        enc_t,
        Far(mesh_lat),
        enc,
        halo_g,
        flops=3 * 10**9,
    )
    moved = first_level(halo_out, halo_step)
    halo_in = second_level(moved)
    proc = finish(mesh_one, moved, halo_in[1:])
    mesh_two, part, ga, *grad_halo = call(
        process_kernel,
        [
            shape(mesh_rows, features, BF16),
            shape(mesh_rows, features, F32),
            shape(mesh_edges, features, BF16),
        ]
        + [shape(graph * halo_step, features, BF16)] * mp,
        Far(cotangent),
        mesh_one,
        halo_in,
        sender_g,
        proc_g,
        proc,
        proc_t,
        sender_t,
        last=(0,),
        flops=5 * 10**9,
        scratch=[
            pltpu.VMEM((mesh_edges, features), BF16),
            pltpu.VMEM((mesh_edges, features), BF16),
            pltpu.VMEM((mesh_edges, LANES), F32),
        ],
    )
    halo_back, half_way = exchange_back(grad_halo, halo_step)
    part, _ = lax.optimization_barrier((part, half_way))
    (grad_one,) = call(
        receive_kernel, [shape(mesh_rows, features, F32)], part, ga, proc_t, proc, flops=3 * 10**8
    )
    part, ga, *grad_slots = call(
        decode_kernel,
        [shape(mesh_rows, features, F32), shape(edges, features, BF16)]
        + [shape(graph * step, features, BF16)] * mp,
        halo_back,
        halo_t,
        grad_one,
        slope_n,
        normed_n,
        scale_n,
        enc_g,
        slope_e,
        normed_e,
        scale_e,
        enc,
        slot_t,
        flops=3 * 10**9,
    )
    returned, half_way = exchange_back(grad_slots, step)
    part, _ = lax.optimization_barrier((part, half_way))
    (mesh_grad,) = call(
        receive_kernel, [shape(mesh_rows, features, F32)], part, ga, enc_t, enc, last=(0,), flops=3 * 10**8
    )
    (grid_grad,) = call(
        grid_kernel, [shape(grid_rows, features, F32)], returned, grid_t, last=(0,)
    )
    return (mesh_two, grid_grad, mesh_grad)


def solution(mesh):
    rows = P(AXES, None)
    flat = P(AXES)
    in_specs = (rows,) * 4 + (flat,) * 2 + (rows,) + (flat,) * 2 + (P(None, "mp"), P("mp", None)) * 4
    return jax.shard_map(
        local, mesh=mesh, in_specs=in_specs, out_specs=(rows,) * 3, check_vma=False
    )
```

```python
import jax
import jax.numpy as jnp
from jax import lax
from jax.experimental import pallas as pl
from jax.experimental.pallas import tpu as pltpu
from jax.sharding import PartitionSpec as P

F32 = jnp.float32
BF16 = jnp.bfloat16
LANES = 128
ROWS = 512
FEATURES = 512
AXES = ("groups", "graph", "mp")


def dot(left, right):
    return jnp.dot(left, right, preferred_element_type=F32)


def dot_trans(left, right):
    return lax.dot_general(left, right, (((1,), (1,)), ((), ())), preferred_element_type=F32)


def shape(rows, columns, dtype):
    return jax.ShapeDtypeStruct((rows, columns), dtype)


class Far:
    def __init__(self, array):
        self.array = pltpu.with_memory_space_constraint(array, pltpu.HBM)


class Input:
    def __init__(self, copy, ref):
        self.copy, self.ref = copy, ref

    def __call__(self):
        if self.copy is not None:
            self.copy.wait()
            self.copy = None
        return self.ref


class Output:
    def __init__(self, ref, copy, part=None):
        self.ref, self.copy, self.part = ref, copy, part

    def send_part(self, low, value):
        rows = value.shape[0]
        self.ref[pl.ds(low, rows), :] = value
        self.part(low, rows).start()

    def send(self, value=None):
        if value is not None:
            self.ref[...] = value
        if self.copy is not None:
            self.copy.start()


def call(kernel, out_shape, *args, last=(), scratch=(), flops=0):
    groups = [a if isinstance(a, list) else [a] for a in args]
    flat = [a for group in groups for a in group]
    far = [isinstance(a, Far) for a in flat]
    arrays = [a.array if isinstance(a, Far) else a for a in flat]
    count, outs = len(arrays), len(out_shape)

    def body(*refs):
        ins, refs = refs[:count], refs[count:]
        out_refs, refs = refs[:outs], refs[outs:]
        places, refs = list(refs[: sum(far)]), refs[sum(far) :]
        results, refs = list(refs[: len(last)]), refs[len(last) :]
        sem_in, sem_out, refs = refs[0], refs[1], refs[2:]
        inputs = []
        for ref, away in zip(ins, far):
            copy = None
            if away:
                place = places.pop(0)
                copy = pltpu.make_async_copy(ref, place, sem_in.at[len(places)])
                copy.start()
                ref = place
            inputs.append(Input(copy, ref))
        outputs = []
        for i, ref in enumerate(out_refs):
            copy = part = None
            if i in last:
                place = results.pop(0)
                sem = sem_out.at[len(results)]
                copy = pltpu.make_async_copy(place, ref, sem)

                def part(low, rows, place=place, ref=ref, sem=sem):
                    at = pl.ds(low, rows)
                    return pltpu.make_async_copy(place.at[at, :], ref.at[at, :], sem)

                ref = place
            outputs.append(Output(ref, copy, part))
        given = []
        for arg, group in zip(args, groups):
            part, inputs = inputs[: len(group)], inputs[len(group) :]
            given.append(part if isinstance(arg, list) else part[0])
        kernel(*given, *outputs, *refs)
        for output in outputs:
            if output.copy is not None:
                output.copy.wait()

    vmem, hbm = pl.BlockSpec(memory_space=pltpu.VMEM), pl.BlockSpec(memory_space=pl.ANY)
    total = sum(a.size * a.dtype.itemsize for a in arrays)
    return pl.pallas_call(
        body,
        out_shape=out_shape,
        in_specs=[hbm if away else vmem for away in far],
        out_specs=[hbm if i in last else vmem for i in range(outs)],
        scratch_shapes=[pltpu.VMEM(a.shape, a.dtype) for a, away in zip(arrays, far) if away]
        + [pltpu.VMEM(out_shape[i].shape, out_shape[i].dtype) for i in last]
        + [pltpu.SemaphoreType.DMA((max(sum(far), 1),)), pltpu.SemaphoreType.DMA((max(len(last), 1),))]
        + list(scratch),
        name=kernel.__name__,
        cost_estimate=pl.CostEstimate(flops=flops, bytes_accessed=total, transcendentals=0),
        compiler_params=pltpu.CompilerParams(vmem_limit_bytes=24 * 1024 * 1024),
    )(*arrays)


def layers(blocks, which):
    low = which * 3 * FEATURES
    middle = low + 2 * FEATURES
    return (
        jnp.concatenate([block()[:, low:middle] for block in blocks], axis=0),
        jnp.concatenate([block()[:, middle : middle + FEATURES] for block in blocks], axis=0),
    )


def turned(first, select):
    return dot_trans(select, first).astype(BF16)


def prepare_kernel(grid, send, shards, kept, *messages):
    width = 3 * FEATURES
    outgoing = send_rows(grid, send)
    size = kept.ref.shape[0]
    kept.ref[...] = outgoing[:size, :].astype(BF16)
    for i, out in enumerate(messages):
        out.ref[:, 2 * width :] = outgoing[(i + 1) * size : (i + 2) * size, :].astype(BF16)
    for i in range(2):
        first, second = piece_of(shards[2 * i], shards[2 * i + 1], messages[0].ref.shape[0])
        low = i * width
        for out in messages:
            out.ref[:, low : low + 2 * FEATURES] = first
            out.ref[:, low + 2 * FEATURES : low + width] = second


def piece_of(one, two, rows):
    plane = lax.axis_index("groups") * lax.axis_size("graph") + lax.axis_index("graph")
    base = plane * rows
    hidden = two().shape[0]
    select = jnp.where(
        lax.broadcasted_iota(jnp.int32, (rows, hidden), 0) + base
        == lax.broadcasted_iota(jnp.int32, (rows, hidden), 1),
        1.0,
        0.0,
    ).astype(BF16)
    return turned(one()[...], select), two()[pl.ds(pl.multiple_of(base, rows), rows), :]


def join_kernel(kept, messages, near, block, both):
    width = 6 * FEATURES
    weights = jnp.concatenate([m()[:, :width] for m in messages], axis=0)
    rows = jnp.concatenate([kept()[...]] + [m()[:, width:] for m in messages], axis=0)
    step = rows.shape[0] // 16
    block.ref[...] = weights
    both.ref[:, :width] = weights
    size = near.ref.shape[0]
    for j in range(4):
        moved = dot(turn_table(4, 4, step, j), rows).astype(BF16)
        if j == 0:
            near.ref[...] = moved
        else:
            both.ref[(j - 1) * size : j * size, width:] = moved


def own_kernel(shards, enc_own, proc_own, proc_piece):
    width = 3 * FEATURES
    for i in range(4):
        one, two = shards[2 * i](), shards[2 * i + 1]()
        hidden = one.shape[1]
        select = jnp.where(
            lax.broadcasted_iota(jnp.int32, (hidden, hidden), 0)
            == lax.broadcasted_iota(jnp.int32, (hidden, hidden), 1),
            1.0,
            0.0,
        ).astype(BF16)
        out, low = (enc_own, proc_own)[i // 2], i % 2 * width
        out.ref[:, low : low + 2 * FEATURES] = turned(one[...], select)
        out.ref[:, low + 2 * FEATURES : low + width] = two[...]
    for i in (2, 3):
        first, second = piece_of(shards[2 * i], shards[2 * i + 1], proc_piece.ref.shape[0])
        low = i % 2 * width
        proc_piece.ref[:, low : low + 2 * FEATURES] = first
        proc_piece.ref[:, low + 2 * FEATURES : low + width] = second


def across(x, flip):
    planes = lax.axis_size("groups") * lax.axis_size("graph")
    return lax.ppermute(x, ("groups", "graph"), [(p, p ^ flip) for p in range(planes)])


def start(grid_lat, grid_send, shards, tables):
    grid_rows, features = grid_lat.shape
    mp, graph = lax.axis_size("mp"), lax.axis_size("graph")
    step = stride(grid_send.shape[1])
    sent = [shape(graph * step, features, BF16)] * mp
    planes = lax.axis_size("groups") * graph
    hidden = shards[1].shape[0]
    if planes != 8 or mp != 4 or hidden != 128 or features != FEATURES:
        outgoing = call(send_kernel, sent, Far(grid_lat), Far(grid_send.T))
        rows = []
        for i in range(4):
            rows.append(lax.all_gather(shards[2 * i], "mp", axis=1, tiled=True).T)
            rows.append(lax.all_gather(shards[2 * i + 1], "mp", axis=0, tiled=True))
        enc, proc = jnp.concatenate(rows[:4], axis=1), jnp.concatenate(rows[4:], axis=1)
        arrived = exchange(outgoing, step)
        return [enc], lambda one, moved, came: [proc], arrived, tables
    far = [Far(s) for s in shards]
    piece = hidden // planes
    width = 6 * features
    kept, *messages = call(
        prepare_kernel,
        sent[:1] + [shape(piece, width + features, BF16)] * 3,
        Far(grid_lat),
        Far(grid_send.T),
        far[:4],
    )
    enc_own, proc_own, proc_piece = call(
        own_kernel, [shape(hidden, width, BF16)] * 2 + [shape(piece, width, BF16)], far
    )
    messages = [along(m, i + 1, True) for i, m in enumerate(messages)]
    kept, enc_own, *tables = lax.optimization_barrier((kept, enc_own, *tables))
    rows = mp * step
    near, first, both = call(
        join_kernel,
        [shape(rows, features, BF16), shape(3 * piece, width, BF16), shape(3 * rows, width + features, BF16)],
        kept,
        messages,
    )
    x, y, corner = across(both, 2), across(first, 4), across(first, 6)
    proc_piece, _ = lax.optimization_barrier((proc_piece, near))
    beside_me = lax.ppermute(proc_piece, "mp", [(m, m ^ 1) for m in range(mp)])
    pair = jnp.concatenate([proc_piece, beside_me])
    pairs = lax.ppermute(pair, "mp", [(m, m ^ 2) for m in range(mp)])
    proc_first = jnp.concatenate([beside_me, pairs])
    both, x, y, corner, _ = lax.optimization_barrier((both, x, y, corner, pairs))
    core, x_core, others = across(both, 1), across(x, 1), across(jnp.concatenate([y, corner]), 1)
    enc = [enc_own, first, core, x, y, corner, x_core, others]
    arrived = [near, core, x, x_core]
    proc_first, *_ = lax.optimization_barrier((proc_first, x, y, corner))
    proc_x, proc_y = across(proc_first, 2), across(proc_first, 4)

    def finish(one, moved, came):
        late, _ = lax.optimization_barrier((proc_x, one))
        corner = across(late, 4)
        x, y, *_ = lax.optimization_barrier((proc_x, proc_y, *moved))
        sides = across(jnp.concatenate([x, y]), 1)
        corner, *_ = lax.optimization_barrier((corner, *came))
        return [proc_own, proc_first, across(proc_first, 1), x, y, sides, corner, across(corner, 1)]

    return enc, finish, arrived, tables


def forward(inputs, first, second):
    before = dot_trans(inputs, first)
    logistic = 0.5 + 0.5 * jnp.tanh(0.5 * before)
    wide = before * logistic
    hidden = wide.astype(BF16)
    slope = logistic + wide * (1.0 - logistic)
    summed = dot(hidden, second)
    centered = summed - jnp.mean(summed, axis=-1, keepdims=True)
    rescale = lax.rsqrt(jnp.mean(centered * centered, axis=-1, keepdims=True) + 1e-05)
    normed = centered * rescale
    return normed, slope.astype(BF16), normed.astype(BF16), rescale


def backward_hidden(incoming, slope, normed, rescale, second):
    normed = normed.astype(F32)
    g_out = (
        incoming
        - jnp.mean(incoming, axis=-1, keepdims=True)
        - normed * jnp.mean(incoming * normed, axis=-1, keepdims=True)
    ) * rescale
    return (dot_trans(g_out.astype(BF16), second) * slope.astype(F32)).astype(BF16)


def table(index_row, count):
    n = index_row.shape[1]
    return jnp.where(lax.broadcasted_iota(jnp.int32, (count, n), 0) == index_row, 1.0, 0.0)


def stride(capacity):
    return max(capacity, 16 // min(lax.axis_size("mp"), lax.axis_size("graph")))


def sent_at(peer, slot, step, paired=False):
    mp, graph = lax.axis_size("mp"), lax.axis_size("graph")
    me, other = lax.axis_index("mp"), peer % mp
    shift = other ^ me if paired else (other + mp - me) % mp
    return (shift * graph + (peer // mp ^ lax.axis_index("graph"))) * step + slot


def arrived_at(peer, slot, step, paired=False):
    mp = lax.axis_size("mp")
    me, other = lax.axis_index("mp"), peer % mp
    shift = other ^ me if paired else (me + mp - other) % mp
    return ((peer // mp ^ lax.axis_index("graph")) * mp + shift) * step + slot


def sent_row(index, step, paired=False, order=sent_at):
    width, count = index.shape
    index = index.astype(F32).T
    at = lax.broadcasted_iota(jnp.int32, (count, count * step), 1)
    peer = lax.broadcasted_iota(jnp.int32, (count, count * step), 0)
    row = jnp.zeros(at.shape, F32)
    for slot in range(width):
        hit = order(peer, slot, step, paired) == at
        row = jnp.where(hit, index[:, slot : slot + 1] + 1.0, row)
    return jnp.sum(row, axis=0, keepdims=True).astype(jnp.int32) - 1


def stacked(blocks):
    return jnp.concatenate([block()[...] for block in blocks], axis=0)


def split(rows, outs):
    size = rows.shape[0] // len(outs)
    for i, out in enumerate(outs):
        out.ref[...] = rows[i * size : (i + 1) * size, :].astype(BF16)


def send_rows(grid, send):
    index = send()[...]
    one = table(sent_row(index, stride(index.shape[0]), True), grid().shape[0])
    return dot(one.T.astype(BF16), grid()[...])


def send_kernel(grid, send, *outgoing):
    split(send_rows(grid, send), outgoing)


def turn_table(sources, targets, step, j):
    row = lax.broadcasted_iota(jnp.int32, (sources * step, sources * targets * step), 0)
    at = lax.broadcasted_iota(jnp.int32, row.shape, 1)
    source = (row // step * targets + j) * step + row % step
    return jnp.where(at == source, 1.0, 0.0).astype(BF16)


def turn_kernel(blocks, *outs):
    rows = stacked(blocks)
    step = rows.shape[0] // (len(blocks) * len(outs))
    for j, out in enumerate(outs):
        out.ref[...] = dot(turn_table(len(blocks), len(outs), step, j), rows).astype(BF16)


def tables_kernel(mesh, slot, recv_e, halo, sender, recv_p, send, *outs):
    mesh_rows = mesh().shape[0]
    peers = halo().shape[1]
    slot_step, halo_step = outs[0].ref.shape[0] // peers, outs[4].ref.shape[1] // peers
    capacity, halo_capacity = slot_step, halo().shape[0]
    slots = slot()[...]
    coming = arrived_at(slots // capacity, slots % capacity, slot_step, True)
    slots = sent_at(slots // capacity, slots % capacity, slot_step)
    senders = sender()[...]
    remote = jnp.maximum(senders - mesh_rows, 0)
    own, peer, place = senders < mesh_rows, remote // halo_capacity, remote % halo_capacity
    back = jnp.where(own, senders, mesh_rows + sent_at(peer, place, halo_step))
    senders = jnp.where(own, senders, mesh_rows + arrived_at(peer, place, halo_step))
    halo_back = sent_row(halo()[...], halo_step, order=arrived_at)
    halo_rows = sent_row(halo()[...], halo_step)
    rows = (slots, recv_e()[...], halo_back, back, recv_p()[...])
    gathered = (coming, rows[1], halo_rows, senders, rows[4])
    for i, row in enumerate(rows):
        scatter, gather = outs[2 * i : 2 * i + 2]
        count = scatter.ref.shape[0]
        one = table(row, count)
        scatter.ref[...] = one.astype(BF16)
        other = one if gathered[i] is row else table(gathered[i], count)
        gather.ref[...] = other.T.astype(BF16)
    outs[10].ref[...] = dot(outs[3].ref[...], mesh()[...]).astype(BF16)
    returned = sent_row(send()[...], slot_step, order=arrived_at)
    outs[11].ref[...] = table(returned, outs[11].ref.shape[0]).astype(BF16)


def arrived_rows(blocks):
    size = blocks[0]().shape[0]
    rows = [blocks[0]()[...]]
    for t, block in enumerate(blocks[1:]):
        if block().shape[1] == FEATURES:
            rows.append(block()[...])
        else:
            rows.append(block()[t * size : (t + 1) * size, 6 * FEATURES :])
    return jnp.concatenate(rows, axis=0)


def encode_kernel(
    recv_rows, arrived, slot_g, enc_t, mesh, weights, halo_g,
    one_out, slope_e, normed_e, scale_e, slope_n, normed_n, scale_n, *halo_out,
):
    rows_in = arrived_rows(arrived)
    edges = slot_g().shape[0]
    first, second = layers(weights, 0)
    for low in range(0, edges, ROWS):
        rows = pl.ds(low, ROWS)
        sent = dot(slot_g()[rows, :], rows_in).astype(BF16)
        inputs = jnp.concatenate([sent, recv_rows()[rows, :]], axis=1)
        _, slope, normed, rescale = forward(inputs, first, second)
        slope_e.ref[rows, :] = slope
        normed_e.ref[rows, :] = normed
        scale_e.ref[rows, :] = jnp.broadcast_to(rescale, (ROWS, LANES))
    aggregate = dot(enc_t()[...], normed_e.ref[...]).astype(BF16)
    first, second = layers(weights, 1)
    own = mesh()[...]
    normed, slope, rounded, rescale = forward(
        jnp.concatenate([own, aggregate], axis=1), first, second
    )
    one = (own.astype(F32) + normed).astype(BF16)
    one_out.ref[...] = one
    split(dot(halo_g()[...], one), halo_out)
    slope_n.ref[...] = slope
    normed_n.ref[...] = rounded
    scale_n.ref[...] = jnp.broadcast_to(rescale, scale_n.ref.shape)


def process_kernel(
    cotangent_in, one_in, halo, sender_g, proc_g, weights, proc_t, sender_t, two, part, ga, *refs
):
    grad_halo, (slope_p, normed_p, scale_p) = refs[:-3], refs[-3:]
    ga_p = ga.ref
    features = FEATURES
    one = one_in()[...]
    mesh_rows = one.shape[0]
    lookup = jnp.concatenate([one, stacked(halo)], axis=0)
    edges = sender_g().shape[0]
    first, second = layers(weights, 0)
    for low in range(0, edges, ROWS):
        rows = pl.ds(low, ROWS)
        sent = dot(sender_g()[rows, :], lookup).astype(BF16)
        got = dot(proc_g()[rows, :], one).astype(BF16)
        _, slope, normed, rescale = forward(jnp.concatenate([sent, got], axis=1), first, second)
        slope_p[rows, :] = slope
        normed_p[rows, :] = normed
        scale_p[rows, :] = jnp.broadcast_to(rescale, (ROWS, LANES))
    aggregate = dot(proc_t()[...], normed_p[...]).astype(BF16)
    first_n, second_n = layers(weights, 1)
    normed, slope, rounded, rescale = forward(
        jnp.concatenate([one, aggregate], axis=1), first_n, second_n
    )
    two.send((one.astype(F32) + normed).astype(BF16))
    cotangent = cotangent_in()[...].astype(F32)
    g_q = dot(backward_hidden(cotangent, slope, rounded, rescale, second_n), first_n)
    g_msg = g_q[:, features:].astype(BF16)
    for low in range(0, edges, ROWS):
        rows = pl.ds(low, ROWS)
        incoming = dot(proc_g()[rows, :], g_msg)
        ga_p[rows, :] = backward_hidden(
            incoming, slope_p[rows, :], normed_p[rows, :], scale_p[rows, 0:1], second
        )
    by_send = dot(sender_t()[...], ga_p[...]).astype(BF16)
    g_send = dot(by_send, first[:, :features])
    split(g_send[mesh_rows:, :], grad_halo)
    part.ref[...] = cotangent + g_q[:, :features] + g_send[:mesh_rows, :]


def receive_kernel(part, ga, scatter, weights, out):
    by_recv = dot(scatter()[...], ga()[...]).astype(BF16)
    first, _ = layers(weights, 0)
    out.send(part()[...] + dot(by_recv, first[:, FEATURES:]))


def decode_kernel(
    back, halo_t, grad_in, slope_n, normed_n, scale_n, enc_g, slope_e, normed_e, scale_e,
    weights, slot_t, part, ga, *grad_slots
):
    ga_e = ga.ref
    features = FEATURES
    edges = enc_g().shape[0]
    grad_one = grad_in()[...] + dot(halo_t()[...], stacked(back))
    first_n, second_n = layers(weights, 1)
    ga_n = backward_hidden(grad_one, slope_n()[...], normed_n()[...], scale_n()[:, 0:1], second_n)
    g_n = dot(ga_n, first_n)
    part.ref[...] = grad_one + g_n[:, :features]
    g_edge = g_n[:, features:].astype(BF16)
    first, second = layers(weights, 0)
    for low in range(0, edges, ROWS):
        rows = pl.ds(low, ROWS)
        incoming = dot(enc_g()[rows, :], g_edge)
        ga_e[rows, :] = backward_hidden(
            incoming, slope_e()[rows, :], normed_e()[rows, :], scale_e()[rows, 0:1], second
        )
    by_slot = dot(slot_t()[...], ga_e[...]).astype(BF16)
    split(dot(by_slot, first[:, :features]), grad_slots)


def grid_kernel(back, table_in, out):
    rows = stacked(back)
    size = out.ref.shape[0] // 4
    for low in range(0, 4 * size, size):
        out.send_part(low, dot(table_in()[pl.ds(low, size), :], rows))


def along(block, shift, paired=False):
    size = lax.axis_size("mp")
    if shift % size == 0:
        return block
    to = [m ^ shift if paired else (m + shift) % size for m in range(size)]
    return lax.ppermute(block, "mp", list(enumerate(to)))


def beside(block, flip):
    if flip == 0:
        return block
    return lax.ppermute(block, "graph", [(g, g ^ flip) for g in range(lax.axis_size("graph"))])


def turn(blocks, count, step):
    out = shape(len(blocks) * step, blocks[0].shape[1], BF16)
    return call(turn_kernel, [out] * count, list(blocks))


def exchange(blocks, step):
    return second_level(first_level(blocks, step, True))


def first_level(blocks, step, paired=False):
    return turn([along(b, s, paired) for s, b in enumerate(blocks)], lax.axis_size("graph"), step)


def second_level(blocks):
    return [beside(b, t) for t, b in enumerate(blocks)]


def exchange_back(blocks, step):
    moved = first_level(blocks, step)
    return second_level(moved), moved[0]


def local(
    grid_lat,
    mesh_lat,
    cotangent,
    grid_send,
    g2m_slot,
    g2m_receiver,
    halo_send,
    mesh_sender,
    mesh_receiver,
    *shards,
):
    grid_rows, features = grid_lat.shape
    mesh_rows = mesh_lat.shape[0]
    edges = g2m_slot.shape[0]
    mesh_edges = mesh_sender.shape[0]
    mp, graph = lax.axis_size("mp"), lax.axis_size("graph")
    step, halo_step = stride(grid_send.shape[1]), stride(halo_send.shape[1])
    slots, halos = mp * graph * step, mp * graph * halo_step
    tables = call(
        tables_kernel,
        [
            shape(slots, edges, BF16),
            shape(edges, slots, BF16),
            shape(mesh_rows, edges, BF16),
            shape(edges, mesh_rows, BF16),
            shape(mesh_rows, halos, BF16),
            shape(halos, mesh_rows, BF16),
            shape(mesh_rows + halos, mesh_edges, BF16),
            shape(mesh_edges, mesh_rows + halos, BF16),
            shape(mesh_rows, mesh_edges, BF16),
            shape(mesh_edges, mesh_rows, BF16),
            shape(edges, features, BF16),
            shape(grid_rows, slots, BF16),
        ],
        Far(mesh_lat),
        Far(g2m_slot.reshape(1, edges)),
        Far(g2m_receiver.reshape(1, edges)),
        Far(halo_send.T),
        Far(mesh_sender.reshape(1, mesh_edges)),
        Far(mesh_receiver.reshape(1, mesh_edges)),
        Far(grid_send.T),
    )
    enc, finish, arrived, tables = start(grid_lat, grid_send, shards, tables)
    slot_t, slot_g, enc_t, enc_g, halo_t, halo_g, sender_t, sender_g, proc_t, proc_g = tables[:10]
    recv_rows, grid_t = tables[10:]
    saved = [
        shape(edges, features, BF16),
        shape(edges, features, BF16),
        shape(edges, LANES, F32),
        shape(mesh_rows, features, BF16),
        shape(mesh_rows, features, BF16),
        shape(mesh_rows, LANES, F32),
    ]
    mesh_one, slope_e, normed_e, scale_e, slope_n, normed_n, scale_n, *halo_out = call(
        encode_kernel,
        [shape(mesh_rows, features, BF16)] + saved + [shape(graph * halo_step, features, BF16)] * mp,
        recv_rows,
        arrived,
        slot_g,
        enc_t,
        Far(mesh_lat),
        enc,
        halo_g,
        flops=3 * 10**9,
    )
    moved = first_level(halo_out, halo_step)
    halo_in = second_level(moved)
    proc = finish(mesh_one, moved, halo_in[1:])
    mesh_two, part, ga, *grad_halo = call(
        process_kernel,
        [
            shape(mesh_rows, features, BF16),
            shape(mesh_rows, features, F32),
            shape(mesh_edges, features, BF16),
        ]
        + [shape(graph * halo_step, features, BF16)] * mp,
        Far(cotangent),
        mesh_one,
        halo_in,
        sender_g,
        proc_g,
        proc,
        proc_t,
        sender_t,
        last=(0,),
        flops=5 * 10**9,
        scratch=[
            pltpu.VMEM((mesh_edges, features), BF16),
            pltpu.VMEM((mesh_edges, features), BF16),
            pltpu.VMEM((mesh_edges, LANES), F32),
        ],
    )
    halo_back, half_way = exchange_back(grad_halo, halo_step)
    part, _ = lax.optimization_barrier((part, half_way))
    (grad_one,) = call(
        receive_kernel, [shape(mesh_rows, features, F32)], part, ga, proc_t, proc, flops=3 * 10**8
    )
    part, ga, *grad_slots = call(
        decode_kernel,
        [shape(mesh_rows, features, F32), shape(edges, features, BF16)]
        + [shape(graph * step, features, BF16)] * mp,
        halo_back,
        halo_t,
        grad_one,
        slope_n,
        normed_n,
        scale_n,
        enc_g,
        slope_e,
        normed_e,
        scale_e,
        enc,
        slot_t,
        flops=3 * 10**9,
    )
    returned, half_way = exchange_back(grad_slots, step)
    part, _ = lax.optimization_barrier((part, half_way))
    (mesh_grad,) = call(
        receive_kernel, [shape(mesh_rows, features, F32)], part, ga, enc_t, enc, last=(0,), flops=3 * 10**8
    )
    (grid_grad,) = call(
        grid_kernel, [shape(grid_rows, features, F32)], returned, grid_t, last=(0,)
    )
    return (mesh_two, grid_grad, mesh_grad)


def solution(mesh):
    rows = P(AXES, None)
    flat = P(AXES)
    in_specs = (rows,) * 4 + (flat,) * 2 + (rows,) + (flat,) * 2 + (P(None, "mp"), P("mp", None)) * 4
    return jax.shard_map(
        local, mesh=mesh, in_specs=in_specs, out_specs=(rows,) * 3, check_vma=False
    )
```

```python
import jax
import jax.numpy as jnp
from jax import lax
from jax.experimental import pallas as pl
from jax.experimental.pallas import tpu as pltpu
from jax.sharding import PartitionSpec as P

F32 = jnp.float32
BF16 = jnp.bfloat16
LANES = 128
ROWS = 512
FEATURES = 512
AXES = ("groups", "graph", "mp")


def dot(left, right):
    return jnp.dot(left, right, preferred_element_type=F32)


def dot_trans(left, right):
    return lax.dot_general(left, right, (((1,), (1,)), ((), ())), preferred_element_type=F32)


def shape(rows, columns, dtype):
    return jax.ShapeDtypeStruct((rows, columns), dtype)


class Far:
    def __init__(self, array):
        self.array = pltpu.with_memory_space_constraint(array, pltpu.HBM)


class Input:
    def __init__(self, copy, ref):
        self.copy, self.ref = copy, ref

    def __call__(self):
        if self.copy is not None:
            self.copy.wait()
            self.copy = None
        return self.ref


class Output:
    def __init__(self, ref, copy, part=None):
        self.ref, self.copy, self.part = ref, copy, part

    def send_part(self, low, value):
        rows = value.shape[0]
        self.ref[pl.ds(low, rows), :] = value
        self.part(low, rows).start()

    def send(self, value=None):
        if value is not None:
            self.ref[...] = value
        if self.copy is not None:
            self.copy.start()


def call(kernel, out_shape, *args, last=(), scratch=(), flops=0):
    groups = [a if isinstance(a, list) else [a] for a in args]
    flat = [a for group in groups for a in group]
    far = [isinstance(a, Far) for a in flat]
    arrays = [a.array if isinstance(a, Far) else a for a in flat]
    count, outs = len(arrays), len(out_shape)

    def body(*refs):
        ins, refs = refs[:count], refs[count:]
        out_refs, refs = refs[:outs], refs[outs:]
        places, refs = list(refs[: sum(far)]), refs[sum(far) :]
        results, refs = list(refs[: len(last)]), refs[len(last) :]
        sem_in, sem_out, refs = refs[0], refs[1], refs[2:]
        inputs = []
        for ref, away in zip(ins, far):
            copy = None
            if away:
                place = places.pop(0)
                copy = pltpu.make_async_copy(ref, place, sem_in.at[len(places)])
                copy.start()
                ref = place
            inputs.append(Input(copy, ref))
        outputs = []
        for i, ref in enumerate(out_refs):
            copy = part = None
            if i in last:
                place = results.pop(0)
                sem = sem_out.at[len(results)]
                copy = pltpu.make_async_copy(place, ref, sem)

                def part(low, rows, place=place, ref=ref, sem=sem):
                    at = pl.ds(low, rows)
                    return pltpu.make_async_copy(place.at[at, :], ref.at[at, :], sem)

                ref = place
            outputs.append(Output(ref, copy, part))
        given = []
        for arg, group in zip(args, groups):
            part, inputs = inputs[: len(group)], inputs[len(group) :]
            given.append(part if isinstance(arg, list) else part[0])
        kernel(*given, *outputs, *refs)
        for output in outputs:
            if output.copy is not None:
                output.copy.wait()

    vmem, hbm = pl.BlockSpec(memory_space=pltpu.VMEM), pl.BlockSpec(memory_space=pl.ANY)
    total = sum(a.size * a.dtype.itemsize for a in arrays)
    return pl.pallas_call(
        body,
        out_shape=out_shape,
        in_specs=[hbm if away else vmem for away in far],
        out_specs=[hbm if i in last else vmem for i in range(outs)],
        scratch_shapes=[pltpu.VMEM(a.shape, a.dtype) for a, away in zip(arrays, far) if away]
        + [pltpu.VMEM(out_shape[i].shape, out_shape[i].dtype) for i in last]
        + [pltpu.SemaphoreType.DMA((max(sum(far), 1),)), pltpu.SemaphoreType.DMA((max(len(last), 1),))]
        + list(scratch),
        name=kernel.__name__,
        cost_estimate=pl.CostEstimate(flops=flops, bytes_accessed=total, transcendentals=0),
        compiler_params=pltpu.CompilerParams(vmem_limit_bytes=24 * 1024 * 1024),
    )(*arrays)


def layers(blocks, which):
    low = which * 3 * FEATURES
    middle = low + 2 * FEATURES
    return (
        jnp.concatenate([block()[:, low:middle] for block in blocks], axis=0),
        jnp.concatenate([block()[:, middle : middle + FEATURES] for block in blocks], axis=0),
    )


def turned(first, select):
    return dot_trans(select, first).astype(BF16)


def prepare_kernel(grid, send, shards, kept, *messages):
    width = 3 * FEATURES
    outgoing = send_rows(grid, send)
    size = kept.ref.shape[0]
    kept.ref[...] = outgoing[:size, :].astype(BF16)
    for i, out in enumerate(messages):
        out.ref[:, 2 * width :] = outgoing[(i + 1) * size : (i + 2) * size, :].astype(BF16)
    for i in range(2):
        first, second = piece_of(shards[2 * i], shards[2 * i + 1], messages[0].ref.shape[0])
        low = i * width
        for out in messages:
            out.ref[:, low : low + 2 * FEATURES] = first
            out.ref[:, low + 2 * FEATURES : low + width] = second


def piece_of(one, two, rows):
    plane = lax.axis_index("groups") * lax.axis_size("graph") + lax.axis_index("graph")
    base = plane * rows
    hidden = two().shape[0]
    select = jnp.where(
        lax.broadcasted_iota(jnp.int32, (rows, hidden), 0) + base
        == lax.broadcasted_iota(jnp.int32, (rows, hidden), 1),
        1.0,
        0.0,
    ).astype(BF16)
    return turned(one()[...], select), two()[pl.ds(pl.multiple_of(base, rows), rows), :]


def join_kernel(kept, messages, near, block, both):
    width = 6 * FEATURES
    weights = jnp.concatenate([m()[:, :width] for m in messages], axis=0)
    rows = jnp.concatenate([kept()[...]] + [m()[:, width:] for m in messages], axis=0)
    step = rows.shape[0] // 16
    block.ref[...] = weights
    both.ref[:, :width] = weights
    size = near.ref.shape[0]
    for j in range(4):
        moved = dot(turn_table(4, 4, step, j), rows).astype(BF16)
        if j == 0:
            near.ref[...] = moved
        else:
            both.ref[(j - 1) * size : j * size, width:] = moved


def own_kernel(shards, enc_own, proc_own, proc_piece):
    width = 3 * FEATURES
    for i in range(4):
        one, two = shards[2 * i](), shards[2 * i + 1]()
        hidden = one.shape[1]
        select = jnp.where(
            lax.broadcasted_iota(jnp.int32, (hidden, hidden), 0)
            == lax.broadcasted_iota(jnp.int32, (hidden, hidden), 1),
            1.0,
            0.0,
        ).astype(BF16)
        out, low = (enc_own, proc_own)[i // 2], i % 2 * width
        out.ref[:, low : low + 2 * FEATURES] = turned(one[...], select)
        out.ref[:, low + 2 * FEATURES : low + width] = two[...]
    for i in (2, 3):
        first, second = piece_of(shards[2 * i], shards[2 * i + 1], proc_piece.ref.shape[0])
        low = i % 2 * width
        proc_piece.ref[:, low : low + 2 * FEATURES] = first
        proc_piece.ref[:, low + 2 * FEATURES : low + width] = second


def across(x, flip):
    planes = lax.axis_size("groups") * lax.axis_size("graph")
    return lax.ppermute(x, ("groups", "graph"), [(p, p ^ flip) for p in range(planes)])


def start(grid_lat, grid_send, shards, tables):
    grid_rows, features = grid_lat.shape
    mp, graph = lax.axis_size("mp"), lax.axis_size("graph")
    step = stride(grid_send.shape[1])
    sent = [shape(graph * step, features, BF16)] * mp
    planes = lax.axis_size("groups") * graph
    hidden = shards[1].shape[0]
    if planes != 8 or mp != 4 or hidden != 128 or features != FEATURES:
        outgoing = call(send_kernel, sent, Far(grid_lat), Far(grid_send.T))
        rows = []
        for i in range(4):
            rows.append(lax.all_gather(shards[2 * i], "mp", axis=1, tiled=True).T)
            rows.append(lax.all_gather(shards[2 * i + 1], "mp", axis=0, tiled=True))
        enc, proc = jnp.concatenate(rows[:4], axis=1), jnp.concatenate(rows[4:], axis=1)
        arrived = exchange(outgoing, step)
        return [enc], lambda one, moved, came: [proc], arrived, tables
    far = [Far(s) for s in shards]
    piece = hidden // planes
    width = 6 * features
    kept, *messages = call(
        prepare_kernel,
        sent[:1] + [shape(piece, width + features, BF16)] * 3,
        Far(grid_lat),
        Far(grid_send.T),
        far[:4],
    )
    enc_own, proc_own, proc_piece = call(
        own_kernel, [shape(hidden, width, BF16)] * 2 + [shape(piece, width, BF16)], far
    )
    messages = [along(m, i + 1, True) for i, m in enumerate(messages)]
    kept, enc_own, *tables = lax.optimization_barrier((kept, enc_own, *tables))
    rows = mp * step
    near, first, both = call(
        join_kernel,
        [shape(rows, features, BF16), shape(3 * piece, width, BF16), shape(3 * rows, width + features, BF16)],
        kept,
        messages,
    )
    x, y, corner = across(both, 2), across(first, 4), across(first, 6)
    proc_piece, _ = lax.optimization_barrier((proc_piece, near))
    beside_me = lax.ppermute(proc_piece, "mp", [(m, m ^ 1) for m in range(mp)])
    pair = jnp.concatenate([proc_piece, beside_me])
    pairs = lax.ppermute(pair, "mp", [(m, m ^ 2) for m in range(mp)])
    proc_first = jnp.concatenate([beside_me, pairs])
    both, x, y, corner, _ = lax.optimization_barrier((both, x, y, corner, pairs))
    core, x_core, others = across(both, 1), across(x, 1), across(jnp.concatenate([y, corner]), 1)
    enc = [enc_own, first, core, x, y, corner, x_core, others]
    arrived = [near, core, x, x_core]
    proc_first, *_ = lax.optimization_barrier((proc_first, x, y, corner))
    proc_x, proc_y = across(proc_first, 2), across(proc_first, 4)

    def finish(one, moved, came):
        late, _ = lax.optimization_barrier((proc_x, one))
        corner = across(late, 4)
        x, y, *_ = lax.optimization_barrier((proc_x, proc_y, *moved))
        sides = across(jnp.concatenate([x, y]), 1)
        corner, *_ = lax.optimization_barrier((corner, *came))
        return [proc_own, proc_first, across(proc_first, 1), x, y, sides, corner, across(corner, 1)]

    return enc, finish, arrived, tables


def forward(inputs, first, second):
    before = dot_trans(inputs, first)
    logistic = 0.5 + 0.5 * jnp.tanh(0.5 * before)
    wide = before * logistic
    hidden = wide.astype(BF16)
    slope = logistic + wide * (1.0 - logistic)
    summed = dot(hidden, second)
    centered = summed - jnp.mean(summed, axis=-1, keepdims=True)
    rescale = lax.rsqrt(jnp.mean(centered * centered, axis=-1, keepdims=True) + 1e-05)
    normed = centered * rescale
    return normed, slope.astype(BF16), normed.astype(BF16), rescale


def backward_hidden(incoming, slope, normed, rescale, second):
    normed = normed.astype(F32)
    g_out = (
        incoming
        - jnp.mean(incoming, axis=-1, keepdims=True)
        - normed * jnp.mean(incoming * normed, axis=-1, keepdims=True)
    ) * rescale
    return (dot_trans(g_out.astype(BF16), second) * slope.astype(F32)).astype(BF16)


def table(index_row, count):
    n = index_row.shape[1]
    return jnp.where(lax.broadcasted_iota(jnp.int32, (count, n), 0) == index_row, 1.0, 0.0)


def stride(capacity):
    return max(capacity, 16 // min(lax.axis_size("mp"), lax.axis_size("graph")))


def sent_at(peer, slot, step, paired=False):
    mp, graph = lax.axis_size("mp"), lax.axis_size("graph")
    me, other = lax.axis_index("mp"), peer % mp
    shift = other ^ me if paired else (other + mp - me) % mp
    return (shift * graph + (peer // mp ^ lax.axis_index("graph"))) * step + slot


def arrived_at(peer, slot, step, paired=False):
    mp = lax.axis_size("mp")
    me, other = lax.axis_index("mp"), peer % mp
    shift = other ^ me if paired else (me + mp - other) % mp
    return ((peer // mp ^ lax.axis_index("graph")) * mp + shift) * step + slot


def sent_row(index, step, paired=False, order=sent_at):
    width, count = index.shape
    index = index.astype(F32).T
    at = lax.broadcasted_iota(jnp.int32, (count, count * step), 1)
    peer = lax.broadcasted_iota(jnp.int32, (count, count * step), 0)
    row = jnp.zeros(at.shape, F32)
    for slot in range(width):
        hit = order(peer, slot, step, paired) == at
        row = jnp.where(hit, index[:, slot : slot + 1] + 1.0, row)
    return jnp.sum(row, axis=0, keepdims=True).astype(jnp.int32) - 1


def stacked(blocks):
    return jnp.concatenate([block()[...] for block in blocks], axis=0)


def split(rows, outs):
    size = rows.shape[0] // len(outs)
    for i, out in enumerate(outs):
        out.ref[...] = rows[i * size : (i + 1) * size, :].astype(BF16)


def send_rows(grid, send):
    index = send()[...]
    one = table(sent_row(index, stride(index.shape[0]), True), grid().shape[0])
    return dot(one.T.astype(BF16), grid()[...])


def send_kernel(grid, send, *outgoing):
    split(send_rows(grid, send), outgoing)


def turn_table(sources, targets, step, j):
    row = lax.broadcasted_iota(jnp.int32, (sources * step, sources * targets * step), 0)
    at = lax.broadcasted_iota(jnp.int32, row.shape, 1)
    source = (row // step * targets + j) * step + row % step
    return jnp.where(at == source, 1.0, 0.0).astype(BF16)


def turn_kernel(blocks, *outs):
    rows = stacked(blocks[::-1])
    step = rows.shape[0] // (len(blocks) * len(outs))
    for j, out in enumerate(outs):
        out.ref[...] = dot(turn_table(len(blocks), len(outs), step, j), rows).astype(BF16)


def tables_kernel(mesh, slot, recv_e, halo, sender, recv_p, send, *outs):
    mesh_rows = mesh().shape[0]
    peers = halo().shape[1]
    slot_step, halo_step = outs[0].ref.shape[0] // peers, outs[4].ref.shape[1] // peers
    capacity, halo_capacity = slot_step, halo().shape[0]
    slots = slot()[...]
    coming = arrived_at(slots // capacity, slots % capacity, slot_step, True)
    slots = sent_at(slots // capacity, slots % capacity, slot_step)
    senders = sender()[...]
    remote = jnp.maximum(senders - mesh_rows, 0)
    own, peer, place = senders < mesh_rows, remote // halo_capacity, remote % halo_capacity
    back = jnp.where(own, senders, mesh_rows + sent_at(peer, place, halo_step))
    senders = jnp.where(own, senders, mesh_rows + arrived_at(peer, place, halo_step))
    halo_back = sent_row(halo()[...], halo_step, order=arrived_at)
    halo_rows = sent_row(halo()[...], halo_step)
    rows = (slots, recv_e()[...], halo_back, back, recv_p()[...])
    gathered = (coming, rows[1], halo_rows, senders, rows[4])
    for i, row in enumerate(rows):
        scatter, gather = outs[2 * i : 2 * i + 2]
        count = scatter.ref.shape[0]
        one = table(row, count)
        scatter.ref[...] = one.astype(BF16)
        other = one if gathered[i] is row else table(gathered[i], count)
        gather.ref[...] = other.T.astype(BF16)
    outs[10].ref[...] = dot(outs[3].ref[...], mesh()[...]).astype(BF16)
    returned = sent_row(send()[...], slot_step, order=arrived_at)
    outs[11].ref[...] = table(returned, outs[11].ref.shape[0]).astype(BF16)


def arrived_rows(blocks):
    size = blocks[0]().shape[0]
    rows = [blocks[0]()[...]]
    for t, block in enumerate(blocks[1:]):
        if block().shape[1] == FEATURES:
            rows.append(block()[...])
        else:
            rows.append(block()[t * size : (t + 1) * size, 6 * FEATURES :])
    return jnp.concatenate(rows, axis=0)


def encode_kernel(
    recv_rows, arrived, slot_g, enc_t, mesh, weights, halo_g,
    one_out, slope_e, normed_e, scale_e, slope_n, normed_n, scale_n, *halo_out,
):
    rows_in = arrived_rows(arrived)
    edges = slot_g().shape[0]
    first, second = layers(weights, 0)
    for low in range(0, edges, ROWS):
        rows = pl.ds(low, ROWS)
        sent = dot(slot_g()[rows, :], rows_in).astype(BF16)
        inputs = jnp.concatenate([sent, recv_rows()[rows, :]], axis=1)
        _, slope, normed, rescale = forward(inputs, first, second)
        slope_e.ref[rows, :] = slope
        normed_e.ref[rows, :] = normed
        scale_e.ref[rows, :] = jnp.broadcast_to(rescale, (ROWS, LANES))
    aggregate = dot(enc_t()[...], normed_e.ref[...]).astype(BF16)
    first, second = layers(weights, 1)
    own = mesh()[...]
    normed, slope, rounded, rescale = forward(
        jnp.concatenate([own, aggregate], axis=1), first, second
    )
    one = (own.astype(F32) + normed).astype(BF16)
    one_out.ref[...] = one
    split(dot(halo_g()[...], one), halo_out)
    slope_n.ref[...] = slope
    normed_n.ref[...] = rounded
    scale_n.ref[...] = jnp.broadcast_to(rescale, scale_n.ref.shape)


def process_kernel(
    cotangent_in, one_in, halo, sender_g, proc_g, weights, proc_t, sender_t, two, part, ga, *refs
):
    grad_halo, (slope_p, normed_p, scale_p) = refs[:-3], refs[-3:]
    ga_p = ga.ref
    features = FEATURES
    one = one_in()[...]
    mesh_rows = one.shape[0]
    lookup = jnp.concatenate([one, stacked(halo)], axis=0)
    edges = sender_g().shape[0]
    first, second = layers(weights, 0)
    for low in range(0, edges, ROWS):
        rows = pl.ds(low, ROWS)
        sent = dot(sender_g()[rows, :], lookup).astype(BF16)
        got = dot(proc_g()[rows, :], one).astype(BF16)
        _, slope, normed, rescale = forward(jnp.concatenate([sent, got], axis=1), first, second)
        slope_p[rows, :] = slope
        normed_p[rows, :] = normed
        scale_p[rows, :] = jnp.broadcast_to(rescale, (ROWS, LANES))
    aggregate = dot(proc_t()[...], normed_p[...]).astype(BF16)
    first_n, second_n = layers(weights, 1)
    normed, slope, rounded, rescale = forward(
        jnp.concatenate([one, aggregate], axis=1), first_n, second_n
    )
    two.send((one.astype(F32) + normed).astype(BF16))
    cotangent = cotangent_in()[...].astype(F32)
    g_q = dot(backward_hidden(cotangent, slope, rounded, rescale, second_n), first_n)
    g_msg = g_q[:, features:].astype(BF16)
    for low in range(0, edges, ROWS):
        rows = pl.ds(low, ROWS)
        incoming = dot(proc_g()[rows, :], g_msg)
        ga_p[rows, :] = backward_hidden(
            incoming, slope_p[rows, :], normed_p[rows, :], scale_p[rows, 0:1], second
        )
    by_send = dot(sender_t()[...], ga_p[...]).astype(BF16)
    g_send = dot(by_send, first[:, :features])
    split(g_send[mesh_rows:, :], grad_halo)
    part.ref[...] = cotangent + g_q[:, :features] + g_send[:mesh_rows, :]


def receive_kernel(part, ga, scatter, weights, out):
    by_recv = dot(scatter()[...], ga()[...]).astype(BF16)
    first, _ = layers(weights, 0)
    out.send(part()[...] + dot(by_recv, first[:, FEATURES:]))


def decode_kernel(
    back, halo_t, grad_in, slope_n, normed_n, scale_n, enc_g, slope_e, normed_e, scale_e,
    weights, slot_t, part, ga, *grad_slots
):
    ga_e = ga.ref
    features = FEATURES
    edges = enc_g().shape[0]
    grad_one = grad_in()[...] + dot(halo_t()[...], stacked(back))
    first_n, second_n = layers(weights, 1)
    ga_n = backward_hidden(grad_one, slope_n()[...], normed_n()[...], scale_n()[:, 0:1], second_n)
    g_n = dot(ga_n, first_n)
    part.ref[...] = grad_one + g_n[:, :features]
    g_edge = g_n[:, features:].astype(BF16)
    first, second = layers(weights, 0)
    for low in range(0, edges, ROWS):
        rows = pl.ds(low, ROWS)
        incoming = dot(enc_g()[rows, :], g_edge)
        ga_e[rows, :] = backward_hidden(
            incoming, slope_e()[rows, :], normed_e()[rows, :], scale_e()[rows, 0:1], second
        )
    by_slot = dot(slot_t()[...], ga_e[...]).astype(BF16)
    split(dot(by_slot, first[:, :features]), grad_slots)


def grid_kernel(back, table_in, out):
    rows = stacked(back)
    size = out.ref.shape[0] // 4
    for low in range(0, 4 * size, size):
        out.send_part(low, dot(table_in()[pl.ds(low, size), :], rows))


def along(block, shift, paired=False):
    size = lax.axis_size("mp")
    if shift % size == 0:
        return block
    to = [m ^ shift if paired else (m + shift) % size for m in range(size)]
    return lax.ppermute(block, "mp", list(enumerate(to)))


def beside(block, flip):
    if flip == 0:
        return block
    return lax.ppermute(block, "graph", [(g, g ^ flip) for g in range(lax.axis_size("graph"))])


def turn(blocks, count, step):
    out = shape(len(blocks) * step, blocks[0].shape[1], BF16)
    return call(turn_kernel, [out] * count, list(blocks)[::-1])


def exchange(blocks, step):
    return second_level(first_level(blocks, step, True))


def first_level(blocks, step, paired=False):
    return turn([along(b, s, paired) for s, b in enumerate(blocks)], lax.axis_size("graph"), step)


def second_level(blocks):
    return [beside(b, t) for t, b in enumerate(blocks)]


def exchange_back(blocks, step):
    moved = first_level(blocks, step)
    return second_level(moved), moved[0]


def local(
    grid_lat,
    mesh_lat,
    cotangent,
    grid_send,
    g2m_slot,
    g2m_receiver,
    halo_send,
    mesh_sender,
    mesh_receiver,
    *shards,
):
    grid_rows, features = grid_lat.shape
    mesh_rows = mesh_lat.shape[0]
    edges = g2m_slot.shape[0]
    mesh_edges = mesh_sender.shape[0]
    mp, graph = lax.axis_size("mp"), lax.axis_size("graph")
    step, halo_step = stride(grid_send.shape[1]), stride(halo_send.shape[1])
    slots, halos = mp * graph * step, mp * graph * halo_step
    tables = call(
        tables_kernel,
        [
            shape(slots, edges, BF16),
            shape(edges, slots, BF16),
            shape(mesh_rows, edges, BF16),
            shape(edges, mesh_rows, BF16),
            shape(mesh_rows, halos, BF16),
            shape(halos, mesh_rows, BF16),
            shape(mesh_rows + halos, mesh_edges, BF16),
            shape(mesh_edges, mesh_rows + halos, BF16),
            shape(mesh_rows, mesh_edges, BF16),
            shape(mesh_edges, mesh_rows, BF16),
            shape(edges, features, BF16),
            shape(grid_rows, slots, BF16),
        ],
        Far(mesh_lat),
        Far(g2m_slot.reshape(1, edges)),
        Far(g2m_receiver.reshape(1, edges)),
        Far(halo_send.T),
        Far(mesh_sender.reshape(1, mesh_edges)),
        Far(mesh_receiver.reshape(1, mesh_edges)),
        Far(grid_send.T),
    )
    enc, finish, arrived, tables = start(grid_lat, grid_send, shards, tables)
    slot_t, slot_g, enc_t, enc_g, halo_t, halo_g, sender_t, sender_g, proc_t, proc_g = tables[:10]
    recv_rows, grid_t = tables[10:]
    saved = [
        shape(edges, features, BF16),
        shape(edges, features, BF16),
        shape(edges, LANES, F32),
        shape(mesh_rows, features, BF16),
        shape(mesh_rows, features, BF16),
        shape(mesh_rows, LANES, F32),
    ]
    mesh_one, slope_e, normed_e, scale_e, slope_n, normed_n, scale_n, *halo_out = call(
        encode_kernel,
        [shape(mesh_rows, features, BF16)] + saved + [shape(graph * halo_step, features, BF16)] * mp,
        recv_rows,
        arrived,
        slot_g,
        enc_t,
        Far(mesh_lat),
        enc,
        halo_g,
        flops=3 * 10**9,
    )
    moved = first_level(halo_out, halo_step)
    halo_in = second_level(moved)
    proc = finish(mesh_one, moved, halo_in[1:])
    mesh_two, part, ga, *grad_halo = call(
        process_kernel,
        [
            shape(mesh_rows, features, BF16),
            shape(mesh_rows, features, F32),
            shape(mesh_edges, features, BF16),
        ]
        + [shape(graph * halo_step, features, BF16)] * mp,
        Far(cotangent),
        mesh_one,
        halo_in,
        sender_g,
        proc_g,
        proc,
        proc_t,
        sender_t,
        last=(0,),
        flops=5 * 10**9,
        scratch=[
            pltpu.VMEM((mesh_edges, features), BF16),
            pltpu.VMEM((mesh_edges, features), BF16),
            pltpu.VMEM((mesh_edges, LANES), F32),
        ],
    )
    halo_back, half_way = exchange_back(grad_halo, halo_step)
    part, _ = lax.optimization_barrier((part, half_way))
    (grad_one,) = call(
        receive_kernel, [shape(mesh_rows, features, F32)], part, ga, proc_t, proc, flops=3 * 10**8
    )
    part, ga, *grad_slots = call(
        decode_kernel,
        [shape(mesh_rows, features, F32), shape(edges, features, BF16)]
        + [shape(graph * step, features, BF16)] * mp,
        halo_back,
        halo_t,
        grad_one,
        slope_n,
        normed_n,
        scale_n,
        enc_g,
        slope_e,
        normed_e,
        scale_e,
        enc,
        slot_t,
        flops=3 * 10**9,
    )
    returned, half_way = exchange_back(grad_slots, step)
    part, _ = lax.optimization_barrier((part, half_way))
    (mesh_grad,) = call(
        receive_kernel, [shape(mesh_rows, features, F32)], part, ga, enc_t, enc, last=(0,), flops=3 * 10**8
    )
    (grid_grad,) = call(
        grid_kernel, [shape(grid_rows, features, F32)], returned, grid_t, last=(0,)
    )
    return (mesh_two, grid_grad, mesh_grad)


def solution(mesh):
    rows = P(AXES, None)
    flat = P(AXES)
    in_specs = (rows,) * 4 + (flat,) * 2 + (rows,) + (flat,) * 2 + (P(None, "mp"), P("mp", None)) * 4
    return jax.shard_map(
        local, mesh=mesh, in_specs=in_specs, out_specs=(rows,) * 3, check_vma=False
    )
```
